32 devices in a mesh: stream: 4 (over z), cy: 4 (over y, x), cz: 2 (over core).
Axes of the slice: x: 2, y: 2, z: 4, core: 2. Of those that a mesh axis runs over, the one named last changes fastest.
Arguments:
- populations: float32 [384, 19, 4096], P(('stream', 'cy', 'cz')), may hold values from 0.2 to 1
- solid_cells: int32 [384, 4096], P(('stream', 'cy', 'cz')), may hold values 0 or 1
- block_pos: int32 [384, 3], P(('stream', 'cy', 'cz')), may hold values from -1 to 7, as said below
Outputs:
- populations_out: float32 [19, 128, 64, 128], P(None, 'stream', 'cy', 'cz')
The draws below stay inside these ranges and needn't reach their ends.
Inputs may be any that keep to these rules, and one draw needn't show every extreme that they name: `block_pos`: row r belongs to device r // 12 in mesh order. A device's rows hold, in order, a run of its (cy, cz) group's block list followed by rows of -1. The list names once every block with by in the group's 1 block and bz in its 4 blocks, ordered by bx, blocks of one bx in any order. The device at index s of stream holds the entries from s * 8 + d_s up to (s + 1) * 8 + d_(s+1), where d is 0 at both ends of the axis and |d_s| <= 2; so its rows name at most 2 blocks with bx // 2 equal to each of s - 1 and s + 1, no other foreign ones, and at most 4 of its own blocks lie on other devices.
All inputs are finite; a program needn't handle non-finite values. No bound on the sum of `solid_cells` on one device may be relied on, other than what follows from the above.
Results may differ from the reference program's by a relative error of at most 0.0001.
Values sent between devices are 32-bit elements; how exact they have to be, the bound alone decides.
No kernel may reach another device: no remote copies, remote signals or barrier semaphores. Data moves between devices by JAX's collectives and lax.ppermute only.
A program may use at most 128 MiB of HBM per device.

```python
import jax
import jax.numpy as jnp

EDGE = 16
BXD = 2
BYD = 1
BZD = 4
STEPS = 2
MOVE_CAP = 2
SLOTS = 8
OLD_SLOTS = 12
ROWS = 384
NXC = 128
NYC = 64
NZC = 128
N_STREAM = 4
N_CY = 4
N_CZ = 2


def draw_block_pos(key, part):
    groups = N_CY * N_CZ
    per_layer = BYD * BZD
    layers = BXD * N_STREAM
    key_delta = jax.random.fold_in(key, 11)
    key_spot = jax.random.fold_in(key, 12)
    key_order = jax.random.fold_in(key, 13)
    offsets = jax.random.randint(key_delta, (groups, N_STREAM + 1), -MOVE_CAP, MOVE_CAP + 1)
    column = jnp.arange(N_STREAM + 1)[None, :]
    spot = jax.random.randint(key_spot, (groups, 1), 1, N_STREAM - 2)
    offsets = jnp.where(column == spot, MOVE_CAP, offsets)
    offsets = jnp.where(column == spot + 1, -MOVE_CAP, offsets)
    offsets = jnp.where(column == spot + 2, MOVE_CAP, offsets)
    offsets = jnp.where((column == 0) | (column == N_STREAM), 0, offsets)
    cuts = column * SLOTS + offsets
    starts = cuts[:, :-1]
    counts = cuts[:, 1:] - cuts[:, :-1]
    slot_index = jnp.arange(OLD_SLOTS)
    entry = starts[:, :, None] + slot_index[None, None, :]
    occupied = slot_index[None, None, :] < counts[:, :, None]
    entry = jnp.where(occupied, entry, 0)
    scores = jax.random.randint(key_order, (groups, layers, per_layer), 0, 1 << 20) * per_layer
    scores = scores + jnp.arange(per_layer)[None, None, :]
    ordering = jnp.argsort(scores, axis=-1)
    layer = entry // per_layer
    within = entry % per_layer
    group_index = jnp.arange(groups)[:, None, None]
    placed = ordering[group_index, layer, within]
    group_y = group_index // N_CZ
    group_z = group_index % N_CZ
    coord_x = layer
    coord_y = group_y * BYD + placed // BZD
    coord_z = group_z * BZD + placed % BZD
    coords = jnp.stack([coord_x, coord_y, coord_z], axis=-1)
    coords = jnp.where(occupied[..., None], coords, -1)
    coords = jnp.transpose(coords, (1, 0, 2, 3))
    return coords.reshape(N_STREAM * groups * OLD_SLOTS, 3).astype(jnp.int32)


def with_ends(array, stream_key, low, high):
    index_at = [jax.random.randint(jax.random.fold_in(stream_key, axis), (), 0, length) for axis, length in enumerate(array.shape)]
    widest = array.shape.index(max(array.shape))
    beside = index_at[:widest] + [(index_at[widest] + 1) % array.shape[widest]] + index_at[widest + 1:]
    return array.at[tuple(index_at)].set(low).at[tuple(beside)].set(high)


def shard_levels(own_key, shape, cuts, least, top_value):
    factor_of = 1.0
    for position, shards_of in cuts:
        draws = jax.random.uniform(jax.random.fold_in(jax.random.fold_in(own_key, 6), position), (shards_of,), jnp.float32, least / len(cuts), top_value / len(cuts))
        factor_of = factor_of * jnp.repeat(jnp.exp(draws), shape[position] // shards_of).reshape((-1,) + (1,) * (len(shape) - 1 - position))
    return factor_of


def setup_inputs(seed: int = 0) -> dict:
    key_list = jax.random.split(jax.random.key(seed), 4)
    return {
        "populations": jnp.clip(0.2 + 0.8 * jax.random.uniform(key_list[0], (ROWS, 19, EDGE**3), jnp.float32) ** shard_levels(key_list[0], (ROWS, 19, EDGE**3), ((0, 32),), -0.2, 0.2), 0.2, 1.0),
        "solid_cells": with_ends((jax.random.randint(key_list[1], (ROWS, EDGE**3), 0, 8) < 1).astype(jnp.int32), jax.random.fold_in(key_list[1], 1), 0, 1),
        "block_pos": draw_block_pos(jax.random.fold_in(key_list[3], 71), 0),
    }


VELOCITIES = ((0, 0, 0), (1, 0, 0), (-1, 0, 0), (0, 1, 0), (0, -1, 0), (0, 0, 1), (0, 0, -1),
              (1, 1, 0), (-1, -1, 0), (1, -1, 0), (-1, 1, 0), (1, 0, 1), (-1, 0, -1),
              (1, 0, -1), (-1, 0, 1), (0, 1, 1), (0, -1, -1), (0, 1, -1), (0, -1, 1))
WEIGHTS = (1.0 / 3.0,) + (1.0 / 18.0,) * 6 + (1.0 / 36.0,) * 12
OPPOSITE = (0, 2, 1, 4, 3, 6, 5, 8, 7, 10, 9, 12, 11, 14, 13, 16, 15, 18, 17)
OMEGA_EVEN = 1.25
OMEGA_ODD = 1.0 / 1.125


def moment(lattice, component):
    summed = jnp.zeros_like(lattice[0])
    for member in range(19):
        factor = VELOCITIES[member][component]
        if factor == 1:
            summed = summed + lattice[member]
        elif factor == -1:
            summed = summed - lattice[member]
    return summed


def collide(lattice):
    density = jnp.sum(lattice, axis=0)
    velocity = [moment(lattice, component) / density for component in range(3)]
    square = velocity[0] * velocity[0] + velocity[1] * velocity[1] + velocity[2] * velocity[2]
    outputs = []
    for member in range(19):
        step_x, step_y, step_z = VELOCITIES[member]
        projected = step_x * velocity[0] + step_y * velocity[1] + step_z * velocity[2]
        even_eq = WEIGHTS[member] * density * (1.0 + 4.5 * projected * projected - 1.5 * square)
        odd_eq = WEIGHTS[member] * density * 3.0 * projected
        mirror = lattice[OPPOSITE[member]]
        even_part = 0.5 * (lattice[member] + mirror)
        odd_part = 0.5 * (lattice[member] - mirror)
        outputs.append(lattice[member] - OMEGA_EVEN * (even_part - even_eq) - OMEGA_ODD * (odd_part - odd_eq))
    return jnp.stack(outputs), density


def propagate(lattice, widened, wall_ext, drift_y, drift_z, density, rotor_here):
    size_x, size_y, size_z = lattice.shape[1:]
    outputs = []
    for member in range(19):
        step_x, step_y, step_z = VELOCITIES[member]
        window = (slice(1 - step_x, 1 - step_x + size_x), slice(1 - step_y, 1 - step_y + size_y),
                  slice(1 - step_z, 1 - step_z + size_z))
        pulled = widened[member][window]
        blocked = wall_ext[window]
        wall_push = 6.0 * WEIGHTS[member] * density * (step_y * drift_y[window] + step_z * drift_z[window])
        bounced = widened[OPPOSITE[member]][1:1 + size_x, 1:1 + size_y, 1:1 + size_z] + wall_push
        read = jnp.where(blocked, bounced, pulled)
        outputs.append(jnp.where(rotor_here, lattice[member], read))
    return jnp.stack(outputs)


def reference(populations, solid_cells, block_pos):
    block_cells = EDGE ** 3
    count_x = BXD * N_STREAM
    count_y = BYD * N_CY
    count_z = BZD * N_CZ
    blocks_all = count_x * count_y * count_z
    occupied = block_pos[:, 0] >= 0
    ident = (block_pos[:, 0] * count_y + block_pos[:, 1]) * count_z + block_pos[:, 2]
    ident = jnp.where(occupied, ident, blocks_all).astype(jnp.int32)
    placed = jnp.zeros((blocks_all + 1, 19, block_cells), jnp.float32).at[ident].set(populations)[:blocks_all]
    lattice = placed.reshape(count_x, count_y, count_z, 19, EDGE, EDGE, EDGE)
    lattice = lattice.transpose(3, 0, 4, 1, 5, 2, 6).reshape(19, NXC, NYC, NZC)
    placed_marks = jnp.zeros((blocks_all + 1, block_cells), jnp.int32).at[ident].set(solid_cells)[:blocks_all]
    marks = placed_marks.reshape(count_x, count_y, count_z, EDGE, EDGE, EDGE)
    marks = marks.transpose(0, 3, 1, 4, 2, 5).reshape(NXC, NYC, NZC)
    rotor_here = marks == 1
    wall_ext = jnp.pad(rotor_here, 1, constant_values=True)
    rotor_ext = jnp.pad(rotor_here, 1, constant_values=False)
    spin = 0.2 / (NYC + NZC)
    centre_y = (NYC - 1) / 2.0
    centre_z = (NZC - 1) / 2.0
    coord_y = (jnp.arange(NYC + 2) - 1).astype(jnp.float32)
    coord_z = (jnp.arange(NZC + 2) - 1).astype(jnp.float32)
    drift_y = jnp.where(rotor_ext, -spin * (coord_z - centre_z)[None, None, :], 0.0)
    drift_z = jnp.where(rotor_ext, spin * (coord_y - centre_y)[None, :, None], 0.0)
    for sweep in range(STEPS):
        post, density = collide(lattice)
        widened = jnp.pad(post, ((0, 0), (1, 1), (1, 1), (1, 1)))
        lattice = propagate(lattice, widened, wall_ext, drift_y, drift_z, density, rotor_here)
    return lattice
```

```python
import functools

import jax
import jax.numpy as jnp
from jax import lax
from jax.experimental import pallas as pl
from jax.experimental.pallas import tpu as pltpu
from jax.sharding import PartitionSpec as P

EDGE = 16
BXD = 2
BYD = 1
BZD = 4
MOVE_CAP = 2

VELOCITIES = (
    (0, 0, 0),
    (1, 0, 0),
    (-1, 0, 0),
    (0, 1, 0),
    (0, -1, 0),
    (0, 0, 1),
    (0, 0, -1),
    (1, 1, 0),
    (-1, -1, 0),
    (1, -1, 0),
    (-1, 1, 0),
    (1, 0, 1),
    (-1, 0, -1),
    (1, 0, -1),
    (-1, 0, 1),
    (0, 1, 1),
    (0, -1, -1),
    (0, 1, -1),
    (0, -1, 1),
)
WEIGHTS = (1.0 / 3.0,) + (1.0 / 18.0,) * 6 + (1.0 / 36.0,) * 12
OPPOSITE = (0, 2, 1, 4, 3, 6, 5, 8, 7, 10, 9, 12, 11, 14, 13, 16, 15, 18, 17)
OMEGA_EVEN = 1.25
OMEGA_ODD = 1.0 / 1.125

POPS = 19
PLANES = 20
LANE = 128
TILES = EDGE**3 // LANE
BLOCK = PLANES * TILES
YLO = LANE // EDGE
SLAB = 4
SENT_SLABS = MOVE_CAP * BLOCK
SENT_META = SENT_SLABS + BZD * PLANES * SLAB
SENT_ROWS = SENT_META + 8
LAYERS = BXD + 2
ZGROUPS = 3
ZROWS = ZGROUPS * TILES
ZMETA = LAYERS * ZROWS
DIAG = ZROWS + ZGROUPS * SLAB

SPAN_X = BXD * EDGE
SPAN_Y = BYD * EDGE
SPAN_Z = BZD * EDGE
PITCH = SPAN_Y + 8
FIRST = 8
FIELD = (SPAN_X + 4) * PITCH + 16
EXT_X = SPAN_X + 4
EXT_Z = SPAN_Z + 2
RIM_UP = tuple(i for i in range(POPS) if VELOCITIES[i][1] == 1)
RIM_DOWN = tuple(i for i in range(POPS) if VELOCITIES[i][1] == -1)
RIM = POPS + len(RIM_UP)
RIM_BLOCKS = -(-RIM * EXT_Z // LANE)
RIM_ROWS = RIM_BLOCKS * EXT_X + 4
GRID_X = 48

ROTOR = -1.0e30
OUTSIDE = -2.0e30
WALL_BELOW = -1.0e20
OUT_BELOW = -1.5e30

VMEM = pltpu.VMEM
SMEM = pltpu.SMEM


def lanes():
    return lax.broadcasted_iota(jnp.int32, (8, LANE), 1)


def collide(f):
    even = [None] * POPS
    odd = [None] * POPS
    for i in range(1, POPS, 2):
        even[i] = f[i] + f[i + 1]
        odd[i] = f[i] - f[i + 1]
    density = f[0]
    for i in range(1, POPS, 2):
        density = density + even[i]
    flow = []
    for axis in range(3):
        total = None
        for i in range(1, POPS, 2):
            sign = VELOCITIES[i][axis]
            if sign == 0:
                continue
            if total is None:
                total = odd[i] if sign == 1 else -odd[i]
            else:
                total = total + odd[i] if sign == 1 else total - odd[i]
        flow.append(total)
    inverse = 1.0 / density
    velocity = [part * inverse for part in flow]
    square = velocity[0] * velocity[0] + velocity[1] * velocity[1] + velocity[2] * velocity[2]
    base = density * (1.0 - 1.5 * square)
    post = [None] * POPS
    post[0] = (1.0 - OMEGA_EVEN) * f[0] + (OMEGA_EVEN * WEIGHTS[0]) * base
    shared = {}
    for weight in (WEIGHTS[1], WEIGHTS[7]):
        shared[weight] = ((OMEGA_EVEN * weight) * base, (OMEGA_EVEN * weight * 4.5) * density,
                          (OMEGA_ODD * weight * 3.0) * density)
    for i in range(1, POPS, 2):
        projected = None
        for axis in range(3):
            sign = VELOCITIES[i][axis]
            if sign == 0:
                continue
            if projected is None:
                projected = velocity[axis] if sign == 1 else -velocity[axis]
            else:
                projected = projected + velocity[axis] if sign == 1 else projected - velocity[axis]
        low, curve, slope = shared[WEIGHTS[i]]
        even_part = (0.5 - 0.5 * OMEGA_EVEN) * even[i] + (low + curve * (projected * projected))
        odd_part = (0.5 - 0.5 * OMEGA_ODD) * odd[i] + slope * projected
        post[i] = even_part + odd_part
        post[i + 1] = even_part - odd_part
    return post, density


def pushes(density, drift_y, drift_z):
    along_y = density * drift_y
    along_z = density * drift_z
    out = [None] * POPS
    for i in range(1, POPS):
        _, step_y, step_z = VELOCITIES[i]
        total = None
        for sign, part in ((step_y, along_y), (step_z, along_z)):
            if sign == 0:
                continue
            if total is None:
                total = part if sign == 1 else -part
            else:
                total = total + part if sign == 1 else total - part
        if total is not None:
            out[i] = (6.0 * WEIGHTS[i]) * total
    return out


def streamed(pull, own, density, drift_y, drift_z):
    push = pushes(density, drift_y, drift_z)
    out = [own(0)]
    for i in range(1, POPS):
        pulled = pull(i)
        bounced = own(OPPOSITE[i])
        blocked = pulled < WALL_BELOW
        if push[i] is not None:
            bounced = jnp.where(pulled < OUT_BELOW, bounced, bounced + push[i])
        out.append(jnp.where(blocked, bounced, pulled))
    return out


def place():
    return lax.axis_index("stream"), lax.axis_index("cy"), lax.axis_index("cz")


def slot_of(pos, row, layer, column_z):
    slot = (pos[row, 0] - (layer * BXD - 1)) * BZD + (pos[row, 2] - column_z * BZD)
    return jnp.clip(slot, 0, LAYERS * BZD - 1)


def fill_table(pos, table):
    layer, _, column_z = place()
    for entry in range(LAYERS * BZD):
        table[entry] = -1
    for row in range(pos.shape[0]):

        @pl.when(pos[row, 0] >= 0)
        def _(row=row):
            table[slot_of(pos, row, layer, column_z)] = row


def spread_marks(marks, dense):
    rows = marks.shape[0]
    for first in range(0, rows, 8):
        size = min(8, rows - first)
        for tile in range(TILES):
            value = marks[first : first + size, tile * LANE : (tile + 1) * LANE].astype(jnp.float32)
            dense[pl.ds(first * TILES + tile, size, stride=TILES), :] = value


def pack_stream(pos, marks, pops, up, down, table, dense, blocks, slabs, sems):
    fill_table(pos, table)
    count = 0
    for row in range(pos.shape[0]):
        count = count + jnp.where(pos[row, 0] >= 0, 1, 0)
    last = jnp.clip(count - MOVE_CAP, 0, pos.shape[0] - MOVE_CAP)
    sources = [last, last + 1, 0, 1]
    copies = []
    for n, row in enumerate(sources):
        copies.append(pltpu.make_async_copy(pops.at[row], blocks.at[n], sems.at[n]))
    slab_rows = []
    for side in range(2):
        for bz in range(BZD):
            row = jnp.maximum(table[(2 - side) * BZD + bz], 0)
            n = side * BZD + bz
            first = (TILES - SLAB) * LANE if side == 0 else 0
            slab_rows.append(row)
            copies.append(
                pltpu.make_async_copy(
                    pops.at[row, :, pl.ds(first, SLAB * LANE)], slabs.at[n], sems.at[4 + n]
                )
            )
    for copy in copies:
        copy.start()
    spread_marks(marks, dense)
    for side, out in enumerate((up, down)):
        for j in range(MOVE_CAP):
            row = sources[side * MOVE_CAP + j]
            out[pl.ds(j * BLOCK + POPS * TILES, TILES), :] = dense[pl.ds(row * TILES, TILES), :]
            for part, column in ((0, 0), (1, 2)):
                value = jnp.full((1, LANE), pos[row, column], jnp.int32).astype(jnp.float32)
                out[pl.ds(SENT_META + 2 * j + part, 1), :] = value
        for bz in range(BZD):
            row = slab_rows[side * BZD + bz]
            first = TILES - SLAB if side == 0 else 0
            target = SENT_SLABS + (bz * PLANES + POPS) * SLAB
            out[pl.ds(target, SLAB), :] = dense[pl.ds(row * TILES + first, SLAB), :]
    for side, out in enumerate((up, down)):
        for j in range(MOVE_CAP):
            copies[side * MOVE_CAP + j].wait()
            for group, size in ((0, 8), (8, 8), (16, 3)):
                for tile in range(TILES):
                    value = blocks[side * MOVE_CAP + j, group : group + size, tile * LANE : (tile + 1) * LANE]
                    out[pl.ds(j * BLOCK + group * TILES + tile, size, stride=TILES), :] = value
        for bz in range(BZD):
            n = side * BZD + bz
            copies[4 + n].wait()
            for group, size in ((0, 8), (8, 8), (16, 3)):
                for q in range(SLAB):
                    value = slabs[n, group : group + size, q * LANE : (q + 1) * LANE]
                    target = SENT_SLABS + (bz * PLANES + group) * SLAB + q
                    out[pl.ds(target, size, stride=SLAB), :] = value


def pack_own(pos, marks, pops, own, zpack, zup, zdown, dense, stage, sems):
    layer, _, column_z = place()
    rows = pos.shape[0]
    copies = [pltpu.make_async_copy(pops.at[r], stage.at[r], sems.at[r]) for r in range(rows)]
    for copy in copies:
        copy.start()
    spread_marks(marks, dense)

    def settle(row, carry):
        pltpu.make_async_copy(pops.at[row], stage.at[row], sems.at[row]).wait()

        @pl.when(pos[row, 0] >= 0)
        def _():
            base = slot_of(pos, row, layer, column_z) * BLOCK
            for tile in range(TILES):
                for group, size in ((0, 8), (8, 8), (16, 3)):
                    value = stage[row, group : group + size, tile * LANE : (tile + 1) * LANE]
                    own[pl.ds(base + group * TILES + tile, size, stride=TILES), :] = value
            own[pl.ds(base + POPS * TILES, TILES), :] = dense[pl.ds(row * TILES, TILES), :]

        return carry

    lax.fori_loop(0, rows, settle, 0)
    edge_bz = jnp.where(column_z == 0, BZD - 1, 0)
    first_c = jnp.where(column_z == 0, EDGE - 2, 0)
    spot = (lanes() % EDGE) // 2
    for held in range(LAYERS):
        base = (held * BZD + edge_bz) * BLOCK
        for group in range(ZGROUPS):
            for part in range(TILES // 8):
                total = jnp.zeros((8, LANE), jnp.float32)
                for k in range(min(8, PLANES - group * 8)):
                    value = own[pl.ds(base + (group * 8 + k) * TILES + part * 8, 8), :]
                    value = pltpu.roll(value, (2 * k - first_c + LANE) % LANE, 1)
                    total = jnp.where(spot == k, value, total)
                zpack[pl.ds(held * ZROWS + group * TILES + part * 8, 8), :] = total
    present = [jnp.int32(0)] * LAYERS
    for row in range(rows):
        slot = slot_of(pos, row, layer, column_z)
        for held in range(LAYERS):
            hit = (pos[row, 0] >= 0) & (slot == held * BZD + edge_bz)
            present[held] = jnp.where(hit, 1, present[held])
    sublane = lax.broadcasted_iota(jnp.int32, (8, LANE), 0)
    flags = jnp.zeros((8, LANE), jnp.int32)
    for held in range(LAYERS):
        flags = jnp.where(sublane == held, present[held], flags)
    zpack[pl.ds(ZMETA, 8), :] = flags.astype(jnp.float32)
    zup[pl.ds(0, ZROWS), :] = zpack[pl.ds(3 * ZROWS, ZROWS), :]
    zdown[pl.ds(0, ZROWS), :] = zpack[pl.ds(0, ZROWS), :]
    for group in range(ZGROUPS):
        target = pl.ds(ZROWS + group * SLAB, SLAB)
        zup[target, :] = zpack[pl.ds(2 * ZROWS + group * TILES + TILES - SLAB, SLAB), :]
        zdown[target, :] = zpack[pl.ds(ZROWS + group * TILES, SLAB), :]


def gathered(load, zload, ylo, column_z):
    lane = lanes()
    parts = [load(bz) for bz in range(BZD)]
    rows = parts[0].shape[0]
    lane = lane[:rows]
    total = None
    for bz in range(BZD):
        shift = (bz * EDGE - ylo * EDGE) % LANE
        value = pltpu.roll(parts[bz], shift, 1) if shift else parts[bz]
        total = value if total is None else jnp.where(lane // EDGE == bz, value, total)
    zvalue, spot = zload
    goal = jnp.where(column_z == 0, SPAN_Z, LANE - 2)
    zvalue = pltpu.roll(zvalue, (goal - (ylo * EDGE + 2 * spot) + LANE) % LANE, 1)
    return jnp.where(lane >= SPAN_Z, zvalue, total)


def inside_lanes(rows, column_z):
    lane = lanes()[:rows]
    low = (column_z == 0) & (lane >= SPAN_Z) & (lane < SPAN_Z + 2)
    high = (column_z != 0) & (lane >= LANE - 2)
    return (lane < SPAN_Z) | low | high


def marked(post, mark, inside):
    flag = jnp.where(inside, jnp.where(mark > 0.5, ROTOR, 0.0), OUTSIDE)
    wall = flag < WALL_BELOW
    return [jnp.where(wall, flag, value) for value in post]


def chunk_values(own, edge, zall, zedge, chunk, yhi, ylo, column_z):
    out = []
    for plane in range(PLANES):
        group, spot = plane // 8, plane % 8
        if chunk is None:

            def load(bz):
                return edge[pl.ds((bz * PLANES + plane) * 8 + yhi, 4, stride=2), :]

            zvalue = zedge[pl.ds(group * 8 + yhi, 4, stride=2), :]
        else:
            held, half = 1 + chunk // 2, chunk % 2

            def load(bz):
                base = (held * BZD + bz) * BLOCK + plane * TILES + half * EDGE + yhi
                return own[pl.ds(base, 8, stride=2), :]

            zvalue = zall[pl.ds(held * ZROWS + group * TILES + half * EDGE + yhi, 8, stride=2), :]
        out.append(gathered(load, (zvalue, spot), ylo, column_z))
    return out


def halo_x_inside(layer, layers):
    row = lax.broadcasted_iota(jnp.int32, (4, LANE), 0)
    low = (row < 2) & (layer > 0)
    high = (row >= 2) & (layer < layers - 1)
    return low | high


def settle_rim(layers, pos, up, down, zin, zup, zdown, own_in, own, edge, zall, zedge, rim_up, rim_down, post_up, post_down):
    del own_in
    layer, _, column_z = place()
    for arrived in (up, down):
        for j in range(MOVE_CAP):
            bx = arrived[pl.ds(SENT_META + 2 * j, 1), :].astype(jnp.int32)
            bz = arrived[pl.ds(SENT_META + 2 * j + 1, 1), :].astype(jnp.int32)
            code = (bx - layer * BXD) * BZD + (bz - column_z * BZD)
            mine = (bx >= layer * BXD) & (bx < (layer + 1) * BXD)
            first = layer == 0 if arrived is up else layer == layers - 1
            code = jnp.max(jnp.where(mine, code, -1))

            @pl.when((code >= 0) & jnp.logical_not(first))
            def _(arrived=arrived, j=j, code=code):
                base = (jnp.clip(code, 0, BXD * BZD - 1) + BZD) * BLOCK

                def move(n, carry):
                    for k in range(4):
                        rows = n * 32 + 8 * k
                        own[pl.ds(base + rows, 8), :] = arrived[pl.ds(j * BLOCK + rows, 8), :]
                    return carry

                lax.fori_loop(0, BLOCK // 32, move, 0)

    for side, arrived in enumerate((up, down)):
        for bz in range(BZD):
            here = jnp.int32(0)
            goal = (0 if side == 0 else LAYERS - 1) * BZD + bz
            for row in range(pos.shape[0]):
                hit = (pos[row, 0] >= 0) & (slot_of(pos, row, layer, column_z) == goal)
                here = jnp.where(hit, 1, here)
            first = TILES - SLAB if side == 0 else 0
            for plane in range(PLANES):
                mine = own[pl.ds(goal * BLOCK + plane * TILES + first, SLAB), :]
                other = arrived[pl.ds(SENT_SLABS + (bz * PLANES + plane) * SLAB, SLAB), :]
                edge[pl.ds((bz * PLANES + plane) * 8 + side * SLAB, SLAB), :] = jnp.where(here == 1, mine, other)
    for held in range(LAYERS):
        flag = zin[pl.ds(ZMETA + held, 1), :] > 0.5
        for group in range(ZGROUPS):
            if held == 1 or held == 2:
                for part in range(TILES // 8):
                    rows = pl.ds(held * ZROWS + group * TILES + part * 8, 8)
                    source = zup if held == 1 else zdown
                    other = source[pl.ds(group * TILES + part * 8, 8), :]
                    zall[rows, :] = jnp.where(flag, zin[rows, :], other)
            else:
                side = 0 if held == 0 else 1
                source = zup if held == 0 else zdown
                first = TILES - SLAB if held == 0 else 0
                mine = zin[pl.ds(held * ZROWS + group * TILES + first, SLAB), :]
                other = source[pl.ds(ZROWS + group * SLAB, SLAB), :]
                zedge[pl.ds(group * 8 + side * SLAB, SLAB), :] = jnp.where(flag, mine, other)
    for chunk in (0, 1, 2, 3, None):
        for y in (0, 1, SPAN_Y - 2, SPAN_Y - 1):
            values = chunk_values(own, edge, zall, zedge, chunk, y // YLO, y % YLO, column_z)
            post, _ = collide(values[:POPS])
            rows = values[0].shape[0]
            inside = inside_lanes(rows, column_z)
            if chunk is None:
                inside = inside & halo_x_inside(layer, layers)
            post = marked(post, values[POPS], inside)
            target = post_down if y < 2 else post_up
            rim = RIM_DOWN if y < 2 else RIM_UP
            if y in (0, SPAN_Y - 1):
                pairs = [(i, i) for i in range(POPS)]
            else:
                pairs = [(POPS + n, i) for n, i in enumerate(rim)]
            for plane, i in pairs:
                if chunk is None:
                    target[pl.ds(plane * GRID_X, 2), :] = post[i][:2]
                    target[pl.ds(plane * GRID_X + EXT_X - 2, 2), :] = post[i][2:]
                else:
                    target[pl.ds(plane * GRID_X + 2 + 8 * chunk, 8), :] = post[i]
    lane = lanes()
    for source, target in ((post_up, rim_up), (post_down, rim_down)):
        for chunk in range(5):
            size = min(8, EXT_X - 8 * chunk)
            for block in range(RIM_BLOCKS):
                total = jnp.zeros((8, LANE), jnp.float32)
                for plane in range(RIM):
                    begin = plane * EXT_Z - block * LANE
                    if begin >= LANE or begin + EXT_Z <= 0:
                        continue
                    value = source[pl.ds(plane * GRID_X + 8 * chunk, 8), :]
                    value = pltpu.roll(value, (begin + LANE + 2 * column_z) % LANE, 1)
                    total = jnp.where((lane >= begin) & (lane < begin + EXT_Z), value, total)
                target[pl.ds(block * EXT_X + 8 * chunk, size), :] = total[:size]


def settle_all(layers, own, edge, zall, zedge, field, start, density):
    layer, _, column_z = place()

    def halves(yhi, carry):
        def chunks(chunk, carry):
            held = 1 + chunk // 2
            half = chunk % 2
            for ylo in range(YLO):
                values = []
                for plane in range(PLANES):
                    group, spot = plane // 8, plane % 8

                    def load(bz):
                        base = (held * BZD + bz) * BLOCK + plane * TILES + half * EDGE + yhi
                        return own[pl.ds(base, 8, stride=2), :]

                    zrow = held * ZROWS + group * TILES + half * EDGE + yhi
                    zvalue = zall[pl.ds(zrow, 8, stride=2), :]
                    values.append(gathered(load, (zvalue, spot), ylo, column_z))
                post, rho = collide(values[:POPS])
                post = marked(post, values[POPS], inside_lanes(8, column_z))
                row = (8 * chunk + 2) * PITCH + FIRST + YLO * yhi + ylo
                for i in range(POPS):
                    field[pl.ds(i * FIELD + row, 8, stride=PITCH), :] = post[i]
                    start[pl.ds((i * SPAN_X + 8 * chunk) * SPAN_Y + YLO * yhi + ylo, 8, stride=SPAN_Y), :] = values[i]
                density[pl.ds(row, 8, stride=PITCH), :] = rho
            return carry

        lax.fori_loop(0, SPAN_X // 8, chunks, 0)
        for ylo in range(YLO):
            values = []
            for plane in range(PLANES):
                group, spot = plane // 8, plane % 8

                def load(bz):
                    return edge[pl.ds((bz * PLANES + plane) * 8 + yhi, 4, stride=2), :]

                zvalue = zedge[pl.ds(group * 8 + yhi, 4, stride=2), :]
                values.append(gathered(load, (zvalue, spot), ylo, column_z))
            post, rho = collide(values[:POPS])
            inside = inside_lanes(4, column_z) & halo_x_inside(layer, layers)
            post = marked(post, values[POPS], inside)
            for first, side in ((0, 0), (EXT_X - 2, 2)):
                row = first * PITCH + FIRST + YLO * yhi + ylo
                for i in range(POPS):
                    field[pl.ds(i * FIELD + row, 2, stride=PITCH), :] = post[i][side : side + 2]
                density[pl.ds(row, 2, stride=PITCH), :] = rho[side : side + 2]
        return carry

    lax.fori_loop(0, SPAN_Y // YLO, halves, 0)


def finish(columns, depth, rim_low, rim_high, field_in, start, density, out, field, later, thick, low, high):
    del field_in
    _, column_y, column_z = place()
    lane = lanes()
    total_y = SPAN_Y * columns
    total_z = SPAN_Z * depth
    spin = 0.2 / (total_y + total_z)
    centre_y = (total_y - 1) / 2.0
    centre_z = (total_z - 1) / 2.0
    here_z = jnp.where(lane < SPAN_Z + 8, lane, lane - LANE) + column_z * SPAN_Z
    drift_y = -spin * (here_z.astype(jnp.float32) - centre_z)
    flat = (lane + 2 * column_z) % LANE
    for source, target, there in ((rim_low, low, column_y > 0), (rim_high, high, column_y < columns - 1)):
        for chunk in range(5):
            size = min(8, EXT_X - 8 * chunk)
            blocks = [source[pl.ds(block * EXT_X + 8 * chunk, 8), :] for block in range(RIM_BLOCKS)]
            for plane in range(RIM):
                block, begin = divmod(plane * EXT_Z, LANE)
                shift = (2 * LANE - begin - 2 * column_z) % LANE
                value = pltpu.roll(blocks[block], shift, 1)
                if begin + EXT_Z > LANE:
                    value = jnp.where(flat < LANE - begin, value, pltpu.roll(blocks[block + 1], shift, 1))
                value = jnp.where((flat < EXT_Z) & there, value, OUTSIDE)
                target[pl.ds(plane * GRID_X + 8 * chunk, 8), :] = value
    for source, y, rim in ((low, -1, RIM_UP), (high, SPAN_Y, RIM_DOWN)):
        for i in rim:
            for chunk in range(5):
                size = min(8, EXT_X - 8 * chunk)
                row = i * FIELD + 8 * chunk * PITCH + FIRST + y
                field[pl.ds(row, size, stride=PITCH), :] = source[pl.ds(i * GRID_X + 8 * chunk, size), :]

    def turned(value, step_z):
        return pltpu.roll(value, step_z % LANE, 1) if step_z else value

    for source, y, rim in ((low, -1, RIM_UP), (high, SPAN_Y, RIM_DOWN)):
        outer = {i: POPS + n for n, i in enumerate(rim)}
        toward = VELOCITIES[rim[0]][1]
        drift_z = spin * ((column_y * SPAN_Y + y).astype(jnp.float32) - centre_y)
        for chunk in range(5):
            first = 1 + 8 * chunk
            size = min(8, EXT_X - 1 - first)

            def pull(i):
                step_x, step_y, step_z = VELOCITIES[i]
                if step_y == toward:
                    value = source[pl.ds(outer[i] * GRID_X + first - step_x, 8), :]
                elif step_y == 0:
                    value = source[pl.ds(i * GRID_X + first - step_x, 8), :]
                else:
                    row = i * FIELD + (first - step_x) * PITCH + FIRST + y - step_y
                    if size == 8:
                        value = field[pl.ds(row, 8, stride=PITCH), :]
                    else:
                        value = field[pl.ds(row, size, stride=PITCH), :]
                if size < 8 and value.shape[0] == 8:
                    value = value[:size]
                return turned(value, step_z)

            posts = [source[pl.ds(i * GRID_X + first, 8), :][:size] for i in range(POPS)]
            rho = posts[0]
            for i in range(1, POPS):
                rho = rho + posts[i]
            values = streamed(pull, lambda i: posts[i], rho, drift_y[:size], drift_z)
            post, _ = collide(values)
            wall = posts[0] < WALL_BELOW
            for i in rim:
                row = i * FIELD + first * PITCH + FIRST + y
                later[pl.ds(row, size, stride=PITCH), :] = jnp.where(wall, posts[0], post[i])

    sublane = lax.broadcasted_iota(jnp.int32, (8, LANE), 0)
    drifts = []
    for half in range(SPAN_Y // 8):
        here_y = sublane + (column_y * SPAN_Y + 8 * half)
        drifts.append(spin * (here_y.astype(jnp.float32) - centre_y))

    def first_step(x, carry):
        for half in range(SPAN_Y // 8):
            base = x * PITCH + FIRST + 8 * half

            def pull(i):
                step_x, step_y, step_z = VELOCITIES[i]
                return turned(field[pl.ds(i * FIELD + base - step_x * PITCH - step_y, 8), :], step_z)

            def own(i):
                return field[pl.ds(i * FIELD + base, 8), :]

            rho = density[pl.ds(base, 8), :]
            values = streamed(pull, own, rho, drift_y, drifts[half])
            post, rho = collide(values)
            flag = own(0)
            wall = flag < WALL_BELOW
            for i in range(POPS):
                later[pl.ds(i * FIELD + base, 8), :] = jnp.where(wall, flag, post[i])
            thick[pl.ds(base, 8), :] = rho
        return carry

    lax.fori_loop(1, EXT_X - 1, first_step, 0)

    def second_step(x, carry):
        for half in range(SPAN_Y // 8):
            base = (x + 2) * PITCH + FIRST + 8 * half

            def pull(i):
                step_x, step_y, step_z = VELOCITIES[i]
                return turned(later[pl.ds(i * FIELD + base - step_x * PITCH - step_y, 8), :], step_z)

            def own(i):
                return later[pl.ds(i * FIELD + base, 8), :]

            values = streamed(pull, own, thick[pl.ds(base, 8), :], drift_y, drifts[half])
            wall = own(0) < WALL_BELOW
            for i in range(POPS):
                first = start[pl.ds((i * SPAN_X + x) * SPAN_Y + 8 * half, 8), :]
                value = jnp.where(wall, first, values[i])
                out[i, x, pl.ds(8 * half, 8), :] = value[:, :SPAN_Z]
        return carry

    lax.fori_loop(0, SPAN_X, second_step, 0)


def rows_of(count):
    return jax.ShapeDtypeStruct((count, LANE), jnp.float32)


def kept(count):
    return VMEM((count, LANE), jnp.float32)


def params(mib):
    return pltpu.CompilerParams(vmem_limit_bytes=mib * 2**20)


def shards(populations, solid_cells, block_pos):
    layers = lax.axis_size("stream")
    columns = lax.axis_size("cy")
    depth = lax.axis_size("cz")
    rows = block_pos.shape[0]
    smem = pl.BlockSpec(memory_space=SMEM)
    vmem = pl.BlockSpec(memory_space=VMEM)
    anywhere = pl.BlockSpec(memory_space=pl.ANY)

    send_up, send_down = pl.pallas_call(
        pack_stream,
        out_shape=(rows_of(SENT_ROWS), rows_of(SENT_ROWS)),
        in_specs=[smem, vmem, anywhere],
        out_specs=(vmem, vmem),
        scratch_shapes=[
            SMEM((LAYERS * BZD,), jnp.int32),
            VMEM((rows * TILES, LANE), jnp.float32),
            VMEM((2 * MOVE_CAP, POPS, EDGE**3), jnp.float32),
            VMEM((2 * BZD, POPS, SLAB * LANE), jnp.float32),
            pltpu.SemaphoreType.DMA((2 * MOVE_CAP + 2 * BZD,)),
        ],
        compiler_params=params(24),
        name="pack_stream",
    )(block_pos, solid_cells, populations)
    up = [(i, i + 1) for i in range(layers - 1)]
    down = [(i + 1, i) for i in range(layers - 1)]
    from_low = lax.ppermute(send_up, "stream", up)
    from_high = lax.ppermute(send_down, "stream", down)

    own, zpack, zsend_up, zsend_down = pl.pallas_call(
        pack_own,
        out_shape=(kept(LAYERS * BZD * BLOCK), rows_of(ZMETA + 8), rows_of(DIAG), rows_of(DIAG)),
        in_specs=[smem, vmem, anywhere],
        out_specs=(vmem,) * 4,
        scratch_shapes=[
            VMEM((rows * TILES, LANE), jnp.float32),
            VMEM((rows, POPS, EDGE**3), jnp.float32),
            pltpu.SemaphoreType.DMA((rows,)),
        ],
        compiler_params=params(24),
        name="pack_own",
    )(block_pos, solid_cells, populations)
    swap = [(i, depth - 1 - i) for i in range(depth)]
    zin = lax.ppermute(zpack, "cz", swap)
    zup_pairs = [(s * depth + c, t * depth + d) for s, t in up for c, d in swap]
    zdown_pairs = [(s * depth + c, t * depth + d) for s, t in down for c, d in swap]
    z_low = lax.ppermute(zsend_up, ("stream", "cz"), zup_pairs)
    z_high = lax.ppermute(zsend_down, ("stream", "cz"), zdown_pairs)

    own, edge, zall, zedge, rim_up, rim_down = pl.pallas_call(
        functools.partial(settle_rim, layers),
        out_shape=(
            kept(LAYERS * BZD * BLOCK),
            kept(BZD * PLANES * 8),
            kept(LAYERS * ZROWS),
            kept(ZGROUPS * 8),
            rows_of(RIM_ROWS),
            rows_of(RIM_ROWS),
        ),
        in_specs=[smem] + [vmem] * 6,
        out_specs=(vmem,) * 6,
        scratch_shapes=[
            VMEM((RIM * GRID_X, LANE), jnp.float32),
            VMEM((RIM * GRID_X, LANE), jnp.float32),
        ],
        input_output_aliases={6: 0},
        compiler_params=params(24),
        name="settle_rim",
    )(block_pos, from_low, from_high, zin, z_low, z_high, own)
    cy_up = [(i, i + 1) for i in range(columns - 1)]
    cy_down = [(i + 1, i) for i in range(columns - 1)]
    rim_low = lax.ppermute(rim_up, "cy", cy_up)
    rim_high = lax.ppermute(rim_down, "cy", cy_down)

    field, start, density = pl.pallas_call(
        functools.partial(settle_all, layers),
        out_shape=(kept(POPS * FIELD), kept(POPS * SPAN_X * SPAN_Y), kept(FIELD)),
        in_specs=[vmem] * 4,
        out_specs=(vmem,) * 3,
        compiler_params=params(24),
        name="settle_all",
    )(own, edge, zall, zedge)

    out, _ = pl.pallas_call(
        functools.partial(finish, columns, depth),
        out_shape=(
            jax.ShapeDtypeStruct((POPS, SPAN_X, SPAN_Y, SPAN_Z), jnp.float32),
            kept(POPS * FIELD),
        ),
        in_specs=[vmem] * 5,
        out_specs=(vmem, vmem),
        scratch_shapes=[
            VMEM((POPS * FIELD, LANE), jnp.float32),
            VMEM((FIELD, LANE), jnp.float32),
            VMEM((RIM * GRID_X, LANE), jnp.float32),
            VMEM((RIM * GRID_X, LANE), jnp.float32),
        ],
        input_output_aliases={2: 1},
        compiler_params=params(32),
        name="finish",
    )(rim_low, rim_high, field, start, density)
    return out


def solution(mesh):
    in_specs = (
        P(("stream", "cy", "cz"), None, None),
        P(("stream", "cy", "cz"), None),
        P(("stream", "cy", "cz"), None),
    )
    out_specs = P(None, "stream", "cy", "cz")
    return jax.shard_map(shards, mesh=mesh, in_specs=in_specs, out_specs=out_specs, check_vma=False)
```

```python
import functools

import jax
import jax.numpy as jnp
from jax import lax
from jax.experimental import pallas as pl
from jax.experimental.pallas import tpu as pltpu
from jax.sharding import PartitionSpec as P

EDGE = 16
BXD = 2
BYD = 1
BZD = 4
MOVE_CAP = 2

VELOCITIES = (
    (0, 0, 0),
    (1, 0, 0),
    (-1, 0, 0),
    (0, 1, 0),
    (0, -1, 0),
    (0, 0, 1),
    (0, 0, -1),
    (1, 1, 0),
    (-1, -1, 0),
    (1, -1, 0),
    (-1, 1, 0),
    (1, 0, 1),
    (-1, 0, -1),
    (1, 0, -1),
    (-1, 0, 1),
    (0, 1, 1),
    (0, -1, -1),
    (0, 1, -1),
    (0, -1, 1),
)
WEIGHTS = (1.0 / 3.0,) + (1.0 / 18.0,) * 6 + (1.0 / 36.0,) * 12
OPPOSITE = (0, 2, 1, 4, 3, 6, 5, 8, 7, 10, 9, 12, 11, 14, 13, 16, 15, 18, 17)
OMEGA_EVEN = 1.25
OMEGA_ODD = 1.0 / 1.125

POPS = 19
PLANES = 20
LANE = 128
TILES = EDGE**3 // LANE
BLOCK = PLANES * TILES
YLO = LANE // EDGE
SLAB = 4
SENT_SLABS = MOVE_CAP * BLOCK
LAYERS = BXD + 2
ZGROUPS = 3
ZROWS = ZGROUPS * TILES
ZMETA = LAYERS * ZROWS
DIAG = ZROWS + ZGROUPS * SLAB

SPAN_X = BXD * EDGE
SPAN_Y = BYD * EDGE
SPAN_Z = BZD * EDGE
PITCH = SPAN_Y + 8
FIRST = 8
FIELD = (SPAN_X + 4) * PITCH + 16
EXT_X = SPAN_X + 4
EXT_Z = SPAN_Z + 2
RIM_UP = tuple(i for i in range(POPS) if VELOCITIES[i][1] == 1)
RIM_DOWN = tuple(i for i in range(POPS) if VELOCITIES[i][1] == -1)
RIM = POPS + len(RIM_UP)
AHEAD = tuple(i for i in range(POPS) if VELOCITIES[i][0] == 1)
BACK = tuple(i for i in range(POPS) if VELOCITIES[i][0] == -1)
FACE = 2 * BZD
SENT_META = SENT_SLABS + RIM * FACE
SENT_ROWS = SENT_META + 8
RIM_BLOCKS = -(-RIM * EXT_Z // LANE)
RIM_ROWS = RIM_BLOCKS * EXT_X + 4
GRID_X = 48

ROTOR = -1.0e30
OUTSIDE = -2.0e30
WALL_BELOW = -1.0e20
OUT_BELOW = -1.5e30

VMEM = pltpu.VMEM
SMEM = pltpu.SMEM


def lanes():
    return lax.broadcasted_iota(jnp.int32, (8, LANE), 1)


def collide(f):
    even = [None] * POPS
    odd = [None] * POPS
    for i in range(1, POPS, 2):
        even[i] = f[i] + f[i + 1]
        odd[i] = f[i] - f[i + 1]
    density = f[0]
    for i in range(1, POPS, 2):
        density = density + even[i]
    flow = []
    for axis in range(3):
        total = None
        for i in range(1, POPS, 2):
            sign = VELOCITIES[i][axis]
            if sign == 0:
                continue
            if total is None:
                total = odd[i] if sign == 1 else -odd[i]
            else:
                total = total + odd[i] if sign == 1 else total - odd[i]
        flow.append(total)
    inverse = 1.0 / density
    velocity = [part * inverse for part in flow]
    square = velocity[0] * velocity[0] + velocity[1] * velocity[1] + velocity[2] * velocity[2]
    base = density * (1.0 - 1.5 * square)
    post = [None] * POPS
    post[0] = (1.0 - OMEGA_EVEN) * f[0] + (OMEGA_EVEN * WEIGHTS[0]) * base
    shared = {}
    for weight in (WEIGHTS[1], WEIGHTS[7]):
        shared[weight] = ((OMEGA_EVEN * weight) * base, (OMEGA_EVEN * weight * 4.5) * density,
                          (OMEGA_ODD * weight * 3.0) * density)
    for i in range(1, POPS, 2):
        projected = None
        for axis in range(3):
            sign = VELOCITIES[i][axis]
            if sign == 0:
                continue
            if projected is None:
                projected = velocity[axis] if sign == 1 else -velocity[axis]
            else:
                projected = projected + velocity[axis] if sign == 1 else projected - velocity[axis]
        low, curve, slope = shared[WEIGHTS[i]]
        even_part = (0.5 - 0.5 * OMEGA_EVEN) * even[i] + (low + curve * (projected * projected))
        odd_part = (0.5 - 0.5 * OMEGA_ODD) * odd[i] + slope * projected
        post[i] = even_part + odd_part
        post[i + 1] = even_part - odd_part
    return post, density


def pushes(density, drift_y, drift_z):
    along_y = density * drift_y
    along_z = density * drift_z
    out = [None] * POPS
    for i in range(1, POPS):
        _, step_y, step_z = VELOCITIES[i]
        total = None
        for sign, part in ((step_y, along_y), (step_z, along_z)):
            if sign == 0:
                continue
            if total is None:
                total = part if sign == 1 else -part
            else:
                total = total + part if sign == 1 else total - part
        if total is not None:
            out[i] = (6.0 * WEIGHTS[i]) * total
    return out


def total_of(parts):
    parts = list(parts)
    while len(parts) > 1:
        pairs = [parts[n] + parts[n + 1] for n in range(0, len(parts) - 1, 2)]
        parts = pairs + parts[len(parts) - len(parts) % 2 :]
    return parts[0]


def streamed(pull, own, drift_y, drift_z):
    push = pushes(total_of(own), drift_y, drift_z)
    out = [own[0]]
    for i in range(1, POPS):
        pulled = pull(i)
        bounced = own[OPPOSITE[i]]
        blocked = pulled < WALL_BELOW
        if push[i] is not None:
            bounced = jnp.where(pulled < OUT_BELOW, bounced, bounced + push[i])
        out.append(jnp.where(blocked, bounced, pulled))
    return out


def place():
    return lax.axis_index("stream"), lax.axis_index("cy"), lax.axis_index("cz")


def slot_of(pos, row, layer, column_z):
    slot = (pos[0, row] - (layer * BXD - 1)) * BZD + (pos[2, row] - column_z * BZD)
    return jnp.clip(slot, 0, LAYERS * BZD - 1)


def fill_table(pos, table):
    layer, _, column_z = place()
    for entry in range(LAYERS * BZD):
        table[entry] = -1
    for row in range(pos.shape[1]):

        @pl.when(pos[0, row] >= 0)
        def _(row=row):
            table[slot_of(pos, row, layer, column_z)] = row


def spread_marks(marks, dense):
    rows = marks.shape[0]
    for first in range(0, rows, 8):
        size = min(8, rows - first)
        for tile in range(TILES):
            value = marks[first : first + size, tile * LANE : (tile + 1) * LANE].astype(jnp.float32)
            dense[pl.ds(first * TILES + tile, size, stride=TILES), :] = value


def collide_block(ref, base):
    for part in range(TILES // 8):
        old = [ref[pl.ds(base + i * TILES + 8 * part, 8), :] for i in range(POPS)]
        mark = ref[pl.ds(base + POPS * TILES + 8 * part, 8), :] > 0.5
        post, _ = collide(old)
        for i in range(POPS):
            ref[pl.ds(base + i * TILES + 8 * part, 8), :] = jnp.where(mark, old[i], post[i])


def pack_stream(places, marks_in, pops, up, down, pos, table, marks, dense, blocks, slabs, strip, sems):
    mark_copy = pltpu.make_async_copy(marks_in, marks, sems.at[2 * MOVE_CAP + 2 * BZD])
    mark_copy.start()
    place_copy = pltpu.make_async_copy(places, pos, sems.at[2 * MOVE_CAP + 2 * BZD + 1])
    place_copy.start()
    place_copy.wait()
    fill_table(pos, table)
    rows = pos.shape[1]
    count = 0
    for row in range(rows):
        count = count + jnp.where(pos[0, row] >= 0, 1, 0)
    last = jnp.clip(count - MOVE_CAP, 0, rows - MOVE_CAP)
    sources = [last, last + 1, 0, 1]
    copies = []
    for n, row in enumerate(sources):
        copies.append(pltpu.make_async_copy(pops.at[row], blocks.at[n], sems.at[n]))
    slab_rows = []
    for side in range(2):
        for bz in range(BZD):
            row = jnp.maximum(table[(2 - side) * BZD + bz], 0)
            n = side * BZD + bz
            first = (TILES - SLAB) * LANE if side == 0 else 0
            slab_rows.append(row)
            copies.append(
                pltpu.make_async_copy(
                    pops.at[row, :, pl.ds(first, SLAB * LANE)], slabs.at[n], sems.at[4 + n]
                )
            )
    for copy in copies:
        copy.start()
    mark_copy.wait()
    spread_marks(marks, dense)
    groups = ((0, 8), (8, 8), (16, 3))
    for side, out in enumerate((up, down)):
        for j in range(MOVE_CAP):
            row = sources[side * MOVE_CAP + j]
            out[pl.ds(j * BLOCK + POPS * TILES, TILES), :] = dense[pl.ds(row * TILES, TILES), :]
            for part, axis in ((0, 0), (1, 2)):
                value = jnp.full((1, LANE), pos[axis, row], jnp.int32).astype(jnp.float32)
                out[pl.ds(SENT_META + 2 * j + part, 1), :] = value
            copies[side * MOVE_CAP + j].wait()
            for group, size in groups:
                for tile in range(TILES):
                    value = blocks[side * MOVE_CAP + j, group : group + size, tile * LANE : (tile + 1) * LANE]
                    out[pl.ds(j * BLOCK + group * TILES + tile, size, stride=TILES), :] = value
            collide_block(out, j * BLOCK)
        for bz in range(BZD):
            n = side * BZD + bz
            first = slab_rows[n] * TILES + (TILES - SLAB if side == 0 else 0)
            copies[4 + n].wait()
            for x in range(2):
                for yhi in range(2):
                    q = 2 * x + yhi
                    row = x * FACE + 2 * bz + yhi
                    for group, size in groups:
                        value = slabs[n, group : group + size, q * LANE : (q + 1) * LANE]
                        strip[pl.ds(group * 2 * FACE + row, size, stride=2 * FACE), :] = value
                row = POPS * 2 * FACE + x * FACE + 2 * bz
                strip[pl.ds(row, 2), :] = dense[pl.ds(first + 2 * x, 2), :]
        inner = 1 if side == 0 else 0
        for x in range(2):
            old = [strip[pl.ds(i * 2 * FACE + x * FACE, FACE), :] for i in range(POPS)]
            mark = strip[pl.ds(POPS * 2 * FACE + x * FACE, FACE), :] > 0.5
            post, _ = collide(old)
            if x == inner:
                pairs = [(i, i) for i in range(POPS)]
            else:
                pairs = [(POPS + n, i) for n, i in enumerate(AHEAD if side == 0 else BACK)]
            for plane, i in pairs:
                out[pl.ds(SENT_SLABS + plane * FACE, FACE), :] = jnp.where(mark, ROTOR, post[i])


def pack_own(places, marks_in, pops, own, zpack, zup, zdown, pos, marks, dense, stage, sems):
    layer, _, column_z = place()
    rows = pos.shape[1]
    mark_copy = pltpu.make_async_copy(marks_in, marks, sems.at[rows])
    mark_copy.start()
    place_copy = pltpu.make_async_copy(places, pos, sems.at[rows + 1])
    place_copy.start()
    copies = [pltpu.make_async_copy(pops.at[r], stage.at[r], sems.at[r]) for r in range(rows)]
    for copy in copies:
        copy.start()
    mark_copy.wait()
    spread_marks(marks, dense)
    place_copy.wait()

    def settle(row, carry):
        pltpu.make_async_copy(pops.at[row], stage.at[row], sems.at[row]).wait()

        @pl.when(pos[0, row] >= 0)
        def _():
            base = pl.multiple_of(slot_of(pos, row, layer, column_z) * BLOCK, 8)
            for tile in range(TILES):
                for group, size in ((0, 8), (8, 8), (16, 3)):
                    value = stage[row, group : group + size, tile * LANE : (tile + 1) * LANE]
                    own[pl.ds(base + group * TILES + tile, size, stride=TILES), :] = value
            from_row = pl.multiple_of(row * TILES, 8)
            own[pl.ds(base + POPS * TILES, TILES), :] = dense[pl.ds(from_row, TILES), :]
            collide_block(own, base)

        return carry

    lax.fori_loop(0, rows, settle, 0)
    edge_bz = jnp.where(column_z == 0, BZD - 1, 0)
    first_c = jnp.where(column_z == 0, EDGE - 2, 0)
    spot = (lanes() % EDGE) // 2
    for held in range(LAYERS):
        base = pl.multiple_of((held * BZD + edge_bz) * BLOCK, 8)
        for group in range(ZGROUPS):
            for part in range(TILES // 8):
                total = jnp.zeros((8, LANE), jnp.float32)
                for k in range(min(8, PLANES - group * 8)):
                    value = own[pl.ds(base + (group * 8 + k) * TILES + part * 8, 8), :]
                    value = pltpu.roll(value, (2 * k - first_c + LANE) % LANE, 1)
                    total = jnp.where(spot == k, value, total)
                zpack[pl.ds(held * ZROWS + group * TILES + part * 8, 8), :] = total
    present = [jnp.int32(0)] * LAYERS
    for row in range(rows):
        slot = slot_of(pos, row, layer, column_z)
        for held in range(LAYERS):
            hit = (pos[0, row] >= 0) & (slot == held * BZD + edge_bz)
            present[held] = jnp.where(hit, 1, present[held])
    sublane = lax.broadcasted_iota(jnp.int32, (8, LANE), 0)
    flags = jnp.zeros((8, LANE), jnp.int32)
    for held in range(LAYERS):
        flags = jnp.where(sublane == held, present[held], flags)
    zpack[pl.ds(ZMETA, 8), :] = flags.astype(jnp.float32)
    zup[pl.ds(0, ZROWS), :] = zpack[pl.ds(3 * ZROWS, ZROWS), :]
    zdown[pl.ds(0, ZROWS), :] = zpack[pl.ds(0, ZROWS), :]
    for group in range(ZGROUPS):
        target = pl.ds(ZROWS + group * SLAB, SLAB)
        zup[target, :] = zpack[pl.ds(2 * ZROWS + group * TILES + TILES - SLAB, SLAB), :]
        zdown[target, :] = zpack[pl.ds(ZROWS + group * TILES, SLAB), :]


def gathered(load, zload, ylo, column_z):
    lane = lanes()
    parts = [load(bz) for bz in range(BZD)]
    rows = parts[0].shape[0]
    lane = lane[:rows]
    total = None
    for bz in range(BZD):
        shift = (bz * EDGE - ylo * EDGE) % LANE
        value = pltpu.roll(parts[bz], shift, 1) if shift else parts[bz]
        total = value if total is None else jnp.where(lane // EDGE == bz, value, total)
    zvalue, spot = zload
    goal = jnp.where(column_z == 0, SPAN_Z, LANE - 2)
    zvalue = pltpu.roll(zvalue, (goal - (ylo * EDGE + 2 * spot) + LANE) % LANE, 1)
    return jnp.where(lane >= SPAN_Z, zvalue, total)


def inside_lanes(rows, column_z):
    lane = lanes()[:rows]
    low = (column_z == 0) & (lane >= SPAN_Z) & (lane < SPAN_Z + 2)
    high = (column_z != 0) & (lane >= LANE - 2)
    return (lane < SPAN_Z) | low | high


def marked(post, mark, inside):
    flag = jnp.where(inside, jnp.where(mark > 0.5, ROTOR, 0.0), OUTSIDE)
    wall = flag < WALL_BELOW
    return [jnp.where(wall, flag, value) for value in post]


def chunk_values(own, edge, zall, zedge, chunk, yhi, ylo, column_z):
    out = []
    for plane in range(PLANES):
        group, spot = plane // 8, plane % 8
        if chunk is None:

            def load(bz):
                if plane == POPS:
                    return jnp.zeros((4, LANE), jnp.float32)
                return edge[pl.ds(plane * 4 * FACE + 2 * bz + yhi, 4, stride=FACE), :]

            zvalue = zedge[pl.ds(group * 8 + yhi, 4, stride=2), :]
        else:
            held, half = 1 + chunk // 2, chunk % 2

            def load(bz):
                base = (held * BZD + bz) * BLOCK + plane * TILES + half * EDGE + yhi
                return own[pl.ds(base, 8, stride=2), :]

            zvalue = zall[pl.ds(held * ZROWS + group * TILES + half * EDGE + yhi, 8, stride=2), :]
        out.append(gathered(load, (zvalue, spot), ylo, column_z))
    return out


def halo_x_inside(layer, layers):
    row = lax.broadcasted_iota(jnp.int32, (4, LANE), 0)
    low = (row < 2) & (layer > 0)
    high = (row >= 2) & (layer < layers - 1)
    return low | high


def settle_rim(layers, places, up, down, zin, zup, zdown, own_in, own, edge, zall, zedge, rim_up, rim_down, pos, post_up, post_down, sem):
    del own_in
    layer, _, column_z = place()
    place_copy = pltpu.make_async_copy(places, pos, sem)
    place_copy.start()
    for arrived in (up, down):
        for j in range(MOVE_CAP):
            bx = arrived[pl.ds(SENT_META + 2 * j, 1), :].astype(jnp.int32)
            bz = arrived[pl.ds(SENT_META + 2 * j + 1, 1), :].astype(jnp.int32)
            code = (bx - layer * BXD) * BZD + (bz - column_z * BZD)
            mine = (bx >= layer * BXD) & (bx < (layer + 1) * BXD)
            first = layer == 0 if arrived is up else layer == layers - 1
            code = jnp.max(jnp.where(mine, code, -1))

            @pl.when((code >= 0) & jnp.logical_not(first))
            def _(arrived=arrived, j=j, code=code):
                base = pl.multiple_of((jnp.clip(code, 0, BXD * BZD - 1) + BZD) * BLOCK, 8)
                for n in range(BLOCK // 8):
                    own[pl.ds(base + 8 * n, 8), :] = arrived[pl.ds(j * BLOCK + 8 * n, 8), :]

    place_copy.wait()
    for side, arrived in enumerate((up, down)):
        inner, outer = (1, 0) if side == 0 else (2, 3)
        pairs = [(i, i, inner) for i in range(POPS)]
        pairs += [(POPS + n, i, outer) for n, i in enumerate(AHEAD if side == 0 else BACK)]
        for plane, i, x in pairs:
            edge[pl.ds((i * 4 + x) * FACE, FACE), :] = arrived[pl.ds(SENT_SLABS + plane * FACE, FACE), :]
        for bz in range(BZD):
            here = jnp.int32(0)
            goal = (0 if side == 0 else LAYERS - 1) * BZD + bz
            for row in range(pos.shape[1]):
                hit = (pos[0, row] >= 0) & (slot_of(pos, row, layer, column_z) == goal)
                here = jnp.where(hit, 1, here)

            @pl.when(here == 1)
            def _(side=side, pairs=pairs, goal=goal, bz=bz):
                first = goal * BLOCK + (TILES - SLAB if side == 0 else 0)
                for _, i, x in pairs:
                    shift = 2 * (x if side == 0 else x - 2)
                    mark = own[pl.ds(first + POPS * TILES + shift, 2), :] > 0.5
                    value = own[pl.ds(first + i * TILES + shift, 2), :]
                    edge[pl.ds((i * 4 + x) * FACE + 2 * bz, 2), :] = jnp.where(mark, ROTOR, value)

    for held in range(LAYERS):
        flag = zin[pl.ds(ZMETA + held, 1), :] > 0.5
        for group in range(ZGROUPS):
            if held == 1 or held == 2:
                for part in range(TILES // 8):
                    rows = pl.ds(held * ZROWS + group * TILES + part * 8, 8)
                    source = zup if held == 1 else zdown
                    other = source[pl.ds(group * TILES + part * 8, 8), :]
                    zall[rows, :] = jnp.where(flag, zin[rows, :], other)
            else:
                side = 0 if held == 0 else 1
                source = zup if held == 0 else zdown
                first = TILES - SLAB if held == 0 else 0
                mine = zin[pl.ds(held * ZROWS + group * TILES + first, SLAB), :]
                other = source[pl.ds(ZROWS + group * SLAB, SLAB), :]
                zedge[pl.ds(group * 8 + side * SLAB, SLAB), :] = jnp.where(flag, mine, other)
    for chunk in (0, 1, 2, 3, None):
        for y in (0, 1, SPAN_Y - 2, SPAN_Y - 1):
            values = chunk_values(own, edge, zall, zedge, chunk, y // YLO, y % YLO, column_z)
            inside = inside_lanes(values[0].shape[0], column_z)
            if chunk is None:
                inside = inside & halo_x_inside(layer, layers)
            post = marked(values[:POPS], values[POPS], inside)
            target = post_down if y < 2 else post_up
            rim = RIM_DOWN if y < 2 else RIM_UP
            if y in (0, SPAN_Y - 1):
                pairs = [(i, i) for i in range(POPS)]
            else:
                pairs = [(POPS + n, i) for n, i in enumerate(rim)]
            for plane, i in pairs:
                if chunk is None:
                    target[pl.ds(plane * GRID_X, 2), :] = post[i][:2]
                    target[pl.ds(plane * GRID_X + EXT_X - 2, 2), :] = post[i][2:]
                else:
                    target[pl.ds(plane * GRID_X + 2 + 8 * chunk, 8), :] = post[i]
    lane = lanes()
    for source, target in ((post_up, rim_up), (post_down, rim_down)):
        for chunk in range(5):
            size = min(8, EXT_X - 8 * chunk)
            for block in range(RIM_BLOCKS):
                total = jnp.zeros((8, LANE), jnp.float32)
                for plane in range(RIM):
                    begin = plane * EXT_Z - block * LANE
                    if begin >= LANE or begin + EXT_Z <= 0:
                        continue
                    value = source[pl.ds(plane * GRID_X + 8 * chunk, 8), :]
                    value = pltpu.roll(value, (begin + LANE + 2 * column_z) % LANE, 1)
                    total = jnp.where((lane >= begin) & (lane < begin + EXT_Z), value, total)
                target[pl.ds(block * EXT_X + 8 * chunk, size), :] = total[:size]


def turned(value, step_z):
    return pltpu.roll(value, step_z % LANE, 1) if step_z else value


def drifts_of(columns, depth):
    _, _, column_z = place()
    lane = lanes()
    total_y = SPAN_Y * columns
    total_z = SPAN_Z * depth
    spin = 0.2 / (total_y + total_z)
    here_z = jnp.where(lane < SPAN_Z + 8, lane, lane - LANE) + column_z * SPAN_Z
    drift_y = -spin * (here_z.astype(jnp.float32) - (total_z - 1) / 2.0)
    return drift_y, spin, (total_y - 1) / 2.0


def drifts_by_half(columns, depth):
    _, column_y, _ = place()
    drift_y, spin, centre_y = drifts_of(columns, depth)
    sublane = lax.broadcasted_iota(jnp.int32, (8, LANE), 0)
    halves = []
    for half in range(SPAN_Y // 8):
        here_y = sublane + (column_y * SPAN_Y + 8 * half)
        halves.append(spin * (here_y.astype(jnp.float32) - centre_y))
    return drift_y, halves


def pull_from(field, base):
    def pull(i):
        step_x, step_y, step_z = VELOCITIES[i]
        return turned(field[pl.ds(i * FIELD + base - step_x * PITCH - step_y, 8), :], step_z)

    return pull


def settle_all(layers, columns, depth, own, edge, zall, zedge, field, start, later):
    layer, _, column_z = place()

    def halves(yhi, carry):
        def chunks(chunk, carry):
            for ylo in range(YLO):
                values = chunk_values(own, edge, zall, zedge, chunk, yhi, ylo, column_z)
                post = marked(values[:POPS], values[POPS], inside_lanes(8, column_z))
                row = (8 * chunk + 2) * PITCH + FIRST + YLO * yhi + ylo
                for i in range(POPS):
                    field[pl.ds(i * FIELD + row, 8, stride=PITCH), :] = post[i]
                    target = (i * SPAN_X + 8 * chunk) * SPAN_Y + YLO * yhi + ylo
                    start[pl.ds(target, 8, stride=SPAN_Y), :] = values[i]
            return carry

        lax.fori_loop(0, SPAN_X // 8, chunks, 0)
        for ylo in range(YLO):
            values = chunk_values(own, edge, zall, zedge, None, yhi, ylo, column_z)
            inside = inside_lanes(4, column_z) & halo_x_inside(layer, layers)
            post = marked(values[:POPS], values[POPS], inside)
            for first, side in ((0, 0), (EXT_X - 2, 2)):
                row = first * PITCH + FIRST + YLO * yhi + ylo
                for i in range(POPS):
                    field[pl.ds(i * FIELD + row, 2, stride=PITCH), :] = post[i][side : side + 2]
        return carry

    lax.fori_loop(0, SPAN_Y // YLO, halves, 0)
    drift_y, drifts = drifts_by_half(columns, depth)

    def first_step(x, carry):
        for half in range(SPAN_Y // 8):
            base = pl.multiple_of(x * PITCH + FIRST + 8 * half, 8)
            old = [field[pl.ds(i * FIELD + base, 8), :] for i in range(POPS)]
            values = streamed(pull_from(field, base), old, drift_y, drifts[half])
            post, _ = collide(values)
            wall = old[0] < WALL_BELOW
            for i in range(POPS):
                later[pl.ds(i * FIELD + base, 8), :] = jnp.where(wall, old[0], post[i])
        return carry

    lax.fori_loop(1, EXT_X - 1, first_step, 0)


def finish(columns, depth, rim_low, rim_high, field, start, later_in, out, later, low, high, result, sems):
    del later_in
    _, column_y, column_z = place()
    flat = (lanes() + 2 * column_z) % LANE
    for source, target, there in ((rim_low, low, column_y > 0), (rim_high, high, column_y < columns - 1)):
        for chunk in range(5):
            blocks = [source[pl.ds(block * EXT_X + 8 * chunk, 8), :] for block in range(RIM_BLOCKS)]
            for plane in range(RIM):
                block, begin = divmod(plane * EXT_Z, LANE)
                shift = (2 * LANE - begin - 2 * column_z) % LANE
                value = pltpu.roll(blocks[block], shift, 1)
                if begin + EXT_Z > LANE:
                    value = jnp.where(flat < LANE - begin, value, pltpu.roll(blocks[block + 1], shift, 1))
                value = jnp.where((flat < EXT_Z) & there, value, OUTSIDE)
                target[pl.ds(plane * GRID_X + 8 * chunk, 8), :] = value

    drift_y, spin, centre_y = drifts_of(columns, depth)
    for source, face, rim in ((low, 0, RIM_UP), (high, SPAN_Y - 1, RIM_DOWN)):
        outer = {i: POPS + n for n, i in enumerate(rim)}
        toward = VELOCITIES[rim[0]][1]
        for y in (face - toward, face):
            drift_z = spin * ((column_y * SPAN_Y + y).astype(jnp.float32) - centre_y)
            for chunk in range(5):
                first = 1 + 8 * chunk
                size = min(8, EXT_X - 1 - first)

                def value_at(i, x, y):
                    if y == face - 2 * toward:
                        return source[pl.ds(outer[i] * GRID_X + x, size), :]
                    if y == face - toward:
                        return source[pl.ds(i * GRID_X + x, size), :]
                    return field[pl.ds(i * FIELD + x * PITCH + FIRST + y, size, stride=PITCH), :]

                def pull(i):
                    step_x, step_y, step_z = VELOCITIES[i]
                    return turned(value_at(i, first - step_x, y - step_y), step_z)

                old = [value_at(i, first, y) for i in range(POPS)]
                values = streamed(pull, old, drift_y[:size], drift_z)
                post, _ = collide(values)
                wall = old[0] < WALL_BELOW
                for i in range(POPS) if y == face else rim:
                    row = i * FIELD + first * PITCH + FIRST + y
                    later[pl.ds(row, size, stride=PITCH), :] = jnp.where(wall, old[0], post[i])

    drift_y, drifts = drifts_by_half(columns, depth)
    quarter = SPAN_X // 4

    def leave(n):
        part = pl.ds(n * quarter, quarter)
        return pltpu.make_async_copy(result.at[:, part], out.at[:, part], sems.at[n])

    def second_step(x, carry):
        for half in range(SPAN_Y // 8):
            base = pl.multiple_of((x + 2) * PITCH + FIRST + 8 * half, 8)
            old = [later[pl.ds(i * FIELD + base, 8), :] for i in range(POPS)]
            values = streamed(pull_from(later, base), old, drift_y, drifts[half])
            wall = old[0] < WALL_BELOW
            for i in range(POPS):
                first = pl.multiple_of((i * SPAN_X + x) * SPAN_Y + 8 * half, 8)
                value = jnp.where(wall, start[pl.ds(first, 8), :], values[i])
                result[i, x, pl.ds(8 * half, 8), :] = value[:, :SPAN_Z]
        return carry

    for n in range(4):
        lax.fori_loop(n * quarter, (n + 1) * quarter, second_step, 0)
        leave(n).start()
    for n in range(4):
        leave(n).wait()


def rows_of(count):
    return jax.ShapeDtypeStruct((count, LANE), jnp.float32)


def kept(count):
    return VMEM((count, LANE), jnp.float32)


def params(mib):
    return pltpu.CompilerParams(vmem_limit_bytes=mib * 2**20)


def shards(populations, solid_cells, block_pos):
    layers = lax.axis_size("stream")
    columns = lax.axis_size("cy")
    depth = lax.axis_size("cz")
    rows = block_pos.shape[0]
    vmem = pl.BlockSpec(memory_space=VMEM)
    hbm = pl.BlockSpec(memory_space=pltpu.HBM)
    populations = pltpu.with_memory_space_constraint(populations, pltpu.HBM)
    solid_cells = pltpu.with_memory_space_constraint(solid_cells, pltpu.HBM)
    places = pltpu.with_memory_space_constraint(block_pos.T, pltpu.HBM)
    place_scratch = SMEM((3, rows), jnp.int32)
    mark_scratch = [VMEM((rows, EDGE**3), jnp.int32), VMEM((rows * TILES, LANE), jnp.float32)]

    send_up, send_down = pl.pallas_call(
        pack_stream,
        out_shape=(kept(SENT_ROWS), kept(SENT_ROWS)),
        in_specs=[hbm, hbm, hbm],
        out_specs=(vmem, vmem),
        scratch_shapes=[place_scratch, SMEM((LAYERS * BZD,), jnp.int32)]
        + mark_scratch
        + [
            VMEM((2 * MOVE_CAP, POPS, EDGE**3), jnp.float32),
            VMEM((2 * BZD, POPS, SLAB * LANE), jnp.float32),
            VMEM((PLANES * 2 * FACE, LANE), jnp.float32),
            pltpu.SemaphoreType.DMA((2 * MOVE_CAP + 2 * BZD + 2,)),
        ],
        compiler_params=params(16),
        name="pack_stream",
    )(places, solid_cells, populations)
    up = [(i, i + 1) for i in range(layers - 1)]
    down = [(i + 1, i) for i in range(layers - 1)]
    from_low = lax.ppermute(send_up, "stream", up)
    from_high = lax.ppermute(send_down, "stream", down)

    own, zpack, zsend_up, zsend_down = pl.pallas_call(
        pack_own,
        out_shape=(kept(LAYERS * BZD * BLOCK), kept(ZMETA + 8), kept(DIAG), kept(DIAG)),
        in_specs=[hbm, hbm, hbm],
        out_specs=(vmem,) * 4,
        scratch_shapes=[place_scratch]
        + mark_scratch
        + [
            VMEM((rows, POPS, EDGE**3), jnp.float32),
            pltpu.SemaphoreType.DMA((rows + 2,)),
        ],
        compiler_params=params(16),
        name="pack_own",
    )(places, solid_cells, populations)
    swap = [(i, depth - 1 - i) for i in range(depth)]
    zin = lax.ppermute(zpack, "cz", swap)
    zup_pairs = [(s * depth + c, t * depth + d) for s, t in up for c, d in swap]
    zdown_pairs = [(s * depth + c, t * depth + d) for s, t in down for c, d in swap]
    z_low = lax.ppermute(zsend_up, ("stream", "cz"), zup_pairs)
    z_high = lax.ppermute(zsend_down, ("stream", "cz"), zdown_pairs)

    own, edge, zall, zedge, rim_up, rim_down = pl.pallas_call(
        functools.partial(settle_rim, layers),
        out_shape=(
            kept(LAYERS * BZD * BLOCK),
            kept(POPS * 4 * FACE),
            kept(LAYERS * ZROWS),
            kept(ZGROUPS * 8),
            kept(RIM_ROWS),
            kept(RIM_ROWS),
        ),
        in_specs=[hbm] + [vmem] * 6,
        out_specs=(vmem,) * 6,
        scratch_shapes=[
            place_scratch,
            VMEM((RIM * GRID_X, LANE), jnp.float32),
            VMEM((RIM * GRID_X, LANE), jnp.float32),
            pltpu.SemaphoreType.DMA,
        ],
        input_output_aliases={6: 0},
        compiler_params=params(16),
        name="settle_rim",
    )(places, from_low, from_high, zin, z_low, z_high, own)
    cy_up = [(i, i + 1) for i in range(columns - 1)]
    cy_down = [(i + 1, i) for i in range(columns - 1)]
    rim_low = lax.ppermute(rim_up, "cy", cy_up)
    rim_high = lax.ppermute(rim_down, "cy", cy_down)

    field, start, later = pl.pallas_call(
        functools.partial(settle_all, layers, columns, depth),
        out_shape=(kept(POPS * FIELD), kept(POPS * SPAN_X * SPAN_Y), kept(POPS * FIELD)),
        in_specs=[vmem] * 4,
        out_specs=(vmem,) * 3,
        compiler_params=params(16),
        name="settle_all",
    )(own, edge, zall, zedge)

    out, _ = pl.pallas_call(
        functools.partial(finish, columns, depth),
        out_shape=(
            jax.ShapeDtypeStruct((POPS, SPAN_X, SPAN_Y, SPAN_Z), jnp.float32),
            kept(POPS * FIELD),
        ),
        in_specs=[vmem] * 5,
        out_specs=(hbm, vmem),
        scratch_shapes=[
            VMEM((RIM * GRID_X, LANE), jnp.float32),
            VMEM((RIM * GRID_X, LANE), jnp.float32),
            VMEM((POPS, SPAN_X, SPAN_Y, SPAN_Z), jnp.float32),
            pltpu.SemaphoreType.DMA((4,)),
        ],
        input_output_aliases={4: 1},
        compiler_params=params(16),
        name="finish",
    )(rim_low, rim_high, field, start, later)
    return out


def solution(mesh):
    in_specs = (
        P(("stream", "cy", "cz"), None, None),
        P(("stream", "cy", "cz"), None),
        P(("stream", "cy", "cz"), None),
    )
    out_specs = P(None, "stream", "cy", "cz")
    return jax.shard_map(shards, mesh=mesh, in_specs=in_specs, out_specs=out_specs, check_vma=False)
```

```python
import functools

import jax
import jax.numpy as jnp
from jax import lax
from jax.experimental import pallas as pl
from jax.experimental.pallas import tpu as pltpu
from jax.sharding import PartitionSpec as P

EDGE = 16
BXD = 2
BYD = 1
BZD = 4
MOVE_CAP = 2

VELOCITIES = (
    (0, 0, 0),
    (1, 0, 0),
    (-1, 0, 0),
    (0, 1, 0),
    (0, -1, 0),
    (0, 0, 1),
    (0, 0, -1),
    (1, 1, 0),
    (-1, -1, 0),
    (1, -1, 0),
    (-1, 1, 0),
    (1, 0, 1),
    (-1, 0, -1),
    (1, 0, -1),
    (-1, 0, 1),
    (0, 1, 1),
    (0, -1, -1),
    (0, 1, -1),
    (0, -1, 1),
)
WEIGHTS = (1.0 / 3.0,) + (1.0 / 18.0,) * 6 + (1.0 / 36.0,) * 12
OPPOSITE = (0, 2, 1, 4, 3, 6, 5, 8, 7, 10, 9, 12, 11, 14, 13, 16, 15, 18, 17)
OMEGA_EVEN = 1.25
OMEGA_ODD = 1.0 / 1.125

POPS = 19
PLANES = 20
LANE = 128
TILES = EDGE**3 // LANE
BLOCK = PLANES * TILES
YLO = LANE // EDGE
SLAB = 4
GROUPS = ((0, 8), (8, 8), (16, 3))
SENT_SLABS = BLOCK + 8
LAYERS = BXD + 2
ZGROUPS = 3
ZROWS = ZGROUPS * TILES
ZMETA = LAYERS * ZROWS
DIAG = ZROWS + ZGROUPS * SLAB

SPAN_X = BXD * EDGE
SPAN_Y = BYD * EDGE
SPAN_Z = BZD * EDGE
PITCH = SPAN_Y + 8
FIRST = 8
FIELD = (SPAN_X + 4) * PITCH + 16
EXT_X = SPAN_X + 4
EXT_Z = SPAN_Z + 2
RIM_UP = tuple(i for i in range(POPS) if VELOCITIES[i][1] == 1)
RIM_DOWN = tuple(i for i in range(POPS) if VELOCITIES[i][1] == -1)
RIM = POPS + len(RIM_UP)
AHEAD = tuple(i for i in range(POPS) if VELOCITIES[i][0] == 1)
BACK = tuple(i for i in range(POPS) if VELOCITIES[i][0] == -1)
FACE = 2 * BZD
SENT_ROWS = SENT_SLABS + RIM * FACE
RIM_BLOCKS = -(-RIM * EXT_Z // LANE)
RIM_ROWS = RIM_BLOCKS * EXT_X + 4
GRID_X = 48

ROTOR = -1.0e30
OUTSIDE = -2.0e30
WALL_BELOW = -1.0e20
OUT_BELOW = -1.5e30

VMEM = pltpu.VMEM
SMEM = pltpu.SMEM


def lanes():
    return lax.broadcasted_iota(jnp.int32, (8, LANE), 1)


def collide(f):
    even = [None] * POPS
    odd = [None] * POPS
    for i in range(1, POPS, 2):
        even[i] = f[i] + f[i + 1]
        odd[i] = f[i] - f[i + 1]
    density = f[0]
    for i in range(1, POPS, 2):
        density = density + even[i]
    flow = []
    for axis in range(3):
        total = None
        for i in range(1, POPS, 2):
            sign = VELOCITIES[i][axis]
            if sign == 0:
                continue
            if total is None:
                total = odd[i] if sign == 1 else -odd[i]
            else:
                total = total + odd[i] if sign == 1 else total - odd[i]
        flow.append(total)
    inverse = 1.0 / density
    velocity = [part * inverse for part in flow]
    square = velocity[0] * velocity[0] + velocity[1] * velocity[1] + velocity[2] * velocity[2]
    base = density * (1.0 - 1.5 * square)
    post = [None] * POPS
    post[0] = (1.0 - OMEGA_EVEN) * f[0] + (OMEGA_EVEN * WEIGHTS[0]) * base
    shared = {}
    for weight in (WEIGHTS[1], WEIGHTS[7]):
        shared[weight] = ((OMEGA_EVEN * weight) * base, (OMEGA_EVEN * weight * 4.5) * density,
                          (OMEGA_ODD * weight * 3.0) * density)
    for i in range(1, POPS, 2):
        projected = None
        for axis in range(3):
            sign = VELOCITIES[i][axis]
            if sign == 0:
                continue
            if projected is None:
                projected = velocity[axis] if sign == 1 else -velocity[axis]
            else:
                projected = projected + velocity[axis] if sign == 1 else projected - velocity[axis]
        low, curve, slope = shared[WEIGHTS[i]]
        even_part = (0.5 - 0.5 * OMEGA_EVEN) * even[i] + (low + curve * (projected * projected))
        odd_part = (0.5 - 0.5 * OMEGA_ODD) * odd[i] + slope * projected
        post[i] = even_part + odd_part
        post[i + 1] = even_part - odd_part
    return post, density


def pushes(density, drift_y, drift_z):
    along_y = density * drift_y
    along_z = density * drift_z
    out = [None] * POPS
    for i in range(1, POPS):
        _, step_y, step_z = VELOCITIES[i]
        total = None
        for sign, part in ((step_y, along_y), (step_z, along_z)):
            if sign == 0:
                continue
            if total is None:
                total = part if sign == 1 else -part
            else:
                total = total + part if sign == 1 else total - part
        if total is not None:
            out[i] = (6.0 * WEIGHTS[i]) * total
    return out


def total_of(parts):
    parts = list(parts)
    while len(parts) > 1:
        pairs = [parts[n] + parts[n + 1] for n in range(0, len(parts) - 1, 2)]
        parts = pairs + parts[len(parts) - len(parts) % 2 :]
    return parts[0]


def streamed(pull, own, drift_y, drift_z):
    push = pushes(total_of(own), drift_y, drift_z)
    out = [own[0]]
    for i in range(1, POPS):
        pulled = pull(i)
        bounced = own[OPPOSITE[i]]
        blocked = pulled < WALL_BELOW
        if push[i] is not None:
            bounced = jnp.where(pulled < OUT_BELOW, bounced, bounced + push[i])
        out.append(jnp.where(blocked, bounced, pulled))
    return out


def place():
    return lax.axis_index("stream"), lax.axis_index("cy"), lax.axis_index("cz")


def slot_of(pos, row, layer, column_z):
    slot = (pos[0, row] - (layer * BXD - 1)) * BZD + (pos[2, row] - column_z * BZD)
    return jnp.clip(slot, 0, LAYERS * BZD - 1)


def fill_table(pos, table):
    layer, _, column_z = place()
    for entry in range(LAYERS * BZD):
        table[entry] = -1
    for row in range(pos.shape[1]):

        @pl.when(pos[0, row] >= 0)
        def _(row=row):
            table[slot_of(pos, row, layer, column_z)] = row


def spread_marks(marks, dense):
    rows = marks.shape[0]
    for first in range(0, rows, 8):
        size = min(8, rows - first)
        for tile in range(TILES):
            value = marks[first : first + size, tile * LANE : (tile + 1) * LANE].astype(jnp.float32)
            dense[pl.ds(first * TILES + tile, size, stride=TILES), :] = value


def collide_block(ref, base):
    for part in range(TILES // 8):
        old = [ref[pl.ds(base + i * TILES + 8 * part, 8), :] for i in range(POPS)]
        mark = ref[pl.ds(base + POPS * TILES + 8 * part, 8), :] > 0.5
        post, _ = collide(old)
        for i in range(POPS):
            ref[pl.ds(base + i * TILES + 8 * part, 8), :] = jnp.where(mark, old[i], post[i])


def pack_block(out, base, stage, dense, row):
    out[pl.ds(base + POPS * TILES, TILES), :] = dense[pl.ds(pl.multiple_of(row * TILES, 8), TILES), :]
    for tile in range(TILES):
        for group, size in GROUPS:
            value = stage[group : group + size, tile * LANE : (tile + 1) * LANE]
            out[pl.ds(base + group * TILES + tile, size, stride=TILES), :] = value
    collide_block(out, base)


def pack_stream(part, places, marks_in, pops, up, down, pos, table, marks, dense, blocks, slabs, strip, sems):
    mark_copy = pltpu.make_async_copy(marks_in, marks, sems.at[0])
    mark_copy.start()
    place_copy = pltpu.make_async_copy(places, pos, sems.at[1])
    place_copy.start()
    down_copy = pltpu.make_async_copy(pops.at[part], blocks.at[1], sems.at[3])
    down_copy.start()
    place_copy.wait()
    rows = pos.shape[1]
    count = 0
    for row in range(rows):
        count = count + jnp.where(pos[0, row] >= 0, 1, 0)
    last = jnp.clip(count - MOVE_CAP, 0, rows - MOVE_CAP) + part
    up_copy = pltpu.make_async_copy(pops.at[last], blocks.at[0], sems.at[2])
    up_copy.start()
    slab_rows = []
    slab_copies = []
    if part == MOVE_CAP - 1:
        fill_table(pos, table)
        for side in range(2):
            for bz in range(BZD):
                row = jnp.maximum(table[(2 - side) * BZD + bz], 0)
                n = side * BZD + bz
                first = (TILES - SLAB) * LANE if side == 0 else 0
                slab_rows.append(row)
                slab_copies.append(
                    pltpu.make_async_copy(
                        pops.at[row, :, pl.ds(first, SLAB * LANE)], slabs.at[n], sems.at[4 + n]
                    )
                )
        for copy in slab_copies:
            copy.start()
    mark_copy.wait()
    spread_marks(marks, dense)
    for n, (out, row, copy) in ((1, (down, part, down_copy)), (0, (up, last, up_copy))):
        for k, axis in ((0, 0), (1, 2)):
            value = jnp.full((1, LANE), pos[axis, row], jnp.int32).astype(jnp.float32)
            out[pl.ds(BLOCK + k, 1), :] = value
        copy.wait()
        pack_block(out, 0, blocks.at[n], dense, row)
    if part < MOVE_CAP - 1:
        return
    for side, out in enumerate((up, down)):
        for bz in range(BZD):
            n = side * BZD + bz
            first = slab_rows[n] * TILES + (TILES - SLAB if side == 0 else 0)
            slab_copies[n].wait()
            for x in range(2):
                for yhi in range(2):
                    q = 2 * x + yhi
                    row = x * FACE + 2 * bz + yhi
                    for group, size in GROUPS:
                        value = slabs[n, group : group + size, q * LANE : (q + 1) * LANE]
                        strip[pl.ds(group * 2 * FACE + row, size, stride=2 * FACE), :] = value
                row = POPS * 2 * FACE + x * FACE + 2 * bz
                strip[pl.ds(row, 2), :] = dense[pl.ds(first + 2 * x, 2), :]
        inner = 1 if side == 0 else 0
        for x in range(2):
            old = [strip[pl.ds(i * 2 * FACE + x * FACE, FACE), :] for i in range(POPS)]
            mark = strip[pl.ds(POPS * 2 * FACE + x * FACE, FACE), :] > 0.5
            post, _ = collide(old)
            if x == inner:
                pairs = [(i, i) for i in range(POPS)]
            else:
                pairs = [(POPS + n, i) for n, i in enumerate(AHEAD if side == 0 else BACK)]
            for plane, i in pairs:
                out[pl.ds(SENT_SLABS + plane * FACE, FACE), :] = jnp.where(mark, ROTOR, post[i])


def pack_own(places, marks_in, pops, own, zpack, zup, zdown, pos, marks, dense, stage, sems):
    layer, _, column_z = place()
    rows = pos.shape[1]
    mark_copy = pltpu.make_async_copy(marks_in, marks, sems.at[rows])
    mark_copy.start()
    place_copy = pltpu.make_async_copy(places, pos, sems.at[rows + 1])
    place_copy.start()
    copies = [pltpu.make_async_copy(pops.at[r], stage.at[r], sems.at[r]) for r in range(rows)]
    for copy in copies:
        copy.start()
    mark_copy.wait()
    spread_marks(marks, dense)
    place_copy.wait()

    def settle(row, carry):
        pltpu.make_async_copy(pops.at[row], stage.at[row], sems.at[row]).wait()

        @pl.when(pos[0, row] >= 0)
        def _():
            base = pl.multiple_of(slot_of(pos, row, layer, column_z) * BLOCK, 8)
            pack_block(own, base, stage.at[row], dense, row)

        return carry

    lax.fori_loop(0, rows, settle, 0)
    edge_bz = jnp.where(column_z == 0, BZD - 1, 0)
    first_c = jnp.where(column_z == 0, EDGE - 2, 0)
    spot = (lanes() % EDGE) // 2
    for held in range(LAYERS):
        base = pl.multiple_of((held * BZD + edge_bz) * BLOCK, 8)
        for group in range(ZGROUPS):
            for part in range(TILES // 8):
                total = jnp.zeros((8, LANE), jnp.float32)
                for k in range(min(8, PLANES - group * 8)):
                    value = own[pl.ds(base + (group * 8 + k) * TILES + part * 8, 8), :]
                    value = pltpu.roll(value, (2 * k - first_c + LANE) % LANE, 1)
                    total = jnp.where(spot == k, value, total)
                zpack[pl.ds(held * ZROWS + group * TILES + part * 8, 8), :] = total
    present = [jnp.int32(0)] * LAYERS
    for row in range(rows):
        slot = slot_of(pos, row, layer, column_z)
        for held in range(LAYERS):
            hit = (pos[0, row] >= 0) & (slot == held * BZD + edge_bz)
            present[held] = jnp.where(hit, 1, present[held])
    sublane = lax.broadcasted_iota(jnp.int32, (8, LANE), 0)
    flags = jnp.zeros((8, LANE), jnp.int32)
    for held in range(LAYERS):
        flags = jnp.where(sublane == held, present[held], flags)
    zpack[pl.ds(ZMETA, 8), :] = flags.astype(jnp.float32)
    zup[pl.ds(0, ZROWS), :] = zpack[pl.ds(3 * ZROWS, ZROWS), :]
    zdown[pl.ds(0, ZROWS), :] = zpack[pl.ds(0, ZROWS), :]
    for group in range(ZGROUPS):
        target = pl.ds(ZROWS + group * SLAB, SLAB)
        zup[target, :] = zpack[pl.ds(2 * ZROWS + group * TILES + TILES - SLAB, SLAB), :]
        zdown[target, :] = zpack[pl.ds(ZROWS + group * TILES, SLAB), :]


def gathered(parts, zvalue, spot, ylo, column_z):
    lane = lanes()
    rows = parts[0].shape[0]
    lane = lane[:rows]
    total = None
    for bz in range(BZD):
        shift = (bz * EDGE - ylo * EDGE) % LANE
        value = pltpu.roll(parts[bz], shift, 1) if shift else parts[bz]
        total = value if total is None else jnp.where(lane // EDGE == bz, value, total)
    goal = jnp.where(column_z == 0, SPAN_Z, LANE - 2)
    zvalue = pltpu.roll(zvalue, (goal - (ylo * EDGE + 2 * spot) + LANE) % LANE, 1)
    return jnp.where(lane >= SPAN_Z, zvalue, total)


def gathered_rows(parts, zvalue, spot, column_z):
    lane = lanes()[: parts[0].shape[0]]
    single = (lane // EDGE) % 2 == 1
    double = (lane // (2 * EDGE)) % 2 == 1
    main = lane < SPAN_Z
    pairs = []
    for n in (0, 2):
        even = jnp.where(single, pltpu.roll(parts[n + 1], EDGE, 1), parts[n])
        odd = jnp.where(single, parts[n + 1], pltpu.roll(parts[n], LANE - EDGE, 1))
        pairs.append((even, odd))
    goal = jnp.where(column_z == 0, SPAN_Z, LANE - 2)
    out = [None] * YLO
    for r in range(4):
        low, high = pairs[0][r % 2], pairs[1][r % 2]
        if r < 2:
            both = jnp.where(double, pltpu.roll(high, 2 * EDGE, 1), low)
        else:
            both = jnp.where(double, high, pltpu.roll(low, LANE - 2 * EDGE, 1))
        beyond = pltpu.roll(zvalue, (goal - (r * EDGE + 2 * spot) + LANE) % LANE, 1)
        out[r] = jnp.where(main, both, beyond)
        out[r + 4] = pltpu.roll(jnp.where(main, beyond, both), SPAN_Z, 1)
    return out


def inside_lanes(rows, column_z):
    lane = lanes()[:rows]
    low = (column_z == 0) & (lane >= SPAN_Z) & (lane < SPAN_Z + 2)
    high = (column_z != 0) & (lane >= LANE - 2)
    return (lane < SPAN_Z) | low | high


def marked(post, mark, inside):
    flag = jnp.where(inside, jnp.where(mark > 0.5, ROTOR, 0.0), OUTSIDE)
    wall = flag < WALL_BELOW
    return [jnp.where(wall, flag, value) for value in post]


def plane_parts(own, edge, zall, zedge, chunk, yhi, plane):
    group = plane // 8
    if chunk is None:
        if plane == POPS:
            parts = [jnp.zeros((4, LANE), jnp.float32)] * BZD
        else:
            parts = [edge[pl.ds(plane * 4 * FACE + 2 * bz + yhi, 4, stride=FACE), :] for bz in range(BZD)]
        return parts, zedge[pl.ds(group * 8 + yhi, 4, stride=2), :]
    held, half = 1 + chunk // 2, chunk % 2
    parts = []
    for bz in range(BZD):
        base = (held * BZD + bz) * BLOCK + plane * TILES + half * EDGE + yhi
        parts.append(own[pl.ds(base, 8, stride=2), :])
    return parts, zall[pl.ds(held * ZROWS + group * TILES + half * EDGE + yhi, 8, stride=2), :]


def chunk_values(own, edge, zall, zedge, chunk, yhi, ylo, column_z):
    out = []
    for plane in range(PLANES):
        parts, zvalue = plane_parts(own, edge, zall, zedge, chunk, yhi, plane)
        out.append(gathered(parts, zvalue, plane % 8, ylo, column_z))
    return out


def halo_x_inside(layer, layers):
    row = lax.broadcasted_iota(jnp.int32, (4, LANE), 0)
    low = (row < 2) & (layer > 0)
    high = (row >= 2) & (layer < layers - 1)
    return low | high


def settle_rim(layers, places, up_first, down_first, up, down, zin, zup, zdown, own_in, own, edge, zall, zedge, rim_up, rim_down, pos, post_up, post_down, sem):
    del own_in
    layer, _, column_z = place()
    place_copy = pltpu.make_async_copy(places, pos, sem)
    place_copy.start()
    for n, arrived in enumerate((up_first, down_first, up, down)):
        bx = arrived[pl.ds(BLOCK, 1), :].astype(jnp.int32)
        bz = arrived[pl.ds(BLOCK + 1, 1), :].astype(jnp.int32)
        code = (bx - layer * BXD) * BZD + (bz - column_z * BZD)
        mine = (bx >= layer * BXD) & (bx < (layer + 1) * BXD)
        first = layer == 0 if n % 2 == 0 else layer == layers - 1
        code = jnp.max(jnp.where(mine, code, -1))

        @pl.when((code >= 0) & jnp.logical_not(first))
        def _(arrived=arrived, code=code):
            base = pl.multiple_of((jnp.clip(code, 0, BXD * BZD - 1) + BZD) * BLOCK, 8)
            for k in range(BLOCK // 8):
                own[pl.ds(base + 8 * k, 8), :] = arrived[pl.ds(8 * k, 8), :]

    place_copy.wait()
    for side, arrived in enumerate((up, down)):
        inner, outer = (1, 0) if side == 0 else (2, 3)
        pairs = [(i, i, inner) for i in range(POPS)]
        pairs += [(POPS + n, i, outer) for n, i in enumerate(AHEAD if side == 0 else BACK)]
        for plane, i, x in pairs:
            edge[pl.ds((i * 4 + x) * FACE, FACE), :] = arrived[pl.ds(SENT_SLABS + plane * FACE, FACE), :]
        for bz in range(BZD):
            here = jnp.int32(0)
            goal = (0 if side == 0 else LAYERS - 1) * BZD + bz
            for row in range(pos.shape[1]):
                hit = (pos[0, row] >= 0) & (slot_of(pos, row, layer, column_z) == goal)
                here = jnp.where(hit, 1, here)

            @pl.when(here == 1)
            def _(side=side, pairs=pairs, goal=goal, bz=bz):
                first = goal * BLOCK + (TILES - SLAB if side == 0 else 0)
                for _, i, x in pairs:
                    shift = 2 * (x if side == 0 else x - 2)
                    mark = own[pl.ds(first + POPS * TILES + shift, 2), :] > 0.5
                    value = own[pl.ds(first + i * TILES + shift, 2), :]
                    edge[pl.ds((i * 4 + x) * FACE + 2 * bz, 2), :] = jnp.where(mark, ROTOR, value)

    for held in range(LAYERS):
        flag = zin[pl.ds(ZMETA + held, 1), :] > 0.5
        for group in range(ZGROUPS):
            if held == 1 or held == 2:
                for part in range(TILES // 8):
                    rows = pl.ds(held * ZROWS + group * TILES + part * 8, 8)
                    source = zup if held == 1 else zdown
                    other = source[pl.ds(group * TILES + part * 8, 8), :]
                    zall[rows, :] = jnp.where(flag, zin[rows, :], other)
            else:
                side = 0 if held == 0 else 1
                source = zup if held == 0 else zdown
                first = TILES - SLAB if held == 0 else 0
                mine = zin[pl.ds(held * ZROWS + group * TILES + first, SLAB), :]
                other = source[pl.ds(ZROWS + group * SLAB, SLAB), :]
                zedge[pl.ds(group * 8 + side * SLAB, SLAB), :] = jnp.where(flag, mine, other)
    for chunk in (0, 1, 2, 3, None):
        for y in (0, 1, SPAN_Y - 2, SPAN_Y - 1):
            values = chunk_values(own, edge, zall, zedge, chunk, y // YLO, y % YLO, column_z)
            inside = inside_lanes(values[0].shape[0], column_z)
            if chunk is None:
                inside = inside & halo_x_inside(layer, layers)
            post = marked(values[:POPS], values[POPS], inside)
            target = post_down if y < 2 else post_up
            rim = RIM_DOWN if y < 2 else RIM_UP
            if y in (0, SPAN_Y - 1):
                pairs = [(i, i) for i in range(POPS)]
            else:
                pairs = [(POPS + n, i) for n, i in enumerate(rim)]
            for plane, i in pairs:
                if chunk is None:
                    target[pl.ds(plane * GRID_X, 2), :] = post[i][:2]
                    target[pl.ds(plane * GRID_X + EXT_X - 2, 2), :] = post[i][2:]
                else:
                    target[pl.ds(plane * GRID_X + 2 + 8 * chunk, 8), :] = post[i]
    lane = lanes()
    for source, target in ((post_up, rim_up), (post_down, rim_down)):
        for chunk in range(5):
            size = min(8, EXT_X - 8 * chunk)
            for block in range(RIM_BLOCKS):
                total = jnp.zeros((8, LANE), jnp.float32)
                for plane in range(RIM):
                    begin = plane * EXT_Z - block * LANE
                    if begin >= LANE or begin + EXT_Z <= 0:
                        continue
                    value = source[pl.ds(plane * GRID_X + 8 * chunk, 8), :]
                    value = pltpu.roll(value, (begin + LANE + 2 * column_z) % LANE, 1)
                    total = jnp.where((lane >= begin) & (lane < begin + EXT_Z), value, total)
                target[pl.ds(block * EXT_X + 8 * chunk, size), :] = total[:size]


def turned(value, step_z):
    return pltpu.roll(value, step_z % LANE, 1) if step_z else value


def drifts_of(columns, depth):
    _, _, column_z = place()
    lane = lanes()
    total_y = SPAN_Y * columns
    total_z = SPAN_Z * depth
    spin = 0.2 / (total_y + total_z)
    here_z = jnp.where(lane < SPAN_Z + 8, lane, lane - LANE) + column_z * SPAN_Z
    drift_y = -spin * (here_z.astype(jnp.float32) - (total_z - 1) / 2.0)
    return drift_y, spin, (total_y - 1) / 2.0


def drifts_by_half(columns, depth):
    _, column_y, _ = place()
    drift_y, spin, centre_y = drifts_of(columns, depth)
    sublane = lax.broadcasted_iota(jnp.int32, (8, LANE), 0)
    halves = []
    for half in range(SPAN_Y // 8):
        here_y = sublane + (column_y * SPAN_Y + 8 * half)
        halves.append(spin * (here_y.astype(jnp.float32) - centre_y))
    return drift_y, halves


def pull_from(field, base):
    def pull(i):
        step_x, step_y, step_z = VELOCITIES[i]
        return turned(field[pl.ds(i * FIELD + base - step_x * PITCH - step_y, 8), :], step_z)

    return pull


def settle_all(layers, columns, depth, own, edge, zall, zedge, field, start, later):
    layer, _, column_z = place()

    def flags_of(mark, inside):
        return [jnp.where(inside, jnp.where(value > 0.5, ROTOR, 0.0), OUTSIDE) for value in mark]

    def halves(yhi, carry):
        def rows_of_plane(chunk, plane):
            parts, zvalue = plane_parts(own, edge, zall, zedge, chunk, yhi, plane)
            return gathered_rows(parts, zvalue, plane % 8, column_z)

        def chunks(chunk, carry):
            flags = flags_of(rows_of_plane(chunk, POPS), inside_lanes(8, column_z))
            for i in range(POPS):
                values = rows_of_plane(chunk, i)
                for ylo in range(YLO):
                    row = i * FIELD + (8 * chunk + 2) * PITCH + FIRST + YLO * yhi + ylo
                    value = jnp.where(flags[ylo] < WALL_BELOW, flags[ylo], values[ylo])
                    field[pl.ds(row, 8, stride=PITCH), :] = value
                    target = (i * SPAN_X + 8 * chunk) * SPAN_Y + YLO * yhi + ylo
                    start[pl.ds(target, 8, stride=SPAN_Y), :] = values[ylo]
            return carry

        lax.fori_loop(0, SPAN_X // 8, chunks, 0)
        inside = inside_lanes(4, column_z) & halo_x_inside(layer, layers)
        flags = flags_of(rows_of_plane(None, POPS), inside)
        for i in range(POPS):
            values = rows_of_plane(None, i)
            for ylo in range(YLO):
                value = jnp.where(flags[ylo] < WALL_BELOW, flags[ylo], values[ylo])
                for first, side in ((0, 0), (EXT_X - 2, 2)):
                    row = i * FIELD + first * PITCH + FIRST + YLO * yhi + ylo
                    field[pl.ds(row, 2, stride=PITCH), :] = value[side : side + 2]
        return carry

    lax.fori_loop(0, SPAN_Y // YLO, halves, 0)
    drift_y, drifts = drifts_by_half(columns, depth)

    def first_step(x, carry):
        for half in range(SPAN_Y // 8):
            base = pl.multiple_of(x * PITCH + FIRST + 8 * half, 8)
            old = [field[pl.ds(i * FIELD + base, 8), :] for i in range(POPS)]
            values = streamed(pull_from(field, base), old, drift_y, drifts[half])
            post, _ = collide(values)
            wall = old[0] < WALL_BELOW
            for i in range(POPS):
                later[pl.ds(i * FIELD + base, 8), :] = jnp.where(wall, old[0], post[i])
        return carry

    lax.fori_loop(1, EXT_X - 1, first_step, 0)


def finish(columns, depth, rim_low, rim_high, field, start, later_in, out, later, low, high, result, sems):
    del later_in
    _, column_y, column_z = place()
    flat = (lanes() + 2 * column_z) % LANE
    for source, target, there in ((rim_low, low, column_y > 0), (rim_high, high, column_y < columns - 1)):
        for chunk in range(5):
            blocks = [source[pl.ds(block * EXT_X + 8 * chunk, 8), :] for block in range(RIM_BLOCKS)]
            for plane in range(RIM):
                block, begin = divmod(plane * EXT_Z, LANE)
                shift = (2 * LANE - begin - 2 * column_z) % LANE
                value = pltpu.roll(blocks[block], shift, 1)
                if begin + EXT_Z > LANE:
                    value = jnp.where(flat < LANE - begin, value, pltpu.roll(blocks[block + 1], shift, 1))
                value = jnp.where((flat < EXT_Z) & there, value, OUTSIDE)
                target[pl.ds(plane * GRID_X + 8 * chunk, 8), :] = value

    drift_y, spin, centre_y = drifts_of(columns, depth)
    for source, face, rim in ((low, 0, RIM_UP), (high, SPAN_Y - 1, RIM_DOWN)):
        outer = {i: POPS + n for n, i in enumerate(rim)}
        toward = VELOCITIES[rim[0]][1]
        for y in (face - toward, face):
            drift_z = spin * ((column_y * SPAN_Y + y).astype(jnp.float32) - centre_y)
            for chunk in range(5):
                first = 1 + 8 * chunk
                size = min(8, EXT_X - 1 - first)

                def value_at(i, x, y):
                    if y == face - 2 * toward:
                        return source[pl.ds(outer[i] * GRID_X + x, size), :]
                    if y == face - toward:
                        return source[pl.ds(i * GRID_X + x, size), :]
                    return field[pl.ds(i * FIELD + x * PITCH + FIRST + y, size, stride=PITCH), :]

                def pull(i):
                    step_x, step_y, step_z = VELOCITIES[i]
                    return turned(value_at(i, first - step_x, y - step_y), step_z)

                old = [value_at(i, first, y) for i in range(POPS)]
                values = streamed(pull, old, drift_y[:size], drift_z)
                post, _ = collide(values)
                wall = old[0] < WALL_BELOW
                for i in range(POPS) if y == face else rim:
                    row = i * FIELD + first * PITCH + FIRST + y
                    later[pl.ds(row, size, stride=PITCH), :] = jnp.where(wall, old[0], post[i])

    drift_y, drifts = drifts_by_half(columns, depth)
    quarter = SPAN_X // 4

    def leave(n):
        part = pl.ds(n * quarter, quarter)
        return pltpu.make_async_copy(result.at[:, part], out.at[:, part], sems.at[n])

    def second_step(x, carry):
        for half in range(SPAN_Y // 8):
            base = pl.multiple_of((x + 2) * PITCH + FIRST + 8 * half, 8)
            old = [later[pl.ds(i * FIELD + base, 8), :] for i in range(POPS)]
            values = streamed(pull_from(later, base), old, drift_y, drifts[half])
            wall = old[0] < WALL_BELOW
            for i in range(POPS):
                first = pl.multiple_of((i * SPAN_X + x) * SPAN_Y + 8 * half, 8)
                value = jnp.where(wall, start[pl.ds(first, 8), :], values[i])
                result[i, x, pl.ds(8 * half, 8), :] = value[:, :SPAN_Z]
        return carry

    for n in range(4):
        lax.fori_loop(n * quarter, (n + 1) * quarter, second_step, 0)
        leave(n).start()
    for n in range(4):
        leave(n).wait()


def rows_of(count):
    return jax.ShapeDtypeStruct((count, LANE), jnp.float32)


def kept(count):
    return VMEM((count, LANE), jnp.float32)


def params(mib):
    return pltpu.CompilerParams(vmem_limit_bytes=mib * 2**20)


def shards(populations, solid_cells, block_pos):
    layers = lax.axis_size("stream")
    columns = lax.axis_size("cy")
    depth = lax.axis_size("cz")
    rows = block_pos.shape[0]
    vmem = pl.BlockSpec(memory_space=VMEM)
    hbm = pl.BlockSpec(memory_space=pltpu.HBM)
    populations = pltpu.with_memory_space_constraint(populations, pltpu.HBM)
    solid_cells = pltpu.with_memory_space_constraint(solid_cells, pltpu.HBM)
    places = pltpu.with_memory_space_constraint(block_pos.T, pltpu.HBM)
    place_scratch = SMEM((3, rows), jnp.int32)
    mark_scratch = [VMEM((rows, EDGE**3), jnp.int32), VMEM((rows * TILES, LANE), jnp.float32)]

    up = [(i, i + 1) for i in range(layers - 1)]
    down = [(i + 1, i) for i in range(layers - 1)]
    from_low = []
    from_high = []
    for part in range(MOVE_CAP):
        sent = BLOCK + 8 if part < MOVE_CAP - 1 else SENT_ROWS
        send_up, send_down = pl.pallas_call(
            functools.partial(pack_stream, part),
            out_shape=(kept(sent), kept(sent)),
            in_specs=[hbm, hbm, hbm],
            out_specs=(vmem, vmem),
            scratch_shapes=[place_scratch, SMEM((LAYERS * BZD,), jnp.int32)]
            + mark_scratch
            + [
                VMEM((2, POPS, EDGE**3), jnp.float32),
                VMEM((2 * BZD, POPS, SLAB * LANE), jnp.float32),
                VMEM((PLANES * 2 * FACE, LANE), jnp.float32),
                pltpu.SemaphoreType.DMA((4 + 2 * BZD,)),
            ],
            compiler_params=params(16),
            name="pack_stream",
        )(places, solid_cells, populations)
        if part < MOVE_CAP - 1:
            send_up, send_down, places = lax.optimization_barrier((send_up, send_down, places))
            places = pltpu.with_memory_space_constraint(places, pltpu.HBM)
        from_low.append(lax.ppermute(send_up, "stream", up))
        from_high.append(lax.ppermute(send_down, "stream", down))

    own, zpack, zsend_up, zsend_down = pl.pallas_call(
        pack_own,
        out_shape=(kept(LAYERS * BZD * BLOCK), kept(ZMETA + 8), kept(DIAG), kept(DIAG)),
        in_specs=[hbm, hbm, hbm],
        out_specs=(vmem,) * 4,
        scratch_shapes=[place_scratch]
        + mark_scratch
        + [
            VMEM((rows, POPS, EDGE**3), jnp.float32),
            pltpu.SemaphoreType.DMA((rows + 2,)),
        ],
        compiler_params=params(16),
        name="pack_own",
    )(places, solid_cells, populations)
    zpack, zsend_up, zsend_down, from_low[0], from_high[0] = lax.optimization_barrier(
        (zpack, zsend_up, zsend_down, from_low[0], from_high[0])
    )
    swap = [(i, depth - 1 - i) for i in range(depth)]
    zin = lax.ppermute(zpack, "cz", swap)
    zup_pairs = [(s * depth + c, t * depth + d) for s, t in up for c, d in swap]
    zdown_pairs = [(s * depth + c, t * depth + d) for s, t in down for c, d in swap]
    z_low = lax.ppermute(zsend_up, ("stream", "cz"), zup_pairs)
    z_high = lax.ppermute(zsend_down, ("stream", "cz"), zdown_pairs)

    own, edge, zall, zedge, rim_up, rim_down = pl.pallas_call(
        functools.partial(settle_rim, layers),
        out_shape=(
            kept(LAYERS * BZD * BLOCK),
            kept(POPS * 4 * FACE),
            kept(LAYERS * ZROWS),
            kept(ZGROUPS * 8),
            kept(RIM_ROWS),
            kept(RIM_ROWS),
        ),
        in_specs=[hbm] + [vmem] * 8,
        out_specs=(vmem,) * 6,
        scratch_shapes=[
            place_scratch,
            VMEM((RIM * GRID_X, LANE), jnp.float32),
            VMEM((RIM * GRID_X, LANE), jnp.float32),
            pltpu.SemaphoreType.DMA,
        ],
        input_output_aliases={8: 0},
        compiler_params=params(16),
        name="settle_rim",
    )(places, from_low[0], from_high[0], from_low[1], from_high[1], zin, z_low, z_high, own)
    cy_up = [(i, i + 1) for i in range(columns - 1)]
    cy_down = [(i + 1, i) for i in range(columns - 1)]
    rim_low = lax.ppermute(rim_up, "cy", cy_up)
    rim_high = lax.ppermute(rim_down, "cy", cy_down)

    field, start, later = pl.pallas_call(
        functools.partial(settle_all, layers, columns, depth),
        out_shape=(kept(POPS * FIELD), kept(POPS * SPAN_X * SPAN_Y), kept(POPS * FIELD)),
        in_specs=[vmem] * 4,
        out_specs=(vmem,) * 3,
        compiler_params=params(16),
        name="settle_all",
    )(own, edge, zall, zedge)

    out, _ = pl.pallas_call(
        functools.partial(finish, columns, depth),
        out_shape=(
            jax.ShapeDtypeStruct((POPS, SPAN_X, SPAN_Y, SPAN_Z), jnp.float32),
            kept(POPS * FIELD),
        ),
        in_specs=[vmem] * 5,
        out_specs=(hbm, vmem),
        scratch_shapes=[
            VMEM((RIM * GRID_X, LANE), jnp.float32),
            VMEM((RIM * GRID_X, LANE), jnp.float32),
            VMEM((POPS, SPAN_X, SPAN_Y, SPAN_Z), jnp.float32),
            pltpu.SemaphoreType.DMA((4,)),
        ],
        input_output_aliases={4: 1},
        compiler_params=params(16),
        name="finish",
    )(rim_low, rim_high, field, start, later)
    return out


def solution(mesh):
    in_specs = (
        P(("stream", "cy", "cz"), None, None),
        P(("stream", "cy", "cz"), None),
        P(("stream", "cy", "cz"), None),
    )
    out_specs = P(None, "stream", "cy", "cz")
    return jax.shard_map(shards, mesh=mesh, in_specs=in_specs, out_specs=out_specs, check_vma=False)
```

```python
import functools

import jax
import jax.numpy as jnp
from jax import lax
from jax.experimental import pallas as pl
from jax.experimental.pallas import tpu as pltpu
from jax.sharding import PartitionSpec as P

EDGE = 16
BXD = 2
BYD = 1
BZD = 4
MOVE_CAP = 2

VELOCITIES = (
    (0, 0, 0),
    (1, 0, 0),
    (-1, 0, 0),
    (0, 1, 0),
    (0, -1, 0),
    (0, 0, 1),
    (0, 0, -1),
    (1, 1, 0),
    (-1, -1, 0),
    (1, -1, 0),
    (-1, 1, 0),
    (1, 0, 1),
    (-1, 0, -1),
    (1, 0, -1),
    (-1, 0, 1),
    (0, 1, 1),
    (0, -1, -1),
    (0, 1, -1),
    (0, -1, 1),
)
WEIGHTS = (1.0 / 3.0,) + (1.0 / 18.0,) * 6 + (1.0 / 36.0,) * 12
OPPOSITE = (0, 2, 1, 4, 3, 6, 5, 8, 7, 10, 9, 12, 11, 14, 13, 16, 15, 18, 17)
OMEGA_EVEN = 1.25
OMEGA_ODD = 1.0 / 1.125

POPS = 19
PLANES = 20
LANE = 128
TILES = EDGE**3 // LANE
BLOCK = PLANES * TILES
YLO = LANE // EDGE
SLAB = 4
GROUPS = ((0, 8), (8, 8), (16, 3))
SENT_SLABS = MOVE_CAP * BLOCK
LAYERS = BXD + 2
ZGROUPS = 3
ZROWS = ZGROUPS * TILES
ZMETA = LAYERS * ZROWS
DIAG = ZROWS + ZGROUPS * SLAB

SPAN_X = BXD * EDGE
SPAN_Y = BYD * EDGE
SPAN_Z = BZD * EDGE
PITCH = SPAN_Y + 8
FIRST = 8
FIELD = (SPAN_X + 4) * PITCH + 16
EXT_X = SPAN_X + 4
EXT_Z = SPAN_Z + 2
RIM_UP = tuple(i for i in range(POPS) if VELOCITIES[i][1] == 1)
RIM_DOWN = tuple(i for i in range(POPS) if VELOCITIES[i][1] == -1)
RIM = POPS + len(RIM_UP)
AHEAD = tuple(i for i in range(POPS) if VELOCITIES[i][0] == 1)
BACK = tuple(i for i in range(POPS) if VELOCITIES[i][0] == -1)
FACE = 2 * BZD
SENT_META = SENT_SLABS + RIM * FACE
SENT_ROWS = SENT_META + 8
RIM_BLOCKS = -(-RIM * EXT_Z // LANE)
RIM_ROWS = RIM_BLOCKS * EXT_X + 4
GRID_X = 48

ROTOR = -1.0e30
OUTSIDE = -2.0e30
WALL_BELOW = -1.0e20
OUT_BELOW = -1.5e30

VMEM = pltpu.VMEM
SMEM = pltpu.SMEM


def lanes():
    return lax.broadcasted_iota(jnp.int32, (8, LANE), 1)


def collide(f):
    even = [None] * POPS
    odd = [None] * POPS
    for i in range(1, POPS, 2):
        even[i] = f[i] + f[i + 1]
        odd[i] = f[i] - f[i + 1]
    density = f[0]
    for i in range(1, POPS, 2):
        density = density + even[i]
    flow = []
    for axis in range(3):
        total = None
        for i in range(1, POPS, 2):
            sign = VELOCITIES[i][axis]
            if sign == 0:
                continue
            if total is None:
                total = odd[i] if sign == 1 else -odd[i]
            else:
                total = total + odd[i] if sign == 1 else total - odd[i]
        flow.append(total)
    inverse = 1.0 / density
    velocity = [part * inverse for part in flow]
    square = velocity[0] * velocity[0] + velocity[1] * velocity[1] + velocity[2] * velocity[2]
    base = density * (1.0 - 1.5 * square)
    post = [None] * POPS
    post[0] = (1.0 - OMEGA_EVEN) * f[0] + (OMEGA_EVEN * WEIGHTS[0]) * base
    shared = {}
    for weight in (WEIGHTS[1], WEIGHTS[7]):
        shared[weight] = ((OMEGA_EVEN * weight) * base, (OMEGA_EVEN * weight * 4.5) * density,
                          (OMEGA_ODD * weight * 3.0) * density)
    for i in range(1, POPS, 2):
        projected = None
        for axis in range(3):
            sign = VELOCITIES[i][axis]
            if sign == 0:
                continue
            if projected is None:
                projected = velocity[axis] if sign == 1 else -velocity[axis]
            else:
                projected = projected + velocity[axis] if sign == 1 else projected - velocity[axis]
        low, curve, slope = shared[WEIGHTS[i]]
        even_part = (0.5 - 0.5 * OMEGA_EVEN) * even[i] + (low + curve * (projected * projected))
        odd_part = (0.5 - 0.5 * OMEGA_ODD) * odd[i] + slope * projected
        post[i] = even_part + odd_part
        post[i + 1] = even_part - odd_part
    return post, density


def pushes(density, drift_y, drift_z):
    along_y = density * drift_y
    along_z = density * drift_z
    out = [None] * POPS
    for i in range(1, POPS):
        _, step_y, step_z = VELOCITIES[i]
        total = None
        for sign, part in ((step_y, along_y), (step_z, along_z)):
            if sign == 0:
                continue
            if total is None:
                total = part if sign == 1 else -part
            else:
                total = total + part if sign == 1 else total - part
        if total is not None:
            out[i] = (6.0 * WEIGHTS[i]) * total
    return out


def total_of(parts):
    parts = list(parts)
    while len(parts) > 1:
        pairs = [parts[n] + parts[n + 1] for n in range(0, len(parts) - 1, 2)]
        parts = pairs + parts[len(parts) - len(parts) % 2 :]
    return parts[0]


def streamed(pull, own, drift_y, drift_z):
    push = pushes(total_of(own), drift_y, drift_z)
    out = [own[0]]
    for i in range(1, POPS):
        pulled = pull(i)
        bounced = own[OPPOSITE[i]]
        blocked = pulled < WALL_BELOW
        if push[i] is not None:
            bounced = jnp.where(pulled < OUT_BELOW, bounced, bounced + push[i])
        out.append(jnp.where(blocked, bounced, pulled))
    return out


def ahead(items, take, leave, depth):
    waiting = []
    for n in items:
        waiting.append((n, take(n)))
        if len(waiting) > depth:
            leave(*waiting.pop(0))
    for pair in waiting:
        leave(*pair)


def place():
    return lax.axis_index("stream"), lax.axis_index("cy"), lax.axis_index("cz")


def slot_of(pos, row, layer, column_z):
    slot = (pos[0, row] - (layer * BXD - 1)) * BZD + (pos[2, row] - column_z * BZD)
    return jnp.clip(slot, 0, LAYERS * BZD - 1)


def fill_table(pos, table):
    layer, _, column_z = place()
    for entry in range(LAYERS * BZD):
        table[entry] = -1
    for row in range(pos.shape[1]):

        @pl.when(pos[0, row] >= 0)
        def _(row=row):
            table[slot_of(pos, row, layer, column_z)] = row


def spread_marks(marks, dense):
    rows = marks.shape[0]
    for first in range(0, rows, 8):
        size = min(8, rows - first)
        for begin in range(0, TILES, 8):
            values = [marks[first : first + size, t * LANE : (t + 1) * LANE] for t in range(begin, begin + 8)]
            for k, value in enumerate(values):
                dense[pl.ds(first * TILES + begin + k, size, stride=TILES), :] = value.astype(jnp.float32)


def collide_block(ref, base):
    for part in range(TILES // 8):
        old = [ref[pl.ds(base + i * TILES + 8 * part, 8), :] for i in range(POPS)]
        mark = ref[pl.ds(base + POPS * TILES + 8 * part, 8), :] > 0.5
        post, _ = collide(old)
        for i in range(POPS):
            ref[pl.ds(base + i * TILES + 8 * part, 8), :] = jnp.where(mark, old[i], post[i])


def pack_block(out, base, stage, dense, row):
    out[pl.ds(base + POPS * TILES, TILES), :] = dense[pl.ds(pl.multiple_of(row * TILES, 8), TILES), :]
    for first in range(0, TILES, 4):
        moves = []
        for tile in range(first, first + 4):
            for group, size in GROUPS:
                value = stage[group : group + size, tile * LANE : (tile + 1) * LANE]
                moves.append((pl.ds(base + group * TILES + tile, size, stride=TILES), value))
        for target, value in moves:
            out[target, :] = value
    collide_block(out, base)


def pack_stream(places, marks_in, pops, up, down, pos, table, marks, dense, blocks, slabs, strip, sems):
    mark_copy = pltpu.make_async_copy(marks_in, marks, sems.at[0])
    mark_copy.start()
    place_copy = pltpu.make_async_copy(places, pos, sems.at[1])
    place_copy.start()
    rows = pos.shape[1]
    copies = [None] * 4
    for j in range(MOVE_CAP):
        copies[MOVE_CAP + j] = pltpu.make_async_copy(pops.at[j], blocks.at[MOVE_CAP + j], sems.at[2 + MOVE_CAP + j])
        copies[MOVE_CAP + j].start()
    place_copy.wait()
    count = 0
    for row in range(rows):
        count = count + jnp.where(pos[0, row] >= 0, 1, 0)
    last = jnp.clip(count - MOVE_CAP, 0, rows - MOVE_CAP)
    for j in range(MOVE_CAP):
        copies[j] = pltpu.make_async_copy(pops.at[last + j], blocks.at[j], sems.at[2 + j])
        copies[j].start()
    fill_table(pos, table)
    slab_rows = []
    slab_copies = []
    for side in range(2):
        for bz in range(BZD):
            row = jnp.maximum(table[(2 - side) * BZD + bz], 0)
            n = side * BZD + bz
            first = (TILES - SLAB) * LANE if side == 0 else 0
            slab_rows.append(row)
            slab_copies.append(
                pltpu.make_async_copy(
                    pops.at[row, :, pl.ds(first, SLAB * LANE)], slabs.at[n], sems.at[2 + 2 * MOVE_CAP + n]
                )
            )
            slab_copies[n].start()
    mark_copy.wait()
    spread_marks(marks, dense)
    for side, out in ((1, down), (0, up)):
        for j in range(MOVE_CAP):
            row = j if side == 1 else last + j
            for k, axis in ((0, 0), (1, 2)):
                value = jnp.full((1, LANE), pos[axis, row], jnp.int32).astype(jnp.float32)
                out[pl.ds(SENT_META + 2 * j + k, 1), :] = value
            n = side * MOVE_CAP + j
            copies[n].wait()
            pack_block(out, j * BLOCK, blocks.at[n], dense, row)
    for side, out in enumerate((up, down)):
        for bz in range(BZD):
            n = side * BZD + bz
            first = slab_rows[n] * TILES + (TILES - SLAB if side == 0 else 0)
            slab_copies[n].wait()
            moves = []
            for x in range(2):
                for yhi in range(2):
                    q = 2 * x + yhi
                    row = x * FACE + 2 * bz + yhi
                    for group, size in GROUPS:
                        value = slabs[n, group : group + size, q * LANE : (q + 1) * LANE]
                        moves.append((pl.ds(group * 2 * FACE + row, size, stride=2 * FACE), value))
                row = POPS * 2 * FACE + x * FACE + 2 * bz
                moves.append((pl.ds(row, 2), dense[pl.ds(first + 2 * x, 2), :]))
            for target, value in moves:
                strip[target, :] = value
        inner = 1 if side == 0 else 0
        for x in range(2):
            old = [strip[pl.ds(i * 2 * FACE + x * FACE, FACE), :] for i in range(POPS)]
            mark = strip[pl.ds(POPS * 2 * FACE + x * FACE, FACE), :] > 0.5
            post, _ = collide(old)
            if x == inner:
                pairs = [(i, i) for i in range(POPS)]
            else:
                pairs = [(POPS + n, i) for n, i in enumerate(AHEAD if side == 0 else BACK)]
            for plane, i in pairs:
                out[pl.ds(SENT_SLABS + plane * FACE, FACE), :] = jnp.where(mark, ROTOR, post[i])


def pack_edge(places, marks_in, pops, own, zpack, zup, zdown, pos, table, marks, dense, stage, sems):
    column_z = lax.axis_index("cz")
    mark_copy = pltpu.make_async_copy(marks_in, marks, sems.at[LAYERS])
    mark_copy.start()
    place_copy = pltpu.make_async_copy(places, pos, sems.at[LAYERS + 1])
    place_copy.start()
    place_copy.wait()
    fill_table(pos, table)
    edge_bz = jnp.where(column_z == 0, BZD - 1, 0)
    first_c = jnp.where(column_z == 0, EDGE - 2, 0)
    found = [table[held * BZD + edge_bz] for held in range(LAYERS)]
    row_of = [jnp.maximum(row, 0) for row in found]
    copies = []
    for held in range(LAYERS):
        copies.append(pltpu.make_async_copy(pops.at[row_of[held]], stage.at[held], sems.at[held]))
        copies[held].start()
    mark_copy.wait()
    spread_marks(marks, dense)
    spot = (lanes() % EDGE) // 2
    sublane = lax.broadcasted_iota(jnp.int32, (8, LANE), 0)
    flags = jnp.zeros((8, LANE), jnp.int32)
    for held in range(LAYERS):
        copies[held].wait()
        base = pl.multiple_of((held * BZD + edge_bz) * BLOCK, 8)

        @pl.when(found[held] >= 0)
        def _(held=held, base=base):
            pack_block(own, base, stage.at[held], dense, row_of[held])
            totals = []
            for group in range(ZGROUPS):
                for part in range(TILES // 8):
                    total = jnp.zeros((8, LANE), jnp.float32)
                    for k in range(min(8, PLANES - group * 8)):
                        value = own[pl.ds(base + (group * 8 + k) * TILES + part * 8, 8), :]
                        value = pltpu.roll(value, (2 * k - first_c + LANE) % LANE, 1)
                        total = jnp.where(spot == k, value, total)
                    totals.append((held * ZROWS + group * TILES + part * 8, total))
            for row, total in totals:
                zpack[pl.ds(row, 8), :] = total

        flags = jnp.where((sublane == held) & (found[held] >= 0), 1, flags)
    zpack[pl.ds(ZMETA, 8), :] = flags.astype(jnp.float32)
    zup[pl.ds(0, ZROWS), :] = zpack[pl.ds(3 * ZROWS, ZROWS), :]
    zdown[pl.ds(0, ZROWS), :] = zpack[pl.ds(0, ZROWS), :]
    for group in range(ZGROUPS):
        target = pl.ds(ZROWS + group * SLAB, SLAB)
        zup[target, :] = zpack[pl.ds(2 * ZROWS + group * TILES + TILES - SLAB, SLAB), :]
        zdown[target, :] = zpack[pl.ds(ZROWS + group * TILES, SLAB), :]


def pack_own(places, marks_in, pops, own_in, own, pos, marks, dense, stage, sems):
    del own_in
    layer, _, column_z = place()
    edge_bz = jnp.where(column_z == 0, BZD - 1, 0)
    rows = pos.shape[1]
    mark_copy = pltpu.make_async_copy(marks_in, marks, sems.at[rows])
    mark_copy.start()
    place_copy = pltpu.make_async_copy(places, pos, sems.at[rows + 1])
    place_copy.start()
    copies = [pltpu.make_async_copy(pops.at[r], stage.at[r], sems.at[r]) for r in range(rows)]
    for copy in copies:
        copy.start()
    mark_copy.wait()
    spread_marks(marks, dense)
    place_copy.wait()

    def settle(row, carry):
        pltpu.make_async_copy(pops.at[row], stage.at[row], sems.at[row]).wait()
        slot = slot_of(pos, row, layer, column_z)

        @pl.when((pos[0, row] >= 0) & (slot % BZD != edge_bz))
        def _():
            pack_block(own, pl.multiple_of(slot * BLOCK, 8), stage.at[row], dense, row)

        return carry

    lax.fori_loop(0, rows, settle, 0)


def gathered(parts, zvalue, spot, ylo, column_z):
    lane = lanes()
    rows = parts[0].shape[0]
    lane = lane[:rows]
    total = None
    for bz in range(BZD):
        shift = (bz * EDGE - ylo * EDGE) % LANE
        value = pltpu.roll(parts[bz], shift, 1) if shift else parts[bz]
        total = value if total is None else jnp.where(lane // EDGE == bz, value, total)
    goal = jnp.where(column_z == 0, SPAN_Z, LANE - 2)
    zvalue = pltpu.roll(zvalue, (goal - (ylo * EDGE + 2 * spot) + LANE) % LANE, 1)
    return jnp.where(lane >= SPAN_Z, zvalue, total)


def gathered_rows(parts, zvalue, spot, column_z):
    lane = lanes()[: parts[0].shape[0]]
    single = (lane // EDGE) % 2 == 1
    double = (lane // (2 * EDGE)) % 2 == 1
    main = lane < SPAN_Z
    pairs = []
    for n in (0, 2):
        even = jnp.where(single, pltpu.roll(parts[n + 1], EDGE, 1), parts[n])
        odd = jnp.where(single, parts[n + 1], pltpu.roll(parts[n], LANE - EDGE, 1))
        pairs.append((even, odd))
    goal = jnp.where(column_z == 0, SPAN_Z, LANE - 2)
    out = [None] * YLO
    for r in range(4):
        low, high = pairs[0][r % 2], pairs[1][r % 2]
        if r < 2:
            both = jnp.where(double, pltpu.roll(high, 2 * EDGE, 1), low)
        else:
            both = jnp.where(double, high, pltpu.roll(low, LANE - 2 * EDGE, 1))
        beyond = pltpu.roll(zvalue, (goal - (r * EDGE + 2 * spot) + LANE) % LANE, 1)
        out[r] = jnp.where(main, both, beyond)
        out[r + 4] = pltpu.roll(jnp.where(main, beyond, both), SPAN_Z, 1)
    return out


def inside_lanes(rows, column_z):
    lane = lanes()[:rows]
    low = (column_z == 0) & (lane >= SPAN_Z) & (lane < SPAN_Z + 2)
    high = (column_z != 0) & (lane >= LANE - 2)
    return (lane < SPAN_Z) | low | high


def marked(post, mark, inside):
    flag = jnp.where(inside, jnp.where(mark > 0.5, ROTOR, 0.0), OUTSIDE)
    wall = flag < WALL_BELOW
    return [jnp.where(wall, flag, value) for value in post]


def plane_parts(own, edge, zall, zedge, chunk, yhi, plane):
    group = plane // 8
    if chunk is None:
        if plane == POPS:
            parts = [jnp.zeros((4, LANE), jnp.float32)] * BZD
        else:
            parts = [edge[pl.ds(plane * 4 * FACE + 2 * bz + yhi, 4, stride=FACE), :] for bz in range(BZD)]
        return parts, zedge[pl.ds(group * 8 + yhi, 4, stride=2), :]
    held, half = 1 + chunk // 2, chunk % 2
    parts = []
    for bz in range(BZD):
        base = (held * BZD + bz) * BLOCK + plane * TILES + half * EDGE + yhi
        parts.append(own[pl.ds(base, 8, stride=2), :])
    return parts, zall[pl.ds(held * ZROWS + group * TILES + half * EDGE + yhi, 8, stride=2), :]


def chunk_values(own, edge, zall, zedge, chunk, yhi, ylo, column_z):
    out = []
    for plane in range(PLANES):
        parts, zvalue = plane_parts(own, edge, zall, zedge, chunk, yhi, plane)
        out.append(gathered(parts, zvalue, plane % 8, ylo, column_z))
    return out


def halo_x_inside(layer, layers):
    row = lax.broadcasted_iota(jnp.int32, (4, LANE), 0)
    low = (row < 2) & (layer > 0)
    high = (row >= 2) & (layer < layers - 1)
    return low | high


def settle_rim(layers, places, up, down, zin, zup, zdown, own_in, own, edge, zall, zedge, rim_up, rim_down, pos, post_up, post_down, sem):
    del own_in
    layer, _, column_z = place()
    place_copy = pltpu.make_async_copy(places, pos, sem)
    place_copy.start()
    for arrived in (up, down):
        for j in range(MOVE_CAP):
            bx = arrived[pl.ds(SENT_META + 2 * j, 1), :].astype(jnp.int32)
            bz = arrived[pl.ds(SENT_META + 2 * j + 1, 1), :].astype(jnp.int32)
            code = (bx - layer * BXD) * BZD + (bz - column_z * BZD)
            mine = (bx >= layer * BXD) & (bx < (layer + 1) * BXD)
            first = layer == 0 if arrived is up else layer == layers - 1
            code = jnp.max(jnp.where(mine, code, -1))

            @pl.when((code >= 0) & jnp.logical_not(first))
            def _(arrived=arrived, j=j, code=code):
                base = pl.multiple_of((jnp.clip(code, 0, BXD * BZD - 1) + BZD) * BLOCK, 8)
                for k in range(0, BLOCK, 128):
                    values = [arrived[pl.ds(j * BLOCK + k + 8 * n, 8), :] for n in range(16)]
                    for n, value in enumerate(values):
                        own[pl.ds(base + k + 8 * n, 8), :] = value

    place_copy.wait()
    for side, arrived in enumerate((up, down)):
        inner, outer = (1, 0) if side == 0 else (2, 3)
        pairs = [(i, i, inner) for i in range(POPS)]
        pairs += [(POPS + n, i, outer) for n, i in enumerate(AHEAD if side == 0 else BACK)]
        values = [arrived[pl.ds(SENT_SLABS + plane * FACE, FACE), :] for plane, _, _ in pairs]
        for (_, i, x), value in zip(pairs, values):
            edge[pl.ds((i * 4 + x) * FACE, FACE), :] = value
        for bz in range(BZD):
            here = jnp.int32(0)
            goal = (0 if side == 0 else LAYERS - 1) * BZD + bz
            for row in range(pos.shape[1]):
                hit = (pos[0, row] >= 0) & (slot_of(pos, row, layer, column_z) == goal)
                here = jnp.where(hit, 1, here)

            @pl.when(here == 1)
            def _(side=side, pairs=pairs, goal=goal, bz=bz):
                first = goal * BLOCK + (TILES - SLAB if side == 0 else 0)
                values = []
                for _, i, x in pairs:
                    shift = 2 * (x if side == 0 else x - 2)
                    mark = own[pl.ds(first + POPS * TILES + shift, 2), :] > 0.5
                    values.append(jnp.where(mark, ROTOR, own[pl.ds(first + i * TILES + shift, 2), :]))
                for (_, i, x), value in zip(pairs, values):
                    edge[pl.ds((i * 4 + x) * FACE + 2 * bz, 2), :] = value

    moves = []
    for held in range(LAYERS):
        flag = zin[pl.ds(ZMETA + held, 1), :] > 0.5
        for group in range(ZGROUPS):
            if held == 1 or held == 2:
                for part in range(TILES // 8):
                    rows = pl.ds(held * ZROWS + group * TILES + part * 8, 8)
                    source = zup if held == 1 else zdown
                    other = source[pl.ds(group * TILES + part * 8, 8), :]
                    moves.append((zall, rows, jnp.where(flag, zin[rows, :], other)))
            else:
                side = 0 if held == 0 else 1
                source = zup if held == 0 else zdown
                first = TILES - SLAB if held == 0 else 0
                mine = zin[pl.ds(held * ZROWS + group * TILES + first, SLAB), :]
                other = source[pl.ds(ZROWS + group * SLAB, SLAB), :]
                moves.append((zedge, pl.ds(group * 8 + side * SLAB, SLAB), jnp.where(flag, mine, other)))
    for target, rows, value in moves:
        target[rows, :] = value
    for chunk in (0, 1, 2, 3, None):
        for y in (0, 1, SPAN_Y - 2, SPAN_Y - 1):
            values = chunk_values(own, edge, zall, zedge, chunk, y // YLO, y % YLO, column_z)
            inside = inside_lanes(values[0].shape[0], column_z)
            if chunk is None:
                inside = inside & halo_x_inside(layer, layers)
            post = marked(values[:POPS], values[POPS], inside)
            target = post_down if y < 2 else post_up
            rim = RIM_DOWN if y < 2 else RIM_UP
            if y in (0, SPAN_Y - 1):
                pairs = [(i, i) for i in range(POPS)]
            else:
                pairs = [(POPS + n, i) for n, i in enumerate(rim)]
            for plane, i in pairs:
                if chunk is None:
                    target[pl.ds(plane * GRID_X, 2), :] = post[i][:2]
                    target[pl.ds(plane * GRID_X + EXT_X - 2, 2), :] = post[i][2:]
                else:
                    target[pl.ds(plane * GRID_X + 2 + 8 * chunk, 8), :] = post[i]
    lane = lanes()
    for source, target in ((post_up, rim_up), (post_down, rim_down)):
        for chunk in range(5):
            size = min(8, EXT_X - 8 * chunk)
            values = []
            for plane in range(RIM):
                value = source[pl.ds(plane * GRID_X + 8 * chunk, 8), :]
                values.append(pltpu.roll(value, (plane * EXT_Z + 2 * column_z) % LANE, 1))
            totals = []
            for block in range(RIM_BLOCKS):
                total = jnp.zeros((8, LANE), jnp.float32)
                for plane in range(RIM):
                    begin = plane * EXT_Z - block * LANE
                    if begin >= LANE or begin + EXT_Z <= 0:
                        continue
                    total = jnp.where((lane >= begin) & (lane < begin + EXT_Z), values[plane], total)
                totals.append(total)
            for block in range(RIM_BLOCKS):
                target[pl.ds(block * EXT_X + 8 * chunk, size), :] = totals[block][:size]


def turned(value, step_z):
    return pltpu.roll(value, step_z % LANE, 1) if step_z else value


def drifts_of(columns, depth):
    _, _, column_z = place()
    lane = lanes()
    total_y = SPAN_Y * columns
    total_z = SPAN_Z * depth
    spin = 0.2 / (total_y + total_z)
    here_z = jnp.where(lane < SPAN_Z + 8, lane, lane - LANE) + column_z * SPAN_Z
    drift_y = -spin * (here_z.astype(jnp.float32) - (total_z - 1) / 2.0)
    return drift_y, spin, (total_y - 1) / 2.0


def drifts_by_half(columns, depth):
    _, column_y, _ = place()
    drift_y, spin, centre_y = drifts_of(columns, depth)
    sublane = lax.broadcasted_iota(jnp.int32, (8, LANE), 0)
    halves = []
    for half in range(SPAN_Y // 8):
        here_y = sublane + (column_y * SPAN_Y + 8 * half)
        halves.append(spin * (here_y.astype(jnp.float32) - centre_y))
    return drift_y, halves


def pull_from(field, base):
    def pull(i):
        step_x, step_y, step_z = VELOCITIES[i]
        return turned(field[pl.ds(i * FIELD + base - step_x * PITCH - step_y, 8), :], step_z)

    return pull


def settle_all(layers, columns, depth, own, edge, zall, zedge, field, start, later):
    layer, _, column_z = place()

    def flags_of(mark, inside):
        return [jnp.where(inside, jnp.where(value > 0.5, ROTOR, 0.0), OUTSIDE) for value in mark]

    def halves(yhi, carry):
        def rows_of_plane(chunk, plane):
            parts, zvalue = plane_parts(own, edge, zall, zedge, chunk, yhi, plane)
            return gathered_rows(parts, zvalue, plane % 8, column_z)

        def chunks(chunk, carry):
            flags = flags_of(rows_of_plane(chunk, POPS), inside_lanes(8, column_z))

            def leave(i, values):
                for ylo in range(YLO):
                    row = i * FIELD + (8 * chunk + 2) * PITCH + FIRST + YLO * yhi + ylo
                    value = jnp.where(flags[ylo] < WALL_BELOW, flags[ylo], values[ylo])
                    field[pl.ds(row, 8, stride=PITCH), :] = value
                    target = (i * SPAN_X + 8 * chunk) * SPAN_Y + YLO * yhi + ylo
                    start[pl.ds(target, 8, stride=SPAN_Y), :] = values[ylo]

            ahead(range(POPS), lambda i: rows_of_plane(chunk, i), leave, 3)
            return carry

        lax.fori_loop(0, SPAN_X // 8, chunks, 0)
        inside = inside_lanes(4, column_z) & halo_x_inside(layer, layers)
        flags = flags_of(rows_of_plane(None, POPS), inside)

        def leave(i, values):
            for ylo in range(YLO):
                value = jnp.where(flags[ylo] < WALL_BELOW, flags[ylo], values[ylo])
                for first, side in ((0, 0), (EXT_X - 2, 2)):
                    row = i * FIELD + first * PITCH + FIRST + YLO * yhi + ylo
                    field[pl.ds(row, 2, stride=PITCH), :] = value[side : side + 2]

        ahead(range(POPS), lambda i: rows_of_plane(None, i), leave, 3)
        return carry

    lax.fori_loop(0, SPAN_Y // YLO, halves, 0)
    drift_y, drifts = drifts_by_half(columns, depth)

    def first_step(x, carry):
        for half in range(SPAN_Y // 8):
            base = pl.multiple_of(x * PITCH + FIRST + 8 * half, 8)
            old = [field[pl.ds(i * FIELD + base, 8), :] for i in range(POPS)]
            values = streamed(pull_from(field, base), old, drift_y, drifts[half])
            post, _ = collide(values)
            wall = old[0] < WALL_BELOW
            for i in range(POPS):
                later[pl.ds(i * FIELD + base, 8), :] = jnp.where(wall, old[0], post[i])
        return carry

    lax.fori_loop(1, EXT_X - 1, first_step, 0)


def finish(columns, depth, rim_low, rim_high, field, start, later_in, out, later, low, high, result, sems):
    del later_in
    _, column_y, column_z = place()
    flat = (lanes() + 2 * column_z) % LANE
    for source, target, there in ((rim_low, low, column_y > 0), (rim_high, high, column_y < columns - 1)):
        for chunk in range(5):
            blocks = [source[pl.ds(block * EXT_X + 8 * chunk, 8), :] for block in range(RIM_BLOCKS)]
            for plane in range(RIM):
                block, begin = divmod(plane * EXT_Z, LANE)
                shift = (2 * LANE - begin - 2 * column_z) % LANE
                value = pltpu.roll(blocks[block], shift, 1)
                if begin + EXT_Z > LANE:
                    value = jnp.where(flat < LANE - begin, value, pltpu.roll(blocks[block + 1], shift, 1))
                value = jnp.where((flat < EXT_Z) & there, value, OUTSIDE)
                target[pl.ds(plane * GRID_X + 8 * chunk, 8), :] = value

    drift_y, spin, centre_y = drifts_of(columns, depth)
    for source, face, rim in ((low, 0, RIM_UP), (high, SPAN_Y - 1, RIM_DOWN)):
        outer = {i: POPS + n for n, i in enumerate(rim)}
        toward = VELOCITIES[rim[0]][1]
        for y in (face - toward, face):
            drift_z = spin * ((column_y * SPAN_Y + y).astype(jnp.float32) - centre_y)
            for chunk in range(5):
                first = 1 + 8 * chunk
                size = min(8, EXT_X - 1 - first)

                def value_at(i, x, y):
                    if y == face - 2 * toward:
                        return source[pl.ds(outer[i] * GRID_X + x, size), :]
                    if y == face - toward:
                        return source[pl.ds(i * GRID_X + x, size), :]
                    return field[pl.ds(i * FIELD + x * PITCH + FIRST + y, size, stride=PITCH), :]

                def pull(i):
                    step_x, step_y, step_z = VELOCITIES[i]
                    return turned(value_at(i, first - step_x, y - step_y), step_z)

                old = [value_at(i, first, y) for i in range(POPS)]
                values = streamed(pull, old, drift_y[:size], drift_z)
                post, _ = collide(values)
                wall = old[0] < WALL_BELOW
                for i in range(POPS) if y == face else rim:
                    row = i * FIELD + first * PITCH + FIRST + y
                    later[pl.ds(row, size, stride=PITCH), :] = jnp.where(wall, old[0], post[i])

    drift_y, drifts = drifts_by_half(columns, depth)
    quarter = SPAN_X // 4

    def leave(n):
        part = pl.ds(n * quarter, quarter)
        return pltpu.make_async_copy(result.at[:, part], out.at[:, part], sems.at[n])

    def second_step(x, carry):
        for half in range(SPAN_Y // 8):
            base = pl.multiple_of((x + 2) * PITCH + FIRST + 8 * half, 8)
            old = [later[pl.ds(i * FIELD + base, 8), :] for i in range(POPS)]
            values = streamed(pull_from(later, base), old, drift_y, drifts[half])
            wall = old[0] < WALL_BELOW
            for i in range(POPS):
                first = pl.multiple_of((i * SPAN_X + x) * SPAN_Y + 8 * half, 8)
                value = jnp.where(wall, start[pl.ds(first, 8), :], values[i])
                result[i, x, pl.ds(8 * half, 8), :] = value[:, :SPAN_Z]
        return carry

    for n in range(4):
        lax.fori_loop(n * quarter, (n + 1) * quarter, second_step, 0)
        leave(n).start()
    for n in range(4):
        leave(n).wait()


def rows_of(count):
    return jax.ShapeDtypeStruct((count, LANE), jnp.float32)


def kept(count):
    return VMEM((count, LANE), jnp.float32)


def params(mib):
    return pltpu.CompilerParams(vmem_limit_bytes=mib * 2**20)


def shards(populations, solid_cells, block_pos):
    layers = lax.axis_size("stream")
    columns = lax.axis_size("cy")
    depth = lax.axis_size("cz")
    rows = block_pos.shape[0]
    vmem = pl.BlockSpec(memory_space=VMEM)
    hbm = pl.BlockSpec(memory_space=pltpu.HBM)
    populations = pltpu.with_memory_space_constraint(populations, pltpu.HBM)
    solid_cells = pltpu.with_memory_space_constraint(solid_cells, pltpu.HBM)
    places = pltpu.with_memory_space_constraint(block_pos.T, pltpu.HBM)
    place_scratch = SMEM((3, rows), jnp.int32)
    table_scratch = SMEM((LAYERS * BZD,), jnp.int32)
    mark_scratch = [VMEM((rows, EDGE**3), jnp.int32), VMEM((rows * TILES, LANE), jnp.float32)]

    up = [(i, i + 1) for i in range(layers - 1)]
    down = [(i + 1, i) for i in range(layers - 1)]
    send_up, send_down = pl.pallas_call(
        pack_stream,
        out_shape=(kept(SENT_ROWS), kept(SENT_ROWS)),
        in_specs=[hbm, hbm, hbm],
        out_specs=(vmem, vmem),
        scratch_shapes=[place_scratch, table_scratch]
        + mark_scratch
        + [
            VMEM((2 * MOVE_CAP, POPS, EDGE**3), jnp.float32),
            VMEM((2 * BZD, POPS, SLAB * LANE), jnp.float32),
            VMEM((PLANES * 2 * FACE, LANE), jnp.float32),
            pltpu.SemaphoreType.DMA((2 + 2 * MOVE_CAP + 2 * BZD,)),
        ],
        compiler_params=params(16),
        name="pack_stream",
    )(places, solid_cells, populations)
    from_low = lax.ppermute(send_up, "stream", up)
    from_high = lax.ppermute(send_down, "stream", down)

    own, zpack, zsend_up, zsend_down = pl.pallas_call(
        pack_edge,
        out_shape=(kept(LAYERS * BZD * BLOCK), kept(ZMETA + 8), kept(DIAG), kept(DIAG)),
        in_specs=[hbm, hbm, hbm],
        out_specs=(vmem,) * 4,
        scratch_shapes=[place_scratch, table_scratch]
        + mark_scratch
        + [
            VMEM((LAYERS, POPS, EDGE**3), jnp.float32),
            pltpu.SemaphoreType.DMA((LAYERS + 2,)),
        ],
        compiler_params=params(16),
        name="pack_edge",
    )(places, solid_cells, populations)
    swap = [(i, depth - 1 - i) for i in range(depth)]
    zin = lax.ppermute(zpack, "cz", swap)
    zup_pairs = [(s * depth + c, t * depth + d) for s, t in up for c, d in swap]
    zdown_pairs = [(s * depth + c, t * depth + d) for s, t in down for c, d in swap]
    z_low = lax.ppermute(zsend_up, ("stream", "cz"), zup_pairs)
    z_high = lax.ppermute(zsend_down, ("stream", "cz"), zdown_pairs)

    own = pl.pallas_call(
        pack_own,
        out_shape=kept(LAYERS * BZD * BLOCK),
        in_specs=[hbm, hbm, hbm, vmem],
        out_specs=vmem,
        scratch_shapes=[place_scratch]
        + mark_scratch
        + [
            VMEM((rows, POPS, EDGE**3), jnp.float32),
            pltpu.SemaphoreType.DMA((rows + 2,)),
        ],
        input_output_aliases={3: 0},
        compiler_params=params(16),
        name="pack_own",
    )(places, solid_cells, populations, own)

    own, edge, zall, zedge, rim_up, rim_down = pl.pallas_call(
        functools.partial(settle_rim, layers),
        out_shape=(
            kept(LAYERS * BZD * BLOCK),
            kept(POPS * 4 * FACE),
            kept(LAYERS * ZROWS),
            kept(ZGROUPS * 8),
            kept(RIM_ROWS),
            kept(RIM_ROWS),
        ),
        in_specs=[hbm] + [vmem] * 6,
        out_specs=(vmem,) * 6,
        scratch_shapes=[
            place_scratch,
            VMEM((RIM * GRID_X, LANE), jnp.float32),
            VMEM((RIM * GRID_X, LANE), jnp.float32),
            pltpu.SemaphoreType.DMA,
        ],
        input_output_aliases={6: 0},
        compiler_params=params(16),
        name="settle_rim",
    )(places, from_low, from_high, zin, z_low, z_high, own)
    cy_up = [(i, i + 1) for i in range(columns - 1)]
    cy_down = [(i + 1, i) for i in range(columns - 1)]
    rim_low = lax.ppermute(rim_up, "cy", cy_up)
    rim_high = lax.ppermute(rim_down, "cy", cy_down)

    field, start, later = pl.pallas_call(
        functools.partial(settle_all, layers, columns, depth),
        out_shape=(kept(POPS * FIELD), kept(POPS * SPAN_X * SPAN_Y), kept(POPS * FIELD)),
        in_specs=[vmem] * 4,
        out_specs=(vmem,) * 3,
        compiler_params=params(16),
        name="settle_all",
    )(own, edge, zall, zedge)

    out, _ = pl.pallas_call(
        functools.partial(finish, columns, depth),
        out_shape=(
            jax.ShapeDtypeStruct((POPS, SPAN_X, SPAN_Y, SPAN_Z), jnp.float32),
            kept(POPS * FIELD),
        ),
        in_specs=[vmem] * 5,
        out_specs=(hbm, vmem),
        scratch_shapes=[
            VMEM((RIM * GRID_X, LANE), jnp.float32),
            VMEM((RIM * GRID_X, LANE), jnp.float32),
            VMEM((POPS, SPAN_X, SPAN_Y, SPAN_Z), jnp.float32),
            pltpu.SemaphoreType.DMA((4,)),
        ],
        input_output_aliases={4: 1},
        compiler_params=params(16),
        name="finish",
    )(rim_low, rim_high, field, start, later)
    return out


def solution(mesh):
    in_specs = (
        P(("stream", "cy", "cz"), None, None),
        P(("stream", "cy", "cz"), None),
        P(("stream", "cy", "cz"), None),
    )
    out_specs = P(None, "stream", "cy", "cz")
    return jax.shard_map(shards, mesh=mesh, in_specs=in_specs, out_specs=out_specs, check_vma=False)
```

```python
import functools

import jax
import jax.numpy as jnp
from jax import lax
from jax.experimental import pallas as pl
from jax.experimental.pallas import tpu as pltpu
from jax.sharding import PartitionSpec as P

EDGE = 16
BXD = 2
BYD = 1
BZD = 4
MOVE_CAP = 2

VELOCITIES = (
    (0, 0, 0),
    (1, 0, 0),
    (-1, 0, 0),
    (0, 1, 0),
    (0, -1, 0),
    (0, 0, 1),
    (0, 0, -1),
    (1, 1, 0),
    (-1, -1, 0),
    (1, -1, 0),
    (-1, 1, 0),
    (1, 0, 1),
    (-1, 0, -1),
    (1, 0, -1),
    (-1, 0, 1),
    (0, 1, 1),
    (0, -1, -1),
    (0, 1, -1),
    (0, -1, 1),
)
WEIGHTS = (1.0 / 3.0,) + (1.0 / 18.0,) * 6 + (1.0 / 36.0,) * 12
OPPOSITE = (0, 2, 1, 4, 3, 6, 5, 8, 7, 10, 9, 12, 11, 14, 13, 16, 15, 18, 17)
OMEGA_EVEN = 1.25
OMEGA_ODD = 1.0 / 1.125

POPS = 19
PLANES = 20
LANE = 128
TILES = EDGE**3 // LANE
BLOCK = PLANES * TILES
YLO = LANE // EDGE
SLAB = 4
GROUPS = ((0, 8), (8, 8), (16, 3))
SENT_SLABS = MOVE_CAP * BLOCK
LAYERS = BXD + 2
ZGROUPS = 3
ZROWS = ZGROUPS * TILES
ZMETA = LAYERS * ZROWS
DIAG = ZROWS + ZGROUPS * SLAB

SPAN_X = BXD * EDGE
SPAN_Y = BYD * EDGE
SPAN_Z = BZD * EDGE
PITCH = SPAN_X + 8
STEP = PITCH // 8
FIRST = 96
FIELD = FIRST + (SPAN_Y + 1) * PITCH + 48
TURN = 9
EXT_X = SPAN_X + 4
EXT_Z = SPAN_Z + 2
RIM_UP = tuple(i for i in range(POPS) if VELOCITIES[i][1] == 1)
RIM_DOWN = tuple(i for i in range(POPS) if VELOCITIES[i][1] == -1)
RIM = POPS + len(RIM_UP)
AHEAD = tuple(i for i in range(POPS) if VELOCITIES[i][0] == 1)
BACK = tuple(i for i in range(POPS) if VELOCITIES[i][0] == -1)
FACE = 2 * BZD
SENT_META = SENT_SLABS + RIM * FACE
SENT_ROWS = SENT_META + 8
RIM_BLOCKS = -(-RIM * EXT_Z // LANE)
RIM_ROWS = RIM_BLOCKS * EXT_X + 4
GRID_X = 48

ROTOR = -1.0e30
OUTSIDE = -2.0e30
WALL_BELOW = -1.0e20
OUT_BELOW = -1.5e30

VMEM = pltpu.VMEM
SMEM = pltpu.SMEM


def lanes():
    return lax.broadcasted_iota(jnp.int32, (8, LANE), 1)


def collide(f):
    even = [None] * POPS
    odd = [None] * POPS
    for i in range(1, POPS, 2):
        even[i] = f[i] + f[i + 1]
        odd[i] = f[i] - f[i + 1]
    density = f[0]
    for i in range(1, POPS, 2):
        density = density + even[i]
    flow = []
    for axis in range(3):
        total = None
        for i in range(1, POPS, 2):
            sign = VELOCITIES[i][axis]
            if sign == 0:
                continue
            if total is None:
                total = odd[i] if sign == 1 else -odd[i]
            else:
                total = total + odd[i] if sign == 1 else total - odd[i]
        flow.append(total)
    inverse = 1.0 / density
    velocity = [part * inverse for part in flow]
    square = velocity[0] * velocity[0] + velocity[1] * velocity[1] + velocity[2] * velocity[2]
    base = density * (1.0 - 1.5 * square)
    post = [None] * POPS
    post[0] = (1.0 - OMEGA_EVEN) * f[0] + (OMEGA_EVEN * WEIGHTS[0]) * base
    shared = {}
    for weight in (WEIGHTS[1], WEIGHTS[7]):
        shared[weight] = ((OMEGA_EVEN * weight) * base, (OMEGA_EVEN * weight * 4.5) * density,
                          (OMEGA_ODD * weight * 3.0) * density)
    for i in range(1, POPS, 2):
        projected = None
        for axis in range(3):
            sign = VELOCITIES[i][axis]
            if sign == 0:
                continue
            if projected is None:
                projected = velocity[axis] if sign == 1 else -velocity[axis]
            else:
                projected = projected + velocity[axis] if sign == 1 else projected - velocity[axis]
        low, curve, slope = shared[WEIGHTS[i]]
        even_part = (0.5 - 0.5 * OMEGA_EVEN) * even[i] + (low + curve * (projected * projected))
        odd_part = (0.5 - 0.5 * OMEGA_ODD) * odd[i] + slope * projected
        post[i] = even_part + odd_part
        post[i + 1] = even_part - odd_part
    return post, density


def pushes(density, drift_y, drift_z):
    along_y = density * drift_y
    along_z = density * drift_z
    out = [None] * POPS
    for i in range(1, POPS):
        _, step_y, step_z = VELOCITIES[i]
        total = None
        for sign, part in ((step_y, along_y), (step_z, along_z)):
            if sign == 0:
                continue
            if total is None:
                total = part if sign == 1 else -part
            else:
                total = total + part if sign == 1 else total - part
        if total is not None:
            out[i] = (6.0 * WEIGHTS[i]) * total
    return out


def total_of(parts):
    parts = list(parts)
    while len(parts) > 1:
        pairs = [parts[n] + parts[n + 1] for n in range(0, len(parts) - 1, 2)]
        parts = pairs + parts[len(parts) - len(parts) % 2 :]
    return parts[0]


def streamed(pull, own, drift_y, drift_z):
    push = pushes(total_of(own), drift_y, drift_z)
    out = [own[0]]
    for i in range(1, POPS):
        pulled = pull(i)
        bounced = own[OPPOSITE[i]]
        blocked = pulled < WALL_BELOW
        if push[i] is not None:
            bounced = jnp.where(pulled < OUT_BELOW, bounced, bounced + push[i])
        out.append(jnp.where(blocked, bounced, pulled))
    return out


def ahead(items, take, leave, depth):
    waiting = []
    for n in items:
        waiting.append((n, take(n)))
        if len(waiting) > depth:
            leave(*waiting.pop(0))
    for pair in waiting:
        leave(*pair)


def place():
    return lax.axis_index("stream"), lax.axis_index("cy"), lax.axis_index("cz")


def slot_of(pos, row, layer, column_z):
    slot = (pos[0, row] - (layer * BXD - 1)) * BZD + (pos[2, row] - column_z * BZD)
    return jnp.clip(slot, 0, LAYERS * BZD - 1)


def fill_table(pos, table):
    layer, _, column_z = place()
    for entry in range(LAYERS * BZD):
        table[entry] = -1
    for row in range(pos.shape[1]):

        @pl.when(pos[0, row] >= 0)
        def _(row=row):
            table[slot_of(pos, row, layer, column_z)] = row


def spread_marks(marks, dense):
    rows = marks.shape[0]
    for first in range(0, rows, 8):
        size = min(8, rows - first)
        for begin in range(0, TILES, 8):
            values = [marks[first : first + size, t * LANE : (t + 1) * LANE] for t in range(begin, begin + 8)]
            for k, value in enumerate(values):
                dense[pl.ds(first * TILES + begin + k, size, stride=TILES), :] = value.astype(jnp.float32)


def collide_block(ref, base):
    for part in range(TILES // 8):
        old = [ref[pl.ds(base + i * TILES + 8 * part, 8), :] for i in range(POPS)]
        mark = ref[pl.ds(base + POPS * TILES + 8 * part, 8), :] > 0.5
        post, _ = collide(old)
        for i in range(POPS):
            ref[pl.ds(base + i * TILES + 8 * part, 8), :] = jnp.where(mark, old[i], post[i])


def pack_block(out, base, stage, dense, row):
    out[pl.ds(base + POPS * TILES, TILES), :] = dense[pl.ds(pl.multiple_of(row * TILES, 8), TILES), :]
    for first in range(0, TILES, 4):
        moves = []
        for tile in range(first, first + 4):
            for group, size in GROUPS:
                value = stage[group : group + size, tile * LANE : (tile + 1) * LANE]
                moves.append((pl.ds(base + group * TILES + tile, size, stride=TILES), value))
        for target, value in moves:
            out[target, :] = value
    collide_block(out, base)


def pack_stream(places, marks_in, pops, up, down, pos, table, marks, dense, blocks, slabs, strip, sems):
    mark_copy = pltpu.make_async_copy(marks_in, marks, sems.at[0])
    mark_copy.start()
    place_copy = pltpu.make_async_copy(places, pos, sems.at[1])
    place_copy.start()
    rows = pos.shape[1]
    copies = [None] * 4
    for j in range(MOVE_CAP):
        copies[MOVE_CAP + j] = pltpu.make_async_copy(pops.at[j], blocks.at[MOVE_CAP + j], sems.at[2 + MOVE_CAP + j])
        copies[MOVE_CAP + j].start()
    place_copy.wait()
    count = 0
    for row in range(rows):
        count = count + jnp.where(pos[0, row] >= 0, 1, 0)
    last = jnp.clip(count - MOVE_CAP, 0, rows - MOVE_CAP)
    for j in range(MOVE_CAP):
        copies[j] = pltpu.make_async_copy(pops.at[last + j], blocks.at[j], sems.at[2 + j])
        copies[j].start()
    fill_table(pos, table)
    slab_rows = []
    slab_copies = []
    for side in range(2):
        for bz in range(BZD):
            row = jnp.maximum(table[(2 - side) * BZD + bz], 0)
            n = side * BZD + bz
            first = (TILES - SLAB) * LANE if side == 0 else 0
            slab_rows.append(row)
            slab_copies.append(
                pltpu.make_async_copy(
                    pops.at[row, :, pl.ds(first, SLAB * LANE)], slabs.at[n], sems.at[2 + 2 * MOVE_CAP + n]
                )
            )
            slab_copies[n].start()
    mark_copy.wait()
    spread_marks(marks, dense)
    for side, out in ((1, down), (0, up)):
        for j in range(MOVE_CAP):
            row = j if side == 1 else last + j
            for k, axis in ((0, 0), (1, 2)):
                value = jnp.full((1, LANE), pos[axis, row], jnp.int32).astype(jnp.float32)
                out[pl.ds(SENT_META + 2 * j + k, 1), :] = value
            n = side * MOVE_CAP + j
            copies[n].wait()
            pack_block(out, j * BLOCK, blocks.at[n], dense, row)
    for side, out in enumerate((up, down)):
        for bz in range(BZD):
            n = side * BZD + bz
            first = slab_rows[n] * TILES + (TILES - SLAB if side == 0 else 0)
            slab_copies[n].wait()
            moves = []
            for x in range(2):
                for yhi in range(2):
                    q = 2 * x + yhi
                    row = x * FACE + 2 * bz + yhi
                    for group, size in GROUPS:
                        value = slabs[n, group : group + size, q * LANE : (q + 1) * LANE]
                        moves.append((pl.ds(group * 2 * FACE + row, size, stride=2 * FACE), value))
                row = POPS * 2 * FACE + x * FACE + 2 * bz
                moves.append((pl.ds(row, 2), dense[pl.ds(first + 2 * x, 2), :]))
            for target, value in moves:
                strip[target, :] = value
        inner = 1 if side == 0 else 0
        for x in range(2):
            old = [strip[pl.ds(i * 2 * FACE + x * FACE, FACE), :] for i in range(POPS)]
            mark = strip[pl.ds(POPS * 2 * FACE + x * FACE, FACE), :] > 0.5
            post, _ = collide(old)
            if x == inner:
                pairs = [(i, i) for i in range(POPS)]
            else:
                pairs = [(POPS + n, i) for n, i in enumerate(AHEAD if side == 0 else BACK)]
            for plane, i in pairs:
                out[pl.ds(SENT_SLABS + plane * FACE, FACE), :] = jnp.where(mark, ROTOR, post[i])


def pack_edge(places, marks_in, pops, own, zpack, zup, zdown, pos, table, marks, dense, stage, sems):
    column_z = lax.axis_index("cz")
    mark_copy = pltpu.make_async_copy(marks_in, marks, sems.at[LAYERS])
    mark_copy.start()
    place_copy = pltpu.make_async_copy(places, pos, sems.at[LAYERS + 1])
    place_copy.start()
    place_copy.wait()
    fill_table(pos, table)
    edge_bz = jnp.where(column_z == 0, BZD - 1, 0)
    first_c = jnp.where(column_z == 0, EDGE - 2, 0)
    found = [table[held * BZD + edge_bz] for held in range(LAYERS)]
    row_of = [jnp.maximum(row, 0) for row in found]
    copies = []
    for held in range(LAYERS):
        copies.append(pltpu.make_async_copy(pops.at[row_of[held]], stage.at[held], sems.at[held]))
        copies[held].start()
    mark_copy.wait()
    spread_marks(marks, dense)
    spot = (lanes() % EDGE) // 2
    sublane = lax.broadcasted_iota(jnp.int32, (8, LANE), 0)
    flags = jnp.zeros((8, LANE), jnp.int32)
    for held in range(LAYERS):
        copies[held].wait()
        base = pl.multiple_of((held * BZD + edge_bz) * BLOCK, 8)

        @pl.when(found[held] >= 0)
        def _(held=held, base=base):
            pack_block(own, base, stage.at[held], dense, row_of[held])
            totals = []
            for group in range(ZGROUPS):
                for part in range(TILES // 8):
                    total = jnp.zeros((8, LANE), jnp.float32)
                    for k in range(min(8, PLANES - group * 8)):
                        value = own[pl.ds(base + (group * 8 + k) * TILES + part * 8, 8), :]
                        value = pltpu.roll(value, (2 * k - first_c + LANE) % LANE, 1)
                        total = jnp.where(spot == k, value, total)
                    totals.append((held * ZROWS + group * TILES + part * 8, total))
            for row, total in totals:
                zpack[pl.ds(row, 8), :] = total

        flags = jnp.where((sublane == held) & (found[held] >= 0), 1, flags)
    zpack[pl.ds(ZMETA, 8), :] = flags.astype(jnp.float32)
    zup[pl.ds(0, ZROWS), :] = zpack[pl.ds(3 * ZROWS, ZROWS), :]
    zdown[pl.ds(0, ZROWS), :] = zpack[pl.ds(0, ZROWS), :]
    for group in range(ZGROUPS):
        target = pl.ds(ZROWS + group * SLAB, SLAB)
        zup[target, :] = zpack[pl.ds(2 * ZROWS + group * TILES + TILES - SLAB, SLAB), :]
        zdown[target, :] = zpack[pl.ds(ZROWS + group * TILES, SLAB), :]


def pack_own(places, marks_in, pops, own_in, own, pos, marks, dense, stage, sems):
    del own_in
    layer, _, column_z = place()
    edge_bz = jnp.where(column_z == 0, BZD - 1, 0)
    rows = pos.shape[1]
    mark_copy = pltpu.make_async_copy(marks_in, marks, sems.at[rows])
    mark_copy.start()
    place_copy = pltpu.make_async_copy(places, pos, sems.at[rows + 1])
    place_copy.start()
    copies = [pltpu.make_async_copy(pops.at[r], stage.at[r], sems.at[r]) for r in range(rows)]
    for copy in copies:
        copy.start()
    mark_copy.wait()
    spread_marks(marks, dense)
    place_copy.wait()

    def settle(row, carry):
        pltpu.make_async_copy(pops.at[row], stage.at[row], sems.at[row]).wait()
        slot = slot_of(pos, row, layer, column_z)

        @pl.when((pos[0, row] >= 0) & (slot % BZD != edge_bz))
        def _():
            pack_block(own, pl.multiple_of(slot * BLOCK, 8), stage.at[row], dense, row)

        return carry

    lax.fori_loop(0, rows, settle, 0)


def gathered(parts, zvalue, spot, ylo, column_z):
    lane = lanes()
    rows = parts[0].shape[0]
    lane = lane[:rows]
    total = None
    for bz in range(BZD):
        shift = (bz * EDGE - ylo * EDGE) % LANE
        value = pltpu.roll(parts[bz], shift, 1) if shift else parts[bz]
        total = value if total is None else jnp.where(lane // EDGE == bz, value, total)
    goal = jnp.where(column_z == 0, SPAN_Z, LANE - 2)
    zvalue = pltpu.roll(zvalue, (goal - (ylo * EDGE + 2 * spot) + LANE) % LANE, 1)
    return jnp.where(lane >= SPAN_Z, zvalue, total)


def gathered_rows(parts, zvalue, spot, column_z):
    lane = lanes()[: parts[0].shape[0]]
    single = (lane // EDGE) % 2 == 1
    double = (lane // (2 * EDGE)) % 2 == 1
    main = lane < SPAN_Z
    pairs = []
    for n in (0, 2):
        even = jnp.where(single, pltpu.roll(parts[n + 1], EDGE, 1), parts[n])
        odd = jnp.where(single, parts[n + 1], pltpu.roll(parts[n], LANE - EDGE, 1))
        pairs.append((even, odd))
    goal = jnp.where(column_z == 0, SPAN_Z, LANE - 2)
    out = [None] * YLO
    for r in range(4):
        low, high = pairs[0][r % 2], pairs[1][r % 2]
        if r < 2:
            both = jnp.where(double, pltpu.roll(high, 2 * EDGE, 1), low)
        else:
            both = jnp.where(double, high, pltpu.roll(low, LANE - 2 * EDGE, 1))
        beyond = pltpu.roll(zvalue, (goal - (r * EDGE + 2 * spot) + LANE) % LANE, 1)
        out[r] = jnp.where(main, both, beyond)
        out[r + 4] = pltpu.roll(jnp.where(main, beyond, both), SPAN_Z, 1)
    return out


def inside_lanes(rows, column_z):
    lane = lanes()[:rows]
    low = (column_z == 0) & (lane >= SPAN_Z) & (lane < SPAN_Z + 2)
    high = (column_z != 0) & (lane >= LANE - 2)
    return (lane < SPAN_Z) | low | high


def marked(post, mark, inside):
    flag = jnp.where(inside, jnp.where(mark > 0.5, ROTOR, 0.0), OUTSIDE)
    wall = flag < WALL_BELOW
    return [jnp.where(wall, flag, value) for value in post]


def plane_parts(own, edge, zall, zedge, chunk, yhi, plane):
    group = plane // 8
    if chunk is None:
        if plane == POPS:
            parts = [jnp.zeros((4, LANE), jnp.float32)] * BZD
        else:
            parts = [edge[pl.ds(plane * 4 * FACE + 2 * bz + yhi, 4, stride=FACE), :] for bz in range(BZD)]
        return parts, zedge[pl.ds(group * 8 + yhi, 4, stride=2), :]
    held, half = 1 + chunk // 2, chunk % 2
    parts = []
    for bz in range(BZD):
        base = (held * BZD + bz) * BLOCK + plane * TILES + half * EDGE + yhi
        parts.append(own[pl.ds(base, 8, stride=2), :])
    return parts, zall[pl.ds(held * ZROWS + group * TILES + half * EDGE + yhi, 8, stride=2), :]


def chunk_values(own, edge, zall, zedge, chunk, yhi, ylo, column_z):
    out = []
    for plane in range(PLANES):
        parts, zvalue = plane_parts(own, edge, zall, zedge, chunk, yhi, plane)
        out.append(gathered(parts, zvalue, plane % 8, ylo, column_z))
    return out


def halo_x_inside(layer, layers):
    row = lax.broadcasted_iota(jnp.int32, (4, LANE), 0)
    low = (row < 2) & (layer > 0)
    high = (row >= 2) & (layer < layers - 1)
    return low | high


def settle_rim(layers, places, up, down, zin, zup, zdown, own_in, own, edge, zall, zedge, rim_up, rim_down, pos, post_up, post_down, sem):
    del own_in
    layer, _, column_z = place()
    place_copy = pltpu.make_async_copy(places, pos, sem)
    place_copy.start()
    for arrived in (up, down):
        for j in range(MOVE_CAP):
            bx = arrived[pl.ds(SENT_META + 2 * j, 1), :].astype(jnp.int32)
            bz = arrived[pl.ds(SENT_META + 2 * j + 1, 1), :].astype(jnp.int32)
            code = (bx - layer * BXD) * BZD + (bz - column_z * BZD)
            mine = (bx >= layer * BXD) & (bx < (layer + 1) * BXD)
            first = layer == 0 if arrived is up else layer == layers - 1
            code = jnp.max(jnp.where(mine, code, -1))

            @pl.when((code >= 0) & jnp.logical_not(first))
            def _(arrived=arrived, j=j, code=code):
                base = pl.multiple_of((jnp.clip(code, 0, BXD * BZD - 1) + BZD) * BLOCK, 8)
                for k in range(0, BLOCK, 128):
                    values = [arrived[pl.ds(j * BLOCK + k + 8 * n, 8), :] for n in range(16)]
                    for n, value in enumerate(values):
                        own[pl.ds(base + k + 8 * n, 8), :] = value

    place_copy.wait()
    for side, arrived in enumerate((up, down)):
        inner, outer = (1, 0) if side == 0 else (2, 3)
        pairs = [(i, i, inner) for i in range(POPS)]
        pairs += [(POPS + n, i, outer) for n, i in enumerate(AHEAD if side == 0 else BACK)]
        values = [arrived[pl.ds(SENT_SLABS + plane * FACE, FACE), :] for plane, _, _ in pairs]
        for (_, i, x), value in zip(pairs, values):
            edge[pl.ds((i * 4 + x) * FACE, FACE), :] = value
        for bz in range(BZD):
            here = jnp.int32(0)
            goal = (0 if side == 0 else LAYERS - 1) * BZD + bz
            for row in range(pos.shape[1]):
                hit = (pos[0, row] >= 0) & (slot_of(pos, row, layer, column_z) == goal)
                here = jnp.where(hit, 1, here)

            @pl.when(here == 1)
            def _(side=side, pairs=pairs, goal=goal, bz=bz):
                first = goal * BLOCK + (TILES - SLAB if side == 0 else 0)
                values = []
                for _, i, x in pairs:
                    shift = 2 * (x if side == 0 else x - 2)
                    mark = own[pl.ds(first + POPS * TILES + shift, 2), :] > 0.5
                    values.append(jnp.where(mark, ROTOR, own[pl.ds(first + i * TILES + shift, 2), :]))
                for (_, i, x), value in zip(pairs, values):
                    edge[pl.ds((i * 4 + x) * FACE + 2 * bz, 2), :] = value

    moves = []
    for held in range(LAYERS):
        flag = zin[pl.ds(ZMETA + held, 1), :] > 0.5
        for group in range(ZGROUPS):
            if held == 1 or held == 2:
                for part in range(TILES // 8):
                    rows = pl.ds(held * ZROWS + group * TILES + part * 8, 8)
                    source = zup if held == 1 else zdown
                    other = source[pl.ds(group * TILES + part * 8, 8), :]
                    moves.append((zall, rows, jnp.where(flag, zin[rows, :], other)))
            else:
                side = 0 if held == 0 else 1
                source = zup if held == 0 else zdown
                first = TILES - SLAB if held == 0 else 0
                mine = zin[pl.ds(held * ZROWS + group * TILES + first, SLAB), :]
                other = source[pl.ds(ZROWS + group * SLAB, SLAB), :]
                moves.append((zedge, pl.ds(group * 8 + side * SLAB, SLAB), jnp.where(flag, mine, other)))
    for target, rows, value in moves:
        target[rows, :] = value
    for chunk in (0, 1, 2, 3, None):
        for y in (0, 1, SPAN_Y - 2, SPAN_Y - 1):
            values = chunk_values(own, edge, zall, zedge, chunk, y // YLO, y % YLO, column_z)
            inside = inside_lanes(values[0].shape[0], column_z)
            if chunk is None:
                inside = inside & halo_x_inside(layer, layers)
            post = marked(values[:POPS], values[POPS], inside)
            target = post_down if y < 2 else post_up
            rim = RIM_DOWN if y < 2 else RIM_UP
            if y in (0, SPAN_Y - 1):
                pairs = [(i, i) for i in range(POPS)]
            else:
                pairs = [(POPS + n, i) for n, i in enumerate(rim)]
            for plane, i in pairs:
                if chunk is None:
                    target[pl.ds(plane * GRID_X, 2), :] = post[i][:2]
                    target[pl.ds(plane * GRID_X + EXT_X - 2, 2), :] = post[i][2:]
                else:
                    target[pl.ds(plane * GRID_X + 2 + 8 * chunk, 8), :] = post[i]
    lane = lanes()
    for source, target in ((post_up, rim_up), (post_down, rim_down)):
        for chunk in range(5):
            size = min(8, EXT_X - 8 * chunk)
            values = []
            for plane in range(RIM):
                value = source[pl.ds(plane * GRID_X + 8 * chunk, 8), :]
                values.append(pltpu.roll(value, (plane * EXT_Z + 2 * column_z) % LANE, 1))
            totals = []
            for block in range(RIM_BLOCKS):
                total = jnp.zeros((8, LANE), jnp.float32)
                for plane in range(RIM):
                    begin = plane * EXT_Z - block * LANE
                    if begin >= LANE or begin + EXT_Z <= 0:
                        continue
                    total = jnp.where((lane >= begin) & (lane < begin + EXT_Z), values[plane], total)
                totals.append(total)
            for block in range(RIM_BLOCKS):
                target[pl.ds(block * EXT_X + 8 * chunk, size), :] = totals[block][:size]


def turned(value, step_z):
    return pltpu.roll(value, step_z % LANE, 1) if step_z else value


def drifts_of(columns, depth):
    _, _, column_z = place()
    lane = lanes()
    total_y = SPAN_Y * columns
    total_z = SPAN_Z * depth
    spin = 0.2 / (total_y + total_z)
    here_z = jnp.where(lane < SPAN_Z + 8, lane, lane - LANE) + column_z * SPAN_Z
    drift_y = -spin * (here_z.astype(jnp.float32) - (total_z - 1) / 2.0)
    return drift_y, spin, (total_y - 1) / 2.0


def first_step(columns, depth, field, later, begin, end):
    _, column_y, _ = place()
    drift_y, spin, centre_y = drifts_of(columns, depth)
    sublane = lax.broadcasted_iota(jnp.int32, (8, LANE), 0)

    def tile(n, carry):
        base = pl.multiple_of(8 * n, 8)
        line = (n - FIRST // 8 + 2 * STEP) // STEP
        next_row = (sublane >= 6) & (n - FIRST // 8 + 2 * STEP - line * STEP == STEP - 1)
        here_y = jnp.where(next_row, line + 1, line) + (column_y * SPAN_Y - 2)
        drift_z = spin * (here_y.astype(jnp.float32) - centre_y)
        old = [field[pl.ds(i * FIELD + base, 8), :] for i in range(POPS)]
        values = streamed(pull_from(field, base), old, drift_y, drift_z)
        post, _ = collide(values)
        wall = old[0] < WALL_BELOW
        for i in range(POPS):
            later[pl.ds(i * FIELD + base, 8), :] = jnp.where(wall, old[0], post[i])
        return carry

    lax.fori_loop(FIRST // 8 + begin, FIRST // 8 + end, tile, 0)


def pull_from(field, base):
    def pull(i):
        step_x, step_y, step_z = VELOCITIES[i]
        return turned(field[pl.ds(i * FIELD + base - step_y * PITCH - step_x, 8), :], step_z)

    return pull


def settle_all(layers, columns, depth, own, edge, zall, zedge, field, start, later):
    layer, _, column_z = place()

    def caps_of(mark, inside):
        return [jnp.where(inside, jnp.where(value > 0.5, ROTOR, -ROTOR), OUTSIDE) for value in mark]

    def halves(yhi, carry):
        def rows_of_plane(chunk, plane):
            parts, zvalue = plane_parts(own, edge, zall, zedge, chunk, yhi, plane)
            return gathered_rows(parts, zvalue, plane % 8, column_z)

        top = yhi * YLO * PITCH + FIRST

        def chunks(chunk, carry):
            caps = caps_of(rows_of_plane(chunk, POPS), inside_lanes(8, column_z))

            def leave(i, values):
                for ylo in range(YLO):
                    row = pl.multiple_of(i * FIELD + top + ylo * PITCH + 8 * chunk, 8)
                    field[pl.ds(row, 8), :] = jnp.minimum(values[ylo], caps[ylo])
                    row = pl.multiple_of((i * SPAN_Y + YLO * yhi + ylo) * SPAN_X + 8 * chunk, 8)
                    start[pl.ds(row, 8), :] = values[ylo]

            ahead(range(POPS), lambda i: rows_of_plane(chunk, i), leave, 1)
            return carry

        lax.fori_loop(0, SPAN_X // 8, chunks, 0)
        inside = inside_lanes(4, column_z) & halo_x_inside(layer, layers)
        caps = caps_of(rows_of_plane(None, POPS), inside)

        def leave(i, values):
            for ylo in range(YLO):
                value = jnp.minimum(values[ylo], caps[ylo])
                row = i * FIELD + top + ylo * PITCH
                field[pl.ds(row - 2, 2), :] = value[:2]
                field[pl.ds(row + SPAN_X, 2), :] = value[2:]

        ahead(range(POPS), lambda i: rows_of_plane(None, i), leave, 1)
        return carry

    lax.fori_loop(0, SPAN_Y // YLO, halves, 0)
    first_step(columns, depth, field, later, STEP, (SPAN_Y - 1) * STEP)


def finish(columns, depth, rim_low, rim_high, field_in, start, later_in, out, field, later, turn, result, sems):
    del field_in, later_in
    _, column_y, column_z = place()
    flat = (lanes() + 2 * column_z) % LANE
    sides = (
        (rim_low, -1, -2, RIM_UP, column_y > 0),
        (rim_high, SPAN_Y, SPAN_Y + 1, RIM_DOWN, column_y < columns - 1),
    )
    for source, near, far, rim, there in sides:
        for chunk in range(5):
            size = min(8, EXT_X - 8 * chunk)
            blocks = [source[pl.ds(block * EXT_X + 8 * chunk, 8), :] for block in range(RIM_BLOCKS)]
            for plane in range(RIM):
                block, begin = divmod(plane * EXT_Z, LANE)
                shift = (2 * LANE - begin - 2 * column_z) % LANE
                value = pltpu.roll(blocks[block], shift, 1)
                if begin + EXT_Z > LANE:
                    value = jnp.where(flat < LANE - begin, value, pltpu.roll(blocks[block + 1], shift, 1))
                value = jnp.where((flat < EXT_Z) & there, value, OUTSIDE)
                i, y = (plane, near) if plane < POPS else (rim[plane - POPS], far)
                row = i * FIELD + FIRST + y * PITCH - 2 + 8 * chunk
                field[pl.ds(row, size), :] = value[:size]

    first_step(columns, depth, field, later, -STEP - 1, STEP)
    first_step(columns, depth, field, later, (SPAN_Y - 1) * STEP - 1, (SPAN_Y + 1) * STEP)

    drift_y, spin, centre_y = drifts_of(columns, depth)

    def leave(n):
        part = pl.ds(n * 8, 8)
        return pltpu.make_async_copy(result.at[:, part], out.at[:, part], sems.at[n])

    def second_step(chunk, carry):
        for half in range(SPAN_Y // 8):
            for k in range(8):
                y = 8 * half + k
                base = pl.multiple_of(FIRST + y * PITCH + 8 * chunk, 8)
                drift_z = spin * ((column_y * SPAN_Y + y).astype(jnp.float32) - centre_y)
                old = [later[pl.ds(i * FIELD + base, 8), :] for i in range(POPS)]
                values = streamed(pull_from(later, base), old, drift_y, drift_z)
                wall = old[0] < WALL_BELOW
                for i in range(POPS):
                    first = pl.multiple_of((i * SPAN_Y + y) * SPAN_X + 8 * chunk, 8)
                    value = jnp.where(wall, start[pl.ds(first, 8), :], values[i])
                    turn[pl.ds(i * 8 * TURN + k * TURN, 8), :] = value
            for k in range(8):
                values = [turn[pl.ds(i * 8 * TURN + k, 8, stride=TURN), :] for i in range(POPS)]
                for i in range(POPS):
                    result[i, 8 * chunk + k, 8 * half : 8 * half + 8, :] = values[i][:, :SPAN_Z]
        leave(chunk).start()
        return carry

    lax.fori_loop(0, SPAN_X // 8, second_step, 0)
    for n in range(SPAN_X // 8):
        leave(n).wait()


def rows_of(count):
    return jax.ShapeDtypeStruct((count, LANE), jnp.float32)


def kept(count):
    return VMEM((count, LANE), jnp.float32)


def params(mib):
    return pltpu.CompilerParams(vmem_limit_bytes=mib * 2**20)


def shards(populations, solid_cells, block_pos):
    layers = lax.axis_size("stream")
    columns = lax.axis_size("cy")
    depth = lax.axis_size("cz")
    rows = block_pos.shape[0]
    vmem = pl.BlockSpec(memory_space=VMEM)
    hbm = pl.BlockSpec(memory_space=pltpu.HBM)
    populations = pltpu.with_memory_space_constraint(populations, pltpu.HBM)
    solid_cells = pltpu.with_memory_space_constraint(solid_cells, pltpu.HBM)
    places = pltpu.with_memory_space_constraint(block_pos.T, pltpu.HBM)
    place_scratch = SMEM((3, rows), jnp.int32)
    table_scratch = SMEM((LAYERS * BZD,), jnp.int32)
    mark_scratch = [VMEM((rows, EDGE**3), jnp.int32), VMEM((rows * TILES, LANE), jnp.float32)]

    up = [(i, i + 1) for i in range(layers - 1)]
    down = [(i + 1, i) for i in range(layers - 1)]
    send_up, send_down = pl.pallas_call(
        pack_stream,
        out_shape=(kept(SENT_ROWS), kept(SENT_ROWS)),
        in_specs=[hbm, hbm, hbm],
        out_specs=(vmem, vmem),
        scratch_shapes=[place_scratch, table_scratch]
        + mark_scratch
        + [
            VMEM((2 * MOVE_CAP, POPS, EDGE**3), jnp.float32),
            VMEM((2 * BZD, POPS, SLAB * LANE), jnp.float32),
            VMEM((PLANES * 2 * FACE, LANE), jnp.float32),
            pltpu.SemaphoreType.DMA((2 + 2 * MOVE_CAP + 2 * BZD,)),
        ],
        compiler_params=params(16),
        name="pack_stream",
    )(places, solid_cells, populations)
    from_low = lax.ppermute(send_up, "stream", up)
    from_high = lax.ppermute(send_down, "stream", down)

    own, zpack, zsend_up, zsend_down = pl.pallas_call(
        pack_edge,
        out_shape=(kept(LAYERS * BZD * BLOCK), kept(ZMETA + 8), kept(DIAG), kept(DIAG)),
        in_specs=[hbm, hbm, hbm],
        out_specs=(vmem,) * 4,
        scratch_shapes=[place_scratch, table_scratch]
        + mark_scratch
        + [
            VMEM((LAYERS, POPS, EDGE**3), jnp.float32),
            pltpu.SemaphoreType.DMA((LAYERS + 2,)),
        ],
        compiler_params=params(16),
        name="pack_edge",
    )(places, solid_cells, populations)
    swap = [(i, depth - 1 - i) for i in range(depth)]
    zin = lax.ppermute(zpack, "cz", swap)
    zup_pairs = [(s * depth + c, t * depth + d) for s, t in up for c, d in swap]
    zdown_pairs = [(s * depth + c, t * depth + d) for s, t in down for c, d in swap]
    z_low = lax.ppermute(zsend_up, ("stream", "cz"), zup_pairs)
    z_high = lax.ppermute(zsend_down, ("stream", "cz"), zdown_pairs)

    own = pl.pallas_call(
        pack_own,
        out_shape=kept(LAYERS * BZD * BLOCK),
        in_specs=[hbm, hbm, hbm, vmem],
        out_specs=vmem,
        scratch_shapes=[place_scratch]
        + mark_scratch
        + [
            VMEM((rows, POPS, EDGE**3), jnp.float32),
            pltpu.SemaphoreType.DMA((rows + 2,)),
        ],
        input_output_aliases={3: 0},
        compiler_params=params(16),
        name="pack_own",
    )(places, solid_cells, populations, own)

    own, edge, zall, zedge, rim_up, rim_down = pl.pallas_call(
        functools.partial(settle_rim, layers),
        out_shape=(
            kept(LAYERS * BZD * BLOCK),
            kept(POPS * 4 * FACE),
            kept(LAYERS * ZROWS),
            kept(ZGROUPS * 8),
            kept(RIM_ROWS),
            kept(RIM_ROWS),
        ),
        in_specs=[hbm] + [vmem] * 6,
        out_specs=(vmem,) * 6,
        scratch_shapes=[
            place_scratch,
            VMEM((RIM * GRID_X, LANE), jnp.float32),
            VMEM((RIM * GRID_X, LANE), jnp.float32),
            pltpu.SemaphoreType.DMA,
        ],
        input_output_aliases={6: 0},
        compiler_params=params(16),
        name="settle_rim",
    )(places, from_low, from_high, zin, z_low, z_high, own)
    cy_up = [(i, i + 1) for i in range(columns - 1)]
    cy_down = [(i + 1, i) for i in range(columns - 1)]
    rim_low = lax.ppermute(rim_up, "cy", cy_up)
    rim_high = lax.ppermute(rim_down, "cy", cy_down)

    field, start, later = pl.pallas_call(
        functools.partial(settle_all, layers, columns, depth),
        out_shape=(kept(POPS * FIELD), kept(POPS * SPAN_X * SPAN_Y), kept(POPS * FIELD)),
        in_specs=[vmem] * 4,
        out_specs=(vmem,) * 3,
        compiler_params=params(16),
        name="settle_all",
    )(own, edge, zall, zedge)

    out, _, _ = pl.pallas_call(
        functools.partial(finish, columns, depth),
        out_shape=(
            jax.ShapeDtypeStruct((POPS, SPAN_X, SPAN_Y, SPAN_Z), jnp.float32),
            kept(POPS * FIELD),
            kept(POPS * FIELD),
        ),
        in_specs=[vmem] * 5,
        out_specs=(hbm, vmem, vmem),
        scratch_shapes=[
            VMEM((POPS * 8 * TURN, LANE), jnp.float32),
            VMEM((POPS, SPAN_X, SPAN_Y, SPAN_Z), jnp.float32),
            pltpu.SemaphoreType.DMA((SPAN_X // 8,)),
        ],
        input_output_aliases={2: 1, 4: 2},
        compiler_params=params(16),
        name="finish",
    )(rim_low, rim_high, field, start, later)
    return out


def solution(mesh):
    in_specs = (
        P(("stream", "cy", "cz"), None, None),
        P(("stream", "cy", "cz"), None),
        P(("stream", "cy", "cz"), None),
    )
    out_specs = P(None, "stream", "cy", "cz")
    return jax.shard_map(shards, mesh=mesh, in_specs=in_specs, out_specs=out_specs, check_vma=False)
```

```python
import functools

import jax
import jax.numpy as jnp
from jax import lax
from jax.experimental import pallas as pl
from jax.experimental.pallas import tpu as pltpu
from jax.sharding import PartitionSpec as P

EDGE = 16
BXD = 2
BYD = 1
BZD = 4
MOVE_CAP = 2

VELOCITIES = (
    (0, 0, 0),
    (1, 0, 0),
    (-1, 0, 0),
    (0, 1, 0),
    (0, -1, 0),
    (0, 0, 1),
    (0, 0, -1),
    (1, 1, 0),
    (-1, -1, 0),
    (1, -1, 0),
    (-1, 1, 0),
    (1, 0, 1),
    (-1, 0, -1),
    (1, 0, -1),
    (-1, 0, 1),
    (0, 1, 1),
    (0, -1, -1),
    (0, 1, -1),
    (0, -1, 1),
)
WEIGHTS = (1.0 / 3.0,) + (1.0 / 18.0,) * 6 + (1.0 / 36.0,) * 12
OPPOSITE = (0, 2, 1, 4, 3, 6, 5, 8, 7, 10, 9, 12, 11, 14, 13, 16, 15, 18, 17)
OMEGA_EVEN = 1.25
OMEGA_ODD = 1.0 / 1.125

POPS = 19
PLANES = 20
LANE = 128
TILES = EDGE**3 // LANE
BLOCK = PLANES * TILES
YLO = LANE // EDGE
SLAB = 4
GROUPS = ((0, 8), (8, 8), (16, 3))
SENT_SLABS = MOVE_CAP * BLOCK
LAYERS = BXD + 2
ZGROUPS = 3
ZROWS = ZGROUPS * TILES
ZMETA = LAYERS * ZROWS
DIAG = ZROWS + ZGROUPS * SLAB

SPAN_X = BXD * EDGE
SPAN_Y = BYD * EDGE
SPAN_Z = BZD * EDGE
PITCH = SPAN_X + 8
STEP = PITCH // 8
FIRST = 96
FIELD = FIRST + (SPAN_Y + 1) * PITCH + 48
TURN = 9
EXT_X = SPAN_X + 4
EXT_Z = SPAN_Z + 2
RIM_UP = tuple(i for i in range(POPS) if VELOCITIES[i][1] == 1)
RIM_DOWN = tuple(i for i in range(POPS) if VELOCITIES[i][1] == -1)
RIM = POPS + len(RIM_UP)
AHEAD = tuple(i for i in range(POPS) if VELOCITIES[i][0] == 1)
BACK = tuple(i for i in range(POPS) if VELOCITIES[i][0] == -1)
FACE = 2 * BZD
SENT_META = SENT_SLABS + RIM * FACE
SENT_ROWS = SENT_META + 8
RIM_BLOCKS = -(-RIM * EXT_Z // LANE)
RIM_ROWS = RIM_BLOCKS * EXT_X + 4
GRID_X = 48

ROTOR = -1.0e30
OUTSIDE = -2.0e30
WALL_BELOW = -1.0e20
OUT_BELOW = -1.5e30

VMEM = pltpu.VMEM
SMEM = pltpu.SMEM


def lanes():
    return lax.broadcasted_iota(jnp.int32, (8, LANE), 1)


def collide(f):
    even = [None] * POPS
    odd = [None] * POPS
    for i in range(1, POPS, 2):
        even[i] = f[i] + f[i + 1]
        odd[i] = f[i] - f[i + 1]
    density = f[0]
    for i in range(1, POPS, 2):
        density = density + even[i]
    flow = []
    for axis in range(3):
        total = None
        for i in range(1, POPS, 2):
            sign = VELOCITIES[i][axis]
            if sign == 0:
                continue
            if total is None:
                total = odd[i] if sign == 1 else -odd[i]
            else:
                total = total + odd[i] if sign == 1 else total - odd[i]
        flow.append(total)
    inverse = 1.0 / density
    velocity = [part * inverse for part in flow]
    square = velocity[0] * velocity[0] + velocity[1] * velocity[1] + velocity[2] * velocity[2]
    base = density * (1.0 - 1.5 * square)
    post = [None] * POPS
    post[0] = (1.0 - OMEGA_EVEN) * f[0] + (OMEGA_EVEN * WEIGHTS[0]) * base
    shared = {}
    for weight in (WEIGHTS[1], WEIGHTS[7]):
        shared[weight] = ((OMEGA_EVEN * weight) * base, (OMEGA_EVEN * weight * 4.5) * density,
                          (OMEGA_ODD * weight * 3.0) * density)
    for i in range(1, POPS, 2):
        projected = None
        for axis in range(3):
            sign = VELOCITIES[i][axis]
            if sign == 0:
                continue
            if projected is None:
                projected = velocity[axis] if sign == 1 else -velocity[axis]
            else:
                projected = projected + velocity[axis] if sign == 1 else projected - velocity[axis]
        low, curve, slope = shared[WEIGHTS[i]]
        even_part = (0.5 - 0.5 * OMEGA_EVEN) * even[i] + (low + curve * (projected * projected))
        odd_part = (0.5 - 0.5 * OMEGA_ODD) * odd[i] + slope * projected
        post[i] = even_part + odd_part
        post[i + 1] = even_part - odd_part
    return post, density


def pushes(density, drift_y, drift_z):
    along_y = density * drift_y
    along_z = density * drift_z
    out = [None] * POPS
    for i in range(1, POPS):
        _, step_y, step_z = VELOCITIES[i]
        total = None
        for sign, part in ((step_y, along_y), (step_z, along_z)):
            if sign == 0:
                continue
            if total is None:
                total = part if sign == 1 else -part
            else:
                total = total + part if sign == 1 else total - part
        if total is not None:
            out[i] = (6.0 * WEIGHTS[i]) * total
    return out


def total_of(parts):
    parts = list(parts)
    while len(parts) > 1:
        pairs = [parts[n] + parts[n + 1] for n in range(0, len(parts) - 1, 2)]
        parts = pairs + parts[len(parts) - len(parts) % 2 :]
    return parts[0]


def streamed(pull, own, drift_y, drift_z):
    push = pushes(total_of(own), drift_y, drift_z)
    out = [own[0]]
    for i in range(1, POPS):
        pulled = pull(i)
        bounced = own[OPPOSITE[i]]
        blocked = pulled < WALL_BELOW
        if push[i] is not None:
            bounced = jnp.where(pulled < OUT_BELOW, bounced, bounced + push[i])
        out.append(jnp.where(blocked, bounced, pulled))
    return out


def ahead(items, take, leave, depth):
    waiting = []
    for n in items:
        waiting.append((n, take(n)))
        if len(waiting) > depth:
            leave(*waiting.pop(0))
    for pair in waiting:
        leave(*pair)


def place():
    return lax.axis_index("stream"), lax.axis_index("cy"), lax.axis_index("cz")


def slot_of(pos, row, layer, column_z):
    slot = (pos[0, row] - (layer * BXD - 1)) * BZD + (pos[2, row] - column_z * BZD)
    return jnp.clip(slot, 0, LAYERS * BZD - 1)


def fill_table(pos, table):
    layer, _, column_z = place()
    for entry in range(LAYERS * BZD):
        table[entry] = -1
    for row in range(pos.shape[1]):

        @pl.when(pos[0, row] >= 0)
        def _(row=row):
            table[slot_of(pos, row, layer, column_z)] = row


def spread_marks(marks, dense):
    rows = marks.shape[0]
    for first in range(0, rows, 8):
        size = min(8, rows - first)
        for begin in range(0, TILES, 8):
            values = [marks[first : first + size, t * LANE : (t + 1) * LANE] for t in range(begin, begin + 8)]
            for k, value in enumerate(values):
                dense[pl.ds(first * TILES + begin + k, size, stride=TILES), :] = value.astype(jnp.float32)


def collide_block(ref, base):
    for part in range(TILES // 8):
        old = [ref[pl.ds(base + i * TILES + 8 * part, 8), :] for i in range(POPS)]
        mark = ref[pl.ds(base + POPS * TILES + 8 * part, 8), :] > 0.5
        post, _ = collide(old)
        for i in range(POPS):
            ref[pl.ds(base + i * TILES + 8 * part, 8), :] = jnp.where(mark, old[i], post[i])


def pack_block(out, base, stage, dense, row):
    out[pl.ds(base + POPS * TILES, TILES), :] = dense[pl.ds(pl.multiple_of(row * TILES, 8), TILES), :]
    for first in range(0, TILES, 4):
        moves = []
        for tile in range(first, first + 4):
            for group, size in GROUPS:
                value = stage[group : group + size, tile * LANE : (tile + 1) * LANE]
                moves.append((pl.ds(base + group * TILES + tile, size, stride=TILES), value))
        for target, value in moves:
            out[target, :] = value
    collide_block(out, base)


def pack_stream(places, marks_in, pops, up, down, pos, table, marks, dense, blocks, slabs, strip, sems):
    mark_copy = pltpu.make_async_copy(marks_in, marks, sems.at[0])
    mark_copy.start()
    place_copy = pltpu.make_async_copy(places, pos, sems.at[1])
    place_copy.start()
    rows = pos.shape[1]
    copies = [None] * 4
    for j in range(MOVE_CAP):
        copies[MOVE_CAP + j] = pltpu.make_async_copy(pops.at[j], blocks.at[MOVE_CAP + j], sems.at[2 + MOVE_CAP + j])
        copies[MOVE_CAP + j].start()
    place_copy.wait()
    count = 0
    for row in range(rows):
        count = count + jnp.where(pos[0, row] >= 0, 1, 0)
    last = jnp.clip(count - MOVE_CAP, 0, rows - MOVE_CAP)
    for j in range(MOVE_CAP):
        copies[j] = pltpu.make_async_copy(pops.at[last + j], blocks.at[j], sems.at[2 + j])
        copies[j].start()
    fill_table(pos, table)
    slab_rows = []
    slab_copies = []
    for side in range(2):
        for bz in range(BZD):
            row = jnp.maximum(table[(2 - side) * BZD + bz], 0)
            n = side * BZD + bz
            first = (TILES - SLAB) * LANE if side == 0 else 0
            slab_rows.append(row)
            slab_copies.append(
                pltpu.make_async_copy(
                    pops.at[row, :, pl.ds(first, SLAB * LANE)], slabs.at[n], sems.at[2 + 2 * MOVE_CAP + n]
                )
            )
            slab_copies[n].start()
    mark_copy.wait()
    spread_marks(marks, dense)
    for side, out in ((1, down), (0, up)):
        for j in range(MOVE_CAP):
            row = j if side == 1 else last + j
            for k, axis in ((0, 0), (1, 2)):
                value = jnp.full((1, LANE), pos[axis, row], jnp.int32).astype(jnp.float32)
                out[pl.ds(SENT_META + 2 * j + k, 1), :] = value
            n = side * MOVE_CAP + j
            copies[n].wait()
            pack_block(out, j * BLOCK, blocks.at[n], dense, row)
    for side, out in enumerate((up, down)):
        for bz in range(BZD):
            n = side * BZD + bz
            first = slab_rows[n] * TILES + (TILES - SLAB if side == 0 else 0)
            slab_copies[n].wait()
            moves = []
            for x in range(2):
                for yhi in range(2):
                    q = 2 * x + yhi
                    row = x * FACE + 2 * bz + yhi
                    for group, size in GROUPS:
                        value = slabs[n, group : group + size, q * LANE : (q + 1) * LANE]
                        moves.append((pl.ds(group * 2 * FACE + row, size, stride=2 * FACE), value))
                row = POPS * 2 * FACE + x * FACE + 2 * bz
                moves.append((pl.ds(row, 2), dense[pl.ds(first + 2 * x, 2), :]))
            for target, value in moves:
                strip[target, :] = value
        inner = 1 if side == 0 else 0
        for x in range(2):
            old = [strip[pl.ds(i * 2 * FACE + x * FACE, FACE), :] for i in range(POPS)]
            mark = strip[pl.ds(POPS * 2 * FACE + x * FACE, FACE), :] > 0.5
            post, _ = collide(old)
            if x == inner:
                pairs = [(i, i) for i in range(POPS)]
            else:
                pairs = [(POPS + n, i) for n, i in enumerate(AHEAD if side == 0 else BACK)]
            for plane, i in pairs:
                out[pl.ds(SENT_SLABS + plane * FACE, FACE), :] = jnp.where(mark, ROTOR, post[i])


def pack_edge(places, marks_in, pops, own, zpack, zup, zdown, pos, table, marks, dense, stage, sems):
    column_z = lax.axis_index("cz")
    mark_copy = pltpu.make_async_copy(marks_in, marks, sems.at[LAYERS])
    mark_copy.start()
    place_copy = pltpu.make_async_copy(places, pos, sems.at[LAYERS + 1])
    place_copy.start()
    place_copy.wait()
    fill_table(pos, table)
    edge_bz = jnp.where(column_z == 0, BZD - 1, 0)
    first_c = jnp.where(column_z == 0, EDGE - 2, 0)
    found = [table[held * BZD + edge_bz] for held in range(LAYERS)]
    row_of = [jnp.maximum(row, 0) for row in found]
    copies = []
    for held in range(LAYERS):
        copies.append(pltpu.make_async_copy(pops.at[row_of[held]], stage.at[held], sems.at[held]))
        copies[held].start()
    mark_copy.wait()
    spread_marks(marks, dense)
    spot = (lanes() & (EDGE - 1)) >> 1
    sublane = lax.broadcasted_iota(jnp.int32, (8, LANE), 0)
    flags = jnp.zeros((8, LANE), jnp.int32)
    for held in range(LAYERS):
        copies[held].wait()
        base = pl.multiple_of((held * BZD + edge_bz) * BLOCK, 8)

        @pl.when(found[held] >= 0)
        def _(held=held, base=base):
            pack_block(own, base, stage.at[held], dense, row_of[held])
            totals = []
            for group in range(ZGROUPS):
                for part in range(TILES // 8):
                    total = jnp.zeros((8, LANE), jnp.float32)
                    for k in range(min(8, PLANES - group * 8)):
                        value = own[pl.ds(base + (group * 8 + k) * TILES + part * 8, 8), :]
                        value = pltpu.roll(value, (2 * k - first_c + LANE) & (LANE - 1), 1)
                        total = jnp.where(spot == k, value, total)
                    totals.append((held * ZROWS + group * TILES + part * 8, total))
            for row, total in totals:
                zpack[pl.ds(row, 8), :] = total

        flags = jnp.where((sublane == held) & (found[held] >= 0), 1, flags)
    zpack[pl.ds(ZMETA, 8), :] = flags.astype(jnp.float32)
    zup[pl.ds(0, ZROWS), :] = zpack[pl.ds(3 * ZROWS, ZROWS), :]
    zdown[pl.ds(0, ZROWS), :] = zpack[pl.ds(0, ZROWS), :]
    for group in range(ZGROUPS):
        target = pl.ds(ZROWS + group * SLAB, SLAB)
        zup[target, :] = zpack[pl.ds(2 * ZROWS + group * TILES + TILES - SLAB, SLAB), :]
        zdown[target, :] = zpack[pl.ds(ZROWS + group * TILES, SLAB), :]


def pack_own(places, marks_in, pops, own_in, own, pos, marks, dense, stage, sems):
    del own_in
    layer, _, column_z = place()
    edge_bz = jnp.where(column_z == 0, BZD - 1, 0)
    rows = pos.shape[1]
    mark_copy = pltpu.make_async_copy(marks_in, marks, sems.at[rows])
    mark_copy.start()
    place_copy = pltpu.make_async_copy(places, pos, sems.at[rows + 1])
    place_copy.start()
    copies = [pltpu.make_async_copy(pops.at[r], stage.at[r], sems.at[r]) for r in range(rows)]
    for copy in copies:
        copy.start()
    mark_copy.wait()
    spread_marks(marks, dense)
    place_copy.wait()

    def settle(row, carry):
        pltpu.make_async_copy(pops.at[row], stage.at[row], sems.at[row]).wait()
        slot = slot_of(pos, row, layer, column_z)

        @pl.when((pos[0, row] >= 0) & (slot % BZD != edge_bz))
        def _():
            pack_block(own, pl.multiple_of(slot * BLOCK, 8), stage.at[row], dense, row)

        return carry

    lax.fori_loop(0, rows, settle, 0)


class Lanes:
    def __init__(self, column_z):
        lane = lanes()
        self.from_bz = [lane >= bz * EDGE for bz in range(BZD)]
        self.main = lane < SPAN_Z
        self.single = (lane & EDGE) != 0
        self.double = (lane & (2 * EDGE)) != 0
        self.goal = jnp.where(column_z == 0, SPAN_Z, LANE - 2)

    def to_halo(self, ylo, spot):
        return (self.goal - (ylo * EDGE + 2 * spot) + LANE) & (LANE - 1)


def gathered(parts, zvalue, spot, ylo, masks):
    rows = parts[0].shape[0]
    total = None
    for bz in range(BZD):
        shift = (bz * EDGE - ylo * EDGE) % LANE
        value = pltpu.roll(parts[bz], shift, 1) if shift else parts[bz]
        total = value if total is None else jnp.where(masks.from_bz[bz][:rows], value, total)
    beyond = pltpu.roll(zvalue, masks.to_halo(ylo, spot), 1)
    return jnp.where(masks.main[:rows], total, beyond)


def gathered_rows(parts, zvalue, spot, masks):
    rows = parts[0].shape[0]
    single, double, main = masks.single[:rows], masks.double[:rows], masks.main[:rows]
    pairs = []
    for n in (0, 2):
        even = jnp.where(single, pltpu.roll(parts[n + 1], EDGE, 1), parts[n])
        odd = jnp.where(single, parts[n + 1], pltpu.roll(parts[n], LANE - EDGE, 1))
        pairs.append((even, odd))
    out = [None] * YLO
    for r in range(4):
        low, high = pairs[0][r % 2], pairs[1][r % 2]
        if r < 2:
            both = jnp.where(double, pltpu.roll(high, 2 * EDGE, 1), low)
        else:
            both = jnp.where(double, high, pltpu.roll(low, LANE - 2 * EDGE, 1))
        beyond = pltpu.roll(zvalue, masks.to_halo(r, spot), 1)
        out[r] = jnp.where(main, both, beyond)
        out[r + 4] = pltpu.roll(jnp.where(main, beyond, both), SPAN_Z, 1)
    return out


def inside_lanes(rows, column_z):
    lane = lanes()[:rows]
    low = (column_z == 0) & (lane >= SPAN_Z) & (lane < SPAN_Z + 2)
    high = (column_z != 0) & (lane >= LANE - 2)
    return (lane < SPAN_Z) | low | high


def marked(post, mark, inside):
    flag = jnp.where(inside, jnp.where(mark > 0.5, ROTOR, 0.0), OUTSIDE)
    wall = flag < WALL_BELOW
    return [jnp.where(wall, flag, value) for value in post]


def plane_parts(own, edge, zall, zedge, chunk, yhi, plane):
    group = plane // 8
    if chunk is None:
        if plane == POPS:
            parts = [jnp.zeros((4, LANE), jnp.float32)] * BZD
        else:
            parts = [edge[pl.ds(plane * 4 * FACE + 2 * bz + yhi, 4, stride=FACE), :] for bz in range(BZD)]
        return parts, zedge[pl.ds(group * 8 + yhi, 4, stride=2), :]
    held, half = 1 + (chunk >> 1), chunk & 1
    first = held * (BZD * BLOCK) + half * EDGE + yhi
    parts = [own[pl.ds(first + bz * BLOCK + plane * TILES, 8, stride=2), :] for bz in range(BZD)]
    first = held * ZROWS + half * EDGE + yhi
    return parts, zall[pl.ds(first + group * TILES, 8, stride=2), :]


def chunk_values(own, edge, zall, zedge, chunk, yhi, ylo, masks):
    out = []
    for plane in range(PLANES):
        parts, zvalue = plane_parts(own, edge, zall, zedge, chunk, yhi, plane)
        out.append(gathered(parts, zvalue, plane % 8, ylo, masks))
    return out


def halo_x_inside(layer, layers):
    row = lax.broadcasted_iota(jnp.int32, (4, LANE), 0)
    low = (row < 2) & (layer > 0)
    high = (row >= 2) & (layer < layers - 1)
    return low | high


def settle_rim(layers, places, up, down, zin, zup, zdown, own_in, own, edge, zall, zedge, rim_up, rim_down, pos, post_up, post_down, sem):
    del own_in
    layer, _, column_z = place()
    place_copy = pltpu.make_async_copy(places, pos, sem)
    place_copy.start()
    for arrived in (up, down):
        for j in range(MOVE_CAP):
            bx = arrived[pl.ds(SENT_META + 2 * j, 1), :].astype(jnp.int32)
            bz = arrived[pl.ds(SENT_META + 2 * j + 1, 1), :].astype(jnp.int32)
            code = (bx - layer * BXD) * BZD + (bz - column_z * BZD)
            mine = (bx >= layer * BXD) & (bx < (layer + 1) * BXD)
            first = layer == 0 if arrived is up else layer == layers - 1
            code = jnp.max(jnp.where(mine, code, -1))

            @pl.when((code >= 0) & jnp.logical_not(first))
            def _(arrived=arrived, j=j, code=code):
                base = pl.multiple_of((jnp.clip(code, 0, BXD * BZD - 1) + BZD) * BLOCK, 8)
                for k in range(0, BLOCK, 128):
                    values = [arrived[pl.ds(j * BLOCK + k + 8 * n, 8), :] for n in range(16)]
                    for n, value in enumerate(values):
                        own[pl.ds(base + k + 8 * n, 8), :] = value

    place_copy.wait()
    for side, arrived in enumerate((up, down)):
        inner, outer = (1, 0) if side == 0 else (2, 3)
        pairs = [(i, i, inner) for i in range(POPS)]
        pairs += [(POPS + n, i, outer) for n, i in enumerate(AHEAD if side == 0 else BACK)]
        values = [arrived[pl.ds(SENT_SLABS + plane * FACE, FACE), :] for plane, _, _ in pairs]
        for (_, i, x), value in zip(pairs, values):
            edge[pl.ds((i * 4 + x) * FACE, FACE), :] = value
        for bz in range(BZD):
            here = jnp.int32(0)
            goal = (0 if side == 0 else LAYERS - 1) * BZD + bz
            for row in range(pos.shape[1]):
                hit = (pos[0, row] >= 0) & (slot_of(pos, row, layer, column_z) == goal)
                here = jnp.where(hit, 1, here)

            @pl.when(here == 1)
            def _(side=side, pairs=pairs, goal=goal, bz=bz):
                first = goal * BLOCK + (TILES - SLAB if side == 0 else 0)
                values = []
                for _, i, x in pairs:
                    shift = 2 * (x if side == 0 else x - 2)
                    mark = own[pl.ds(first + POPS * TILES + shift, 2), :] > 0.5
                    values.append(jnp.where(mark, ROTOR, own[pl.ds(first + i * TILES + shift, 2), :]))
                for (_, i, x), value in zip(pairs, values):
                    edge[pl.ds((i * 4 + x) * FACE + 2 * bz, 2), :] = value

    moves = []
    for held in range(LAYERS):
        flag = zin[pl.ds(ZMETA + held, 1), :] > 0.5
        for group in range(ZGROUPS):
            if held == 1 or held == 2:
                for part in range(TILES // 8):
                    rows = pl.ds(held * ZROWS + group * TILES + part * 8, 8)
                    source = zup if held == 1 else zdown
                    other = source[pl.ds(group * TILES + part * 8, 8), :]
                    moves.append((zall, rows, jnp.where(flag, zin[rows, :], other)))
            else:
                side = 0 if held == 0 else 1
                source = zup if held == 0 else zdown
                first = TILES - SLAB if held == 0 else 0
                mine = zin[pl.ds(held * ZROWS + group * TILES + first, SLAB), :]
                other = source[pl.ds(ZROWS + group * SLAB, SLAB), :]
                moves.append((zedge, pl.ds(group * 8 + side * SLAB, SLAB), jnp.where(flag, mine, other)))
    for target, rows, value in moves:
        target[rows, :] = value
    masks = Lanes(column_z)
    inside_box = inside_lanes(8, column_z)
    inside_halo = inside_lanes(4, column_z) & halo_x_inside(layer, layers)
    for chunk in (0, 1, 2, 3, None):
        for y in (0, 1, SPAN_Y - 2, SPAN_Y - 1):
            values = chunk_values(own, edge, zall, zedge, chunk, y // YLO, y % YLO, masks)
            inside = inside_halo if chunk is None else inside_box
            post = marked(values[:POPS], values[POPS], inside)
            target = post_down if y < 2 else post_up
            rim = RIM_DOWN if y < 2 else RIM_UP
            if y in (0, SPAN_Y - 1):
                pairs = [(i, i) for i in range(POPS)]
            else:
                pairs = [(POPS + n, i) for n, i in enumerate(rim)]
            for plane, i in pairs:
                if chunk is None:
                    target[pl.ds(plane * GRID_X, 2), :] = post[i][:2]
                    target[pl.ds(plane * GRID_X + EXT_X - 2, 2), :] = post[i][2:]
                else:
                    target[pl.ds(plane * GRID_X + 2 + 8 * chunk, 8), :] = post[i]
    lane = lanes()
    for source, target in ((post_up, rim_up), (post_down, rim_down)):
        for chunk in range(5):
            size = min(8, EXT_X - 8 * chunk)
            values = []
            for plane in range(RIM):
                value = source[pl.ds(plane * GRID_X + 8 * chunk, 8), :]
                values.append(pltpu.roll(value, (plane * EXT_Z + 2 * column_z) & (LANE - 1), 1))
            totals = []
            for block in range(RIM_BLOCKS):
                total = jnp.zeros((8, LANE), jnp.float32)
                for plane in range(RIM):
                    begin = plane * EXT_Z - block * LANE
                    if begin >= LANE or begin + EXT_Z <= 0:
                        continue
                    total = jnp.where((lane >= begin) & (lane < begin + EXT_Z), values[plane], total)
                totals.append(total)
            for block in range(RIM_BLOCKS):
                target[pl.ds(block * EXT_X + 8 * chunk, size), :] = totals[block][:size]


def turned(value, step_z):
    return pltpu.roll(value, step_z % LANE, 1) if step_z else value


def drifts_of(columns, depth):
    _, _, column_z = place()
    lane = lanes()
    total_y = SPAN_Y * columns
    total_z = SPAN_Z * depth
    spin = 0.2 / (total_y + total_z)
    here_z = jnp.where(lane < SPAN_Z + 8, lane, lane - LANE) + column_z * SPAN_Z
    drift_y = -spin * (here_z.astype(jnp.float32) - (total_z - 1) / 2.0)
    return drift_y, spin, (total_y - 1) / 2.0


def first_step(columns, depth, field, later, begin, end):
    _, column_y, _ = place()
    drift_y, spin, centre_y = drifts_of(columns, depth)
    sublane = lax.broadcasted_iota(jnp.int32, (8, LANE), 0)

    def tile(n, carry):
        base = pl.multiple_of(8 * n, 8)
        line = (n - FIRST // 8 + 2 * STEP) // STEP
        next_row = (sublane >= 6) & (n - FIRST // 8 + 2 * STEP - line * STEP == STEP - 1)
        here_y = jnp.where(next_row, line + 1, line) + (column_y * SPAN_Y - 2)
        drift_z = spin * (here_y.astype(jnp.float32) - centre_y)
        old = [field[pl.ds(i * FIELD + base, 8), :] for i in range(POPS)]
        values = streamed(pull_from(field, base), old, drift_y, drift_z)
        post, _ = collide(values)
        wall = old[0] < WALL_BELOW
        for i in range(POPS):
            later[pl.ds(i * FIELD + base, 8), :] = jnp.where(wall, old[0], post[i])
        return carry

    lax.fori_loop(FIRST // 8 + begin, FIRST // 8 + end, tile, 0)


def pull_from(field, base):
    def pull(i):
        step_x, step_y, step_z = VELOCITIES[i]
        return turned(field[pl.ds(i * FIELD + base - step_y * PITCH - step_x, 8), :], step_z)

    return pull


def settle_all(layers, columns, depth, own, edge, zall, zedge, field, start, later):
    layer, _, column_z = place()
    masks = Lanes(column_z)
    inside_box = inside_lanes(8, column_z)
    inside_halo = inside_lanes(4, column_z) & halo_x_inside(layer, layers)

    def caps_of(mark, inside):
        return [jnp.where(inside, jnp.where(value > 0.5, ROTOR, -ROTOR), OUTSIDE) for value in mark]

    def halves(yhi, carry):
        def rows_of_plane(chunk, plane):
            parts, zvalue = plane_parts(own, edge, zall, zedge, chunk, yhi, plane)
            return gathered_rows(parts, zvalue, plane % 8, masks)

        top = yhi * YLO * PITCH + FIRST

        def chunks(chunk, carry):
            caps = caps_of(rows_of_plane(chunk, POPS), inside_box)

            def leave(i, values):
                for ylo in range(YLO):
                    row = pl.multiple_of(i * FIELD + top + ylo * PITCH + 8 * chunk, 8)
                    field[pl.ds(row, 8), :] = jnp.minimum(values[ylo], caps[ylo])
                    row = pl.multiple_of((i * SPAN_Y + YLO * yhi + ylo) * SPAN_X + 8 * chunk, 8)
                    start[pl.ds(row, 8), :] = values[ylo]

            ahead(range(POPS), lambda i: rows_of_plane(chunk, i), leave, 1)
            return carry

        lax.fori_loop(0, SPAN_X // 8, chunks, 0)
        caps = caps_of(rows_of_plane(None, POPS), inside_halo)

        def leave(i, values):
            for ylo in range(YLO):
                value = jnp.minimum(values[ylo], caps[ylo])
                row = i * FIELD + top + ylo * PITCH
                field[pl.ds(row - 2, 2), :] = value[:2]
                field[pl.ds(row + SPAN_X, 2), :] = value[2:]

        ahead(range(POPS), lambda i: rows_of_plane(None, i), leave, 1)
        return carry

    lax.fori_loop(0, SPAN_Y // YLO, halves, 0)
    first_step(columns, depth, field, later, STEP, (SPAN_Y - 1) * STEP)


def finish(columns, depth, rim_low, rim_high, field_in, start, later_in, out, field, later, turn, result, sems):
    del field_in, later_in
    _, column_y, column_z = place()
    flat = (lanes() + 2 * column_z) & (LANE - 1)
    sides = (
        (rim_low, -1, -2, RIM_UP, column_y > 0),
        (rim_high, SPAN_Y, SPAN_Y + 1, RIM_DOWN, column_y < columns - 1),
    )
    for source, near, far, rim, there in sides:
        for chunk in range(5):
            size = min(8, EXT_X - 8 * chunk)
            blocks = [source[pl.ds(block * EXT_X + 8 * chunk, 8), :] for block in range(RIM_BLOCKS)]
            for plane in range(RIM):
                block, begin = divmod(plane * EXT_Z, LANE)
                shift = (2 * LANE - begin - 2 * column_z) & (LANE - 1)
                value = pltpu.roll(blocks[block], shift, 1)
                if begin + EXT_Z > LANE:
                    value = jnp.where(flat < LANE - begin, value, pltpu.roll(blocks[block + 1], shift, 1))
                value = jnp.where((flat < EXT_Z) & there, value, OUTSIDE)
                i, y = (plane, near) if plane < POPS else (rim[plane - POPS], far)
                row = i * FIELD + FIRST + y * PITCH - 2 + 8 * chunk
                field[pl.ds(row, size), :] = value[:size]

    first_step(columns, depth, field, later, -STEP - 1, STEP)
    first_step(columns, depth, field, later, (SPAN_Y - 1) * STEP - 1, (SPAN_Y + 1) * STEP)

    drift_y, spin, centre_y = drifts_of(columns, depth)

    def leave(n):
        part = pl.ds(n * 8, 8)
        return pltpu.make_async_copy(result.at[:, part], out.at[:, part], sems.at[n])

    def second_step(chunk, carry):
        for half in range(SPAN_Y // 8):
            for k in range(8):
                y = 8 * half + k
                base = pl.multiple_of(FIRST + y * PITCH + 8 * chunk, 8)
                drift_z = spin * ((column_y * SPAN_Y + y).astype(jnp.float32) - centre_y)
                old = [later[pl.ds(i * FIELD + base, 8), :] for i in range(POPS)]
                values = streamed(pull_from(later, base), old, drift_y, drift_z)
                wall = old[0] < WALL_BELOW
                for i in range(POPS):
                    first = pl.multiple_of((i * SPAN_Y + y) * SPAN_X + 8 * chunk, 8)
                    value = jnp.where(wall, start[pl.ds(first, 8), :], values[i])
                    turn[pl.ds(i * 8 * TURN + k * TURN, 8), :] = value
            for k in range(8):
                values = [turn[pl.ds(i * 8 * TURN + k, 8, stride=TURN), :] for i in range(POPS)]
                for i in range(POPS):
                    result[i, 8 * chunk + k, 8 * half : 8 * half + 8, :] = values[i][:, :SPAN_Z]
        leave(chunk).start()
        return carry

    lax.fori_loop(0, SPAN_X // 8, second_step, 0)
    for n in range(SPAN_X // 8):
        leave(n).wait()


def rows_of(count):
    return jax.ShapeDtypeStruct((count, LANE), jnp.float32)


def kept(count):
    return VMEM((count, LANE), jnp.float32)


def params(mib):
    return pltpu.CompilerParams(vmem_limit_bytes=mib * 2**20)


def shards(populations, solid_cells, block_pos):
    layers = lax.axis_size("stream")
    columns = lax.axis_size("cy")
    depth = lax.axis_size("cz")
    rows = block_pos.shape[0]
    vmem = pl.BlockSpec(memory_space=VMEM)
    hbm = pl.BlockSpec(memory_space=pltpu.HBM)
    populations = pltpu.with_memory_space_constraint(populations, pltpu.HBM)
    solid_cells = pltpu.with_memory_space_constraint(solid_cells, pltpu.HBM)
    places = pltpu.with_memory_space_constraint(block_pos.T, pltpu.HBM)
    place_scratch = SMEM((3, rows), jnp.int32)
    table_scratch = SMEM((LAYERS * BZD,), jnp.int32)
    mark_scratch = [VMEM((rows, EDGE**3), jnp.int32), VMEM((rows * TILES, LANE), jnp.float32)]

    up = [(i, i + 1) for i in range(layers - 1)]
    down = [(i + 1, i) for i in range(layers - 1)]
    send_up, send_down = pl.pallas_call(
        pack_stream,
        out_shape=(kept(SENT_ROWS), kept(SENT_ROWS)),
        in_specs=[hbm, hbm, hbm],
        out_specs=(vmem, vmem),
        scratch_shapes=[place_scratch, table_scratch]
        + mark_scratch
        + [
            VMEM((2 * MOVE_CAP, POPS, EDGE**3), jnp.float32),
            VMEM((2 * BZD, POPS, SLAB * LANE), jnp.float32),
            VMEM((PLANES * 2 * FACE, LANE), jnp.float32),
            pltpu.SemaphoreType.DMA((2 + 2 * MOVE_CAP + 2 * BZD,)),
        ],
        compiler_params=params(16),
        name="pack_stream",
    )(places, solid_cells, populations)
    from_low = lax.ppermute(send_up, "stream", up)
    from_high = lax.ppermute(send_down, "stream", down)

    own, zpack, zsend_up, zsend_down = pl.pallas_call(
        pack_edge,
        out_shape=(kept(LAYERS * BZD * BLOCK), kept(ZMETA + 8), kept(DIAG), kept(DIAG)),
        in_specs=[hbm, hbm, hbm],
        out_specs=(vmem,) * 4,
        scratch_shapes=[place_scratch, table_scratch]
        + mark_scratch
        + [
            VMEM((LAYERS, POPS, EDGE**3), jnp.float32),
            pltpu.SemaphoreType.DMA((LAYERS + 2,)),
        ],
        compiler_params=params(16),
        name="pack_edge",
    )(places, solid_cells, populations)
    swap = [(i, depth - 1 - i) for i in range(depth)]
    zin = lax.ppermute(zpack, "cz", swap)
    zup_pairs = [(s * depth + c, t * depth + d) for s, t in up for c, d in swap]
    zdown_pairs = [(s * depth + c, t * depth + d) for s, t in down for c, d in swap]
    z_low = lax.ppermute(zsend_up, ("stream", "cz"), zup_pairs)
    z_high = lax.ppermute(zsend_down, ("stream", "cz"), zdown_pairs)

    own = pl.pallas_call(
        pack_own,
        out_shape=kept(LAYERS * BZD * BLOCK),
        in_specs=[hbm, hbm, hbm, vmem],
        out_specs=vmem,
        scratch_shapes=[place_scratch]
        + mark_scratch
        + [
            VMEM((rows, POPS, EDGE**3), jnp.float32),
            pltpu.SemaphoreType.DMA((rows + 2,)),
        ],
        input_output_aliases={3: 0},
        compiler_params=params(16),
        name="pack_own",
    )(places, solid_cells, populations, own)

    own, edge, zall, zedge, rim_up, rim_down = pl.pallas_call(
        functools.partial(settle_rim, layers),
        out_shape=(
            kept(LAYERS * BZD * BLOCK),
            kept(POPS * 4 * FACE),
            kept(LAYERS * ZROWS),
            kept(ZGROUPS * 8),
            kept(RIM_ROWS),
            kept(RIM_ROWS),
        ),
        in_specs=[hbm] + [vmem] * 6,
        out_specs=(vmem,) * 6,
        scratch_shapes=[
            place_scratch,
            VMEM((RIM * GRID_X, LANE), jnp.float32),
            VMEM((RIM * GRID_X, LANE), jnp.float32),
            pltpu.SemaphoreType.DMA,
        ],
        input_output_aliases={6: 0},
        compiler_params=params(16),
        name="settle_rim",
    )(places, from_low, from_high, zin, z_low, z_high, own)
    cy_up = [(i, i + 1) for i in range(columns - 1)]
    cy_down = [(i + 1, i) for i in range(columns - 1)]
    rim_low = lax.ppermute(rim_up, "cy", cy_up)
    rim_high = lax.ppermute(rim_down, "cy", cy_down)

    field, start, later = pl.pallas_call(
        functools.partial(settle_all, layers, columns, depth),
        out_shape=(kept(POPS * FIELD), kept(POPS * SPAN_X * SPAN_Y), kept(POPS * FIELD)),
        in_specs=[vmem] * 4,
        out_specs=(vmem,) * 3,
        compiler_params=params(16),
        name="settle_all",
    )(own, edge, zall, zedge)

    out, _, _ = pl.pallas_call(
        functools.partial(finish, columns, depth),
        out_shape=(
            jax.ShapeDtypeStruct((POPS, SPAN_X, SPAN_Y, SPAN_Z), jnp.float32),
            kept(POPS * FIELD),
            kept(POPS * FIELD),
        ),
        in_specs=[vmem] * 5,
        out_specs=(hbm, vmem, vmem),
        scratch_shapes=[
            VMEM((POPS * 8 * TURN, LANE), jnp.float32),
            VMEM((POPS, SPAN_X, SPAN_Y, SPAN_Z), jnp.float32),
            pltpu.SemaphoreType.DMA((SPAN_X // 8,)),
        ],
        input_output_aliases={2: 1, 4: 2},
        compiler_params=params(16),
        name="finish",
    )(rim_low, rim_high, field, start, later)
    return out


def solution(mesh):
    in_specs = (
        P(("stream", "cy", "cz"), None, None),
        P(("stream", "cy", "cz"), None),
        P(("stream", "cy", "cz"), None),
    )
    out_specs = P(None, "stream", "cy", "cz")
    return jax.shard_map(shards, mesh=mesh, in_specs=in_specs, out_specs=out_specs, check_vma=False)
```

```python
import functools

import jax
import jax.numpy as jnp
from jax import lax
from jax.experimental import pallas as pl
from jax.experimental.pallas import tpu as pltpu
from jax.sharding import PartitionSpec as P

EDGE = 16
BXD = 2
BYD = 1
BZD = 4
MOVE_CAP = 2

VELOCITIES = (
    (0, 0, 0),
    (1, 0, 0),
    (-1, 0, 0),
    (0, 1, 0),
    (0, -1, 0),
    (0, 0, 1),
    (0, 0, -1),
    (1, 1, 0),
    (-1, -1, 0),
    (1, -1, 0),
    (-1, 1, 0),
    (1, 0, 1),
    (-1, 0, -1),
    (1, 0, -1),
    (-1, 0, 1),
    (0, 1, 1),
    (0, -1, -1),
    (0, 1, -1),
    (0, -1, 1),
)
WEIGHTS = (1.0 / 3.0,) + (1.0 / 18.0,) * 6 + (1.0 / 36.0,) * 12
OPPOSITE = (0, 2, 1, 4, 3, 6, 5, 8, 7, 10, 9, 12, 11, 14, 13, 16, 15, 18, 17)
OMEGA_EVEN = 1.25
OMEGA_ODD = 1.0 / 1.125

POPS = 19
PLANES = 20
QUAD = 4
LANE = 128
TILES = EDGE**3 // LANE
BLOCK = PLANES * TILES
YLO = LANE // EDGE
SLAB = 4
GROUPS = ((0, 8), (8, 8), (16, 3))
SENT_SLABS = MOVE_CAP * BLOCK
LAYERS = BXD + 2
ZGROUPS = 3
ZROWS = ZGROUPS * TILES
ZMETA = LAYERS * ZROWS
DIAG = ZROWS + ZGROUPS * SLAB

SPAN_X = BXD * EDGE
SPAN_Y = BYD * EDGE
SPAN_Z = BZD * EDGE
PITCH = SPAN_X + 8
STEP = PITCH // 8
FIRST = 96
FIELD = FIRST + (SPAN_Y + 1) * PITCH + 48
TURN = 9
EXT_X = SPAN_X + 4
EXT_Z = SPAN_Z + 2
RIM_UP = tuple(i for i in range(POPS) if VELOCITIES[i][1] == 1)
RIM_DOWN = tuple(i for i in range(POPS) if VELOCITIES[i][1] == -1)
RIM = POPS + len(RIM_UP)
AHEAD = tuple(i for i in range(POPS) if VELOCITIES[i][0] == 1)
BACK = tuple(i for i in range(POPS) if VELOCITIES[i][0] == -1)
FACE = 2 * BZD
SENT_META = SENT_SLABS + RIM * FACE
SENT_ROWS = SENT_META + 8
RIM_BLOCKS = -(-RIM * EXT_Z // LANE)
RIM_ROWS = RIM_BLOCKS * EXT_X + 4
GRID_X = 48

ROTOR = -1.0e30
OUTSIDE = -2.0e30
WALL_BELOW = -1.0e20
OUT_BELOW = -1.5e30

VMEM = pltpu.VMEM
SMEM = pltpu.SMEM


def lanes():
    return lax.broadcasted_iota(jnp.int32, (8, LANE), 1)


def collide(f):
    even = [None] * POPS
    odd = [None] * POPS
    for i in range(1, POPS, 2):
        even[i] = f[i] + f[i + 1]
        odd[i] = f[i] - f[i + 1]
    density = f[0]
    for i in range(1, POPS, 2):
        density = density + even[i]
    flow = []
    for axis in range(3):
        total = None
        for i in range(1, POPS, 2):
            sign = VELOCITIES[i][axis]
            if sign == 0:
                continue
            if total is None:
                total = odd[i] if sign == 1 else -odd[i]
            else:
                total = total + odd[i] if sign == 1 else total - odd[i]
        flow.append(total)
    inverse = 1.0 / density
    velocity = [part * inverse for part in flow]
    square = velocity[0] * velocity[0] + velocity[1] * velocity[1] + velocity[2] * velocity[2]
    base = density * (1.0 - 1.5 * square)
    post = [None] * POPS
    post[0] = (1.0 - OMEGA_EVEN) * f[0] + (OMEGA_EVEN * WEIGHTS[0]) * base
    shared = {}
    for weight in (WEIGHTS[1], WEIGHTS[7]):
        shared[weight] = ((OMEGA_EVEN * weight) * base, (OMEGA_EVEN * weight * 4.5) * density,
                          (OMEGA_ODD * weight * 3.0) * density)
    for i in range(1, POPS, 2):
        projected = None
        for axis in range(3):
            sign = VELOCITIES[i][axis]
            if sign == 0:
                continue
            if projected is None:
                projected = velocity[axis] if sign == 1 else -velocity[axis]
            else:
                projected = projected + velocity[axis] if sign == 1 else projected - velocity[axis]
        low, curve, slope = shared[WEIGHTS[i]]
        even_part = (0.5 - 0.5 * OMEGA_EVEN) * even[i] + (low + curve * (projected * projected))
        odd_part = (0.5 - 0.5 * OMEGA_ODD) * odd[i] + slope * projected
        post[i] = even_part + odd_part
        post[i + 1] = even_part - odd_part
    return post, density


def pushes(density, drift_y, drift_z):
    along_y = density * drift_y
    along_z = density * drift_z
    out = [None] * POPS
    for i in range(1, POPS):
        _, step_y, step_z = VELOCITIES[i]
        total = None
        for sign, part in ((step_y, along_y), (step_z, along_z)):
            if sign == 0:
                continue
            if total is None:
                total = part if sign == 1 else -part
            else:
                total = total + part if sign == 1 else total - part
        if total is not None:
            out[i] = (6.0 * WEIGHTS[i]) * total
    return out


def total_of(parts):
    parts = list(parts)
    while len(parts) > 1:
        pairs = [parts[n] + parts[n + 1] for n in range(0, len(parts) - 1, 2)]
        parts = pairs + parts[len(parts) - len(parts) % 2 :]
    return parts[0]


def streamed(pull, own, drift_y, drift_z):
    push = pushes(total_of(own), drift_y, drift_z)
    out = [own[0]]
    for i in range(1, POPS):
        pulled = pull(i)
        bounced = own[OPPOSITE[i]]
        blocked = pulled < WALL_BELOW
        if push[i] is not None:
            bounced = jnp.where(pulled < OUT_BELOW, bounced, bounced + push[i])
        out.append(jnp.where(blocked, bounced, pulled))
    return out


def ahead(items, take, leave, depth):
    waiting = []
    for n in items:
        waiting.append((n, take(n)))
        if len(waiting) > depth:
            leave(*waiting.pop(0))
    for pair in waiting:
        leave(*pair)


def place():
    return lax.axis_index("stream"), lax.axis_index("cy"), lax.axis_index("cz")


def slot_of(pos, row, layer, column_z):
    slot = (pos[0, row] - (layer * BXD - 1)) * BZD + (pos[2, row] - column_z * BZD)
    return jnp.clip(slot, 0, LAYERS * BZD - 1)


def fill_table(pos, table):
    layer, _, column_z = place()
    for entry in range(LAYERS * BZD):
        table[entry] = -1
    for row in range(pos.shape[1]):

        @pl.when(pos[0, row] >= 0)
        def _(row=row):
            table[slot_of(pos, row, layer, column_z)] = row


def spread_marks(marks, dense):
    rows = marks.shape[0]
    for first in range(0, rows, 8):
        size = min(8, rows - first)
        for begin in range(0, TILES, 8):
            values = [marks[first : first + size, t * LANE : (t + 1) * LANE] for t in range(begin, begin + 8)]
            for k, value in enumerate(values):
                dense[pl.ds(first * TILES + begin + k, size, stride=TILES), :] = value.astype(jnp.float32)


def collide_block(ref, base):
    for part in range(TILES // 8):
        old = [ref[pl.ds(base + i * TILES + 8 * part, 8), :] for i in range(POPS)]
        mark = ref[pl.ds(base + POPS * TILES + 8 * part, 8), :] > 0.5
        post, _ = collide(old)
        for i in range(POPS):
            ref[pl.ds(base + i * TILES + 8 * part, 8), :] = jnp.where(mark, old[i], post[i])


def pack_block(out, base, stage, dense, row):
    out[pl.ds(base + POPS * TILES, TILES), :] = dense[pl.ds(pl.multiple_of(row * TILES, 8), TILES), :]
    for first in range(0, TILES, 4):
        moves = []
        for tile in range(first, first + 4):
            for group, size in GROUPS:
                value = stage[group : group + size, tile * LANE : (tile + 1) * LANE]
                moves.append((pl.ds(base + group * TILES + tile, size, stride=TILES), value))
        for target, value in moves:
            out[target, :] = value
    collide_block(out, base)


def pack_stream(places, marks_in, pops, up, down, pos, table, marks, dense, blocks, slabs, strip, sems):
    mark_copy = pltpu.make_async_copy(marks_in, marks, sems.at[0])
    mark_copy.start()
    place_copy = pltpu.make_async_copy(places, pos, sems.at[1])
    place_copy.start()
    rows = pos.shape[1]
    copies = [None] * 4
    for j in range(MOVE_CAP):
        copies[MOVE_CAP + j] = pltpu.make_async_copy(pops.at[j], blocks.at[MOVE_CAP + j], sems.at[2 + MOVE_CAP + j])
        copies[MOVE_CAP + j].start()
    place_copy.wait()
    count = 0
    for row in range(rows):
        count = count + jnp.where(pos[0, row] >= 0, 1, 0)
    last = jnp.clip(count - MOVE_CAP, 0, rows - MOVE_CAP)
    for j in range(MOVE_CAP):
        copies[j] = pltpu.make_async_copy(pops.at[last + j], blocks.at[j], sems.at[2 + j])
        copies[j].start()
    fill_table(pos, table)
    slab_rows = []
    slab_copies = []
    for side in range(2):
        for bz in range(BZD):
            row = jnp.maximum(table[(2 - side) * BZD + bz], 0)
            n = side * BZD + bz
            first = (TILES - SLAB) * LANE if side == 0 else 0
            slab_rows.append(row)
            slab_copies.append(
                pltpu.make_async_copy(
                    pops.at[row, :, pl.ds(first, SLAB * LANE)], slabs.at[n], sems.at[2 + 2 * MOVE_CAP + n]
                )
            )
            slab_copies[n].start()
    mark_copy.wait()
    spread_marks(marks, dense)
    for side, out in ((1, down), (0, up)):
        for j in range(MOVE_CAP):
            row = j if side == 1 else last + j
            for k, axis in ((0, 0), (1, 2)):
                value = jnp.full((1, LANE), pos[axis, row], jnp.int32).astype(jnp.float32)
                out[pl.ds(SENT_META + 2 * j + k, 1), :] = value
            n = side * MOVE_CAP + j
            copies[n].wait()
            pack_block(out, j * BLOCK, blocks.at[n], dense, row)
    for side, out in enumerate((up, down)):
        for bz in range(BZD):
            n = side * BZD + bz
            first = slab_rows[n] * TILES + (TILES - SLAB if side == 0 else 0)
            slab_copies[n].wait()
            moves = []
            for x in range(2):
                for yhi in range(2):
                    q = 2 * x + yhi
                    row = x * FACE + 2 * bz + yhi
                    for group, size in GROUPS:
                        value = slabs[n, group : group + size, q * LANE : (q + 1) * LANE]
                        moves.append((pl.ds(group * 2 * FACE + row, size, stride=2 * FACE), value))
                row = POPS * 2 * FACE + x * FACE + 2 * bz
                moves.append((pl.ds(row, 2), dense[pl.ds(first + 2 * x, 2), :]))
            for target, value in moves:
                strip[target, :] = value
        inner = 1 if side == 0 else 0
        for x in range(2):
            old = [strip[pl.ds(i * 2 * FACE + x * FACE, FACE), :] for i in range(POPS)]
            mark = strip[pl.ds(POPS * 2 * FACE + x * FACE, FACE), :] > 0.5
            post, _ = collide(old)
            if x == inner:
                pairs = [(i, i) for i in range(POPS)]
            else:
                pairs = [(POPS + n, i) for n, i in enumerate(AHEAD if side == 0 else BACK)]
            for plane, i in pairs:
                out[pl.ds(SENT_SLABS + plane * FACE, FACE), :] = jnp.where(mark, ROTOR, post[i])


def pack_edge(places, marks_in, pops, own, zpack, zup, zdown, pos, table, marks, dense, stage, sems):
    column_z = lax.axis_index("cz")
    mark_copy = pltpu.make_async_copy(marks_in, marks, sems.at[LAYERS])
    mark_copy.start()
    place_copy = pltpu.make_async_copy(places, pos, sems.at[LAYERS + 1])
    place_copy.start()
    place_copy.wait()
    fill_table(pos, table)
    edge_bz = jnp.where(column_z == 0, BZD - 1, 0)
    first_c = jnp.where(column_z == 0, EDGE - 2, 0)
    found = [table[held * BZD + edge_bz] for held in range(LAYERS)]
    row_of = [jnp.maximum(row, 0) for row in found]
    copies = []
    for held in range(LAYERS):
        copies.append(pltpu.make_async_copy(pops.at[row_of[held]], stage.at[held], sems.at[held]))
        copies[held].start()
    mark_copy.wait()
    spread_marks(marks, dense)
    spot = (lanes() & (EDGE - 1)) >> 1
    sublane = lax.broadcasted_iota(jnp.int32, (8, LANE), 0)
    flags = jnp.zeros((8, LANE), jnp.int32)
    for held in range(LAYERS):
        copies[held].wait()
        base = pl.multiple_of((held * BZD + edge_bz) * BLOCK, 8)

        @pl.when(found[held] >= 0)
        def _(held=held, base=base):
            pack_block(own, base, stage.at[held], dense, row_of[held])
            totals = []
            for group in range(ZGROUPS):
                for part in range(TILES // 8):
                    total = jnp.zeros((8, LANE), jnp.float32)
                    for k in range(min(8, PLANES - group * 8)):
                        value = own[pl.ds(base + (group * 8 + k) * TILES + part * 8, 8), :]
                        value = pltpu.roll(value, (2 * k - first_c + LANE) & (LANE - 1), 1)
                        total = jnp.where(spot == k, value, total)
                    totals.append((held * ZROWS + group * TILES + part * 8, total))
            for row, total in totals:
                zpack[pl.ds(row, 8), :] = total

        flags = jnp.where((sublane == held) & (found[held] >= 0), 1, flags)
    zpack[pl.ds(ZMETA, 8), :] = flags.astype(jnp.float32)
    zup[pl.ds(0, ZROWS), :] = zpack[pl.ds(3 * ZROWS, ZROWS), :]
    zdown[pl.ds(0, ZROWS), :] = zpack[pl.ds(0, ZROWS), :]
    for group in range(ZGROUPS):
        target = pl.ds(ZROWS + group * SLAB, SLAB)
        zup[target, :] = zpack[pl.ds(2 * ZROWS + group * TILES + TILES - SLAB, SLAB), :]
        zdown[target, :] = zpack[pl.ds(ZROWS + group * TILES, SLAB), :]


def pack_own(places, marks_in, pops, own_in, own, pos, marks, dense, stage, sems):
    del own_in
    layer, _, column_z = place()
    edge_bz = jnp.where(column_z == 0, BZD - 1, 0)
    rows = pos.shape[1]
    mark_copy = pltpu.make_async_copy(marks_in, marks, sems.at[rows])
    mark_copy.start()
    place_copy = pltpu.make_async_copy(places, pos, sems.at[rows + 1])
    place_copy.start()
    copies = [pltpu.make_async_copy(pops.at[r], stage.at[r], sems.at[r]) for r in range(rows)]
    for copy in copies:
        copy.start()
    mark_copy.wait()
    spread_marks(marks, dense)
    place_copy.wait()

    def settle(row, carry):
        pltpu.make_async_copy(pops.at[row], stage.at[row], sems.at[row]).wait()
        slot = slot_of(pos, row, layer, column_z)

        @pl.when((pos[0, row] >= 0) & (slot % BZD != edge_bz))
        def _():
            pack_block(own, pl.multiple_of(slot * BLOCK, 8), stage.at[row], dense, row)

        return carry

    lax.fori_loop(0, rows, settle, 0)


class Lanes:
    def __init__(self, column_z):
        lane = lanes()
        self.from_bz = [lane >= bz * EDGE for bz in range(BZD)]
        self.main = lane < SPAN_Z
        self.single = (lane & EDGE) != 0
        self.double = (lane & (2 * EDGE)) != 0
        self.goal = jnp.where(column_z == 0, SPAN_Z, LANE - 2)

    def to_halo(self, ylo, spot):
        return (self.goal - (ylo * EDGE + 2 * spot) + LANE) & (LANE - 1)


def gathered(parts, zvalue, spot, ylo, masks):
    rows = parts[0].shape[0]
    total = None
    for bz in range(BZD):
        shift = (bz * EDGE - ylo * EDGE) % LANE
        value = pltpu.roll(parts[bz], shift, 1) if shift else parts[bz]
        total = value if total is None else jnp.where(masks.from_bz[bz][:rows], value, total)
    beyond = pltpu.roll(zvalue, masks.to_halo(ylo, spot), 1)
    return jnp.where(masks.main[:rows], total, beyond)


def gathered_rows(parts, zvalue, spot, masks):
    rows = parts[0].shape[0]
    single, double, main = masks.single[:rows], masks.double[:rows], masks.main[:rows]
    pairs = []
    for n in (0, 2):
        even = jnp.where(single, pltpu.roll(parts[n + 1], EDGE, 1), parts[n])
        odd = jnp.where(single, parts[n + 1], pltpu.roll(parts[n], LANE - EDGE, 1))
        pairs.append((even, odd))
    out = [None] * YLO
    for r in range(4):
        low, high = pairs[0][r % 2], pairs[1][r % 2]
        if r < 2:
            both = jnp.where(double, pltpu.roll(high, 2 * EDGE, 1), low)
        else:
            both = jnp.where(double, high, pltpu.roll(low, LANE - 2 * EDGE, 1))
        beyond = pltpu.roll(zvalue, masks.to_halo(r, spot), 1)
        out[r] = jnp.where(main, both, beyond)
        out[r + 4] = pltpu.roll(jnp.where(main, beyond, both), SPAN_Z, 1)
    return out


def inside_lanes(rows, column_z):
    lane = lanes()[:rows]
    low = (column_z == 0) & (lane >= SPAN_Z) & (lane < SPAN_Z + 2)
    high = (column_z != 0) & (lane >= LANE - 2)
    return (lane < SPAN_Z) | low | high


def marked(post, mark, inside):
    flag = jnp.where(inside, jnp.where(mark > 0.5, ROTOR, 0.0), OUTSIDE)
    wall = flag < WALL_BELOW
    return [jnp.where(wall, flag, value) for value in post]


def plane_parts(own, edge, zall, zedge, chunk, yhi, plane):
    group = plane >> 3
    if chunk is None:
        first = plane * 4 * FACE + yhi
        parts = [edge[pl.ds(first + 2 * bz, 4, stride=FACE), :] for bz in range(BZD)]
        return parts, zedge[pl.ds(group * 8 + yhi, 4, stride=2), :]
    held, half = 1 + (chunk >> 1), chunk & 1
    first = held * (BZD * BLOCK) + half * EDGE + yhi
    parts = [own[pl.ds(first + bz * BLOCK + plane * TILES, 8, stride=2), :] for bz in range(BZD)]
    first = held * ZROWS + half * EDGE + yhi
    return parts, zall[pl.ds(first + group * TILES, 8, stride=2), :]


def chunk_values(own, edge, zall, zedge, chunk, yhi, ylo, masks):
    out = []
    for plane in range(PLANES):
        parts, zvalue = plane_parts(own, edge, zall, zedge, chunk, yhi, plane)
        out.append(gathered(parts, zvalue, plane % 8, ylo, masks))
    return out


def halo_x_inside(layer, layers):
    row = lax.broadcasted_iota(jnp.int32, (4, LANE), 0)
    low = (row < 2) & (layer > 0)
    high = (row >= 2) & (layer < layers - 1)
    return low | high


def settle_rim(layers, places, up, down, zin, zup, zdown, own_in, own, edge, zall, zedge, rim_up, rim_down, pos, post_up, post_down, sem):
    del own_in
    layer, _, column_z = place()
    place_copy = pltpu.make_async_copy(places, pos, sem)
    place_copy.start()
    for arrived in (up, down):
        for j in range(MOVE_CAP):
            bx = arrived[pl.ds(SENT_META + 2 * j, 1), :].astype(jnp.int32)
            bz = arrived[pl.ds(SENT_META + 2 * j + 1, 1), :].astype(jnp.int32)
            code = (bx - layer * BXD) * BZD + (bz - column_z * BZD)
            mine = (bx >= layer * BXD) & (bx < (layer + 1) * BXD)
            first = layer == 0 if arrived is up else layer == layers - 1
            code = jnp.max(jnp.where(mine, code, -1))

            @pl.when((code >= 0) & jnp.logical_not(first))
            def _(arrived=arrived, j=j, code=code):
                base = pl.multiple_of((jnp.clip(code, 0, BXD * BZD - 1) + BZD) * BLOCK, 8)
                for k in range(0, BLOCK, 128):
                    values = [arrived[pl.ds(j * BLOCK + k + 8 * n, 8), :] for n in range(16)]
                    for n, value in enumerate(values):
                        own[pl.ds(base + k + 8 * n, 8), :] = value

    place_copy.wait()
    for side, arrived in enumerate((up, down)):
        inner, outer = (1, 0) if side == 0 else (2, 3)
        pairs = [(i, i, inner) for i in range(POPS)]
        pairs += [(POPS + n, i, outer) for n, i in enumerate(AHEAD if side == 0 else BACK)]
        for x in (2 * side, 2 * side + 1):
            edge[pl.ds((POPS * 4 + x) * FACE, FACE), :] = jnp.zeros((FACE, LANE), jnp.float32)
        values = [arrived[pl.ds(SENT_SLABS + plane * FACE, FACE), :] for plane, _, _ in pairs]
        for (_, i, x), value in zip(pairs, values):
            edge[pl.ds((i * 4 + x) * FACE, FACE), :] = value
        for bz in range(BZD):
            here = jnp.int32(0)
            goal = (0 if side == 0 else LAYERS - 1) * BZD + bz
            for row in range(pos.shape[1]):
                hit = (pos[0, row] >= 0) & (slot_of(pos, row, layer, column_z) == goal)
                here = jnp.where(hit, 1, here)

            @pl.when(here == 1)
            def _(side=side, pairs=pairs, goal=goal, bz=bz):
                first = goal * BLOCK + (TILES - SLAB if side == 0 else 0)
                values = []
                for _, i, x in pairs:
                    shift = 2 * (x if side == 0 else x - 2)
                    mark = own[pl.ds(first + POPS * TILES + shift, 2), :] > 0.5
                    values.append(jnp.where(mark, ROTOR, own[pl.ds(first + i * TILES + shift, 2), :]))
                for (_, i, x), value in zip(pairs, values):
                    edge[pl.ds((i * 4 + x) * FACE + 2 * bz, 2), :] = value

    moves = []
    for held in range(LAYERS):
        flag = zin[pl.ds(ZMETA + held, 1), :] > 0.5
        for group in range(ZGROUPS):
            if held == 1 or held == 2:
                for part in range(TILES // 8):
                    rows = pl.ds(held * ZROWS + group * TILES + part * 8, 8)
                    source = zup if held == 1 else zdown
                    other = source[pl.ds(group * TILES + part * 8, 8), :]
                    moves.append((zall, rows, jnp.where(flag, zin[rows, :], other)))
            else:
                side = 0 if held == 0 else 1
                source = zup if held == 0 else zdown
                first = TILES - SLAB if held == 0 else 0
                mine = zin[pl.ds(held * ZROWS + group * TILES + first, SLAB), :]
                other = source[pl.ds(ZROWS + group * SLAB, SLAB), :]
                moves.append((zedge, pl.ds(group * 8 + side * SLAB, SLAB), jnp.where(flag, mine, other)))
    for target, rows, value in moves:
        target[rows, :] = value
    masks = Lanes(column_z)
    inside_box = inside_lanes(8, column_z)
    inside_halo = inside_lanes(4, column_z) & halo_x_inside(layer, layers)
    for chunk in (0, 1, 2, 3, None):
        for y in (0, 1, SPAN_Y - 2, SPAN_Y - 1):
            values = chunk_values(own, edge, zall, zedge, chunk, y // YLO, y % YLO, masks)
            inside = inside_halo if chunk is None else inside_box
            post = marked(values[:POPS], values[POPS], inside)
            target = post_down if y < 2 else post_up
            rim = RIM_DOWN if y < 2 else RIM_UP
            if y in (0, SPAN_Y - 1):
                pairs = [(i, i) for i in range(POPS)]
            else:
                pairs = [(POPS + n, i) for n, i in enumerate(rim)]
            for plane, i in pairs:
                if chunk is None:
                    target[pl.ds(plane * GRID_X, 2), :] = post[i][:2]
                    target[pl.ds(plane * GRID_X + EXT_X - 2, 2), :] = post[i][2:]
                else:
                    target[pl.ds(plane * GRID_X + 2 + 8 * chunk, 8), :] = post[i]
    lane = lanes()
    for source, target in ((post_up, rim_up), (post_down, rim_down)):
        for chunk in range(5):
            size = min(8, EXT_X - 8 * chunk)
            values = []
            for plane in range(RIM):
                value = source[pl.ds(plane * GRID_X + 8 * chunk, 8), :]
                values.append(pltpu.roll(value, (plane * EXT_Z + 2 * column_z) & (LANE - 1), 1))
            totals = []
            for block in range(RIM_BLOCKS):
                total = jnp.zeros((8, LANE), jnp.float32)
                for plane in range(RIM):
                    begin = plane * EXT_Z - block * LANE
                    if begin >= LANE or begin + EXT_Z <= 0:
                        continue
                    total = jnp.where((lane >= begin) & (lane < begin + EXT_Z), values[plane], total)
                totals.append(total)
            for block in range(RIM_BLOCKS):
                target[pl.ds(block * EXT_X + 8 * chunk, size), :] = totals[block][:size]


def turned(value, step_z):
    return pltpu.roll(value, step_z % LANE, 1) if step_z else value


def drifts_of(columns, depth):
    _, _, column_z = place()
    lane = lanes()
    total_y = SPAN_Y * columns
    total_z = SPAN_Z * depth
    spin = 0.2 / (total_y + total_z)
    here_z = jnp.where(lane < SPAN_Z + 8, lane, lane - LANE) + column_z * SPAN_Z
    drift_y = -spin * (here_z.astype(jnp.float32) - (total_z - 1) / 2.0)
    return drift_y, spin, (total_y - 1) / 2.0


def first_step(columns, depth, field, later, begin, end):
    _, column_y, _ = place()
    drift_y, spin, centre_y = drifts_of(columns, depth)
    sublane = lax.broadcasted_iota(jnp.int32, (8, LANE), 0)

    def tile(n, carry):
        base = pl.multiple_of(8 * n, 8)
        line = (n - FIRST // 8 + 2 * STEP) // STEP
        next_row = (sublane >= 6) & (n - FIRST // 8 + 2 * STEP - line * STEP == STEP - 1)
        here_y = jnp.where(next_row, line + 1, line) + (column_y * SPAN_Y - 2)
        drift_z = spin * (here_y.astype(jnp.float32) - centre_y)
        old = [field[pl.ds(i * FIELD + base, 8), :] for i in range(POPS)]
        values = streamed(pull_from(field, base), old, drift_y, drift_z)
        post, _ = collide(values)
        wall = old[0] < WALL_BELOW
        for i in range(POPS):
            later[pl.ds(i * FIELD + base, 8), :] = jnp.where(wall, old[0], post[i])
        return carry

    lax.fori_loop(FIRST // 8 + begin, FIRST // 8 + end, tile, 0)


def pull_from(field, base):
    def pull(i):
        step_x, step_y, step_z = VELOCITIES[i]
        return turned(field[pl.ds(i * FIELD + base - step_y * PITCH - step_x, 8), :], step_z)

    return pull


def settle_all(layers, columns, depth, own, edge, zall, zedge, field, start, later):
    layer, _, column_z = place()
    masks = Lanes(column_z)
    inside_box = inside_lanes(8, column_z)
    inside_halo = inside_lanes(4, column_z) & halo_x_inside(layer, layers)

    def caps_of(mark, inside):
        return [jnp.where(inside, jnp.where(value > 0.5, ROTOR, -ROTOR), OUTSIDE) for value in mark]

    def halves(yhi, carry):
        top = yhi * YLO * PITCH + FIRST

        def rows_of_plane(chunk, plane):
            parts, zvalue = plane_parts(own, edge, zall, zedge, chunk, yhi, plane)
            return gathered_rows(parts, zvalue, plane & 7, masks)

        def chunks(chunk, carry):
            caps = caps_of(rows_of_plane(chunk, POPS), inside_box)

            def planes(quad, carry):
                taken = [rows_of_plane(chunk, quad * QUAD + k) for k in range(QUAD)]
                for k, values in enumerate(taken):
                    i = quad * QUAD + k
                    for ylo in range(YLO):
                        row = pl.multiple_of(i * FIELD + top + ylo * PITCH + 8 * chunk, 8)
                        field[pl.ds(row, 8), :] = jnp.minimum(values[ylo], caps[ylo])
                        row = pl.multiple_of((i * SPAN_Y + YLO * yhi + ylo) * SPAN_X + 8 * chunk, 8)
                        start[pl.ds(row, 8), :] = values[ylo]
                return carry

            lax.fori_loop(0, PLANES // QUAD, planes, 0)
            return carry

        lax.fori_loop(0, SPAN_X // 8, chunks, 0)
        caps = caps_of(rows_of_plane(None, POPS), inside_halo)

        def planes(quad, carry):
            taken = [rows_of_plane(None, quad * QUAD + k) for k in range(QUAD)]
            for k, values in enumerate(taken):
                for ylo in range(YLO):
                    value = jnp.minimum(values[ylo], caps[ylo])
                    row = (quad * QUAD + k) * FIELD + top + ylo * PITCH
                    field[pl.ds(row - 2, 2), :] = value[:2]
                    field[pl.ds(row + SPAN_X, 2), :] = value[2:]
            return carry

        lax.fori_loop(0, PLANES // QUAD, planes, 0)
        return carry

    lax.fori_loop(0, SPAN_Y // YLO, halves, 0)
    first_step(columns, depth, field, later, STEP, (SPAN_Y - 1) * STEP)


def finish(columns, depth, rim_low, rim_high, field_in, start, later_in, out, field, later, turn, result, sems):
    del field_in, later_in
    _, column_y, column_z = place()
    flat = (lanes() + 2 * column_z) & (LANE - 1)
    sides = (
        (rim_low, -1, -2, RIM_UP, column_y > 0),
        (rim_high, SPAN_Y, SPAN_Y + 1, RIM_DOWN, column_y < columns - 1),
    )
    for source, near, far, rim, there in sides:
        for chunk in range(5):
            size = min(8, EXT_X - 8 * chunk)
            blocks = [source[pl.ds(block * EXT_X + 8 * chunk, 8), :] for block in range(RIM_BLOCKS)]
            for plane in range(RIM):
                block, begin = divmod(plane * EXT_Z, LANE)
                shift = (2 * LANE - begin - 2 * column_z) & (LANE - 1)
                value = pltpu.roll(blocks[block], shift, 1)
                if begin + EXT_Z > LANE:
                    value = jnp.where(flat < LANE - begin, value, pltpu.roll(blocks[block + 1], shift, 1))
                value = jnp.where((flat < EXT_Z) & there, value, OUTSIDE)
                i, y = (plane, near) if plane < POPS else (rim[plane - POPS], far)
                row = i * FIELD + FIRST + y * PITCH - 2 + 8 * chunk
                field[pl.ds(row, size), :] = value[:size]

    first_step(columns, depth, field, later, -STEP - 1, STEP)
    first_step(columns, depth, field, later, (SPAN_Y - 1) * STEP - 1, (SPAN_Y + 1) * STEP)

    drift_y, spin, centre_y = drifts_of(columns, depth)

    def leave(n):
        part = pl.ds(n * 8, 8)
        return pltpu.make_async_copy(result.at[:, part], out.at[:, part], sems.at[n])

    def second_step(chunk, carry):
        for half in range(SPAN_Y // 8):
            for k in range(8):
                y = 8 * half + k
                base = pl.multiple_of(FIRST + y * PITCH + 8 * chunk, 8)
                drift_z = spin * ((column_y * SPAN_Y + y).astype(jnp.float32) - centre_y)
                old = [later[pl.ds(i * FIELD + base, 8), :] for i in range(POPS)]
                values = streamed(pull_from(later, base), old, drift_y, drift_z)
                wall = old[0] < WALL_BELOW
                for i in range(POPS):
                    first = pl.multiple_of((i * SPAN_Y + y) * SPAN_X + 8 * chunk, 8)
                    value = jnp.where(wall, start[pl.ds(first, 8), :], values[i])
                    turn[pl.ds(i * 8 * TURN + k * TURN, 8), :] = value
            for k in range(8):
                values = [turn[pl.ds(i * 8 * TURN + k, 8, stride=TURN), :] for i in range(POPS)]
                for i in range(POPS):
                    result[i, 8 * chunk + k, 8 * half : 8 * half + 8, :] = values[i][:, :SPAN_Z]
        leave(chunk).start()
        return carry

    lax.fori_loop(0, SPAN_X // 8, second_step, 0)
    for n in range(SPAN_X // 8):
        leave(n).wait()


def rows_of(count):
    return jax.ShapeDtypeStruct((count, LANE), jnp.float32)


def kept(count):
    return VMEM((count, LANE), jnp.float32)


def params(mib):
    return pltpu.CompilerParams(vmem_limit_bytes=mib * 2**20)


def shards(populations, solid_cells, block_pos):
    layers = lax.axis_size("stream")
    columns = lax.axis_size("cy")
    depth = lax.axis_size("cz")
    rows = block_pos.shape[0]
    vmem = pl.BlockSpec(memory_space=VMEM)
    hbm = pl.BlockSpec(memory_space=pltpu.HBM)
    populations = pltpu.with_memory_space_constraint(populations, pltpu.HBM)
    solid_cells = pltpu.with_memory_space_constraint(solid_cells, pltpu.HBM)
    places = pltpu.with_memory_space_constraint(block_pos.T, pltpu.HBM)
    place_scratch = SMEM((3, rows), jnp.int32)
    table_scratch = SMEM((LAYERS * BZD,), jnp.int32)
    mark_scratch = [VMEM((rows, EDGE**3), jnp.int32), VMEM((rows * TILES, LANE), jnp.float32)]

    up = [(i, i + 1) for i in range(layers - 1)]
    down = [(i + 1, i) for i in range(layers - 1)]
    send_up, send_down = pl.pallas_call(
        pack_stream,
        out_shape=(kept(SENT_ROWS), kept(SENT_ROWS)),
        in_specs=[hbm, hbm, hbm],
        out_specs=(vmem, vmem),
        scratch_shapes=[place_scratch, table_scratch]
        + mark_scratch
        + [
            VMEM((2 * MOVE_CAP, POPS, EDGE**3), jnp.float32),
            VMEM((2 * BZD, POPS, SLAB * LANE), jnp.float32),
            VMEM((PLANES * 2 * FACE, LANE), jnp.float32),
            pltpu.SemaphoreType.DMA((2 + 2 * MOVE_CAP + 2 * BZD,)),
        ],
        compiler_params=params(16),
        name="pack_stream",
    )(places, solid_cells, populations)
    from_low = lax.ppermute(send_up, "stream", up)
    from_high = lax.ppermute(send_down, "stream", down)

    own, zpack, zsend_up, zsend_down = pl.pallas_call(
        pack_edge,
        out_shape=(kept(LAYERS * BZD * BLOCK), kept(ZMETA + 8), kept(DIAG), kept(DIAG)),
        in_specs=[hbm, hbm, hbm],
        out_specs=(vmem,) * 4,
        scratch_shapes=[place_scratch, table_scratch]
        + mark_scratch
        + [
            VMEM((LAYERS, POPS, EDGE**3), jnp.float32),
            pltpu.SemaphoreType.DMA((LAYERS + 2,)),
        ],
        compiler_params=params(16),
        name="pack_edge",
    )(places, solid_cells, populations)
    swap = [(i, depth - 1 - i) for i in range(depth)]
    zin = lax.ppermute(zpack, "cz", swap)
    zup_pairs = [(s * depth + c, t * depth + d) for s, t in up for c, d in swap]
    zdown_pairs = [(s * depth + c, t * depth + d) for s, t in down for c, d in swap]
    z_low = lax.ppermute(zsend_up, ("stream", "cz"), zup_pairs)
    z_high = lax.ppermute(zsend_down, ("stream", "cz"), zdown_pairs)

    own = pl.pallas_call(
        pack_own,
        out_shape=kept(LAYERS * BZD * BLOCK),
        in_specs=[hbm, hbm, hbm, vmem],
        out_specs=vmem,
        scratch_shapes=[place_scratch]
        + mark_scratch
        + [
            VMEM((rows, POPS, EDGE**3), jnp.float32),
            pltpu.SemaphoreType.DMA((rows + 2,)),
        ],
        input_output_aliases={3: 0},
        compiler_params=params(16),
        name="pack_own",
    )(places, solid_cells, populations, own)

    own, edge, zall, zedge, rim_up, rim_down = pl.pallas_call(
        functools.partial(settle_rim, layers),
        out_shape=(
            kept(LAYERS * BZD * BLOCK),
            kept(PLANES * 4 * FACE),
            kept(LAYERS * ZROWS),
            kept(ZGROUPS * 8),
            kept(RIM_ROWS),
            kept(RIM_ROWS),
        ),
        in_specs=[hbm] + [vmem] * 6,
        out_specs=(vmem,) * 6,
        scratch_shapes=[
            place_scratch,
            VMEM((RIM * GRID_X, LANE), jnp.float32),
            VMEM((RIM * GRID_X, LANE), jnp.float32),
            pltpu.SemaphoreType.DMA,
        ],
        input_output_aliases={6: 0},
        compiler_params=params(16),
        name="settle_rim",
    )(places, from_low, from_high, zin, z_low, z_high, own)
    cy_up = [(i, i + 1) for i in range(columns - 1)]
    cy_down = [(i + 1, i) for i in range(columns - 1)]
    rim_low = lax.ppermute(rim_up, "cy", cy_up)
    rim_high = lax.ppermute(rim_down, "cy", cy_down)

    field, start, later = pl.pallas_call(
        functools.partial(settle_all, layers, columns, depth),
        out_shape=(kept(PLANES * FIELD), kept(PLANES * SPAN_X * SPAN_Y), kept(POPS * FIELD)),
        in_specs=[vmem] * 4,
        out_specs=(vmem,) * 3,
        compiler_params=params(16),
        name="settle_all",
    )(own, edge, zall, zedge)

    out, _, _ = pl.pallas_call(
        functools.partial(finish, columns, depth),
        out_shape=(
            jax.ShapeDtypeStruct((POPS, SPAN_X, SPAN_Y, SPAN_Z), jnp.float32),
            kept(PLANES * FIELD),
            kept(POPS * FIELD),
        ),
        in_specs=[vmem] * 5,
        out_specs=(hbm, vmem, vmem),
        scratch_shapes=[
            VMEM((POPS * 8 * TURN, LANE), jnp.float32),
            VMEM((POPS, SPAN_X, SPAN_Y, SPAN_Z), jnp.float32),
            pltpu.SemaphoreType.DMA((SPAN_X // 8,)),
        ],
        input_output_aliases={2: 1, 4: 2},
        compiler_params=params(16),
        name="finish",
    )(rim_low, rim_high, field, start, later)
    return out


def solution(mesh):
    in_specs = (
        P(("stream", "cy", "cz"), None, None),
        P(("stream", "cy", "cz"), None),
        P(("stream", "cy", "cz"), None),
    )
    out_specs = P(None, "stream", "cy", "cz")
    return jax.shard_map(shards, mesh=mesh, in_specs=in_specs, out_specs=out_specs, check_vma=False)
```

```python
import functools

import jax
import jax.numpy as jnp
from jax import lax
from jax.experimental import pallas as pl
from jax.experimental.pallas import tpu as pltpu
from jax.sharding import PartitionSpec as P

EDGE = 16
BXD = 2
BYD = 1
BZD = 4
MOVE_CAP = 2

VELOCITIES = (
    (0, 0, 0),
    (1, 0, 0),
    (-1, 0, 0),
    (0, 1, 0),
    (0, -1, 0),
    (0, 0, 1),
    (0, 0, -1),
    (1, 1, 0),
    (-1, -1, 0),
    (1, -1, 0),
    (-1, 1, 0),
    (1, 0, 1),
    (-1, 0, -1),
    (1, 0, -1),
    (-1, 0, 1),
    (0, 1, 1),
    (0, -1, -1),
    (0, 1, -1),
    (0, -1, 1),
)
WEIGHTS = (1.0 / 3.0,) + (1.0 / 18.0,) * 6 + (1.0 / 36.0,) * 12
OPPOSITE = (0, 2, 1, 4, 3, 6, 5, 8, 7, 10, 9, 12, 11, 14, 13, 16, 15, 18, 17)
OMEGA_EVEN = 1.25
OMEGA_ODD = 1.0 / 1.125

POPS = 19
PLANES = 20
LANE = 128
TILES = EDGE**3 // LANE
BLOCK = PLANES * TILES
YLO = LANE // EDGE
SLAB = 4
GROUPS = ((0, 8), (8, 8), (16, 3))
SENT_SLABS = MOVE_CAP * BLOCK
LAYERS = BXD + 2
ZGROUPS = 3
ZROWS = ZGROUPS * TILES
ZMETA = LAYERS * ZROWS
DIAG = ZROWS + ZGROUPS * SLAB

SPAN_X = BXD * EDGE
SPAN_Y = BYD * EDGE
SPAN_Z = BZD * EDGE
PITCH = SPAN_X + 8
STEP = PITCH // 8
FIRST = 96
FIELD = FIRST + (SPAN_Y + 1) * PITCH + 48
TURN = 9
EXT_X = SPAN_X + 4
EXT_Z = SPAN_Z + 2
RIM_UP = tuple(i for i in range(POPS) if VELOCITIES[i][1] == 1)
RIM_DOWN = tuple(i for i in range(POPS) if VELOCITIES[i][1] == -1)
RIM = PLANES + len(RIM_UP) + 1
AHEAD = tuple(i for i in range(POPS) if VELOCITIES[i][0] == 1)
BACK = tuple(i for i in range(POPS) if VELOCITIES[i][0] == -1)
FACE = 2 * BZD
SENT_META = SENT_SLABS + RIM * FACE
SENT_ROWS = SENT_META + 8
RIM_BLOCKS = -(-RIM * EXT_Z // LANE)
RIM_ROWS = RIM_BLOCKS * EXT_X + 4
GRID_X = 48

ROTOR = -(2.0**100)
OUTSIDE = -(2.0**110)
WALL_BELOW = -(2.0**80)
OUT_BELOW = -(2.0**105)

VMEM = pltpu.VMEM
SMEM = pltpu.SMEM


def lanes():
    return lax.broadcasted_iota(jnp.int32, (8, LANE), 1)


def collide(f):
    even = [None] * POPS
    odd = [None] * POPS
    for i in range(1, POPS, 2):
        even[i] = f[i] + f[i + 1]
        odd[i] = f[i] - f[i + 1]
    density = f[0]
    for i in range(1, POPS, 2):
        density = density + even[i]
    flow = []
    for axis in range(3):
        total = None
        for i in range(1, POPS, 2):
            sign = VELOCITIES[i][axis]
            if sign == 0:
                continue
            if total is None:
                total = odd[i] if sign == 1 else -odd[i]
            else:
                total = total + odd[i] if sign == 1 else total - odd[i]
        flow.append(total)
    inverse = 1.0 / density
    velocity = [part * inverse for part in flow]
    square = velocity[0] * velocity[0] + velocity[1] * velocity[1] + velocity[2] * velocity[2]
    base = density * (1.0 - 1.5 * square)
    post = [None] * POPS
    post[0] = (1.0 - OMEGA_EVEN) * f[0] + (OMEGA_EVEN * WEIGHTS[0]) * base
    shared = {}
    for weight in (WEIGHTS[1], WEIGHTS[7]):
        shared[weight] = ((OMEGA_EVEN * weight) * base, (OMEGA_EVEN * weight * 4.5) * density,
                          (OMEGA_ODD * weight * 3.0) * density)
    for i in range(1, POPS, 2):
        projected = None
        for axis in range(3):
            sign = VELOCITIES[i][axis]
            if sign == 0:
                continue
            if projected is None:
                projected = velocity[axis] if sign == 1 else -velocity[axis]
            else:
                projected = projected + velocity[axis] if sign == 1 else projected - velocity[axis]
        low, curve, slope = shared[WEIGHTS[i]]
        even_part = (0.5 - 0.5 * OMEGA_EVEN) * even[i] + (low + curve * (projected * projected))
        odd_part = (0.5 - 0.5 * OMEGA_ODD) * odd[i] + slope * projected
        post[i] = even_part + odd_part
        post[i + 1] = even_part - odd_part
    return post, density


def pushes(density, drift_y, drift_z):
    along_y = density * drift_y
    along_z = density * drift_z
    out = [None] * POPS
    for i in range(1, POPS):
        _, step_y, step_z = VELOCITIES[i]
        total = None
        for sign, part in ((step_y, along_y), (step_z, along_z)):
            if sign == 0:
                continue
            if total is None:
                total = part if sign == 1 else -part
            else:
                total = total + part if sign == 1 else total - part
        if total is not None:
            out[i] = (6.0 * WEIGHTS[i]) * total
    return out


def total_of(parts):
    parts = list(parts)
    while len(parts) > 1:
        pairs = [parts[n] + parts[n + 1] for n in range(0, len(parts) - 1, 2)]
        parts = pairs + parts[len(parts) - len(parts) % 2 :]
    return parts[0]


def streamed(pull, own, drift_y, drift_z):
    push = pushes(total_of(own), drift_y, drift_z)
    out = [own[0]]
    for i in range(1, POPS):
        pulled = pull(i)
        bounced = own[OPPOSITE[i]]
        blocked = pulled < WALL_BELOW
        if push[i] is not None:
            bounced = jnp.where(pulled < OUT_BELOW, bounced, bounced + push[i])
        out.append(jnp.where(blocked, bounced, pulled))
    return out


def ahead(items, take, leave, depth):
    waiting = []
    for n in items:
        waiting.append((n, take(n)))
        if len(waiting) > depth:
            leave(*waiting.pop(0))
    for pair in waiting:
        leave(*pair)


def place():
    return lax.axis_index("stream"), lax.axis_index("cy"), lax.axis_index("cz")


def slot_of(pos, row, layer, column_z):
    slot = (pos[0, row] - (layer * BXD - 1)) * BZD + (pos[2, row] - column_z * BZD)
    return jnp.clip(slot, 0, LAYERS * BZD - 1)


def fill_table(pos, table):
    layer, _, column_z = place()
    for entry in range(LAYERS * BZD):
        table[entry] = -1
    for row in range(pos.shape[1]):

        @pl.when(pos[0, row] >= 0)
        def _(row=row):
            table[slot_of(pos, row, layer, column_z)] = row


def spread_marks(marks, dense):
    rows = marks.shape[0]
    for first in range(0, rows, 8):
        size = min(8, rows - first)
        for begin in range(0, TILES, 8):
            values = [marks[first : first + size, t * LANE : (t + 1) * LANE] for t in range(begin, begin + 8)]
            for k, value in enumerate(values):
                dense[pl.ds(first * TILES + begin + k, size, stride=TILES), :] = value.astype(jnp.float32)


def collide_block(ref, base):
    for part in range(TILES // 8):
        old = [ref[pl.ds(base + i * TILES + 8 * part, 8), :] for i in range(POPS)]
        mark = ref[pl.ds(base + POPS * TILES + 8 * part, 8), :] > 0.5
        post, _ = collide(old)
        for i in range(POPS):
            ref[pl.ds(base + i * TILES + 8 * part, 8), :] = jnp.where(mark, old[i], post[i])


def pack_block(out, base, stage, dense, row):
    out[pl.ds(base + POPS * TILES, TILES), :] = dense[pl.ds(pl.multiple_of(row * TILES, 8), TILES), :]
    for first in range(0, TILES, 4):
        moves = []
        for tile in range(first, first + 4):
            for group, size in GROUPS:
                value = stage[group : group + size, tile * LANE : (tile + 1) * LANE]
                moves.append((pl.ds(base + group * TILES + tile, size, stride=TILES), value))
        for target, value in moves:
            out[target, :] = value
    collide_block(out, base)


def pack_stream(places, marks_in, pops, up, down, pos, table, marks, dense, blocks, slabs, strip, sems):
    mark_copy = pltpu.make_async_copy(marks_in, marks, sems.at[0])
    mark_copy.start()
    place_copy = pltpu.make_async_copy(places, pos, sems.at[1])
    place_copy.start()
    rows = pos.shape[1]
    copies = [None] * 4
    for j in range(MOVE_CAP):
        copies[MOVE_CAP + j] = pltpu.make_async_copy(pops.at[j], blocks.at[MOVE_CAP + j], sems.at[2 + MOVE_CAP + j])
        copies[MOVE_CAP + j].start()
    place_copy.wait()
    count = 0
    for row in range(rows):
        count = count + jnp.where(pos[0, row] >= 0, 1, 0)
    last = jnp.clip(count - MOVE_CAP, 0, rows - MOVE_CAP)
    for j in range(MOVE_CAP):
        copies[j] = pltpu.make_async_copy(pops.at[last + j], blocks.at[j], sems.at[2 + j])
        copies[j].start()
    fill_table(pos, table)
    slab_rows = []
    slab_copies = []
    for side in range(2):
        for bz in range(BZD):
            row = jnp.maximum(table[(2 - side) * BZD + bz], 0)
            n = side * BZD + bz
            first = (TILES - SLAB) * LANE if side == 0 else 0
            slab_rows.append(row)
            slab_copies.append(
                pltpu.make_async_copy(
                    pops.at[row, :, pl.ds(first, SLAB * LANE)], slabs.at[n], sems.at[2 + 2 * MOVE_CAP + n]
                )
            )
            slab_copies[n].start()
    mark_copy.wait()
    spread_marks(marks, dense)
    for side, out in ((1, down), (0, up)):
        for j in range(MOVE_CAP):
            row = j if side == 1 else last + j
            for k, axis in ((0, 0), (1, 2)):
                value = jnp.full((1, LANE), pos[axis, row], jnp.int32).astype(jnp.float32)
                out[pl.ds(SENT_META + 2 * j + k, 1), :] = value
            n = side * MOVE_CAP + j
            copies[n].wait()
            pack_block(out, j * BLOCK, blocks.at[n], dense, row)
    for side, out in enumerate((up, down)):
        for bz in range(BZD):
            n = side * BZD + bz
            first = slab_rows[n] * TILES + (TILES - SLAB if side == 0 else 0)
            slab_copies[n].wait()
            moves = []
            for x in range(2):
                for yhi in range(2):
                    q = 2 * x + yhi
                    row = x * FACE + 2 * bz + yhi
                    for group, size in GROUPS:
                        value = slabs[n, group : group + size, q * LANE : (q + 1) * LANE]
                        moves.append((pl.ds(group * 2 * FACE + row, size, stride=2 * FACE), value))
                row = POPS * 2 * FACE + x * FACE + 2 * bz
                moves.append((pl.ds(row, 2), dense[pl.ds(first + 2 * x, 2), :]))
            for target, value in moves:
                strip[target, :] = value
        inner = 1 if side == 0 else 0
        for x in range(2):
            old = [strip[pl.ds(i * 2 * FACE + x * FACE, FACE), :] for i in range(POPS)]
            mark = strip[pl.ds(POPS * 2 * FACE + x * FACE, FACE), :] > 0.5
            post, _ = collide(old)
            if x == inner:
                pairs = [(i, i) for i in range(POPS)]
                marks_at = POPS
            else:
                pairs = [(PLANES + n, i) for n, i in enumerate(AHEAD if side == 0 else BACK)]
                marks_at = RIM - 1
            for plane, i in pairs:
                out[pl.ds(SENT_SLABS + plane * FACE, FACE), :] = jnp.where(mark, old[i], post[i])
            marks_of = strip[pl.ds(POPS * 2 * FACE + x * FACE, FACE), :]
            out[pl.ds(SENT_SLABS + marks_at * FACE, FACE), :] = marks_of


def pack_edge(places, marks_in, pops, own, zpack, zup, zdown, pos, table, marks, dense, stage, sems):
    column_z = lax.axis_index("cz")
    mark_copy = pltpu.make_async_copy(marks_in, marks, sems.at[LAYERS])
    mark_copy.start()
    place_copy = pltpu.make_async_copy(places, pos, sems.at[LAYERS + 1])
    place_copy.start()
    place_copy.wait()
    fill_table(pos, table)
    edge_bz = jnp.where(column_z == 0, BZD - 1, 0)
    first_c = jnp.where(column_z == 0, EDGE - 2, 0)
    found = [table[held * BZD + edge_bz] for held in range(LAYERS)]
    row_of = [jnp.maximum(row, 0) for row in found]
    copies = []
    for held in range(LAYERS):
        copies.append(pltpu.make_async_copy(pops.at[row_of[held]], stage.at[held], sems.at[held]))
        copies[held].start()
    mark_copy.wait()
    spread_marks(marks, dense)
    spot = (lanes() & (EDGE - 1)) >> 1
    sublane = lax.broadcasted_iota(jnp.int32, (8, LANE), 0)
    flags = jnp.zeros((8, LANE), jnp.int32)
    for held in range(LAYERS):
        copies[held].wait()
        base = pl.multiple_of((held * BZD + edge_bz) * BLOCK, 8)

        @pl.when(found[held] >= 0)
        def _(held=held, base=base):
            pack_block(own, base, stage.at[held], dense, row_of[held])
            totals = []
            for group in range(ZGROUPS):
                for part in range(TILES // 8):
                    total = jnp.zeros((8, LANE), jnp.float32)
                    for k in range(min(8, PLANES - group * 8)):
                        value = own[pl.ds(base + (group * 8 + k) * TILES + part * 8, 8), :]
                        value = pltpu.roll(value, (2 * k - first_c + LANE) & (LANE - 1), 1)
                        total = jnp.where(spot == k, value, total)
                    totals.append((held * ZROWS + group * TILES + part * 8, total))
            for row, total in totals:
                zpack[pl.ds(row, 8), :] = total

        flags = jnp.where((sublane == held) & (found[held] >= 0), 1, flags)
    zpack[pl.ds(ZMETA, 8), :] = flags.astype(jnp.float32)
    zup[pl.ds(0, ZROWS), :] = zpack[pl.ds(3 * ZROWS, ZROWS), :]
    zdown[pl.ds(0, ZROWS), :] = zpack[pl.ds(0, ZROWS), :]
    for group in range(ZGROUPS):
        target = pl.ds(ZROWS + group * SLAB, SLAB)
        zup[target, :] = zpack[pl.ds(2 * ZROWS + group * TILES + TILES - SLAB, SLAB), :]
        zdown[target, :] = zpack[pl.ds(ZROWS + group * TILES, SLAB), :]


def pack_own(places, marks_in, pops, own_in, own, pos, marks, dense, stage, sems):
    del own_in
    layer, _, column_z = place()
    edge_bz = jnp.where(column_z == 0, BZD - 1, 0)
    rows = pos.shape[1]
    mark_copy = pltpu.make_async_copy(marks_in, marks, sems.at[rows])
    mark_copy.start()
    place_copy = pltpu.make_async_copy(places, pos, sems.at[rows + 1])
    place_copy.start()
    copies = [pltpu.make_async_copy(pops.at[r], stage.at[r], sems.at[r]) for r in range(rows)]
    for copy in copies:
        copy.start()
    mark_copy.wait()
    spread_marks(marks, dense)
    place_copy.wait()

    def settle(row, carry):
        pltpu.make_async_copy(pops.at[row], stage.at[row], sems.at[row]).wait()
        slot = slot_of(pos, row, layer, column_z)

        @pl.when((pos[0, row] >= 0) & (slot % BZD != edge_bz))
        def _():
            pack_block(own, pl.multiple_of(slot * BLOCK, 8), stage.at[row], dense, row)

        return carry

    lax.fori_loop(0, rows, settle, 0)


class Lanes:
    def __init__(self, column_z):
        lane = lanes()
        self.from_bz = [lane >= bz * EDGE for bz in range(BZD)]
        self.main = lane < SPAN_Z
        self.goal = jnp.where(column_z == 0, SPAN_Z, LANE - 2)

    def to_halo(self, ylo, spot):
        return (self.goal - (ylo * EDGE + 2 * spot) + LANE) & (LANE - 1)


def gathered(parts, zvalue, spot, ylo, masks):
    rows = parts[0].shape[0]
    total = None
    for bz in range(BZD):
        shift = (bz * EDGE - ylo * EDGE) % LANE
        value = pltpu.roll(parts[bz], shift, 1) if shift else parts[bz]
        total = value if total is None else jnp.where(masks.from_bz[bz][:rows], value, total)
    beyond = pltpu.roll(zvalue, masks.to_halo(ylo, spot), 1)
    return jnp.where(masks.main[:rows], total, beyond)


def inside_lanes(rows, column_z):
    lane = lanes()[:rows]
    low = (column_z == 0) & (lane >= SPAN_Z) & (lane < SPAN_Z + 2)
    high = (column_z != 0) & (lane >= LANE - 2)
    return (lane < SPAN_Z) | low | high


def walled(values, mark, inside):
    factor = jnp.where(mark > 0.5, ROTOR, 1.0)
    cap = jnp.where(inside, -OUTSIDE, OUTSIDE)
    return [jnp.minimum(value * factor, cap) for value in values]


def plane_parts(own, edge, zall, zedge, chunk, yhi, plane):
    group = plane >> 3
    if chunk is None:
        first = plane * 4 * FACE + yhi
        parts = [edge[pl.ds(first + 2 * bz, 4, stride=FACE), :] for bz in range(BZD)]
        return parts, zedge[pl.ds(group * 8 + yhi, 4, stride=2), :]
    held, half = 1 + (chunk >> 1), chunk & 1
    first = held * (BZD * BLOCK) + half * EDGE + yhi
    parts = [own[pl.ds(first + bz * BLOCK + plane * TILES, 8, stride=2), :] for bz in range(BZD)]
    first = held * ZROWS + half * EDGE + yhi
    return parts, zall[pl.ds(first + group * TILES, 8, stride=2), :]


def chunk_values(own, edge, zall, zedge, chunk, yhi, ylo, masks, planes=tuple(range(PLANES))):
    out = []
    for plane in planes:
        parts, zvalue = plane_parts(own, edge, zall, zedge, chunk, yhi, plane)
        out.append(gathered(parts, zvalue, plane % 8, ylo, masks))
    return out


def halo_x_inside(layer, layers):
    row = lax.broadcasted_iota(jnp.int32, (4, LANE), 0)
    low = (row < 2) & (layer > 0)
    high = (row >= 2) & (layer < layers - 1)
    return low | high


def settle_rim(layers, places, up, down, zin, zup, zdown, own_in, own, edge, zall, zedge, rim_up, rim_down, pos, post_up, post_down, sem):
    del own_in
    layer, _, column_z = place()
    place_copy = pltpu.make_async_copy(places, pos, sem)
    place_copy.start()
    for arrived in (up, down):
        for j in range(MOVE_CAP):
            bx = arrived[pl.ds(SENT_META + 2 * j, 1), :].astype(jnp.int32)
            bz = arrived[pl.ds(SENT_META + 2 * j + 1, 1), :].astype(jnp.int32)
            code = (bx - layer * BXD) * BZD + (bz - column_z * BZD)
            mine = (bx >= layer * BXD) & (bx < (layer + 1) * BXD)
            first = layer == 0 if arrived is up else layer == layers - 1
            code = jnp.max(jnp.where(mine, code, -1))

            @pl.when((code >= 0) & jnp.logical_not(first))
            def _(arrived=arrived, j=j, code=code):
                base = pl.multiple_of((jnp.clip(code, 0, BXD * BZD - 1) + BZD) * BLOCK, 8)
                for k in range(0, BLOCK, 128):
                    values = [arrived[pl.ds(j * BLOCK + k + 8 * n, 8), :] for n in range(16)]
                    for n, value in enumerate(values):
                        own[pl.ds(base + k + 8 * n, 8), :] = value

    place_copy.wait()
    for side, arrived in enumerate((up, down)):
        inner, outer = (1, 0) if side == 0 else (2, 3)
        pairs = [(i, i, inner) for i in range(PLANES)]
        pairs += [(PLANES + n, i, outer) for n, i in enumerate((AHEAD if side == 0 else BACK) + (POPS,))]
        values = [arrived[pl.ds(SENT_SLABS + plane * FACE, FACE), :] for plane, _, _ in pairs]
        for (_, i, x), value in zip(pairs, values):
            edge[pl.ds((i * 4 + x) * FACE, FACE), :] = value
        for bz in range(BZD):
            here = jnp.int32(0)
            goal = (0 if side == 0 else LAYERS - 1) * BZD + bz
            for row in range(pos.shape[1]):
                hit = (pos[0, row] >= 0) & (slot_of(pos, row, layer, column_z) == goal)
                here = jnp.where(hit, 1, here)

            @pl.when(here == 1)
            def _(side=side, pairs=pairs, goal=goal, bz=bz):
                first = goal * BLOCK + (TILES - SLAB if side == 0 else 0)
                values = []
                for _, i, x in pairs:
                    shift = 2 * (x if side == 0 else x - 2)
                    values.append(own[pl.ds(first + i * TILES + shift, 2), :])
                for (_, i, x), value in zip(pairs, values):
                    edge[pl.ds((i * 4 + x) * FACE + 2 * bz, 2), :] = value

    moves = []
    for held in range(LAYERS):
        flag = zin[pl.ds(ZMETA + held, 1), :] > 0.5
        for group in range(ZGROUPS):
            if held == 1 or held == 2:
                for part in range(TILES // 8):
                    rows = pl.ds(held * ZROWS + group * TILES + part * 8, 8)
                    source = zup if held == 1 else zdown
                    other = source[pl.ds(group * TILES + part * 8, 8), :]
                    moves.append((zall, rows, jnp.where(flag, zin[rows, :], other)))
            else:
                side = 0 if held == 0 else 1
                source = zup if held == 0 else zdown
                first = TILES - SLAB if held == 0 else 0
                mine = zin[pl.ds(held * ZROWS + group * TILES + first, SLAB), :]
                other = source[pl.ds(ZROWS + group * SLAB, SLAB), :]
                moves.append((zedge, pl.ds(group * 8 + side * SLAB, SLAB), jnp.where(flag, mine, other)))
    for target, rows, value in moves:
        target[rows, :] = value
    masks = Lanes(column_z)
    for chunk in (0, 1, 2, 3, None):
        for y in (0, 1, SPAN_Y - 2, SPAN_Y - 1):
            target, rim = (post_down, RIM_DOWN) if y < 2 else (post_up, RIM_UP)
            near = y in (0, SPAN_Y - 1)
            planes = tuple(range(PLANES)) if near else rim + (POPS,)
            values = chunk_values(own, edge, zall, zedge, chunk, y // YLO, y % YLO, masks, planes)
            for n, value in enumerate(values):
                row = (n if near else PLANES + n) * GRID_X
                if chunk is None:
                    target[pl.ds(row, 2), :] = value[:2]
                    target[pl.ds(row + EXT_X - 2, 2), :] = value[2:]
                else:
                    target[pl.ds(row + 2 + 8 * chunk, 8), :] = value
    lane = lanes()
    for source, target in ((post_up, rim_up), (post_down, rim_down)):
        for chunk in range(5):
            size = min(8, EXT_X - 8 * chunk)
            values = []
            for plane in range(RIM):
                value = source[pl.ds(plane * GRID_X + 8 * chunk, 8), :]
                values.append(pltpu.roll(value, (plane * EXT_Z + 2 * column_z) & (LANE - 1), 1))
            totals = []
            for block in range(RIM_BLOCKS):
                total = jnp.zeros((8, LANE), jnp.float32)
                for plane in range(RIM):
                    begin = plane * EXT_Z - block * LANE
                    if begin >= LANE or begin + EXT_Z <= 0:
                        continue
                    total = jnp.where((lane >= begin) & (lane < begin + EXT_Z), values[plane], total)
                totals.append(total)
            for block in range(RIM_BLOCKS):
                target[pl.ds(block * EXT_X + 8 * chunk, size), :] = totals[block][:size]


def turned(value, step_z):
    return pltpu.roll(value, step_z % LANE, 1) if step_z else value


def drifts_of(columns, depth):
    _, _, column_z = place()
    lane = lanes()
    total_y = SPAN_Y * columns
    total_z = SPAN_Z * depth
    spin = 0.2 / (total_y + total_z)
    here_z = jnp.where(lane < SPAN_Z + 8, lane, lane - LANE) + column_z * SPAN_Z
    drift_y = -spin * (here_z.astype(jnp.float32) - (total_z - 1) / 2.0)
    return drift_y, spin, (total_y - 1) / 2.0


def first_step(columns, depth, field, later, begin, end):
    _, column_y, _ = place()
    drift_y, spin, centre_y = drifts_of(columns, depth)
    sublane = lax.broadcasted_iota(jnp.int32, (8, LANE), 0)

    def tile(n, carry):
        base = pl.multiple_of(8 * n, 8)
        line = (n - FIRST // 8 + 2 * STEP) // STEP
        next_row = (sublane >= 6) & (n - FIRST // 8 + 2 * STEP - line * STEP == STEP - 1)
        here_y = jnp.where(next_row, line + 1, line) + (column_y * SPAN_Y - 2)
        drift_z = spin * (here_y.astype(jnp.float32) - centre_y)
        old = [field[pl.ds(i * FIELD + base, 8), :] for i in range(POPS)]
        values = streamed(pull_from(field, base), old, drift_y, drift_z)
        post, _ = collide(values)
        wall = old[0] < WALL_BELOW
        for i in range(POPS):
            later[pl.ds(i * FIELD + base, 8), :] = jnp.where(wall, old[i], post[i])
        return carry

    lax.fori_loop(FIRST // 8 + begin, FIRST // 8 + end, tile, 0)


def pull_from(field, base):
    def pull(i):
        step_x, step_y, step_z = VELOCITIES[i]
        return turned(field[pl.ds(i * FIELD + base - step_y * PITCH - step_x, 8), :], step_z)

    return pull


def settle_all(layers, columns, depth, own, edge, zall, zedge, field, later):
    layer, _, column_z = place()
    masks = Lanes(column_z)
    inside_box = inside_lanes(8, column_z)
    inside_halo = inside_lanes(4, column_z) & halo_x_inside(layer, layers)

    def halves(yhi, carry):
        def chunks(chunk, carry):
            for ylo in range(YLO):
                values = chunk_values(own, edge, zall, zedge, chunk, yhi, ylo, masks)
                values = walled(values[:POPS], values[POPS], inside_box)
                row = pl.multiple_of(FIRST + (YLO * yhi + ylo) * PITCH + 8 * chunk, 8)
                for i in range(POPS):
                    field[pl.ds(i * FIELD + row, 8), :] = values[i]
            return carry

        lax.fori_loop(0, SPAN_X // 8, chunks, 0)
        for ylo in range(YLO):
            values = chunk_values(own, edge, zall, zedge, None, yhi, ylo, masks)
            values = walled(values[:POPS], values[POPS], inside_halo)
            row = FIRST + (YLO * yhi + ylo) * PITCH
            for i in range(POPS):
                field[pl.ds(i * FIELD + row - 2, 2), :] = values[i][:2]
                field[pl.ds(i * FIELD + row + SPAN_X, 2), :] = values[i][2:]
        return carry

    lax.fori_loop(0, SPAN_Y // YLO, halves, 0)
    first_step(columns, depth, field, later, STEP, (SPAN_Y - 1) * STEP)


def finish(layers, columns, depth, rim_low, rim_high, field_in, later_in, out, field, later, turn, result, sems):
    del field_in, later_in
    layer, column_y, column_z = place()
    flat = (lanes() + 2 * column_z) & (LANE - 1)
    sides = (
        (rim_low, -1, -2, RIM_UP, column_y > 0),
        (rim_high, SPAN_Y, SPAN_Y + 1, RIM_DOWN, column_y < columns - 1),
    )
    sublane = lax.broadcasted_iota(jnp.int32, (8, LANE), 0)
    for source, near, far, rim, there in sides:
        for chunk in range(5):
            size = min(8, EXT_X - 8 * chunk)
            blocks = [source[pl.ds(block * EXT_X + 8 * chunk, 8), :] for block in range(RIM_BLOCKS)]

            def plane_of(plane, blocks=blocks):
                block, begin = divmod(plane * EXT_Z, LANE)
                shift = (2 * LANE - begin - 2 * column_z) & (LANE - 1)
                value = pltpu.roll(blocks[block], shift, 1)
                if begin + EXT_Z > LANE:
                    value = jnp.where(flat < LANE - begin, value, pltpu.roll(blocks[block + 1], shift, 1))
                return value

            inside = (flat < EXT_Z) & there
            if chunk == 0:
                inside = inside & ((sublane >= 2) | (layer > 0))
            if chunk == 4:
                inside = inside & ((sublane < 2) | (layer < layers - 1))
            for first, count, y, order in ((0, POPS, near, range(POPS)), (PLANES, len(rim), far, rim)):
                mark = plane_of(POPS if y == near else RIM - 1)
                values = walled([plane_of(first + n) for n in range(count)], mark, inside)
                for i, value in zip(order, values):
                    row = i * FIELD + FIRST + y * PITCH - 2 + 8 * chunk
                    field[pl.ds(row, size), :] = value[:size]

    first_step(columns, depth, field, later, -STEP - 1, STEP)
    first_step(columns, depth, field, later, (SPAN_Y - 1) * STEP - 1, (SPAN_Y + 1) * STEP)

    drift_y, spin, centre_y = drifts_of(columns, depth)

    def leave(n):
        part = pl.ds(n * 8, 8)
        return pltpu.make_async_copy(result.at[:, part], out.at[:, part], sems.at[n])

    def second_step(chunk, carry):
        for half in range(SPAN_Y // 8):
            for k in range(8):
                y = 8 * half + k
                base = pl.multiple_of(FIRST + y * PITCH + 8 * chunk, 8)
                drift_z = spin * ((column_y * SPAN_Y + y).astype(jnp.float32) - centre_y)
                old = [later[pl.ds(i * FIELD + base, 8), :] for i in range(POPS)]
                values = streamed(pull_from(later, base), old, drift_y, drift_z)
                wall = old[0] < WALL_BELOW
                for i in range(POPS):
                    value = jnp.where(wall, old[i] * (1.0 / ROTOR), values[i])
                    turn[pl.ds(i * 8 * TURN + k * TURN, 8), :] = value
            for k in range(8):
                values = [turn[pl.ds(i * 8 * TURN + k, 8, stride=TURN), :] for i in range(POPS)]
                for i in range(POPS):
                    result[i, 8 * chunk + k, 8 * half : 8 * half + 8, :] = values[i][:, :SPAN_Z]
        leave(chunk).start()
        return carry

    lax.fori_loop(0, SPAN_X // 8, second_step, 0)
    for n in range(SPAN_X // 8):
        leave(n).wait()


def rows_of(count):
    return jax.ShapeDtypeStruct((count, LANE), jnp.float32)


def kept(count):
    return VMEM((count, LANE), jnp.float32)


def params(mib):
    return pltpu.CompilerParams(vmem_limit_bytes=mib * 2**20)


def shards(populations, solid_cells, block_pos):
    layers = lax.axis_size("stream")
    columns = lax.axis_size("cy")
    depth = lax.axis_size("cz")
    rows = block_pos.shape[0]
    vmem = pl.BlockSpec(memory_space=VMEM)
    hbm = pl.BlockSpec(memory_space=pltpu.HBM)
    populations = pltpu.with_memory_space_constraint(populations, pltpu.HBM)
    solid_cells = pltpu.with_memory_space_constraint(solid_cells, pltpu.HBM)
    places = pltpu.with_memory_space_constraint(block_pos.T, pltpu.HBM)
    place_scratch = SMEM((3, rows), jnp.int32)
    table_scratch = SMEM((LAYERS * BZD,), jnp.int32)
    mark_scratch = [VMEM((rows, EDGE**3), jnp.int32), VMEM((rows * TILES, LANE), jnp.float32)]

    up = [(i, i + 1) for i in range(layers - 1)]
    down = [(i + 1, i) for i in range(layers - 1)]
    send_up, send_down = pl.pallas_call(
        pack_stream,
        out_shape=(kept(SENT_ROWS), kept(SENT_ROWS)),
        in_specs=[hbm, hbm, hbm],
        out_specs=(vmem, vmem),
        scratch_shapes=[place_scratch, table_scratch]
        + mark_scratch
        + [
            VMEM((2 * MOVE_CAP, POPS, EDGE**3), jnp.float32),
            VMEM((2 * BZD, POPS, SLAB * LANE), jnp.float32),
            VMEM((PLANES * 2 * FACE, LANE), jnp.float32),
            pltpu.SemaphoreType.DMA((2 + 2 * MOVE_CAP + 2 * BZD,)),
        ],
        compiler_params=params(16),
        name="pack_stream",
    )(places, solid_cells, populations)
    from_low = lax.ppermute(send_up, "stream", up)
    from_high = lax.ppermute(send_down, "stream", down)

    own, zpack, zsend_up, zsend_down = pl.pallas_call(
        pack_edge,
        out_shape=(kept(LAYERS * BZD * BLOCK), kept(ZMETA + 8), kept(DIAG), kept(DIAG)),
        in_specs=[hbm, hbm, hbm],
        out_specs=(vmem,) * 4,
        scratch_shapes=[place_scratch, table_scratch]
        + mark_scratch
        + [
            VMEM((LAYERS, POPS, EDGE**3), jnp.float32),
            pltpu.SemaphoreType.DMA((LAYERS + 2,)),
        ],
        compiler_params=params(16),
        name="pack_edge",
    )(places, solid_cells, populations)
    swap = [(i, depth - 1 - i) for i in range(depth)]
    zin = lax.ppermute(zpack, "cz", swap)
    zup_pairs = [(s * depth + c, t * depth + d) for s, t in up for c, d in swap]
    zdown_pairs = [(s * depth + c, t * depth + d) for s, t in down for c, d in swap]
    z_low = lax.ppermute(zsend_up, ("stream", "cz"), zup_pairs)
    z_high = lax.ppermute(zsend_down, ("stream", "cz"), zdown_pairs)

    own = pl.pallas_call(
        pack_own,
        out_shape=kept(LAYERS * BZD * BLOCK),
        in_specs=[hbm, hbm, hbm, vmem],
        out_specs=vmem,
        scratch_shapes=[place_scratch]
        + mark_scratch
        + [
            VMEM((rows, POPS, EDGE**3), jnp.float32),
            pltpu.SemaphoreType.DMA((rows + 2,)),
        ],
        input_output_aliases={3: 0},
        compiler_params=params(16),
        name="pack_own",
    )(places, solid_cells, populations, own)

    own, edge, zall, zedge, rim_up, rim_down = pl.pallas_call(
        functools.partial(settle_rim, layers),
        out_shape=(
            kept(LAYERS * BZD * BLOCK),
            kept(PLANES * 4 * FACE),
            kept(LAYERS * ZROWS),
            kept(ZGROUPS * 8),
            kept(RIM_ROWS),
            kept(RIM_ROWS),
        ),
        in_specs=[hbm] + [vmem] * 6,
        out_specs=(vmem,) * 6,
        scratch_shapes=[
            place_scratch,
            VMEM((RIM * GRID_X, LANE), jnp.float32),
            VMEM((RIM * GRID_X, LANE), jnp.float32),
            pltpu.SemaphoreType.DMA,
        ],
        input_output_aliases={6: 0},
        compiler_params=params(16),
        name="settle_rim",
    )(places, from_low, from_high, zin, z_low, z_high, own)
    cy_up = [(i, i + 1) for i in range(columns - 1)]
    cy_down = [(i + 1, i) for i in range(columns - 1)]
    rim_low = lax.ppermute(rim_up, "cy", cy_up)
    rim_high = lax.ppermute(rim_down, "cy", cy_down)

    field, later = pl.pallas_call(
        functools.partial(settle_all, layers, columns, depth),
        out_shape=(kept(POPS * FIELD), kept(POPS * FIELD)),
        in_specs=[vmem] * 4,
        out_specs=(vmem,) * 2,
        compiler_params=params(16),
        name="settle_all",
    )(own, edge, zall, zedge)

    out, _, _ = pl.pallas_call(
        functools.partial(finish, layers, columns, depth),
        out_shape=(
            jax.ShapeDtypeStruct((POPS, SPAN_X, SPAN_Y, SPAN_Z), jnp.float32),
            kept(POPS * FIELD),
            kept(POPS * FIELD),
        ),
        in_specs=[vmem] * 4,
        out_specs=(hbm, vmem, vmem),
        scratch_shapes=[
            VMEM((POPS * 8 * TURN, LANE), jnp.float32),
            VMEM((POPS, SPAN_X, SPAN_Y, SPAN_Z), jnp.float32),
            pltpu.SemaphoreType.DMA((SPAN_X // 8,)),
        ],
        input_output_aliases={2: 1, 3: 2},
        compiler_params=params(16),
        name="finish",
    )(rim_low, rim_high, field, later)
    return out


def solution(mesh):
    in_specs = (
        P(("stream", "cy", "cz"), None, None),
        P(("stream", "cy", "cz"), None),
        P(("stream", "cy", "cz"), None),
    )
    out_specs = P(None, "stream", "cy", "cz")
    return jax.shard_map(shards, mesh=mesh, in_specs=in_specs, out_specs=out_specs, check_vma=False)
```

```python
import functools

import jax
import jax.numpy as jnp
from jax import lax
from jax.experimental import pallas as pl
from jax.experimental.pallas import tpu as pltpu
from jax.sharding import PartitionSpec as P

EDGE = 16
BXD = 2
BYD = 1
BZD = 4
MOVE_CAP = 2

VELOCITIES = (
    (0, 0, 0),
    (1, 0, 0),
    (-1, 0, 0),
    (0, 1, 0),
    (0, -1, 0),
    (0, 0, 1),
    (0, 0, -1),
    (1, 1, 0),
    (-1, -1, 0),
    (1, -1, 0),
    (-1, 1, 0),
    (1, 0, 1),
    (-1, 0, -1),
    (1, 0, -1),
    (-1, 0, 1),
    (0, 1, 1),
    (0, -1, -1),
    (0, 1, -1),
    (0, -1, 1),
)
WEIGHTS = (1.0 / 3.0,) + (1.0 / 18.0,) * 6 + (1.0 / 36.0,) * 12
OPPOSITE = (0, 2, 1, 4, 3, 6, 5, 8, 7, 10, 9, 12, 11, 14, 13, 16, 15, 18, 17)
OMEGA_EVEN = 1.25
OMEGA_ODD = 1.0 / 1.125

POPS = 19
PLANES = 20
LANE = 128
TILES = EDGE**3 // LANE
BLOCK = PLANES * TILES
YLO = LANE // EDGE
SLAB = 4
GROUPS = ((0, 8), (8, 8), (16, 3))
SENT_SLABS = MOVE_CAP * BLOCK
LAYERS = BXD + 2
ZGROUPS = 3
ZROWS = ZGROUPS * TILES
ZMETA = LAYERS * ZROWS
DIAG = ZROWS + ZGROUPS * SLAB

SPAN_X = BXD * EDGE
SPAN_Y = BYD * EDGE
SPAN_Z = BZD * EDGE
PITCH = SPAN_X + 8
STEP = PITCH // 8
FIRST = 96
FIELD = FIRST + (SPAN_Y + 1) * PITCH + 48
TURN = 9
EXT_X = SPAN_X + 4
EXT_Z = SPAN_Z + 2
RIM_UP = tuple(i for i in range(POPS) if VELOCITIES[i][1] == 1)
RIM_DOWN = tuple(i for i in range(POPS) if VELOCITIES[i][1] == -1)
RIM = PLANES + len(RIM_UP) + 1
AHEAD = tuple(i for i in range(POPS) if VELOCITIES[i][0] == 1)
BACK = tuple(i for i in range(POPS) if VELOCITIES[i][0] == -1)
FACE = 2 * BZD
SENT_META = SENT_SLABS + RIM * FACE
SENT_ROWS = SENT_META + 8
RIM_BLOCKS = -(-RIM * EXT_Z // LANE)
RIM_ROWS = RIM_BLOCKS * EXT_X + 4
GRID_X = 48

ROTOR = -(2.0**100)
OUTSIDE = -(2.0**110)
WALL_BELOW = -(2.0**80)
OUT_BELOW = -(2.0**105)

VMEM = pltpu.VMEM
SMEM = pltpu.SMEM


def lanes():
    return lax.broadcasted_iota(jnp.int32, (8, LANE), 1)


def collide(f):
    even = [None] * POPS
    odd = [None] * POPS
    for i in range(1, POPS, 2):
        even[i] = f[i] + f[i + 1]
        odd[i] = f[i] - f[i + 1]
    density = f[0]
    for i in range(1, POPS, 2):
        density = density + even[i]
    flow = []
    for axis in range(3):
        total = None
        for i in range(1, POPS, 2):
            sign = VELOCITIES[i][axis]
            if sign == 0:
                continue
            if total is None:
                total = odd[i] if sign == 1 else -odd[i]
            else:
                total = total + odd[i] if sign == 1 else total - odd[i]
        flow.append(total)
    inverse = 1.0 / density
    velocity = [part * inverse for part in flow]
    square = velocity[0] * velocity[0] + velocity[1] * velocity[1] + velocity[2] * velocity[2]
    base = density * (1.0 - 1.5 * square)
    post = [None] * POPS
    post[0] = (1.0 - OMEGA_EVEN) * f[0] + (OMEGA_EVEN * WEIGHTS[0]) * base
    shared = {}
    for weight in (WEIGHTS[1], WEIGHTS[7]):
        shared[weight] = ((OMEGA_EVEN * weight) * base, (OMEGA_EVEN * weight * 4.5) * density,
                          (OMEGA_ODD * weight * 3.0) * density)
    for i in range(1, POPS, 2):
        projected = None
        for axis in range(3):
            sign = VELOCITIES[i][axis]
            if sign == 0:
                continue
            if projected is None:
                projected = velocity[axis] if sign == 1 else -velocity[axis]
            else:
                projected = projected + velocity[axis] if sign == 1 else projected - velocity[axis]
        low, curve, slope = shared[WEIGHTS[i]]
        even_part = (0.5 - 0.5 * OMEGA_EVEN) * even[i] + (low + curve * (projected * projected))
        odd_part = (0.5 - 0.5 * OMEGA_ODD) * odd[i] + slope * projected
        post[i] = even_part + odd_part
        post[i + 1] = even_part - odd_part
    return post, density


def pushes(density, drift_y, drift_z):
    along_y = density * drift_y
    along_z = density * drift_z
    out = [None] * POPS
    for i in range(1, POPS):
        _, step_y, step_z = VELOCITIES[i]
        total = None
        for sign, part in ((step_y, along_y), (step_z, along_z)):
            if sign == 0:
                continue
            if total is None:
                total = part if sign == 1 else -part
            else:
                total = total + part if sign == 1 else total - part
        if total is not None:
            out[i] = (6.0 * WEIGHTS[i]) * total
    return out


def total_of(parts):
    parts = list(parts)
    while len(parts) > 1:
        pairs = [parts[n] + parts[n + 1] for n in range(0, len(parts) - 1, 2)]
        parts = pairs + parts[len(parts) - len(parts) % 2 :]
    return parts[0]


def streamed(pull, own, drift_y, drift_z):
    push = pushes(total_of(own), drift_y, drift_z)
    out = [own[0]]
    for i in range(1, POPS):
        pulled = pull(i)
        bounced = own[OPPOSITE[i]]
        blocked = pulled < WALL_BELOW
        if push[i] is not None:
            bounced = jnp.where(pulled < OUT_BELOW, bounced, bounced + push[i])
        out.append(jnp.where(blocked, bounced, pulled))
    return out


def ahead(items, take, leave, depth):
    waiting = []
    for n in items:
        waiting.append((n, take(n)))
        if len(waiting) > depth:
            leave(*waiting.pop(0))
    for pair in waiting:
        leave(*pair)


def place():
    return lax.axis_index("stream"), lax.axis_index("cy"), lax.axis_index("cz")


def slot_of(pos, row, layer, column_z):
    slot = (pos[0, row] - (layer * BXD - 1)) * BZD + (pos[2, row] - column_z * BZD)
    return jnp.clip(slot, 0, LAYERS * BZD - 1)


def fill_table(pos, table):
    layer, _, column_z = place()
    for entry in range(LAYERS * BZD):
        table[entry] = -1
    for row in range(pos.shape[1]):

        @pl.when(pos[0, row] >= 0)
        def _(row=row):
            table[slot_of(pos, row, layer, column_z)] = row


def spread_marks(marks, dense):
    rows = marks.shape[0]
    for first in range(0, rows, 8):
        size = min(8, rows - first)
        for begin in range(0, TILES, 8):
            values = [marks[first : first + size, t * LANE : (t + 1) * LANE] for t in range(begin, begin + 8)]
            for k, value in enumerate(values):
                dense[pl.ds(first * TILES + begin + k, size, stride=TILES), :] = value.astype(jnp.float32)


def collide_block(ref, base):
    for first in range(0, TILES // 8, 2):
        moves = []
        for part in (first, first + 1):
            old = [ref[pl.ds(base + i * TILES + 8 * part, 8), :] for i in range(POPS)]
            mark = ref[pl.ds(base + POPS * TILES + 8 * part, 8), :] > 0.5
            post, _ = collide(old)
            for i in range(POPS):
                moves.append((base + i * TILES + 8 * part, jnp.where(mark, old[i], post[i])))
        for row, value in moves:
            ref[pl.ds(row, 8), :] = value


def pack_block(out, base, stage, dense, row):
    out[pl.ds(base + POPS * TILES, TILES), :] = dense[pl.ds(pl.multiple_of(row * TILES, 8), TILES), :]
    for first in range(0, TILES, 4):
        moves = []
        for tile in range(first, first + 4):
            for group, size in GROUPS:
                value = stage[group : group + size, tile * LANE : (tile + 1) * LANE]
                moves.append((pl.ds(base + group * TILES + tile, size, stride=TILES), value))
        for target, value in moves:
            out[target, :] = value
    collide_block(out, base)


def pack_stream(places, marks_in, pops, up, down, pos, table, marks, dense, blocks, slabs, strip, sems):
    mark_copy = pltpu.make_async_copy(marks_in, marks, sems.at[0])
    mark_copy.start()
    place_copy = pltpu.make_async_copy(places, pos, sems.at[1])
    place_copy.start()
    rows = pos.shape[1]
    copies = [None] * 4
    for j in range(MOVE_CAP):
        copies[MOVE_CAP + j] = pltpu.make_async_copy(pops.at[j], blocks.at[MOVE_CAP + j], sems.at[2 + MOVE_CAP + j])
        copies[MOVE_CAP + j].start()
    place_copy.wait()
    count = 0
    for row in range(rows):
        count = count + jnp.where(pos[0, row] >= 0, 1, 0)
    last = jnp.clip(count - MOVE_CAP, 0, rows - MOVE_CAP)
    for j in range(MOVE_CAP):
        copies[j] = pltpu.make_async_copy(pops.at[last + j], blocks.at[j], sems.at[2 + j])
        copies[j].start()
    fill_table(pos, table)
    slab_rows = []
    slab_copies = []
    for side in range(2):
        for bz in range(BZD):
            row = jnp.maximum(table[(2 - side) * BZD + bz], 0)
            n = side * BZD + bz
            first = (TILES - SLAB) * LANE if side == 0 else 0
            slab_rows.append(row)
            slab_copies.append(
                pltpu.make_async_copy(
                    pops.at[row, :, pl.ds(first, SLAB * LANE)], slabs.at[n], sems.at[2 + 2 * MOVE_CAP + n]
                )
            )
            slab_copies[n].start()
    mark_copy.wait()
    spread_marks(marks, dense)
    for side, out in ((1, down), (0, up)):
        for j in range(MOVE_CAP):
            row = j if side == 1 else last + j
            for k, axis in ((0, 0), (1, 2)):
                value = jnp.full((1, LANE), pos[axis, row], jnp.int32).astype(jnp.float32)
                out[pl.ds(SENT_META + 2 * j + k, 1), :] = value
            n = side * MOVE_CAP + j
            copies[n].wait()
            pack_block(out, j * BLOCK, blocks.at[n], dense, row)
    for side, out in enumerate((up, down)):
        for bz in range(BZD):
            n = side * BZD + bz
            first = slab_rows[n] * TILES + (TILES - SLAB if side == 0 else 0)
            slab_copies[n].wait()
            moves = []
            for x in range(2):
                for yhi in range(2):
                    q = 2 * x + yhi
                    row = x * FACE + 2 * bz + yhi
                    for group, size in GROUPS:
                        value = slabs[n, group : group + size, q * LANE : (q + 1) * LANE]
                        moves.append((pl.ds(group * 2 * FACE + row, size, stride=2 * FACE), value))
                row = POPS * 2 * FACE + x * FACE + 2 * bz
                moves.append((pl.ds(row, 2), dense[pl.ds(first + 2 * x, 2), :]))
            for target, value in moves:
                strip[target, :] = value
        inner = 1 if side == 0 else 0
        for x in range(2):
            old = [strip[pl.ds(i * 2 * FACE + x * FACE, FACE), :] for i in range(POPS)]
            mark = strip[pl.ds(POPS * 2 * FACE + x * FACE, FACE), :] > 0.5
            post, _ = collide(old)
            if x == inner:
                pairs = [(i, i) for i in range(POPS)]
                marks_at = POPS
            else:
                pairs = [(PLANES + n, i) for n, i in enumerate(AHEAD if side == 0 else BACK)]
                marks_at = RIM - 1
            for plane, i in pairs:
                out[pl.ds(SENT_SLABS + plane * FACE, FACE), :] = jnp.where(mark, old[i], post[i])
            marks_of = strip[pl.ds(POPS * 2 * FACE + x * FACE, FACE), :]
            out[pl.ds(SENT_SLABS + marks_at * FACE, FACE), :] = marks_of


def pack_edge(places, marks_in, pops, own, zpack, zup, zdown, pos, table, marks, dense, stage, sems):
    column_z = lax.axis_index("cz")
    mark_copy = pltpu.make_async_copy(marks_in, marks, sems.at[LAYERS])
    mark_copy.start()
    place_copy = pltpu.make_async_copy(places, pos, sems.at[LAYERS + 1])
    place_copy.start()
    place_copy.wait()
    fill_table(pos, table)
    edge_bz = jnp.where(column_z == 0, BZD - 1, 0)
    first_c = jnp.where(column_z == 0, EDGE - 2, 0)
    found = [table[held * BZD + edge_bz] for held in range(LAYERS)]
    row_of = [jnp.maximum(row, 0) for row in found]
    copies = []
    for held in range(LAYERS):
        copies.append(pltpu.make_async_copy(pops.at[row_of[held]], stage.at[held], sems.at[held]))
        copies[held].start()
    mark_copy.wait()
    spread_marks(marks, dense)
    spot = (lanes() & (EDGE - 1)) >> 1
    sublane = lax.broadcasted_iota(jnp.int32, (8, LANE), 0)
    flags = jnp.zeros((8, LANE), jnp.int32)
    for held in range(LAYERS):
        copies[held].wait()
        base = pl.multiple_of((held * BZD + edge_bz) * BLOCK, 8)

        @pl.when(found[held] >= 0)
        def _(held=held, base=base):
            pack_block(own, base, stage.at[held], dense, row_of[held])
            totals = []
            for group in range(ZGROUPS):
                for part in range(TILES // 8):
                    total = jnp.zeros((8, LANE), jnp.float32)
                    for k in range(min(8, PLANES - group * 8)):
                        value = own[pl.ds(base + (group * 8 + k) * TILES + part * 8, 8), :]
                        value = pltpu.roll(value, (2 * k - first_c + LANE) & (LANE - 1), 1)
                        total = jnp.where(spot == k, value, total)
                    totals.append((held * ZROWS + group * TILES + part * 8, total))
            for row, total in totals:
                zpack[pl.ds(row, 8), :] = total

        flags = jnp.where((sublane == held) & (found[held] >= 0), 1, flags)
    zpack[pl.ds(ZMETA, 8), :] = flags.astype(jnp.float32)
    zup[pl.ds(0, ZROWS), :] = zpack[pl.ds(3 * ZROWS, ZROWS), :]
    zdown[pl.ds(0, ZROWS), :] = zpack[pl.ds(0, ZROWS), :]
    for group in range(ZGROUPS):
        target = pl.ds(ZROWS + group * SLAB, SLAB)
        zup[target, :] = zpack[pl.ds(2 * ZROWS + group * TILES + TILES - SLAB, SLAB), :]
        zdown[target, :] = zpack[pl.ds(ZROWS + group * TILES, SLAB), :]


def pack_own(places, marks_in, pops, own_in, own, pos, marks, dense, stage, sems):
    del own_in
    layer, _, column_z = place()
    edge_bz = jnp.where(column_z == 0, BZD - 1, 0)
    rows = pos.shape[1]
    mark_copy = pltpu.make_async_copy(marks_in, marks, sems.at[rows])
    mark_copy.start()
    place_copy = pltpu.make_async_copy(places, pos, sems.at[rows + 1])
    place_copy.start()
    copies = [pltpu.make_async_copy(pops.at[r], stage.at[r], sems.at[r]) for r in range(rows)]
    for copy in copies:
        copy.start()
    mark_copy.wait()
    spread_marks(marks, dense)
    place_copy.wait()

    def settle(row, carry):
        pltpu.make_async_copy(pops.at[row], stage.at[row], sems.at[row]).wait()
        slot = slot_of(pos, row, layer, column_z)

        @pl.when((pos[0, row] >= 0) & (slot % BZD != edge_bz))
        def _():
            pack_block(own, pl.multiple_of(slot * BLOCK, 8), stage.at[row], dense, row)

        return carry

    lax.fori_loop(0, rows, settle, 0)


class Lanes:
    def __init__(self, column_z):
        lane = lanes()
        self.from_bz = [lane >= bz * EDGE for bz in range(BZD)]
        self.main = lane < SPAN_Z
        self.goal = jnp.where(column_z == 0, SPAN_Z, LANE - 2)

    def to_halo(self, ylo, spot):
        return (self.goal - (ylo * EDGE + 2 * spot) + LANE) & (LANE - 1)


def gathered(parts, zvalue, spot, ylo, masks):
    rows = parts[0].shape[0]
    total = None
    for bz in range(BZD):
        shift = (bz * EDGE - ylo * EDGE) % LANE
        value = pltpu.roll(parts[bz], shift, 1) if shift else parts[bz]
        total = value if total is None else jnp.where(masks.from_bz[bz][:rows], value, total)
    beyond = pltpu.roll(zvalue, masks.to_halo(ylo, spot), 1)
    return jnp.where(masks.main[:rows], total, beyond)


def inside_lanes(rows, column_z):
    lane = lanes()[:rows]
    low = (column_z == 0) & (lane >= SPAN_Z) & (lane < SPAN_Z + 2)
    high = (column_z != 0) & (lane >= LANE - 2)
    return (lane < SPAN_Z) | low | high


def walled(values, mark, inside):
    factor = jnp.where(mark > 0.5, ROTOR, 1.0)
    cap = jnp.where(inside, -OUTSIDE, OUTSIDE)
    return [jnp.minimum(value * factor, cap) for value in values]


def plane_parts(own, edge, zall, zedge, chunk, yhi, plane):
    group = plane >> 3
    if chunk is None:
        first = plane * 4 * FACE + yhi
        parts = [edge[pl.ds(first + 2 * bz, 4, stride=FACE), :] for bz in range(BZD)]
        return parts, zedge[pl.ds(group * 8 + yhi, 4, stride=2), :]
    held, half = 1 + (chunk >> 1), chunk & 1
    first = held * (BZD * BLOCK) + half * EDGE + yhi
    parts = [own[pl.ds(first + bz * BLOCK + plane * TILES, 8, stride=2), :] for bz in range(BZD)]
    first = held * ZROWS + half * EDGE + yhi
    return parts, zall[pl.ds(first + group * TILES, 8, stride=2), :]


def chunk_values(own, edge, zall, zedge, chunk, yhi, rows, masks):
    out = [[] for _ in rows]
    for plane in range(PLANES):
        taken = [n for n, (_, planes) in enumerate(rows) if plane in planes]
        if taken:
            parts, zvalue = plane_parts(own, edge, zall, zedge, chunk, yhi, plane)
        for n in taken:
            out[n].append(gathered(parts, zvalue, plane % 8, rows[n][0], masks))
    return out


def halo_x_inside(layer, layers):
    row = lax.broadcasted_iota(jnp.int32, (4, LANE), 0)
    low = (row < 2) & (layer > 0)
    high = (row >= 2) & (layer < layers - 1)
    return low | high


def settle_rim(layers, places, up, down, zin, zup, zdown, own_in, own, edge, zall, zedge, rim_up, rim_down, pos, post_up, post_down, sem):
    del own_in
    layer, _, column_z = place()
    place_copy = pltpu.make_async_copy(places, pos, sem)
    place_copy.start()
    for arrived in (up, down):
        for j in range(MOVE_CAP):
            bx = arrived[pl.ds(SENT_META + 2 * j, 1), :].astype(jnp.int32)
            bz = arrived[pl.ds(SENT_META + 2 * j + 1, 1), :].astype(jnp.int32)
            code = (bx - layer * BXD) * BZD + (bz - column_z * BZD)
            mine = (bx >= layer * BXD) & (bx < (layer + 1) * BXD)
            first = layer == 0 if arrived is up else layer == layers - 1
            code = jnp.max(jnp.where(mine, code, -1))

            @pl.when((code >= 0) & jnp.logical_not(first))
            def _(arrived=arrived, j=j, code=code):
                base = pl.multiple_of((jnp.clip(code, 0, BXD * BZD - 1) + BZD) * BLOCK, 8)
                for k in range(0, BLOCK, 128):
                    values = [arrived[pl.ds(j * BLOCK + k + 8 * n, 8), :] for n in range(16)]
                    for n, value in enumerate(values):
                        own[pl.ds(base + k + 8 * n, 8), :] = value

    place_copy.wait()
    for side, arrived in enumerate((up, down)):
        inner, outer = (1, 0) if side == 0 else (2, 3)
        pairs = [(i, i, inner) for i in range(PLANES)]
        pairs += [(PLANES + n, i, outer) for n, i in enumerate((AHEAD if side == 0 else BACK) + (POPS,))]
        values = [arrived[pl.ds(SENT_SLABS + plane * FACE, FACE), :] for plane, _, _ in pairs]
        for (_, i, x), value in zip(pairs, values):
            edge[pl.ds((i * 4 + x) * FACE, FACE), :] = value
        for bz in range(BZD):
            here = jnp.int32(0)
            goal = (0 if side == 0 else LAYERS - 1) * BZD + bz
            for row in range(pos.shape[1]):
                hit = (pos[0, row] >= 0) & (slot_of(pos, row, layer, column_z) == goal)
                here = jnp.where(hit, 1, here)

            @pl.when(here == 1)
            def _(side=side, pairs=pairs, goal=goal, bz=bz):
                first = goal * BLOCK + (TILES - SLAB if side == 0 else 0)
                values = []
                for _, i, x in pairs:
                    shift = 2 * (x if side == 0 else x - 2)
                    values.append(own[pl.ds(first + i * TILES + shift, 2), :])
                for (_, i, x), value in zip(pairs, values):
                    edge[pl.ds((i * 4 + x) * FACE + 2 * bz, 2), :] = value

    moves = []
    for held in range(LAYERS):
        flag = zin[pl.ds(ZMETA + held, 1), :] > 0.5
        for group in range(ZGROUPS):
            if held == 1 or held == 2:
                for part in range(TILES // 8):
                    rows = pl.ds(held * ZROWS + group * TILES + part * 8, 8)
                    source = zup if held == 1 else zdown
                    other = source[pl.ds(group * TILES + part * 8, 8), :]
                    moves.append((zall, rows, jnp.where(flag, zin[rows, :], other)))
            else:
                side = 0 if held == 0 else 1
                source = zup if held == 0 else zdown
                first = TILES - SLAB if held == 0 else 0
                mine = zin[pl.ds(held * ZROWS + group * TILES + first, SLAB), :]
                other = source[pl.ds(ZROWS + group * SLAB, SLAB), :]
                moves.append((zedge, pl.ds(group * 8 + side * SLAB, SLAB), jnp.where(flag, mine, other)))
    for target, rows, value in moves:
        target[rows, :] = value
    masks = Lanes(column_z)
    for chunk in (0, 1, 2, 3, None):
        for near, far, rim, target in ((0, 1, RIM_DOWN, post_down), (SPAN_Y - 1, SPAN_Y - 2, RIM_UP, post_up)):
            rows = ((near % YLO, range(PLANES)), (far % YLO, rim + (POPS,)))
            first, second = chunk_values(own, edge, zall, zedge, chunk, near // YLO, rows, masks)
            for plane, value in enumerate(first + second):
                row = plane * GRID_X
                if chunk is None:
                    target[pl.ds(row, 2), :] = value[:2]
                    target[pl.ds(row + EXT_X - 2, 2), :] = value[2:]
                else:
                    target[pl.ds(row + 2 + 8 * chunk, 8), :] = value
    lane = lanes()
    for source, target in ((post_up, rim_up), (post_down, rim_down)):
        for chunk in range(5):
            size = min(8, EXT_X - 8 * chunk)
            values = []
            for plane in range(RIM):
                value = source[pl.ds(plane * GRID_X + 8 * chunk, 8), :]
                values.append(pltpu.roll(value, (plane * EXT_Z + 2 * column_z) & (LANE - 1), 1))
            totals = []
            for block in range(RIM_BLOCKS):
                total = jnp.zeros((8, LANE), jnp.float32)
                for plane in range(RIM):
                    begin = plane * EXT_Z - block * LANE
                    if begin >= LANE or begin + EXT_Z <= 0:
                        continue
                    total = jnp.where((lane >= begin) & (lane < begin + EXT_Z), values[plane], total)
                totals.append(total)
            for block in range(RIM_BLOCKS):
                target[pl.ds(block * EXT_X + 8 * chunk, size), :] = totals[block][:size]


def turned(value, step_z):
    return pltpu.roll(value, step_z % LANE, 1) if step_z else value


def drifts_of(columns, depth):
    _, _, column_z = place()
    lane = lanes()
    total_y = SPAN_Y * columns
    total_z = SPAN_Z * depth
    spin = 0.2 / (total_y + total_z)
    here_z = jnp.where(lane < SPAN_Z + 8, lane, lane - LANE) + column_z * SPAN_Z
    drift_y = -spin * (here_z.astype(jnp.float32) - (total_z - 1) / 2.0)
    return drift_y, spin, (total_y - 1) / 2.0


def first_step(columns, depth, field, later, begin, end, last):
    _, column_y, _ = place()
    drift_y, spin, centre_y = drifts_of(columns, depth)
    sublane = lax.broadcasted_iota(jnp.int32, (8, LANE), 0)

    def tile(base, drift_z):
        old = [field[pl.ds(i * FIELD + base, 8), :] for i in range(POPS)]
        values = streamed(pull_from(field, base), old, drift_y, drift_z)
        post, _ = collide(values)
        wall = old[0] < WALL_BELOW
        for i in range(POPS):
            later[pl.ds(i * FIELD + base, 8), :] = jnp.where(wall, old[i], post[i])

    def drift_at(y):
        return spin * ((y + column_y * SPAN_Y).astype(jnp.float32) - centre_y)

    def between(y):
        return jnp.where(sublane < 6, drift_at(y - 1), drift_at(y))

    def row(line, carry):
        y = line - 2
        base = pl.multiple_of(line * PITCH + (FIRST - 2 * PITCH), 8)
        tile(base - 8, between(y))
        for xc in range(STEP - 1):
            tile(base + 8 * xc, drift_at(y))
        return carry

    lax.fori_loop(begin + 2, end + 2, row, 0)
    if last:
        tile(FIRST + end * PITCH - 8, between(jnp.int32(end)))


def pull_from(field, base):
    def pull(i):
        step_x, step_y, step_z = VELOCITIES[i]
        return turned(field[pl.ds(i * FIELD + base - step_y * PITCH - step_x, 8), :], step_z)

    return pull


def settle_all(layers, columns, depth, own, edge, zall, zedge, field, later):
    layer, _, column_z = place()
    masks = Lanes(column_z)
    inside_box = inside_lanes(8, column_z)
    inside_halo = inside_lanes(4, column_z) & halo_x_inside(layer, layers)

    def halves(yhi, carry):
        def chunks(chunk, carry):
            for ylo in range(0, YLO, 2):
                rows = [(ylo + n, range(PLANES)) for n in range(2)]
                pair = chunk_values(own, edge, zall, zedge, chunk, yhi, rows, masks)
                pair = [walled(values[:POPS], values[POPS], inside_box) for values in pair]
                for n, values in enumerate(pair):
                    row = pl.multiple_of(FIRST + (YLO * yhi + ylo + n) * PITCH + 8 * chunk, 8)
                    for i in range(POPS):
                        field[pl.ds(i * FIELD + row, 8), :] = values[i]
            return carry

        lax.fori_loop(0, SPAN_X // 8, chunks, 0)
        for ylo in range(0, YLO, 2):
            rows = [(ylo + n, range(PLANES)) for n in range(2)]
            pair = chunk_values(own, edge, zall, zedge, None, yhi, rows, masks)
            pair = [walled(values[:POPS], values[POPS], inside_halo) for values in pair]
            for n, values in enumerate(pair):
                row = FIRST + (YLO * yhi + ylo + n) * PITCH
                for i in range(POPS):
                    field[pl.ds(i * FIELD + row - 2, 2), :] = values[i][:2]
                    field[pl.ds(i * FIELD + row + SPAN_X, 2), :] = values[i][2:]
        return carry

    lax.fori_loop(0, SPAN_Y // YLO, halves, 0)
    first_step(columns, depth, field, later, 1, SPAN_Y - 1, False)


def finish(layers, columns, depth, rim_low, rim_high, field_in, later_in, out, field, later, turn, result, sems):
    del field_in, later_in
    layer, column_y, column_z = place()
    flat = (lanes() + 2 * column_z) & (LANE - 1)
    sides = (
        (rim_low, -1, -2, RIM_UP, column_y > 0),
        (rim_high, SPAN_Y, SPAN_Y + 1, RIM_DOWN, column_y < columns - 1),
    )
    sublane = lax.broadcasted_iota(jnp.int32, (8, LANE), 0)
    for source, near, far, rim, there in sides:
        for chunk in range(5):
            size = min(8, EXT_X - 8 * chunk)
            blocks = [source[pl.ds(block * EXT_X + 8 * chunk, 8), :] for block in range(RIM_BLOCKS)]

            def plane_of(plane, blocks=blocks):
                block, begin = divmod(plane * EXT_Z, LANE)
                shift = (2 * LANE - begin - 2 * column_z) & (LANE - 1)
                value = pltpu.roll(blocks[block], shift, 1)
                if begin + EXT_Z > LANE:
                    value = jnp.where(flat < LANE - begin, value, pltpu.roll(blocks[block + 1], shift, 1))
                return value

            inside = (flat < EXT_Z) & there
            if chunk == 0:
                inside = inside & ((sublane >= 2) | (layer > 0))
            if chunk == 4:
                inside = inside & ((sublane < 2) | (layer < layers - 1))
            for first, count, y, order in ((0, POPS, near, range(POPS)), (PLANES, len(rim), far, rim)):
                mark = plane_of(POPS if y == near else RIM - 1)
                values = walled([plane_of(first + n) for n in range(count)], mark, inside)
                for i, value in zip(order, values):
                    row = i * FIELD + FIRST + y * PITCH - 2 + 8 * chunk
                    field[pl.ds(row, size), :] = value[:size]

    first_step(columns, depth, field, later, -1, 1, True)
    first_step(columns, depth, field, later, SPAN_Y - 1, SPAN_Y + 1, True)

    drift_y, spin, centre_y = drifts_of(columns, depth)

    def leave(n):
        part = pl.ds(n * 8, 8)
        return pltpu.make_async_copy(result.at[:, part], out.at[:, part], sems.at[n])

    def second_step(chunk, carry):
        for half in range(SPAN_Y // 8):
            for k in range(8):
                y = 8 * half + k
                base = pl.multiple_of(FIRST + y * PITCH + 8 * chunk, 8)
                drift_z = spin * ((column_y * SPAN_Y + y).astype(jnp.float32) - centre_y)
                old = [later[pl.ds(i * FIELD + base, 8), :] for i in range(POPS)]
                values = streamed(pull_from(later, base), old, drift_y, drift_z)
                wall = old[0] < WALL_BELOW
                for i in range(POPS):
                    value = jnp.where(wall, old[i] * (1.0 / ROTOR), values[i])
                    turn[pl.ds(i * 8 * TURN + k * TURN, 8), :] = value
            for k in range(8):
                values = [turn[pl.ds(i * 8 * TURN + k, 8, stride=TURN), :] for i in range(POPS)]
                for i in range(POPS):
                    result[i, 8 * chunk + k, 8 * half : 8 * half + 8, :] = values[i][:, :SPAN_Z]
        leave(chunk).start()
        return carry

    lax.fori_loop(0, SPAN_X // 8, second_step, 0)
    for n in range(SPAN_X // 8):
        leave(n).wait()


def rows_of(count):
    return jax.ShapeDtypeStruct((count, LANE), jnp.float32)


def kept(count):
    return VMEM((count, LANE), jnp.float32)


def params(mib):
    return pltpu.CompilerParams(vmem_limit_bytes=mib * 2**20)


def shards(populations, solid_cells, block_pos):
    layers = lax.axis_size("stream")
    columns = lax.axis_size("cy")
    depth = lax.axis_size("cz")
    rows = block_pos.shape[0]
    vmem = pl.BlockSpec(memory_space=VMEM)
    hbm = pl.BlockSpec(memory_space=pltpu.HBM)
    populations = pltpu.with_memory_space_constraint(populations, pltpu.HBM)
    solid_cells = pltpu.with_memory_space_constraint(solid_cells, pltpu.HBM)
    places = pltpu.with_memory_space_constraint(block_pos.T, pltpu.HBM)
    place_scratch = SMEM((3, rows), jnp.int32)
    table_scratch = SMEM((LAYERS * BZD,), jnp.int32)
    mark_scratch = [VMEM((rows, EDGE**3), jnp.int32), VMEM((rows * TILES, LANE), jnp.float32)]

    up = [(i, i + 1) for i in range(layers - 1)]
    down = [(i + 1, i) for i in range(layers - 1)]
    send_up, send_down = pl.pallas_call(
        pack_stream,
        out_shape=(kept(SENT_ROWS), kept(SENT_ROWS)),
        in_specs=[hbm, hbm, hbm],
        out_specs=(vmem, vmem),
        scratch_shapes=[place_scratch, table_scratch]
        + mark_scratch
        + [
            VMEM((2 * MOVE_CAP, POPS, EDGE**3), jnp.float32),
            VMEM((2 * BZD, POPS, SLAB * LANE), jnp.float32),
            VMEM((PLANES * 2 * FACE, LANE), jnp.float32),
            pltpu.SemaphoreType.DMA((2 + 2 * MOVE_CAP + 2 * BZD,)),
        ],
        compiler_params=params(16),
        name="pack_stream",
    )(places, solid_cells, populations)
    from_low = lax.ppermute(send_up, "stream", up)
    from_high = lax.ppermute(send_down, "stream", down)

    own, zpack, zsend_up, zsend_down = pl.pallas_call(
        pack_edge,
        out_shape=(kept(LAYERS * BZD * BLOCK), kept(ZMETA + 8), kept(DIAG), kept(DIAG)),
        in_specs=[hbm, hbm, hbm],
        out_specs=(vmem,) * 4,
        scratch_shapes=[place_scratch, table_scratch]
        + mark_scratch
        + [
            VMEM((LAYERS, POPS, EDGE**3), jnp.float32),
            pltpu.SemaphoreType.DMA((LAYERS + 2,)),
        ],
        compiler_params=params(16),
        name="pack_edge",
    )(places, solid_cells, populations)
    swap = [(i, depth - 1 - i) for i in range(depth)]
    zin = lax.ppermute(zpack, "cz", swap)
    zup_pairs = [(s * depth + c, t * depth + d) for s, t in up for c, d in swap]
    zdown_pairs = [(s * depth + c, t * depth + d) for s, t in down for c, d in swap]
    z_low = lax.ppermute(zsend_up, ("stream", "cz"), zup_pairs)
    z_high = lax.ppermute(zsend_down, ("stream", "cz"), zdown_pairs)

    own = pl.pallas_call(
        pack_own,
        out_shape=kept(LAYERS * BZD * BLOCK),
        in_specs=[hbm, hbm, hbm, vmem],
        out_specs=vmem,
        scratch_shapes=[place_scratch]
        + mark_scratch
        + [
            VMEM((rows, POPS, EDGE**3), jnp.float32),
            pltpu.SemaphoreType.DMA((rows + 2,)),
        ],
        input_output_aliases={3: 0},
        compiler_params=params(16),
        name="pack_own",
    )(places, solid_cells, populations, own)

    own, edge, zall, zedge, rim_up, rim_down = pl.pallas_call(
        functools.partial(settle_rim, layers),
        out_shape=(
            kept(LAYERS * BZD * BLOCK),
            kept(PLANES * 4 * FACE),
            kept(LAYERS * ZROWS),
            kept(ZGROUPS * 8),
            kept(RIM_ROWS),
            kept(RIM_ROWS),
        ),
        in_specs=[hbm] + [vmem] * 6,
        out_specs=(vmem,) * 6,
        scratch_shapes=[
            place_scratch,
            VMEM((RIM * GRID_X, LANE), jnp.float32),
            VMEM((RIM * GRID_X, LANE), jnp.float32),
            pltpu.SemaphoreType.DMA,
        ],
        input_output_aliases={6: 0},
        compiler_params=params(16),
        name="settle_rim",
    )(places, from_low, from_high, zin, z_low, z_high, own)
    cy_up = [(i, i + 1) for i in range(columns - 1)]
    cy_down = [(i + 1, i) for i in range(columns - 1)]
    rim_low = lax.ppermute(rim_up, "cy", cy_up)
    rim_high = lax.ppermute(rim_down, "cy", cy_down)

    field, later = pl.pallas_call(
        functools.partial(settle_all, layers, columns, depth),
        out_shape=(kept(POPS * FIELD), kept(POPS * FIELD)),
        in_specs=[vmem] * 4,
        out_specs=(vmem,) * 2,
        compiler_params=params(16),
        name="settle_all",
    )(own, edge, zall, zedge)

    out, _, _ = pl.pallas_call(
        functools.partial(finish, layers, columns, depth),
        out_shape=(
            jax.ShapeDtypeStruct((POPS, SPAN_X, SPAN_Y, SPAN_Z), jnp.float32),
            kept(POPS * FIELD),
            kept(POPS * FIELD),
        ),
        in_specs=[vmem] * 4,
        out_specs=(hbm, vmem, vmem),
        scratch_shapes=[
            VMEM((POPS * 8 * TURN, LANE), jnp.float32),
            VMEM((POPS, SPAN_X, SPAN_Y, SPAN_Z), jnp.float32),
            pltpu.SemaphoreType.DMA((SPAN_X // 8,)),
        ],
        input_output_aliases={2: 1, 3: 2},
        compiler_params=params(16),
        name="finish",
    )(rim_low, rim_high, field, later)
    return out


def solution(mesh):
    in_specs = (
        P(("stream", "cy", "cz"), None, None),
        P(("stream", "cy", "cz"), None),
        P(("stream", "cy", "cz"), None),
    )
    out_specs = P(None, "stream", "cy", "cz")
    return jax.shard_map(shards, mesh=mesh, in_specs=in_specs, out_specs=out_specs, check_vma=False)
```

```python
import functools

import jax
import jax.numpy as jnp
from jax import lax
from jax.experimental import pallas as pl
from jax.experimental.pallas import tpu as pltpu
from jax.sharding import PartitionSpec as P

EDGE = 16
BXD = 2
BYD = 1
BZD = 4
MOVE_CAP = 2

VELOCITIES = (
    (0, 0, 0),
    (1, 0, 0),
    (-1, 0, 0),
    (0, 1, 0),
    (0, -1, 0),
    (0, 0, 1),
    (0, 0, -1),
    (1, 1, 0),
    (-1, -1, 0),
    (1, -1, 0),
    (-1, 1, 0),
    (1, 0, 1),
    (-1, 0, -1),
    (1, 0, -1),
    (-1, 0, 1),
    (0, 1, 1),
    (0, -1, -1),
    (0, 1, -1),
    (0, -1, 1),
)
WEIGHTS = (1.0 / 3.0,) + (1.0 / 18.0,) * 6 + (1.0 / 36.0,) * 12
OPPOSITE = (0, 2, 1, 4, 3, 6, 5, 8, 7, 10, 9, 12, 11, 14, 13, 16, 15, 18, 17)
OMEGA_EVEN = 1.25
OMEGA_ODD = 1.0 / 1.125

POPS = 19
PLANES = 20
LANE = 128
TILES = EDGE**3 // LANE
BLOCK = PLANES * TILES
YLO = LANE // EDGE
SLAB = 4
GROUPS = ((0, 8), (8, 8), (16, 3))
SENT_SLABS = MOVE_CAP * BLOCK
LAYERS = BXD + 2
ZGROUPS = 3
ZROWS = ZGROUPS * TILES
ZMETA = LAYERS * ZROWS
DIAG = ZROWS + ZGROUPS * SLAB

SPAN_X = BXD * EDGE
SPAN_Y = BYD * EDGE
SPAN_Z = BZD * EDGE
PITCH = SPAN_X + 8
STEP = PITCH // 8
FIRST = 96
FIELD = FIRST + (SPAN_Y + 1) * PITCH + 48
TURN = 9
EXT_X = SPAN_X + 4
EXT_Z = SPAN_Z + 2
RIM_UP = tuple(i for i in range(POPS) if VELOCITIES[i][1] == 1)
RIM_DOWN = tuple(i for i in range(POPS) if VELOCITIES[i][1] == -1)
RIM = PLANES + len(RIM_UP) + 1
AHEAD = tuple(i for i in range(POPS) if VELOCITIES[i][0] == 1)
BACK = tuple(i for i in range(POPS) if VELOCITIES[i][0] == -1)
FACE = 2 * BZD
SENT_META = SENT_SLABS + RIM * FACE
SENT_ROWS = SENT_META + 8
RIM_BLOCKS = -(-RIM * EXT_Z // LANE)
RIM_ROWS = RIM_BLOCKS * EXT_X + 4
GRID_X = 48

ROTOR = -(2.0**100)
OUTSIDE = -(2.0**110)
WALL_BELOW = -(2.0**80)
OUT_BELOW = -(2.0**105)

VMEM = pltpu.VMEM
SMEM = pltpu.SMEM


def lanes():
    return lax.broadcasted_iota(jnp.int32, (8, LANE), 1)


def collide(f):
    even = [None] * POPS
    odd = [None] * POPS
    for i in range(1, POPS, 2):
        even[i] = f[i] + f[i + 1]
        odd[i] = f[i] - f[i + 1]
    density = f[0]
    for i in range(1, POPS, 2):
        density = density + even[i]
    flow = []
    for axis in range(3):
        total = None
        for i in range(1, POPS, 2):
            sign = VELOCITIES[i][axis]
            if sign == 0:
                continue
            if total is None:
                total = odd[i] if sign == 1 else -odd[i]
            else:
                total = total + odd[i] if sign == 1 else total - odd[i]
        flow.append(total)
    inverse = 1.0 / density
    velocity = [part * inverse for part in flow]
    square = velocity[0] * velocity[0] + velocity[1] * velocity[1] + velocity[2] * velocity[2]
    base = density * (1.0 - 1.5 * square)
    post = [None] * POPS
    post[0] = (1.0 - OMEGA_EVEN) * f[0] + (OMEGA_EVEN * WEIGHTS[0]) * base
    shared = {}
    for weight in (WEIGHTS[1], WEIGHTS[7]):
        shared[weight] = ((OMEGA_EVEN * weight) * base, (OMEGA_EVEN * weight * 4.5) * density,
                          (OMEGA_ODD * weight * 3.0) * density)
    for i in range(1, POPS, 2):
        projected = None
        for axis in range(3):
            sign = VELOCITIES[i][axis]
            if sign == 0:
                continue
            if projected is None:
                projected = velocity[axis] if sign == 1 else -velocity[axis]
            else:
                projected = projected + velocity[axis] if sign == 1 else projected - velocity[axis]
        low, curve, slope = shared[WEIGHTS[i]]
        even_part = (0.5 - 0.5 * OMEGA_EVEN) * even[i] + (low + curve * (projected * projected))
        odd_part = (0.5 - 0.5 * OMEGA_ODD) * odd[i] + slope * projected
        post[i] = even_part + odd_part
        post[i + 1] = even_part - odd_part
    return post, density


def pushes(density, drift_y, drift_z):
    along_y = density * drift_y
    along_z = density * drift_z
    out = [None] * POPS
    for i in range(1, POPS):
        _, step_y, step_z = VELOCITIES[i]
        total = None
        for sign, part in ((step_y, along_y), (step_z, along_z)):
            if sign == 0:
                continue
            if total is None:
                total = part if sign == 1 else -part
            else:
                total = total + part if sign == 1 else total - part
        if total is not None:
            out[i] = (6.0 * WEIGHTS[i]) * total
    return out


def total_of(parts):
    parts = list(parts)
    while len(parts) > 1:
        pairs = [parts[n] + parts[n + 1] for n in range(0, len(parts) - 1, 2)]
        parts = pairs + parts[len(parts) - len(parts) % 2 :]
    return parts[0]


def streamed(pull, own, drift_y, drift_z):
    push = pushes(total_of(own), drift_y, drift_z)
    out = [own[0]]
    for i in range(1, POPS):
        pulled = pull(i)
        bounced = own[OPPOSITE[i]]
        blocked = pulled < WALL_BELOW
        if push[i] is not None:
            bounced = jnp.where(pulled < OUT_BELOW, bounced, bounced + push[i])
        out.append(jnp.where(blocked, bounced, pulled))
    return out


def ahead(items, take, leave, depth):
    waiting = []
    for n in items:
        waiting.append((n, take(n)))
        if len(waiting) > depth:
            leave(*waiting.pop(0))
    for pair in waiting:
        leave(*pair)


def place():
    return lax.axis_index("stream"), lax.axis_index("cy"), lax.axis_index("cz")


def slot_of(pos, row, layer, column_z):
    slot = (pos[0, row] - (layer * BXD - 1)) * BZD + (pos[2, row] - column_z * BZD)
    return jnp.clip(slot, 0, LAYERS * BZD - 1)


def fill_table(pos, table):
    layer, _, column_z = place()
    for entry in range(LAYERS * BZD):
        table[entry] = -1
    for row in range(pos.shape[1]):

        @pl.when(pos[0, row] >= 0)
        def _(row=row):
            table[slot_of(pos, row, layer, column_z)] = row


def spread_marks(marks, dense):
    rows = marks.shape[0]
    for first in range(0, rows, 8):
        size = min(8, rows - first)
        for begin in range(0, TILES, 8):
            values = [marks[first : first + size, t * LANE : (t + 1) * LANE] for t in range(begin, begin + 8)]
            for k, value in enumerate(values):
                dense[pl.ds(first * TILES + begin + k, size, stride=TILES), :] = value.astype(jnp.float32)


def collide_block(ref, base):
    for first in range(0, TILES // 8, 2):
        moves = []
        for part in (first, first + 1):
            old = [ref[pl.ds(base + i * TILES + 8 * part, 8), :] for i in range(POPS)]
            mark = ref[pl.ds(base + POPS * TILES + 8 * part, 8), :] > 0.5
            post, _ = collide(old)
            for i in range(POPS):
                moves.append((base + i * TILES + 8 * part, jnp.where(mark, old[i], post[i])))
        for row, value in moves:
            ref[pl.ds(row, 8), :] = value


def pack_block(out, base, stage, dense, row):
    out[pl.ds(base + POPS * TILES, TILES), :] = dense[pl.ds(pl.multiple_of(row * TILES, 8), TILES), :]
    for first in range(0, TILES, 4):
        moves = []
        for tile in range(first, first + 4):
            for group, size in GROUPS:
                value = stage[group : group + size, tile * LANE : (tile + 1) * LANE]
                moves.append((pl.ds(base + group * TILES + tile, size, stride=TILES), value))
        for target, value in moves:
            out[target, :] = value
    collide_block(out, base)


def pack_stream(places, marks_in, pops, up, down, pos, table, marks, dense, blocks, slabs, strip, sems):
    mark_copy = pltpu.make_async_copy(marks_in, marks, sems.at[0])
    mark_copy.start()
    place_copy = pltpu.make_async_copy(places, pos, sems.at[1])
    place_copy.start()
    rows = pos.shape[1]
    copies = [None] * 4
    for j in range(MOVE_CAP):
        copies[MOVE_CAP + j] = pltpu.make_async_copy(pops.at[j], blocks.at[MOVE_CAP + j], sems.at[2 + MOVE_CAP + j])
        copies[MOVE_CAP + j].start()
    place_copy.wait()
    count = 0
    for row in range(rows):
        count = count + jnp.where(pos[0, row] >= 0, 1, 0)
    last = jnp.clip(count - MOVE_CAP, 0, rows - MOVE_CAP)
    for j in range(MOVE_CAP):
        copies[j] = pltpu.make_async_copy(pops.at[last + j], blocks.at[j], sems.at[2 + j])
        copies[j].start()
    fill_table(pos, table)
    slab_rows = []
    slab_copies = []
    for side in range(2):
        for bz in range(BZD):
            row = jnp.maximum(table[(2 - side) * BZD + bz], 0)
            n = side * BZD + bz
            first = (TILES - SLAB) * LANE if side == 0 else 0
            slab_rows.append(row)
            slab_copies.append(
                pltpu.make_async_copy(
                    pops.at[row, :, pl.ds(first, SLAB * LANE)], slabs.at[n], sems.at[2 + 2 * MOVE_CAP + n]
                )
            )
            slab_copies[n].start()
    mark_copy.wait()
    spread_marks(marks, dense)
    for side, out in ((1, down), (0, up)):
        for j in range(MOVE_CAP):
            row = j if side == 1 else last + j
            for k, axis in ((0, 0), (1, 2)):
                value = jnp.full((1, LANE), pos[axis, row], jnp.int32).astype(jnp.float32)
                out[pl.ds(SENT_META + 2 * j + k, 1), :] = value
            n = side * MOVE_CAP + j
            copies[n].wait()
            pack_block(out, j * BLOCK, blocks.at[n], dense, row)
    for side, out in enumerate((up, down)):
        for bz in range(BZD):
            n = side * BZD + bz
            first = slab_rows[n] * TILES + (TILES - SLAB if side == 0 else 0)
            slab_copies[n].wait()
            moves = []
            for x in range(2):
                for yhi in range(2):
                    q = 2 * x + yhi
                    row = x * FACE + 2 * bz + yhi
                    for group, size in GROUPS:
                        value = slabs[n, group : group + size, q * LANE : (q + 1) * LANE]
                        moves.append((pl.ds(group * 2 * FACE + row, size, stride=2 * FACE), value))
                row = POPS * 2 * FACE + x * FACE + 2 * bz
                moves.append((pl.ds(row, 2), dense[pl.ds(first + 2 * x, 2), :]))
            for target, value in moves:
                strip[target, :] = value
        inner = 1 if side == 0 else 0
        for x in range(2):
            old = [strip[pl.ds(i * 2 * FACE + x * FACE, FACE), :] for i in range(POPS)]
            mark = strip[pl.ds(POPS * 2 * FACE + x * FACE, FACE), :] > 0.5
            post, _ = collide(old)
            if x == inner:
                pairs = [(i, i) for i in range(POPS)]
                marks_at = POPS
            else:
                pairs = [(PLANES + n, i) for n, i in enumerate(AHEAD if side == 0 else BACK)]
                marks_at = RIM - 1
            for plane, i in pairs:
                out[pl.ds(SENT_SLABS + plane * FACE, FACE), :] = jnp.where(mark, old[i], post[i])
            marks_of = strip[pl.ds(POPS * 2 * FACE + x * FACE, FACE), :]
            out[pl.ds(SENT_SLABS + marks_at * FACE, FACE), :] = marks_of


def pack_edge(places, marks_in, pops, own, zpack, zup, zdown, pos, table, marks, dense, stage, sems):
    column_z = lax.axis_index("cz")
    mark_copy = pltpu.make_async_copy(marks_in, marks, sems.at[LAYERS])
    mark_copy.start()
    place_copy = pltpu.make_async_copy(places, pos, sems.at[LAYERS + 1])
    place_copy.start()
    place_copy.wait()
    fill_table(pos, table)
    edge_bz = jnp.where(column_z == 0, BZD - 1, 0)
    first_c = jnp.where(column_z == 0, EDGE - 2, 0)
    found = [table[held * BZD + edge_bz] for held in range(LAYERS)]
    row_of = [jnp.maximum(row, 0) for row in found]
    copies = []
    for held in range(LAYERS):
        copies.append(pltpu.make_async_copy(pops.at[row_of[held]], stage.at[held], sems.at[held]))
        copies[held].start()
    mark_copy.wait()
    spread_marks(marks, dense)
    spot = (lanes() & (EDGE - 1)) >> 1
    sublane = lax.broadcasted_iota(jnp.int32, (8, LANE), 0)
    flags = jnp.zeros((8, LANE), jnp.int32)
    for held in range(LAYERS):
        copies[held].wait()
        base = pl.multiple_of((held * BZD + edge_bz) * BLOCK, 8)

        @pl.when(found[held] >= 0)
        def _(held=held, base=base):
            pack_block(own, base, stage.at[held], dense, row_of[held])
            totals = []
            for group in range(ZGROUPS):
                for part in range(TILES // 8):
                    total = jnp.zeros((8, LANE), jnp.float32)
                    for k in range(min(8, PLANES - group * 8)):
                        value = own[pl.ds(base + (group * 8 + k) * TILES + part * 8, 8), :]
                        value = pltpu.roll(value, (2 * k - first_c + LANE) & (LANE - 1), 1)
                        total = jnp.where(spot == k, value, total)
                    totals.append((held * ZROWS + group * TILES + part * 8, total))
            for row, total in totals:
                zpack[pl.ds(row, 8), :] = total

        flags = jnp.where((sublane == held) & (found[held] >= 0), 1, flags)
    zpack[pl.ds(ZMETA, 8), :] = flags.astype(jnp.float32)
    zup[pl.ds(0, ZROWS), :] = zpack[pl.ds(3 * ZROWS, ZROWS), :]
    zdown[pl.ds(0, ZROWS), :] = zpack[pl.ds(0, ZROWS), :]
    for group in range(ZGROUPS):
        target = pl.ds(ZROWS + group * SLAB, SLAB)
        zup[target, :] = zpack[pl.ds(2 * ZROWS + group * TILES + TILES - SLAB, SLAB), :]
        zdown[target, :] = zpack[pl.ds(ZROWS + group * TILES, SLAB), :]


def pack_own(places, marks_in, pops, own_in, own, edge, flags, pos, table, marks, dense, stage, sems):
    del own_in
    layer, _, column_z = place()
    edge_bz = jnp.where(column_z == 0, BZD - 1, 0)
    rows = pos.shape[1]
    mark_copy = pltpu.make_async_copy(marks_in, marks, sems.at[rows])
    mark_copy.start()
    place_copy = pltpu.make_async_copy(places, pos, sems.at[rows + 1])
    place_copy.start()
    copies = [pltpu.make_async_copy(pops.at[r], stage.at[r], sems.at[r]) for r in range(rows)]
    for copy in copies:
        copy.start()
    mark_copy.wait()
    spread_marks(marks, dense)
    place_copy.wait()

    def settle(row, carry):
        pltpu.make_async_copy(pops.at[row], stage.at[row], sems.at[row]).wait()
        slot = slot_of(pos, row, layer, column_z)

        @pl.when((pos[0, row] >= 0) & (slot % BZD != edge_bz))
        def _():
            pack_block(own, pl.multiple_of(slot * BLOCK, 8), stage.at[row], dense, row)

        return carry

    lax.fori_loop(0, rows, settle, 0)
    fill_table(pos, table)
    line = lax.broadcasted_iota(jnp.int32, (FACE, LANE), 0) >> 1
    for side in range(2):
        here = jnp.zeros((FACE, LANE), jnp.int32)
        for bz in range(BZD):
            goal = (0 if side == 0 else LAYERS - 1) * BZD + bz
            present = table[goal] >= 0
            here = jnp.where((line == bz) & present, 1, here)

            @pl.when(present)
            def _(side=side, goal=goal, bz=bz):
                first = goal * BLOCK + (TILES - SLAB if side == 0 else 0)
                values = []
                for _, i, x in slab_planes(side):
                    shift = 2 * (x if side == 0 else x - 2)
                    values.append(own[pl.ds(first + i * TILES + shift, 2), :])
                for (_, i, x), value in zip(slab_planes(side), values):
                    edge[pl.ds((i * 4 + x) * FACE + 2 * bz, 2), :] = value

        flags[pl.ds(side * FACE, FACE), :] = here.astype(jnp.float32)


def slab_planes(side):
    inner, outer = (1, 0) if side == 0 else (2, 3)
    pairs = [(i, i, inner) for i in range(PLANES)]
    return pairs + [(PLANES + n, i, outer) for n, i in enumerate((AHEAD if side == 0 else BACK) + (POPS,))]


class Lanes:
    def __init__(self, column_z):
        lane = lanes()
        self.from_bz = [lane >= bz * EDGE for bz in range(BZD)]
        self.main = lane < SPAN_Z
        self.goal = jnp.where(column_z == 0, SPAN_Z, LANE - 2)

    def to_halo(self, ylo, spot):
        return (self.goal - (ylo * EDGE + 2 * spot) + LANE) & (LANE - 1)


def gathered(parts, zvalue, spot, ylo, masks):
    rows = parts[0].shape[0]
    total = None
    for bz in range(BZD):
        shift = (bz * EDGE - ylo * EDGE) % LANE
        value = pltpu.roll(parts[bz], shift, 1) if shift else parts[bz]
        total = value if total is None else jnp.where(masks.from_bz[bz][:rows], value, total)
    beyond = pltpu.roll(zvalue, masks.to_halo(ylo, spot), 1)
    return jnp.where(masks.main[:rows], total, beyond)


def inside_lanes(rows, column_z):
    lane = lanes()[:rows]
    low = (column_z == 0) & (lane >= SPAN_Z) & (lane < SPAN_Z + 2)
    high = (column_z != 0) & (lane >= LANE - 2)
    return (lane < SPAN_Z) | low | high


def walled(values, mark, inside):
    factor = jnp.where(mark > 0.5, ROTOR, 1.0)
    cap = jnp.where(inside, -OUTSIDE, OUTSIDE)
    return [jnp.minimum(value * factor, cap) for value in values]


def plane_parts(own, edge, zall, zedge, chunk, yhi, plane):
    group = plane >> 3
    if chunk is None:
        first = plane * 4 * FACE + yhi
        parts = [edge[pl.ds(first + 2 * bz, 4, stride=FACE), :] for bz in range(BZD)]
        return parts, zedge[pl.ds(group * 8 + yhi, 4, stride=2), :]
    held, half = 1 + (chunk >> 1), chunk & 1
    first = held * (BZD * BLOCK) + half * EDGE + yhi
    parts = [own[pl.ds(first + bz * BLOCK + plane * TILES, 8, stride=2), :] for bz in range(BZD)]
    first = held * ZROWS + half * EDGE + yhi
    return parts, zall[pl.ds(first + group * TILES, 8, stride=2), :]


def chunk_values(own, edge, zall, zedge, chunk, yhi, rows, masks):
    out = [[] for _ in rows]
    for plane in range(PLANES):
        taken = [n for n, (_, planes) in enumerate(rows) if plane in planes]
        if taken:
            parts, zvalue = plane_parts(own, edge, zall, zedge, chunk, yhi, plane)
        for n in taken:
            out[n].append(gathered(parts, zvalue, plane % 8, rows[n][0], masks))
    return out


def halo_x_inside(layer, layers):
    row = lax.broadcasted_iota(jnp.int32, (4, LANE), 0)
    low = (row < 2) & (layer > 0)
    high = (row >= 2) & (layer < layers - 1)
    return low | high


def settle_rim(layers, up, down, zin, zup, zdown, edge_own, flags, own_in, own, edge, zall, zedge, rim_up, rim_down, post_up, post_down):
    del own_in
    layer, _, column_z = place()
    codes = []
    for arrived in (up, down):
        first = layer == 0 if arrived is up else layer == layers - 1
        for j in range(MOVE_CAP):
            bx = arrived[pl.ds(SENT_META + 2 * j, 1), :].astype(jnp.int32)
            bz = arrived[pl.ds(SENT_META + 2 * j + 1, 1), :].astype(jnp.int32)
            code = (bx - layer * BXD) * BZD + (bz - column_z * BZD)
            mine = (bx >= layer * BXD) & (bx < (layer + 1) * BXD) & jnp.logical_not(first)
            codes.append((arrived, j, jnp.max(jnp.where(mine, code, -1))))
    for arrived, j, code in codes:

        @pl.when(code >= 0)
        def _(arrived=arrived, j=j, code=code):
            base = pl.multiple_of((jnp.clip(code, 0, BXD * BZD - 1) + BZD) * BLOCK, 8)
            for k in range(0, BLOCK, 128):
                values = [arrived[pl.ds(j * BLOCK + k + 8 * n, 8), :] for n in range(16)]
                for n, value in enumerate(values):
                    own[pl.ds(base + k + 8 * n, 8), :] = value

    for side, arrived in enumerate((up, down)):
        here = flags[pl.ds(side * FACE, FACE), :] > 0.5
        values = []
        for plane, i, x in slab_planes(side):
            row = (i * 4 + x) * FACE
            other = arrived[pl.ds(SENT_SLABS + plane * FACE, FACE), :]
            values.append((row, jnp.where(here, edge_own[pl.ds(row, FACE), :], other)))
        for row, value in values:
            edge[pl.ds(row, FACE), :] = value
    moves = []
    for held in range(LAYERS):
        flag = zin[pl.ds(ZMETA + held, 1), :] > 0.5
        for group in range(ZGROUPS):
            if held == 1 or held == 2:
                for part in range(TILES // 8):
                    rows = pl.ds(held * ZROWS + group * TILES + part * 8, 8)
                    source = zup if held == 1 else zdown
                    other = source[pl.ds(group * TILES + part * 8, 8), :]
                    moves.append((zall, rows, jnp.where(flag, zin[rows, :], other)))
            else:
                side = 0 if held == 0 else 1
                source = zup if held == 0 else zdown
                first = TILES - SLAB if held == 0 else 0
                mine = zin[pl.ds(held * ZROWS + group * TILES + first, SLAB), :]
                other = source[pl.ds(ZROWS + group * SLAB, SLAB), :]
                moves.append((zedge, pl.ds(group * 8 + side * SLAB, SLAB), jnp.where(flag, mine, other)))
    for target, rows, value in moves:
        target[rows, :] = value
    masks = Lanes(column_z)
    for chunk in (0, 1, 2, 3, None):
        for near, far, rim, target in ((0, 1, RIM_DOWN, post_down), (SPAN_Y - 1, SPAN_Y - 2, RIM_UP, post_up)):
            rows = ((near % YLO, range(PLANES)), (far % YLO, rim + (POPS,)))
            first, second = chunk_values(own, edge, zall, zedge, chunk, near // YLO, rows, masks)
            for plane, value in enumerate(first + second):
                row = plane * GRID_X
                if chunk is None:
                    target[pl.ds(row, 2), :] = value[:2]
                    target[pl.ds(row + EXT_X - 2, 2), :] = value[2:]
                else:
                    target[pl.ds(row + 2 + 8 * chunk, 8), :] = value
    lane = lanes()
    for source, target in ((post_up, rim_up), (post_down, rim_down)):
        for chunk in range(5):
            size = min(8, EXT_X - 8 * chunk)
            values = []
            for plane in range(RIM):
                value = source[pl.ds(plane * GRID_X + 8 * chunk, 8), :]
                values.append(pltpu.roll(value, (plane * EXT_Z + 2 * column_z) & (LANE - 1), 1))
            totals = []
            for block in range(RIM_BLOCKS):
                total = jnp.zeros((8, LANE), jnp.float32)
                for plane in range(RIM):
                    begin = plane * EXT_Z - block * LANE
                    if begin >= LANE or begin + EXT_Z <= 0:
                        continue
                    total = jnp.where((lane >= begin) & (lane < begin + EXT_Z), values[plane], total)
                totals.append(total)
            for block in range(RIM_BLOCKS):
                target[pl.ds(block * EXT_X + 8 * chunk, size), :] = totals[block][:size]


def turned(value, step_z):
    return pltpu.roll(value, step_z % LANE, 1) if step_z else value


def drifts_of(columns, depth):
    _, _, column_z = place()
    lane = lanes()
    total_y = SPAN_Y * columns
    total_z = SPAN_Z * depth
    spin = 0.2 / (total_y + total_z)
    here_z = jnp.where(lane < SPAN_Z + 8, lane, lane - LANE) + column_z * SPAN_Z
    drift_y = -spin * (here_z.astype(jnp.float32) - (total_z - 1) / 2.0)
    return drift_y, spin, (total_y - 1) / 2.0


def first_step(columns, depth, field, later, begin, end, last):
    _, column_y, _ = place()
    drift_y, spin, centre_y = drifts_of(columns, depth)
    sublane = lax.broadcasted_iota(jnp.int32, (8, LANE), 0)

    def tile(base, drift_z):
        old = [field[pl.ds(i * FIELD + base, 8), :] for i in range(POPS)]
        values = streamed(pull_from(field, base), old, drift_y, drift_z)
        post, _ = collide(values)
        wall = old[0] < WALL_BELOW
        for i in range(POPS):
            later[pl.ds(i * FIELD + base, 8), :] = jnp.where(wall, old[i], post[i])

    def drift_at(y):
        return spin * ((y + column_y * SPAN_Y).astype(jnp.float32) - centre_y)

    def between(y):
        return jnp.where(sublane < 6, drift_at(y - 1), drift_at(y))

    def row(line, carry):
        y = line - 2
        base = pl.multiple_of(line * PITCH + (FIRST - 2 * PITCH), 8)
        tile(base - 8, between(y))
        for xc in range(STEP - 1):
            tile(base + 8 * xc, drift_at(y))
        return carry

    lax.fori_loop(begin + 2, end + 2, row, 0)
    if last:
        tile(FIRST + end * PITCH - 8, between(jnp.int32(end)))


def pull_from(field, base):
    def pull(i):
        step_x, step_y, step_z = VELOCITIES[i]
        return turned(field[pl.ds(i * FIELD + base - step_y * PITCH - step_x, 8), :], step_z)

    return pull


def settle_all(layers, columns, depth, own, edge, zall, zedge, field, later, turn):
    layer, _, column_z = place()
    masks = Lanes(column_z)
    lane = lanes()
    group_of = [((lane >> 4) & (BZD - 1)) == bz for bz in range(BZD)]
    inside_box = inside_lanes(8, column_z)
    inside_halo = inside_lanes(4, column_z) & halo_x_inside(layer, layers)

    def relay(chunk, yhi, inside, leave):
        for plane in range(PLANES):
            parts, zvalue = plane_parts(own, edge, zall, zedge, chunk, yhi, plane)
            size = zvalue.shape[0]
            main = masks.main[:size]
            for r in range(4):
                both = None
                for bz in range(BZD):
                    shift = (bz - r) * EDGE % LANE
                    value = pltpu.roll(parts[bz], shift, 1) if shift else parts[bz]
                    both = value if both is None else jnp.where(group_of[bz][:size], value, both)
                beyond = pltpu.roll(zvalue, masks.to_halo(r, plane % 8), 1)
                turn[pl.ds((plane * YLO + r) * 8, size), :] = jnp.where(main, both, beyond)
                turn[pl.ds((plane * YLO + r + 4) * 8, size), :] = jnp.where(main, beyond, both)
        for ylo in range(YLO):
            values = [turn[pl.ds((plane * YLO + ylo) * 8, size), :] for plane in range(PLANES)]
            if ylo >= 4:
                values = [pltpu.roll(value, SPAN_Z, 1) for value in values]
            leave(ylo, walled(values[:POPS], values[POPS], inside))

    def halves(yhi, carry):
        def chunks(chunk, carry):
            def leave(ylo, values):
                row = pl.multiple_of(FIRST + (YLO * yhi + ylo) * PITCH + 8 * chunk, 8)
                for i in range(POPS):
                    field[pl.ds(i * FIELD + row, 8), :] = values[i]

            relay(chunk, yhi, inside_box, leave)
            return carry

        lax.fori_loop(0, SPAN_X // 8, chunks, 0)

        def leave(ylo, values):
            row = FIRST + (YLO * yhi + ylo) * PITCH
            for i in range(POPS):
                field[pl.ds(i * FIELD + row - 2, 2), :] = values[i][:2]
                field[pl.ds(i * FIELD + row + SPAN_X, 2), :] = values[i][2:]

        relay(None, yhi, inside_halo, leave)
        return carry

    lax.fori_loop(0, SPAN_Y // YLO, halves, 0)
    first_step(columns, depth, field, later, 1, SPAN_Y - 1, False)


def finish(layers, columns, depth, rim_low, rim_high, field_in, later_in, out, field, later, turn, result, sems):
    del field_in, later_in
    layer, column_y, column_z = place()
    flat = (lanes() + 2 * column_z) & (LANE - 1)
    sides = (
        (rim_low, -1, -2, RIM_UP, column_y > 0),
        (rim_high, SPAN_Y, SPAN_Y + 1, RIM_DOWN, column_y < columns - 1),
    )
    sublane = lax.broadcasted_iota(jnp.int32, (8, LANE), 0)
    for source, near, far, rim, there in sides:
        for chunk in range(5):
            size = min(8, EXT_X - 8 * chunk)
            blocks = [source[pl.ds(block * EXT_X + 8 * chunk, 8), :] for block in range(RIM_BLOCKS)]

            def plane_of(plane, blocks=blocks):
                block, begin = divmod(plane * EXT_Z, LANE)
                shift = (2 * LANE - begin - 2 * column_z) & (LANE - 1)
                value = pltpu.roll(blocks[block], shift, 1)
                if begin + EXT_Z > LANE:
                    value = jnp.where(flat < LANE - begin, value, pltpu.roll(blocks[block + 1], shift, 1))
                return value

            inside = (flat < EXT_Z) & there
            if chunk == 0:
                inside = inside & ((sublane >= 2) | (layer > 0))
            if chunk == 4:
                inside = inside & ((sublane < 2) | (layer < layers - 1))
            for first, count, y, order in ((0, POPS, near, range(POPS)), (PLANES, len(rim), far, rim)):
                mark = plane_of(POPS if y == near else RIM - 1)
                values = walled([plane_of(first + n) for n in range(count)], mark, inside)
                for i, value in zip(order, values):
                    row = i * FIELD + FIRST + y * PITCH - 2 + 8 * chunk
                    field[pl.ds(row, size), :] = value[:size]

    first_step(columns, depth, field, later, -1, 1, True)
    first_step(columns, depth, field, later, SPAN_Y - 1, SPAN_Y + 1, True)

    drift_y, spin, centre_y = drifts_of(columns, depth)

    def leave(chunk, half):
        part = (slice(None), pl.ds(chunk * 8, 8), pl.ds(half * 8, 8))
        return pltpu.make_async_copy(result.at[part], out.at[part], sems.at[chunk, half])

    def second_step(chunk, carry):
        for half in range(SPAN_Y // 8):
            for k in range(8):
                y = 8 * half + k
                base = pl.multiple_of(FIRST + y * PITCH + 8 * chunk, 8)
                drift_z = spin * ((column_y * SPAN_Y + y).astype(jnp.float32) - centre_y)
                old = [later[pl.ds(i * FIELD + base, 8), :] for i in range(POPS)]
                values = streamed(pull_from(later, base), old, drift_y, drift_z)
                wall = old[0] < WALL_BELOW
                for i in range(POPS):
                    value = jnp.where(wall, old[i] * (1.0 / ROTOR), values[i])
                    turn[pl.ds(i * 8 * TURN + k * TURN, 8), :] = value
            for k in range(8):
                values = [turn[pl.ds(i * 8 * TURN + k, 8, stride=TURN), :] for i in range(POPS)]
                for i in range(POPS):
                    result[i, 8 * chunk + k, 8 * half : 8 * half + 8, :] = values[i][:, :SPAN_Z]
            leave(chunk, half).start()
        return carry

    lax.fori_loop(0, SPAN_X // 8, second_step, 0)
    for chunk in range(SPAN_X // 8):
        for half in range(SPAN_Y // 8):
            leave(chunk, half).wait()


def rows_of(count):
    return jax.ShapeDtypeStruct((count, LANE), jnp.float32)


def kept(count):
    return VMEM((count, LANE), jnp.float32)


def params(mib):
    return pltpu.CompilerParams(vmem_limit_bytes=mib * 2**20)


def shards(populations, solid_cells, block_pos):
    layers = lax.axis_size("stream")
    columns = lax.axis_size("cy")
    depth = lax.axis_size("cz")
    rows = block_pos.shape[0]
    vmem = pl.BlockSpec(memory_space=VMEM)
    hbm = pl.BlockSpec(memory_space=pltpu.HBM)
    populations = pltpu.with_memory_space_constraint(populations, pltpu.HBM)
    solid_cells = pltpu.with_memory_space_constraint(solid_cells, pltpu.HBM)
    places = pltpu.with_memory_space_constraint(block_pos.T, pltpu.HBM)
    place_scratch = SMEM((3, rows), jnp.int32)
    table_scratch = SMEM((LAYERS * BZD,), jnp.int32)
    mark_scratch = [VMEM((rows, EDGE**3), jnp.int32), VMEM((rows * TILES, LANE), jnp.float32)]

    up = [(i, i + 1) for i in range(layers - 1)]
    down = [(i + 1, i) for i in range(layers - 1)]
    send_up, send_down = pl.pallas_call(
        pack_stream,
        out_shape=(kept(SENT_ROWS), kept(SENT_ROWS)),
        in_specs=[hbm, hbm, hbm],
        out_specs=(vmem, vmem),
        scratch_shapes=[place_scratch, table_scratch]
        + mark_scratch
        + [
            VMEM((2 * MOVE_CAP, POPS, EDGE**3), jnp.float32),
            VMEM((2 * BZD, POPS, SLAB * LANE), jnp.float32),
            VMEM((PLANES * 2 * FACE, LANE), jnp.float32),
            pltpu.SemaphoreType.DMA((2 + 2 * MOVE_CAP + 2 * BZD,)),
        ],
        compiler_params=params(16),
        name="pack_stream",
    )(places, solid_cells, populations)
    from_low = lax.ppermute(send_up, "stream", up)
    from_high = lax.ppermute(send_down, "stream", down)

    own, zpack, zsend_up, zsend_down = pl.pallas_call(
        pack_edge,
        out_shape=(kept(LAYERS * BZD * BLOCK), kept(ZMETA + 8), kept(DIAG), kept(DIAG)),
        in_specs=[hbm, hbm, hbm],
        out_specs=(vmem,) * 4,
        scratch_shapes=[place_scratch, table_scratch]
        + mark_scratch
        + [
            VMEM((LAYERS, POPS, EDGE**3), jnp.float32),
            pltpu.SemaphoreType.DMA((LAYERS + 2,)),
        ],
        compiler_params=params(16),
        name="pack_edge",
    )(places, solid_cells, populations)
    swap = [(i, depth - 1 - i) for i in range(depth)]
    zin = lax.ppermute(zpack, "cz", swap)
    zup_pairs = [(s * depth + c, t * depth + d) for s, t in up for c, d in swap]
    zdown_pairs = [(s * depth + c, t * depth + d) for s, t in down for c, d in swap]
    z_low = lax.ppermute(zsend_up, ("stream", "cz"), zup_pairs)
    z_high = lax.ppermute(zsend_down, ("stream", "cz"), zdown_pairs)

    own, edge_own, flags = pl.pallas_call(
        pack_own,
        out_shape=(kept(LAYERS * BZD * BLOCK), kept(PLANES * 4 * FACE), kept(2 * FACE)),
        in_specs=[hbm, hbm, hbm, vmem],
        out_specs=(vmem,) * 3,
        scratch_shapes=[place_scratch, table_scratch]
        + mark_scratch
        + [
            VMEM((rows, POPS, EDGE**3), jnp.float32),
            pltpu.SemaphoreType.DMA((rows + 2,)),
        ],
        input_output_aliases={3: 0},
        compiler_params=params(16),
        name="pack_own",
    )(places, solid_cells, populations, own)

    own, edge, zall, zedge, rim_up, rim_down = pl.pallas_call(
        functools.partial(settle_rim, layers),
        out_shape=(
            kept(LAYERS * BZD * BLOCK),
            kept(PLANES * 4 * FACE),
            kept(LAYERS * ZROWS),
            kept(ZGROUPS * 8),
            kept(RIM_ROWS),
            kept(RIM_ROWS),
        ),
        in_specs=[vmem] * 8,
        out_specs=(vmem,) * 6,
        scratch_shapes=[
            VMEM((RIM * GRID_X, LANE), jnp.float32),
            VMEM((RIM * GRID_X, LANE), jnp.float32),
        ],
        input_output_aliases={7: 0},
        compiler_params=params(16),
        name="settle_rim",
    )(from_low, from_high, zin, z_low, z_high, edge_own, flags, own)
    cy_up = [(i, i + 1) for i in range(columns - 1)]
    cy_down = [(i + 1, i) for i in range(columns - 1)]
    rim_low = lax.ppermute(rim_up, "cy", cy_up)
    rim_high = lax.ppermute(rim_down, "cy", cy_down)

    field, later = pl.pallas_call(
        functools.partial(settle_all, layers, columns, depth),
        out_shape=(kept(POPS * FIELD), kept(POPS * FIELD)),
        in_specs=[vmem] * 4,
        out_specs=(vmem,) * 2,
        scratch_shapes=[VMEM((PLANES * YLO * 8, LANE), jnp.float32)],
        compiler_params=params(16),
        name="settle_all",
    )(own, edge, zall, zedge)

    out, _, _ = pl.pallas_call(
        functools.partial(finish, layers, columns, depth),
        out_shape=(
            jax.ShapeDtypeStruct((POPS, SPAN_X, SPAN_Y, SPAN_Z), jnp.float32),
            kept(POPS * FIELD),
            kept(POPS * FIELD),
        ),
        in_specs=[vmem] * 4,
        out_specs=(hbm, vmem, vmem),
        scratch_shapes=[
            VMEM((POPS * 8 * TURN, LANE), jnp.float32),
            VMEM((POPS, SPAN_X, SPAN_Y, SPAN_Z), jnp.float32),
            pltpu.SemaphoreType.DMA((SPAN_X // 8, SPAN_Y // 8)),
        ],
        input_output_aliases={2: 1, 3: 2},
        compiler_params=params(16),
        name="finish",
    )(rim_low, rim_high, field, later)
    return out


def solution(mesh):
    in_specs = (
        P(("stream", "cy", "cz"), None, None),
        P(("stream", "cy", "cz"), None),
        P(("stream", "cy", "cz"), None),
    )
    out_specs = P(None, "stream", "cy", "cz")
    return jax.shard_map(shards, mesh=mesh, in_specs=in_specs, out_specs=out_specs, check_vma=False)
```

```python
import functools

import jax
import jax.numpy as jnp
from jax import lax
from jax.experimental import pallas as pl
from jax.experimental.pallas import tpu as pltpu
from jax.sharding import PartitionSpec as P

EDGE = 16
BXD = 2
BYD = 1
BZD = 4
MOVE_CAP = 2

VELOCITIES = (
    (0, 0, 0),
    (1, 0, 0),
    (-1, 0, 0),
    (0, 1, 0),
    (0, -1, 0),
    (0, 0, 1),
    (0, 0, -1),
    (1, 1, 0),
    (-1, -1, 0),
    (1, -1, 0),
    (-1, 1, 0),
    (1, 0, 1),
    (-1, 0, -1),
    (1, 0, -1),
    (-1, 0, 1),
    (0, 1, 1),
    (0, -1, -1),
    (0, 1, -1),
    (0, -1, 1),
)
WEIGHTS = (1.0 / 3.0,) + (1.0 / 18.0,) * 6 + (1.0 / 36.0,) * 12
OPPOSITE = (0, 2, 1, 4, 3, 6, 5, 8, 7, 10, 9, 12, 11, 14, 13, 16, 15, 18, 17)
OMEGA_EVEN = 1.25
OMEGA_ODD = 1.0 / 1.125

POPS = 19
PLANES = 20
LANE = 128
TILES = EDGE**3 // LANE
BLOCK = PLANES * TILES
YLO = LANE // EDGE
SLAB = 4
GROUPS = ((0, 8), (8, 8), (16, 3))
SENT_SLABS = MOVE_CAP * BLOCK
LAYERS = BXD + 2
ZGROUPS = 3
ZROWS = ZGROUPS * TILES
ZMETA = LAYERS * ZROWS
DIAG = ZROWS + ZGROUPS * SLAB

SPAN_X = BXD * EDGE
SPAN_Y = BYD * EDGE
SPAN_Z = BZD * EDGE
PITCH = SPAN_X + 8
STEP = PITCH // 8
FIRST = 96
FIELD = FIRST + (SPAN_Y + 1) * PITCH + 48
TURN = 9
EXT_X = SPAN_X + 4
EXT_Z = SPAN_Z + 2
RIM_UP = tuple(i for i in range(POPS) if VELOCITIES[i][1] == 1)
RIM_DOWN = tuple(i for i in range(POPS) if VELOCITIES[i][1] == -1)
TOWARD = len(RIM_UP)
SLAB_PLANES = PLANES + TOWARD + 1
STREAMED = POPS - TOWARD
RIM = STREAMED + 1 + TOWARD + 1
KEPT = POPS + TOWARD
AHEAD = tuple(i for i in range(POPS) if VELOCITIES[i][0] == 1)
BACK = tuple(i for i in range(POPS) if VELOCITIES[i][0] == -1)
FACE = 2 * BZD
SENT_META = SENT_SLABS + SLAB_PLANES * FACE
SENT_ROWS = SENT_META + 8
RIM_BLOCKS = -(-RIM * EXT_Z // LANE)
RIM_ROWS = RIM_BLOCKS * EXT_X + 4
GRID_X = 48

ROTOR = -(2.0**100)
OUTSIDE = -(2.0**110)
WALL_BELOW = -(2.0**80)
OUT_BELOW = -(2.0**105)

VMEM = pltpu.VMEM
SMEM = pltpu.SMEM


def lanes():
    return lax.broadcasted_iota(jnp.int32, (8, LANE), 1)


def collide(f):
    even = [None] * POPS
    odd = [None] * POPS
    for i in range(1, POPS, 2):
        even[i] = f[i] + f[i + 1]
        odd[i] = f[i] - f[i + 1]
    density = f[0]
    for i in range(1, POPS, 2):
        density = density + even[i]
    flow = []
    for axis in range(3):
        total = None
        for i in range(1, POPS, 2):
            sign = VELOCITIES[i][axis]
            if sign == 0:
                continue
            if total is None:
                total = odd[i] if sign == 1 else -odd[i]
            else:
                total = total + odd[i] if sign == 1 else total - odd[i]
        flow.append(total)
    inverse = 1.0 / density
    velocity = [part * inverse for part in flow]
    square = velocity[0] * velocity[0] + velocity[1] * velocity[1] + velocity[2] * velocity[2]
    base = density * (1.0 - 1.5 * square)
    post = [None] * POPS
    post[0] = (1.0 - OMEGA_EVEN) * f[0] + (OMEGA_EVEN * WEIGHTS[0]) * base
    shared = {}
    for weight in (WEIGHTS[1], WEIGHTS[7]):
        shared[weight] = ((OMEGA_EVEN * weight) * base, (OMEGA_EVEN * weight * 4.5) * density,
                          (OMEGA_ODD * weight * 3.0) * density)
    for i in range(1, POPS, 2):
        projected = None
        for axis in range(3):
            sign = VELOCITIES[i][axis]
            if sign == 0:
                continue
            if projected is None:
                projected = velocity[axis] if sign == 1 else -velocity[axis]
            else:
                projected = projected + velocity[axis] if sign == 1 else projected - velocity[axis]
        low, curve, slope = shared[WEIGHTS[i]]
        even_part = (0.5 - 0.5 * OMEGA_EVEN) * even[i] + (low + curve * (projected * projected))
        odd_part = (0.5 - 0.5 * OMEGA_ODD) * odd[i] + slope * projected
        post[i] = even_part + odd_part
        post[i + 1] = even_part - odd_part
    return post, density


def pushes(density, drift_y, drift_z):
    along_y = density * drift_y
    along_z = density * drift_z
    out = [None] * POPS
    for i in range(1, POPS):
        _, step_y, step_z = VELOCITIES[i]
        total = None
        for sign, part in ((step_y, along_y), (step_z, along_z)):
            if sign == 0:
                continue
            if total is None:
                total = part if sign == 1 else -part
            else:
                total = total + part if sign == 1 else total - part
        if total is not None:
            out[i] = (6.0 * WEIGHTS[i]) * total
    return out


def total_of(parts):
    parts = list(parts)
    while len(parts) > 1:
        pairs = [parts[n] + parts[n + 1] for n in range(0, len(parts) - 1, 2)]
        parts = pairs + parts[len(parts) - len(parts) % 2 :]
    return parts[0]


def streamed(pull, own, density, drift_y, drift_z, wanted=range(POPS)):
    push = pushes(density, drift_y, drift_z)
    out = {}
    for i in wanted:
        if i == 0:
            out[i] = own[0]
            continue
        pulled = pull(i)
        bounced = own[OPPOSITE[i]]
        blocked = pulled < WALL_BELOW
        if push[i] is not None:
            bounced = jnp.where(pulled < OUT_BELOW, bounced, bounced + push[i])
        out[i] = jnp.where(blocked, bounced, pulled)
    return out


def place():
    return lax.axis_index("stream"), lax.axis_index("cy"), lax.axis_index("cz")


def slot_of(pos, row, layer, column_z):
    slot = (pos[0, row] - (layer * BXD - 1)) * BZD + (pos[2, row] - column_z * BZD)
    return jnp.clip(slot, 0, LAYERS * BZD - 1)


def fill_table(pos, table):
    layer, _, column_z = place()
    for entry in range(LAYERS * BZD):
        table[entry] = -1
    for row in range(pos.shape[1]):

        @pl.when(pos[0, row] >= 0)
        def _(row=row):
            table[slot_of(pos, row, layer, column_z)] = row


def spread_marks(marks, dense):
    rows = marks.shape[0]
    for first in range(0, rows, 8):
        size = min(8, rows - first)
        for begin in range(0, TILES, 8):
            values = [marks[first : first + size, t * LANE : (t + 1) * LANE] for t in range(begin, begin + 8)]
            for k, value in enumerate(values):
                dense[pl.ds(first * TILES + begin + k, size, stride=TILES), :] = value.astype(jnp.float32)


def collide_block(ref, base):
    for first in range(0, TILES // 8, 2):
        moves = []
        for part in (first, first + 1):
            old = [ref[pl.ds(base + i * TILES + 8 * part, 8), :] for i in range(POPS)]
            mark = ref[pl.ds(base + POPS * TILES + 8 * part, 8), :] > 0.5
            post, _ = collide(old)
            for i in range(POPS):
                moves.append((base + i * TILES + 8 * part, jnp.where(mark, old[i], post[i])))
        for row, value in moves:
            ref[pl.ds(row, 8), :] = value


def pack_block(out, base, stage, dense, row):
    out[pl.ds(base + POPS * TILES, TILES), :] = dense[pl.ds(pl.multiple_of(row * TILES, 8), TILES), :]
    for first in range(0, TILES, 4):
        moves = []
        for tile in range(first, first + 4):
            for group, size in GROUPS:
                value = stage[group : group + size, tile * LANE : (tile + 1) * LANE]
                moves.append((pl.ds(base + group * TILES + tile, size, stride=TILES), value))
        for target, value in moves:
            out[target, :] = value
    collide_block(out, base)


def pack_stream(places, marks_in, pops, up, down, pos, table, marks, dense, blocks, slabs, strip, sems):
    mark_copy = pltpu.make_async_copy(marks_in, marks, sems.at[0])
    mark_copy.start()
    place_copy = pltpu.make_async_copy(places, pos, sems.at[1])
    place_copy.start()
    rows = pos.shape[1]
    copies = [None] * 4
    for j in range(MOVE_CAP):
        copies[MOVE_CAP + j] = pltpu.make_async_copy(pops.at[j], blocks.at[MOVE_CAP + j], sems.at[2 + MOVE_CAP + j])
        copies[MOVE_CAP + j].start()
    place_copy.wait()
    count = 0
    for row in range(rows):
        count = count + jnp.where(pos[0, row] >= 0, 1, 0)
    last = jnp.clip(count - MOVE_CAP, 0, rows - MOVE_CAP)
    for j in range(MOVE_CAP):
        copies[j] = pltpu.make_async_copy(pops.at[last + j], blocks.at[j], sems.at[2 + j])
        copies[j].start()
    fill_table(pos, table)
    slab_rows = []
    slab_copies = []
    for side in range(2):
        for bz in range(BZD):
            row = jnp.maximum(table[(2 - side) * BZD + bz], 0)
            n = side * BZD + bz
            first = (TILES - SLAB) * LANE if side == 0 else 0
            slab_rows.append(row)
            slab_copies.append(
                pltpu.make_async_copy(
                    pops.at[row, :, pl.ds(first, SLAB * LANE)], slabs.at[n], sems.at[2 + 2 * MOVE_CAP + n]
                )
            )
            slab_copies[n].start()
    mark_copy.wait()
    spread_marks(marks, dense)
    for side, out in ((1, down), (0, up)):
        for j in range(MOVE_CAP):
            row = j if side == 1 else last + j
            for k, axis in ((0, 0), (1, 2)):
                value = jnp.full((1, LANE), pos[axis, row], jnp.int32).astype(jnp.float32)
                out[pl.ds(SENT_META + 2 * j + k, 1), :] = value
            n = side * MOVE_CAP + j
            copies[n].wait()
            pack_block(out, j * BLOCK, blocks.at[n], dense, row)
    for side, out in enumerate((up, down)):
        for bz in range(BZD):
            n = side * BZD + bz
            first = slab_rows[n] * TILES + (TILES - SLAB if side == 0 else 0)
            slab_copies[n].wait()
            moves = []
            for x in range(2):
                for yhi in range(2):
                    q = 2 * x + yhi
                    row = x * FACE + 2 * bz + yhi
                    for group, size in GROUPS:
                        value = slabs[n, group : group + size, q * LANE : (q + 1) * LANE]
                        moves.append((pl.ds(group * 2 * FACE + row, size, stride=2 * FACE), value))
                row = POPS * 2 * FACE + x * FACE + 2 * bz
                moves.append((pl.ds(row, 2), dense[pl.ds(first + 2 * x, 2), :]))
            for target, value in moves:
                strip[target, :] = value
        inner = 1 if side == 0 else 0
        for x in range(2):
            old = [strip[pl.ds(i * 2 * FACE + x * FACE, FACE), :] for i in range(POPS)]
            mark = strip[pl.ds(POPS * 2 * FACE + x * FACE, FACE), :] > 0.5
            post, _ = collide(old)
            if x == inner:
                pairs = [(i, i) for i in range(POPS)]
                marks_at = POPS
            else:
                pairs = [(PLANES + n, i) for n, i in enumerate(AHEAD if side == 0 else BACK)]
                marks_at = SLAB_PLANES - 1
            for plane, i in pairs:
                out[pl.ds(SENT_SLABS + plane * FACE, FACE), :] = jnp.where(mark, old[i], post[i])
            marks_of = strip[pl.ds(POPS * 2 * FACE + x * FACE, FACE), :]
            out[pl.ds(SENT_SLABS + marks_at * FACE, FACE), :] = marks_of


def pack_edge(places, marks_in, pops, own, zpack, zup, zdown, pos, table, marks, dense, stage, sems):
    column_z = lax.axis_index("cz")
    mark_copy = pltpu.make_async_copy(marks_in, marks, sems.at[LAYERS])
    mark_copy.start()
    place_copy = pltpu.make_async_copy(places, pos, sems.at[LAYERS + 1])
    place_copy.start()
    place_copy.wait()
    fill_table(pos, table)
    edge_bz = jnp.where(column_z == 0, BZD - 1, 0)
    first_c = jnp.where(column_z == 0, EDGE - 2, 0)
    found = [table[held * BZD + edge_bz] for held in range(LAYERS)]
    row_of = [jnp.maximum(row, 0) for row in found]
    copies = []
    for held in range(LAYERS):
        copies.append(pltpu.make_async_copy(pops.at[row_of[held]], stage.at[held], sems.at[held]))
        copies[held].start()
    mark_copy.wait()
    spread_marks(marks, dense)
    spot = (lanes() & (EDGE - 1)) >> 1
    sublane = lax.broadcasted_iota(jnp.int32, (8, LANE), 0)
    flags = jnp.zeros((8, LANE), jnp.int32)
    for held in range(LAYERS):
        copies[held].wait()
        base = pl.multiple_of((held * BZD + edge_bz) * BLOCK, 8)

        @pl.when(found[held] >= 0)
        def _(held=held, base=base):
            pack_block(own, base, stage.at[held], dense, row_of[held])
            totals = []
            for group in range(ZGROUPS):
                for part in range(TILES // 8):
                    total = jnp.zeros((8, LANE), jnp.float32)
                    for k in range(min(8, PLANES - group * 8)):
                        value = own[pl.ds(base + (group * 8 + k) * TILES + part * 8, 8), :]
                        value = pltpu.roll(value, (2 * k - first_c + LANE) & (LANE - 1), 1)
                        total = jnp.where(spot == k, value, total)
                    totals.append((held * ZROWS + group * TILES + part * 8, total))
            for row, total in totals:
                zpack[pl.ds(row, 8), :] = total

        flags = jnp.where((sublane == held) & (found[held] >= 0), 1, flags)
    zpack[pl.ds(ZMETA, 8), :] = flags.astype(jnp.float32)
    zup[pl.ds(0, ZROWS), :] = zpack[pl.ds(3 * ZROWS, ZROWS), :]
    zdown[pl.ds(0, ZROWS), :] = zpack[pl.ds(0, ZROWS), :]
    for group in range(ZGROUPS):
        target = pl.ds(ZROWS + group * SLAB, SLAB)
        zup[target, :] = zpack[pl.ds(2 * ZROWS + group * TILES + TILES - SLAB, SLAB), :]
        zdown[target, :] = zpack[pl.ds(ZROWS + group * TILES, SLAB), :]


def pack_own(places, marks_in, pops, own_in, own, edge, flags, pos, table, marks, dense, stage, sems):
    del own_in
    layer, _, column_z = place()
    edge_bz = jnp.where(column_z == 0, BZD - 1, 0)
    rows = pos.shape[1]
    mark_copy = pltpu.make_async_copy(marks_in, marks, sems.at[rows])
    mark_copy.start()
    place_copy = pltpu.make_async_copy(places, pos, sems.at[rows + 1])
    place_copy.start()
    copies = [pltpu.make_async_copy(pops.at[r], stage.at[r], sems.at[r]) for r in range(rows)]
    for copy in copies:
        copy.start()
    mark_copy.wait()
    spread_marks(marks, dense)
    place_copy.wait()

    def settle(row, carry):
        pltpu.make_async_copy(pops.at[row], stage.at[row], sems.at[row]).wait()
        slot = slot_of(pos, row, layer, column_z)

        @pl.when((pos[0, row] >= 0) & (slot % BZD != edge_bz))
        def _():
            pack_block(own, pl.multiple_of(slot * BLOCK, 8), stage.at[row], dense, row)

        return carry

    lax.fori_loop(0, rows, settle, 0)
    fill_table(pos, table)
    line = lax.broadcasted_iota(jnp.int32, (FACE, LANE), 0) >> 1
    for side in range(2):
        here = jnp.zeros((FACE, LANE), jnp.int32)
        for bz in range(BZD):
            goal = (0 if side == 0 else LAYERS - 1) * BZD + bz
            present = table[goal] >= 0
            here = jnp.where((line == bz) & present, 1, here)

            @pl.when(present)
            def _(side=side, goal=goal, bz=bz):
                first = goal * BLOCK + (TILES - SLAB if side == 0 else 0)
                values = []
                for _, i, x in slab_planes(side):
                    shift = 2 * (x if side == 0 else x - 2)
                    values.append(own[pl.ds(first + i * TILES + shift, 2), :])
                for (_, i, x), value in zip(slab_planes(side), values):
                    edge[pl.ds((i * 4 + x) * FACE + 2 * bz, 2), :] = value

        flags[pl.ds(side * FACE, FACE), :] = here.astype(jnp.float32)


def slab_planes(side):
    inner, outer = (1, 0) if side == 0 else (2, 3)
    pairs = [(i, i, inner) for i in range(PLANES)]
    return pairs + [(PLANES + n, i, outer) for n, i in enumerate((AHEAD if side == 0 else BACK) + (POPS,))]


class Lanes:
    def __init__(self, column_z):
        lane = lanes()
        self.from_bz = [lane >= bz * EDGE for bz in range(BZD)]
        self.main = lane < SPAN_Z
        self.goal = jnp.where(column_z == 0, SPAN_Z, LANE - 2)

    def to_halo(self, ylo, spot):
        return (self.goal - (ylo * EDGE + 2 * spot) + LANE) & (LANE - 1)


def gathered(parts, zvalue, spot, ylo, masks):
    rows = parts[0].shape[0]
    total = None
    for bz in range(BZD):
        shift = (bz * EDGE - ylo * EDGE) % LANE
        value = pltpu.roll(parts[bz], shift, 1) if shift else parts[bz]
        total = value if total is None else jnp.where(masks.from_bz[bz][:rows], value, total)
    beyond = pltpu.roll(zvalue, masks.to_halo(ylo, spot), 1)
    return jnp.where(masks.main[:rows], total, beyond)


def inside_lanes(rows, column_z):
    lane = lanes()[:rows]
    low = (column_z == 0) & (lane >= SPAN_Z) & (lane < SPAN_Z + 2)
    high = (column_z != 0) & (lane >= LANE - 2)
    return (lane < SPAN_Z) | low | high


def walled(values, mark, inside):
    factor = jnp.where(mark > 0.5, ROTOR, 1.0)
    cap = jnp.where(inside, -OUTSIDE, OUTSIDE)
    return [jnp.minimum(value * factor, cap) for value in values]


def plane_parts(own, edge, zall, zedge, chunk, yhi, plane):
    group = plane >> 3
    if chunk is None:
        first = plane * 4 * FACE + yhi
        parts = [edge[pl.ds(first + 2 * bz, 4, stride=FACE), :] for bz in range(BZD)]
        return parts, zedge[pl.ds(group * 8 + yhi, 4, stride=2), :]
    held, half = 1 + (chunk >> 1), chunk & 1
    first = held * (BZD * BLOCK) + half * EDGE + yhi
    parts = [own[pl.ds(first + bz * BLOCK + plane * TILES, 8, stride=2), :] for bz in range(BZD)]
    first = held * ZROWS + half * EDGE + yhi
    return parts, zall[pl.ds(first + group * TILES, 8, stride=2), :]


def chunk_values(own, edge, zall, zedge, chunk, yhi, rows, masks):
    out = [[] for _ in rows]
    for plane in range(PLANES):
        taken = [n for n, (_, planes) in enumerate(rows) if plane in planes]
        if taken:
            parts, zvalue = plane_parts(own, edge, zall, zedge, chunk, yhi, plane)
        for n in taken:
            out[n].append(gathered(parts, zvalue, plane % 8, rows[n][0], masks))
    return out


def halo_x_inside(layer, layers):
    row = lax.broadcasted_iota(jnp.int32, (4, LANE), 0)
    low = (row < 2) & (layer > 0)
    high = (row >= 2) & (layer < layers - 1)
    return low | high


def settle_rim(layers, columns, depth, up, down, zin, zup, zdown, edge_own, flags, own_in, own, edge, zall, zedge, rim_up, rim_down, post_up, post_down):
    del own_in
    layer, column_y, column_z = place()
    codes = []
    for arrived in (up, down):
        first = layer == 0 if arrived is up else layer == layers - 1
        for j in range(MOVE_CAP):
            bx = arrived[pl.ds(SENT_META + 2 * j, 1), :].astype(jnp.int32)
            bz = arrived[pl.ds(SENT_META + 2 * j + 1, 1), :].astype(jnp.int32)
            code = (bx - layer * BXD) * BZD + (bz - column_z * BZD)
            mine = (bx >= layer * BXD) & (bx < (layer + 1) * BXD) & jnp.logical_not(first)
            codes.append((arrived, j, jnp.max(jnp.where(mine, code, -1))))
    for arrived, j, code in codes:

        @pl.when(code >= 0)
        def _(arrived=arrived, j=j, code=code):
            base = pl.multiple_of((jnp.clip(code, 0, BXD * BZD - 1) + BZD) * BLOCK, 8)
            for k in range(0, BLOCK, 128):
                values = [arrived[pl.ds(j * BLOCK + k + 8 * n, 8), :] for n in range(16)]
                for n, value in enumerate(values):
                    own[pl.ds(base + k + 8 * n, 8), :] = value

    for side, arrived in enumerate((up, down)):
        here = flags[pl.ds(side * FACE, FACE), :] > 0.5
        values = []
        for plane, i, x in slab_planes(side):
            row = (i * 4 + x) * FACE
            other = arrived[pl.ds(SENT_SLABS + plane * FACE, FACE), :]
            values.append((row, jnp.where(here, edge_own[pl.ds(row, FACE), :], other)))
        for row, value in values:
            edge[pl.ds(row, FACE), :] = value
    moves = []
    for held in range(LAYERS):
        flag = zin[pl.ds(ZMETA + held, 1), :] > 0.5
        for group in range(ZGROUPS):
            if held == 1 or held == 2:
                for part in range(TILES // 8):
                    rows = pl.ds(held * ZROWS + group * TILES + part * 8, 8)
                    source = zup if held == 1 else zdown
                    other = source[pl.ds(group * TILES + part * 8, 8), :]
                    moves.append((zall, rows, jnp.where(flag, zin[rows, :], other)))
            else:
                side = 0 if held == 0 else 1
                source = zup if held == 0 else zdown
                first = TILES - SLAB if held == 0 else 0
                mine = zin[pl.ds(held * ZROWS + group * TILES + first, SLAB), :]
                other = source[pl.ds(ZROWS + group * SLAB, SLAB), :]
                moves.append((zedge, pl.ds(group * 8 + side * SLAB, SLAB), jnp.where(flag, mine, other)))
    for target, rows, value in moves:
        target[rows, :] = value
    masks = Lanes(column_z)
    inside_box = inside_lanes(8, column_z)
    inside_halo = inside_lanes(4, column_z) & halo_x_inside(layer, layers)
    sides = ((0, 1, RIM_DOWN, RIM_UP, post_down), (SPAN_Y - 1, SPAN_Y - 2, RIM_UP, RIM_DOWN, post_up))
    for chunk in (0, 1, 2, 3, None):
        inside = inside_halo if chunk is None else inside_box
        for near, far, rim, _, target in sides:
            rows = ((near % YLO, range(PLANES)), (far % YLO, rim + (POPS,)))
            first, second = chunk_values(own, edge, zall, zedge, chunk, near // YLO, rows, masks)
            planes = walled(first[:POPS], first[POPS], inside)
            planes += walled(second[:TOWARD], second[TOWARD], inside)
            sent = [first[i] for i in rim] + [first[POPS]]
            spots = list(range(KEPT)) + [KEPT + STREAMED + 1 + n for n in range(len(sent))]
            for plane, value in zip(spots, planes + sent):
                row = plane * GRID_X
                if chunk is None:
                    target[pl.ds(row, 2), :] = value[:2]
                    target[pl.ds(row + EXT_X - 2, 2), :] = value[2:]
                else:
                    target[pl.ds(row + 2 + 8 * chunk, 8), :] = value
    drift_y, spin, centre_y = drifts_of(columns, depth)
    for near, _, rim, away, target in sides:
        drift_z = spin * ((column_y * SPAN_Y + near).astype(jnp.float32) - centre_y)
        wanted = [i for i in range(POPS) if i not in away]
        plane_of = {i: POPS + rim.index(i) if i in rim else i for i in wanted}
        for chunk in range(5):
            first = 1 + 8 * chunk

            def pull(i):
                step_x, _, step_z = VELOCITIES[i]
                return turned(target[pl.ds(plane_of[i] * GRID_X + first - step_x, 8), :], step_z)

            old = [target[pl.ds(i * GRID_X + first, 8), :] for i in range(POPS)]
            rho = total_of(old)
            values = streamed(pull, old, rho, drift_y, drift_z, wanted)
            size = min(8, EXT_X - 1 - first)
            for n, value in enumerate([values[i] for i in wanted] + [rho]):
                target[pl.ds((KEPT + n) * GRID_X + first, size), :] = value[:size]
    lane = lanes()
    for source, target in ((post_up, rim_up), (post_down, rim_down)):
        for chunk in range(5):
            size = min(8, EXT_X - 8 * chunk)
            values = []
            for plane in range(RIM):
                value = source[pl.ds((KEPT + plane) * GRID_X + 8 * chunk, 8), :]
                values.append(pltpu.roll(value, (plane * EXT_Z + 2 * column_z) & (LANE - 1), 1))
            totals = []
            for block in range(RIM_BLOCKS):
                total = jnp.zeros((8, LANE), jnp.float32)
                for plane in range(RIM):
                    begin = plane * EXT_Z - block * LANE
                    if begin >= LANE or begin + EXT_Z <= 0:
                        continue
                    total = jnp.where((lane >= begin) & (lane < begin + EXT_Z), values[plane], total)
                totals.append(total)
            for block in range(RIM_BLOCKS):
                target[pl.ds(block * EXT_X + 8 * chunk, size), :] = totals[block][:size]


def turned(value, step_z):
    return pltpu.roll(value, step_z % LANE, 1) if step_z else value


def drifts_of(columns, depth):
    _, _, column_z = place()
    lane = lanes()
    total_y = SPAN_Y * columns
    total_z = SPAN_Z * depth
    spin = 0.2 / (total_y + total_z)
    here_z = jnp.where(lane < SPAN_Z + 8, lane, lane - LANE) + column_z * SPAN_Z
    drift_y = -spin * (here_z.astype(jnp.float32) - (total_z - 1) / 2.0)
    return drift_y, spin, (total_y - 1) / 2.0


def first_step(columns, depth, field, later, begin, end, last):
    _, column_y, _ = place()
    drift_y, spin, centre_y = drifts_of(columns, depth)
    sublane = lax.broadcasted_iota(jnp.int32, (8, LANE), 0)

    def tile(base, drift_z):
        old = [field[pl.ds(i * FIELD + base, 8), :] for i in range(POPS)]
        values = streamed(pull_from(field, base), old, total_of(old), drift_y, drift_z)
        post, _ = collide(values)
        wall = old[0] < WALL_BELOW
        for i in range(POPS):
            later[pl.ds(i * FIELD + base, 8), :] = jnp.where(wall, old[i], post[i])

    def drift_at(y):
        return spin * ((y + column_y * SPAN_Y).astype(jnp.float32) - centre_y)

    def between(y):
        return jnp.where(sublane < 6, drift_at(y - 1), drift_at(y))

    def row(line, carry):
        y = line - 2
        base = pl.multiple_of(line * PITCH + (FIRST - 2 * PITCH), 8)
        tile(base - 8, between(y))
        for xc in range(STEP - 1):
            tile(base + 8 * xc, drift_at(y))
        return carry

    lax.fori_loop(begin + 2, end + 2, row, 0)
    if last:
        tile(FIRST + end * PITCH - 8, between(jnp.int32(end)))


def pull_from(field, base):
    def pull(i):
        step_x, step_y, step_z = VELOCITIES[i]
        return turned(field[pl.ds(i * FIELD + base - step_y * PITCH - step_x, 8), :], step_z)

    return pull


def settle_all(layers, columns, depth, own, edge, zall, zedge, field, later, turn):
    layer, _, column_z = place()
    masks = Lanes(column_z)
    lane = lanes()
    group_of = [((lane >> 4) & (BZD - 1)) == bz for bz in range(BZD)]
    inside_box = inside_lanes(8, column_z)
    inside_halo = inside_lanes(4, column_z) & halo_x_inside(layer, layers)

    def relay(chunk, yhi, inside, leave):
        for plane in range(PLANES):
            parts, zvalue = plane_parts(own, edge, zall, zedge, chunk, yhi, plane)
            size = zvalue.shape[0]
            main = masks.main[:size]
            for r in range(4):
                both = None
                for bz in range(BZD):
                    shift = (bz - r) * EDGE % LANE
                    value = pltpu.roll(parts[bz], shift, 1) if shift else parts[bz]
                    both = value if both is None else jnp.where(group_of[bz][:size], value, both)
                beyond = pltpu.roll(zvalue, masks.to_halo(r, plane % 8), 1)
                turn[pl.ds((plane * YLO + r) * 8, size), :] = jnp.where(main, both, beyond)
                turn[pl.ds((plane * YLO + r + 4) * 8, size), :] = jnp.where(main, beyond, both)
        for ylo in range(YLO):
            values = [turn[pl.ds((plane * YLO + ylo) * 8, size), :] for plane in range(PLANES)]
            if ylo >= 4:
                values = [pltpu.roll(value, SPAN_Z, 1) for value in values]
            leave(ylo, walled(values[:POPS], values[POPS], inside))

    def halves(yhi, carry):
        def chunks(chunk, carry):
            def leave(ylo, values):
                row = pl.multiple_of(FIRST + (YLO * yhi + ylo) * PITCH + 8 * chunk, 8)
                for i in range(POPS):
                    field[pl.ds(i * FIELD + row, 8), :] = values[i]

            relay(chunk, yhi, inside_box, leave)
            return carry

        lax.fori_loop(0, SPAN_X // 8, chunks, 0)

        def leave(ylo, values):
            row = FIRST + (YLO * yhi + ylo) * PITCH
            for i in range(POPS):
                field[pl.ds(i * FIELD + row - 2, 2), :] = values[i][:2]
                field[pl.ds(i * FIELD + row + SPAN_X, 2), :] = values[i][2:]

        relay(None, yhi, inside_halo, leave)
        return carry

    lax.fori_loop(0, SPAN_Y // YLO, halves, 0)
    first_step(columns, depth, field, later, 1, SPAN_Y - 1, False)


def finish(layers, columns, depth, rim_low, rim_high, field_in, later_in, out, field, later, low, high, turn, result, sems):
    del field_in, later_in
    layer, column_y, column_z = place()
    flat = (lanes() + 2 * column_z) & (LANE - 1)
    sides = (
        (rim_low, low, -1, RIM_UP, RIM_DOWN, column_y > 0),
        (rim_high, high, SPAN_Y, RIM_DOWN, RIM_UP, column_y < columns - 1),
    )
    sublane = lax.broadcasted_iota(jnp.int32, (8, LANE), 0)
    for source, ready, y, rim, _, there in sides:
        for chunk in range(5):
            size = min(8, EXT_X - 8 * chunk)
            blocks = [source[pl.ds(block * EXT_X + 8 * chunk, 8), :] for block in range(RIM_BLOCKS)]
            values = []
            for plane in range(RIM):
                block, begin = divmod(plane * EXT_Z, LANE)
                shift = (2 * LANE - begin - 2 * column_z) & (LANE - 1)
                value = pltpu.roll(blocks[block], shift, 1)
                if begin + EXT_Z > LANE:
                    value = jnp.where(flat < LANE - begin, value, pltpu.roll(blocks[block + 1], shift, 1))
                values.append(value)
            inside = (flat < EXT_Z) & there
            if chunk == 0:
                inside = inside & ((sublane >= 2) | (layer > 0))
            if chunk == 4:
                inside = inside & ((sublane < 2) | (layer < layers - 1))
            for n in range(STREAMED + 1):
                ready[pl.ds(n * GRID_X + 8 * chunk, 8), :] = values[n]
            for i, value in zip(rim, walled(values[STREAMED + 1 : RIM - 1], values[RIM - 1], inside)):
                field[pl.ds(i * FIELD + FIRST + y * PITCH - 2 + 8 * chunk, size), :] = value[:size]

    first_step(columns, depth, field, later, 0, 1, True)
    first_step(columns, depth, field, later, SPAN_Y - 1, SPAN_Y, True)
    drift_y, spin, centre_y = drifts_of(columns, depth)
    for _, ready, y, rim, away, _ in sides:
        drift_z = spin * ((column_y * SPAN_Y + y).astype(jnp.float32) - centre_y)
        for chunk in range(5):
            first = 1 + 8 * chunk
            base = FIRST + y * PITCH - 2 + first
            old = {i: field[pl.ds(i * FIELD + base, 8), :] for i in rim}
            rho = ready[pl.ds(STREAMED * GRID_X + first, 8), :]
            values = streamed(pull_from(field, base), old, rho, drift_y, drift_z, away)
            for n, i in enumerate([i for i in range(POPS) if i not in away]):
                values[i] = ready[pl.ds(n * GRID_X + first, 8), :]
            post, _ = collide(values)
            wall = old[rim[0]] < WALL_BELOW
            size = min(8, EXT_X - 1 - first)
            for i in rim:
                later[pl.ds(i * FIELD + base, size), :] = jnp.where(wall, old[i], post[i])[:size]

    drift_y, spin, centre_y = drifts_of(columns, depth)

    def leave(chunk, half):
        part = (slice(None), pl.ds(chunk * 8, 8), pl.ds(half * 8, 8))
        return pltpu.make_async_copy(result.at[part], out.at[part], sems.at[chunk, half])

    def second_step(chunk, carry):
        for half in range(SPAN_Y // 8):
            for k in range(8):
                y = 8 * half + k
                base = pl.multiple_of(FIRST + y * PITCH + 8 * chunk, 8)
                drift_z = spin * ((column_y * SPAN_Y + y).astype(jnp.float32) - centre_y)
                old = [later[pl.ds(i * FIELD + base, 8), :] for i in range(POPS)]
                values = streamed(pull_from(later, base), old, total_of(old), drift_y, drift_z)
                wall = old[0] < WALL_BELOW
                for i in range(POPS):
                    value = jnp.where(wall, old[i] * (1.0 / ROTOR), values[i])
                    turn[pl.ds(i * 8 * TURN + k * TURN, 8), :] = value
            for k in range(8):
                values = [turn[pl.ds(i * 8 * TURN + k, 8, stride=TURN), :] for i in range(POPS)]
                for i in range(POPS):
                    result[i, 8 * chunk + k, 8 * half : 8 * half + 8, :] = values[i][:, :SPAN_Z]
            leave(chunk, half).start()
        return carry

    lax.fori_loop(0, SPAN_X // 8, second_step, 0)
    for chunk in range(SPAN_X // 8):
        for half in range(SPAN_Y // 8):
            leave(chunk, half).wait()


def rows_of(count):
    return jax.ShapeDtypeStruct((count, LANE), jnp.float32)


def kept(count):
    return VMEM((count, LANE), jnp.float32)


def params(mib):
    return pltpu.CompilerParams(vmem_limit_bytes=mib * 2**20)


def shards(populations, solid_cells, block_pos):
    layers = lax.axis_size("stream")
    columns = lax.axis_size("cy")
    depth = lax.axis_size("cz")
    rows = block_pos.shape[0]
    vmem = pl.BlockSpec(memory_space=VMEM)
    hbm = pl.BlockSpec(memory_space=pltpu.HBM)
    populations = pltpu.with_memory_space_constraint(populations, pltpu.HBM)
    solid_cells = pltpu.with_memory_space_constraint(solid_cells, pltpu.HBM)
    places = pltpu.with_memory_space_constraint(block_pos.T, pltpu.HBM)
    place_scratch = SMEM((3, rows), jnp.int32)
    table_scratch = SMEM((LAYERS * BZD,), jnp.int32)
    mark_scratch = [VMEM((rows, EDGE**3), jnp.int32), VMEM((rows * TILES, LANE), jnp.float32)]

    up = [(i, i + 1) for i in range(layers - 1)]
    down = [(i + 1, i) for i in range(layers - 1)]
    send_up, send_down = pl.pallas_call(
        pack_stream,
        out_shape=(kept(SENT_ROWS), kept(SENT_ROWS)),
        in_specs=[hbm, hbm, hbm],
        out_specs=(vmem, vmem),
        scratch_shapes=[place_scratch, table_scratch]
        + mark_scratch
        + [
            VMEM((2 * MOVE_CAP, POPS, EDGE**3), jnp.float32),
            VMEM((2 * BZD, POPS, SLAB * LANE), jnp.float32),
            VMEM((PLANES * 2 * FACE, LANE), jnp.float32),
            pltpu.SemaphoreType.DMA((2 + 2 * MOVE_CAP + 2 * BZD,)),
        ],
        compiler_params=params(16),
        name="pack_stream",
    )(places, solid_cells, populations)
    from_low = lax.ppermute(send_up, "stream", up)
    from_high = lax.ppermute(send_down, "stream", down)

    own, zpack, zsend_up, zsend_down = pl.pallas_call(
        pack_edge,
        out_shape=(kept(LAYERS * BZD * BLOCK), kept(ZMETA + 8), kept(DIAG), kept(DIAG)),
        in_specs=[hbm, hbm, hbm],
        out_specs=(vmem,) * 4,
        scratch_shapes=[place_scratch, table_scratch]
        + mark_scratch
        + [
            VMEM((LAYERS, POPS, EDGE**3), jnp.float32),
            pltpu.SemaphoreType.DMA((LAYERS + 2,)),
        ],
        compiler_params=params(16),
        name="pack_edge",
    )(places, solid_cells, populations)
    swap = [(i, depth - 1 - i) for i in range(depth)]
    zin = lax.ppermute(zpack, "cz", swap)
    zup_pairs = [(s * depth + c, t * depth + d) for s, t in up for c, d in swap]
    zdown_pairs = [(s * depth + c, t * depth + d) for s, t in down for c, d in swap]
    z_low = lax.ppermute(zsend_up, ("stream", "cz"), zup_pairs)
    z_high = lax.ppermute(zsend_down, ("stream", "cz"), zdown_pairs)

    own, edge_own, flags = pl.pallas_call(
        pack_own,
        out_shape=(kept(LAYERS * BZD * BLOCK), kept(PLANES * 4 * FACE), kept(2 * FACE)),
        in_specs=[hbm, hbm, hbm, vmem],
        out_specs=(vmem,) * 3,
        scratch_shapes=[place_scratch, table_scratch]
        + mark_scratch
        + [
            VMEM((rows, POPS, EDGE**3), jnp.float32),
            pltpu.SemaphoreType.DMA((rows + 2,)),
        ],
        input_output_aliases={3: 0},
        compiler_params=params(16),
        name="pack_own",
    )(places, solid_cells, populations, own)

    own, edge, zall, zedge, rim_up, rim_down = pl.pallas_call(
        functools.partial(settle_rim, layers, columns, depth),
        out_shape=(
            kept(LAYERS * BZD * BLOCK),
            kept(PLANES * 4 * FACE),
            kept(LAYERS * ZROWS),
            kept(ZGROUPS * 8),
            kept(RIM_ROWS),
            kept(RIM_ROWS),
        ),
        in_specs=[vmem] * 8,
        out_specs=(vmem,) * 6,
        scratch_shapes=[
            VMEM(((KEPT + RIM) * GRID_X, LANE), jnp.float32),
            VMEM(((KEPT + RIM) * GRID_X, LANE), jnp.float32),
        ],
        input_output_aliases={7: 0},
        compiler_params=params(16),
        name="settle_rim",
    )(from_low, from_high, zin, z_low, z_high, edge_own, flags, own)
    cy_up = [(i, i + 1) for i in range(columns - 1)]
    cy_down = [(i + 1, i) for i in range(columns - 1)]
    rim_low = lax.ppermute(rim_up, "cy", cy_up)
    rim_high = lax.ppermute(rim_down, "cy", cy_down)

    field, later = pl.pallas_call(
        functools.partial(settle_all, layers, columns, depth),
        out_shape=(kept(POPS * FIELD), kept(POPS * FIELD)),
        in_specs=[vmem] * 4,
        out_specs=(vmem,) * 2,
        scratch_shapes=[VMEM((PLANES * YLO * 8, LANE), jnp.float32)],
        compiler_params=params(16),
        name="settle_all",
    )(own, edge, zall, zedge)

    out, _, _ = pl.pallas_call(
        functools.partial(finish, layers, columns, depth),
        out_shape=(
            jax.ShapeDtypeStruct((POPS, SPAN_X, SPAN_Y, SPAN_Z), jnp.float32),
            kept(POPS * FIELD),
            kept(POPS * FIELD),
        ),
        in_specs=[vmem] * 4,
        out_specs=(hbm, vmem, vmem),
        scratch_shapes=[
            VMEM(((STREAMED + 1) * GRID_X, LANE), jnp.float32),
            VMEM(((STREAMED + 1) * GRID_X, LANE), jnp.float32),
            VMEM((POPS * 8 * TURN, LANE), jnp.float32),
            VMEM((POPS, SPAN_X, SPAN_Y, SPAN_Z), jnp.float32),
            pltpu.SemaphoreType.DMA((SPAN_X // 8, SPAN_Y // 8)),
        ],
        input_output_aliases={2: 1, 3: 2},
        compiler_params=params(16),
        name="finish",
    )(rim_low, rim_high, field, later)
    return out


def solution(mesh):
    in_specs = (
        P(("stream", "cy", "cz"), None, None),
        P(("stream", "cy", "cz"), None),
        P(("stream", "cy", "cz"), None),
    )
    out_specs = P(None, "stream", "cy", "cz")
    return jax.shard_map(shards, mesh=mesh, in_specs=in_specs, out_specs=out_specs, check_vma=False)
```

```python
import functools

import jax
import jax.numpy as jnp
from jax import lax
from jax.experimental import pallas as pl
from jax.experimental.pallas import tpu as pltpu
from jax.sharding import PartitionSpec as P

EDGE = 16
BXD = 2
BYD = 1
BZD = 4
MOVE_CAP = 2

VELOCITIES = (
    (0, 0, 0),
    (1, 0, 0),
    (-1, 0, 0),
    (0, 1, 0),
    (0, -1, 0),
    (0, 0, 1),
    (0, 0, -1),
    (1, 1, 0),
    (-1, -1, 0),
    (1, -1, 0),
    (-1, 1, 0),
    (1, 0, 1),
    (-1, 0, -1),
    (1, 0, -1),
    (-1, 0, 1),
    (0, 1, 1),
    (0, -1, -1),
    (0, 1, -1),
    (0, -1, 1),
)
WEIGHTS = (1.0 / 3.0,) + (1.0 / 18.0,) * 6 + (1.0 / 36.0,) * 12
OPPOSITE = (0, 2, 1, 4, 3, 6, 5, 8, 7, 10, 9, 12, 11, 14, 13, 16, 15, 18, 17)
OMEGA_EVEN = 1.25
OMEGA_ODD = 1.0 / 1.125

POPS = 19
PLANES = 20
LANE = 128
TILES = EDGE**3 // LANE
BLOCK = PLANES * TILES
YLO = LANE // EDGE
SLAB = 4
ODD = TILES + 1
STRIP = 2 * 2 * BZD + 1
GROUPS = ((0, 8), (8, 8), (16, 3))
SENT_SLABS = MOVE_CAP * BLOCK
LAYERS = BXD + 2
ZGROUPS = 3
ZROWS = ZGROUPS * TILES
ZMETA = LAYERS * ZROWS
DIAG = ZROWS + ZGROUPS * SLAB

SPAN_X = BXD * EDGE
SPAN_Y = BYD * EDGE
SPAN_Z = BZD * EDGE
PITCH = SPAN_X + 8
STEP = PITCH // 8
FIRST = 96
FIELD = FIRST + (SPAN_Y + 1) * PITCH + 48
TURN = 9
EXT_X = SPAN_X + 4
EXT_Z = SPAN_Z + 2
RIM_UP = tuple(i for i in range(POPS) if VELOCITIES[i][1] == 1)
RIM_DOWN = tuple(i for i in range(POPS) if VELOCITIES[i][1] == -1)
TOWARD = len(RIM_UP)
SLAB_PLANES = PLANES + TOWARD + 1
STREAMED = POPS - TOWARD
RIM = STREAMED + 1 + TOWARD + 1
KEPT = POPS + TOWARD
AHEAD = tuple(i for i in range(POPS) if VELOCITIES[i][0] == 1)
BACK = tuple(i for i in range(POPS) if VELOCITIES[i][0] == -1)
FACE = 2 * BZD
SENT_META = SENT_SLABS + SLAB_PLANES * FACE
SENT_ROWS = SENT_META + 8
RIM_BLOCKS = -(-RIM * EXT_Z // LANE)
RIM_ROWS = RIM_BLOCKS * EXT_X + 4
GRID_X = 48

ROTOR = -(2.0**100)
OUTSIDE = -(2.0**110)
WALL_BELOW = -(2.0**80)
OUT_BELOW = -(2.0**105)

VMEM = pltpu.VMEM
SMEM = pltpu.SMEM


def lanes():
    return lax.broadcasted_iota(jnp.int32, (8, LANE), 1)


def collide(f):
    even = [None] * POPS
    odd = [None] * POPS
    for i in range(1, POPS, 2):
        even[i] = f[i] + f[i + 1]
        odd[i] = f[i] - f[i + 1]
    density = f[0]
    for i in range(1, POPS, 2):
        density = density + even[i]
    flow = []
    for axis in range(3):
        total = None
        for i in range(1, POPS, 2):
            sign = VELOCITIES[i][axis]
            if sign == 0:
                continue
            if total is None:
                total = odd[i] if sign == 1 else -odd[i]
            else:
                total = total + odd[i] if sign == 1 else total - odd[i]
        flow.append(total)
    inverse = 1.0 / density
    velocity = [part * inverse for part in flow]
    square = velocity[0] * velocity[0] + velocity[1] * velocity[1] + velocity[2] * velocity[2]
    base = density * (1.0 - 1.5 * square)
    post = [None] * POPS
    post[0] = (1.0 - OMEGA_EVEN) * f[0] + (OMEGA_EVEN * WEIGHTS[0]) * base
    shared = {}
    for weight in (WEIGHTS[1], WEIGHTS[7]):
        shared[weight] = ((OMEGA_EVEN * weight) * base, (OMEGA_EVEN * weight * 4.5) * density,
                          (OMEGA_ODD * weight * 3.0) * density)
    for i in range(1, POPS, 2):
        projected = None
        for axis in range(3):
            sign = VELOCITIES[i][axis]
            if sign == 0:
                continue
            if projected is None:
                projected = velocity[axis] if sign == 1 else -velocity[axis]
            else:
                projected = projected + velocity[axis] if sign == 1 else projected - velocity[axis]
        low, curve, slope = shared[WEIGHTS[i]]
        even_part = (0.5 - 0.5 * OMEGA_EVEN) * even[i] + (low + curve * (projected * projected))
        odd_part = (0.5 - 0.5 * OMEGA_ODD) * odd[i] + slope * projected
        post[i] = even_part + odd_part
        post[i + 1] = even_part - odd_part
    return post, density


def pushes(density, drift_y, drift_z):
    along_y = density * drift_y
    along_z = density * drift_z
    out = [None] * POPS
    for i in range(1, POPS):
        _, step_y, step_z = VELOCITIES[i]
        total = None
        for sign, part in ((step_y, along_y), (step_z, along_z)):
            if sign == 0:
                continue
            if total is None:
                total = part if sign == 1 else -part
            else:
                total = total + part if sign == 1 else total - part
        if total is not None:
            out[i] = (6.0 * WEIGHTS[i]) * total
    return out


def total_of(parts):
    parts = list(parts)
    while len(parts) > 1:
        pairs = [parts[n] + parts[n + 1] for n in range(0, len(parts) - 1, 2)]
        parts = pairs + parts[len(parts) - len(parts) % 2 :]
    return parts[0]


def streamed(pull, own, density, drift_y, drift_z, wanted=range(POPS)):
    push = pushes(density, drift_y, drift_z)
    out = {}
    for i in wanted:
        if i == 0:
            out[i] = own[0]
            continue
        pulled = pull(i)
        bounced = own[OPPOSITE[i]]
        blocked = pulled < WALL_BELOW
        if push[i] is not None:
            bounced = jnp.where(pulled < OUT_BELOW, bounced, bounced + push[i])
        out[i] = jnp.where(blocked, bounced, pulled)
    return out


def place():
    return lax.axis_index("stream"), lax.axis_index("cy"), lax.axis_index("cz")


def slot_of(pos, row, layer, column_z):
    slot = (pos[0, row] - (layer * BXD - 1)) * BZD + (pos[2, row] - column_z * BZD)
    return jnp.clip(slot, 0, LAYERS * BZD - 1)


def fill_table(pos, table):
    layer, _, column_z = place()
    for entry in range(LAYERS * BZD):
        table[entry] = -1
    for row in range(pos.shape[1]):

        @pl.when(pos[0, row] >= 0)
        def _(row=row):
            table[slot_of(pos, row, layer, column_z)] = row


def spread_marks(marks, dense):
    rows = marks.shape[0]
    for first in range(0, rows, 8):
        size = min(8, rows - first)
        for begin in range(0, TILES, 8):
            values = [marks[first : first + size, t * LANE : (t + 1) * LANE] for t in range(begin, begin + 8)]
            for k, value in enumerate(values):
                dense[pl.ds(first * ODD + begin + k, size, stride=ODD), :] = value.astype(jnp.float32)


def pack_block(out, base, stage, dense, row, raw):
    for first in range(0, TILES, 4):
        moves = []
        for tile in range(first, first + 4):
            for group, size in GROUPS:
                value = stage[group : group + size, tile * LANE : (tile + 1) * LANE]
                moves.append((pl.ds(group * ODD + tile, size, stride=ODD), value))
        for target, value in moves:
            raw[target, :] = value
    for part in range(TILES // 8):
        old = [raw[pl.ds(i * ODD + 8 * part, 8), :] for i in range(POPS)]
        mark = dense[pl.ds(row * ODD + 8 * part, 8), :]
        post, _ = collide(old)
        for i in range(POPS):
            out[pl.ds(base + i * TILES + 8 * part, 8), :] = jnp.where(mark > 0.5, old[i], post[i])
        out[pl.ds(base + POPS * TILES + 8 * part, 8), :] = mark


def pack_stream(places, marks_in, pops, up, down, pos, table, marks, dense, raw, blocks, slabs, strip, sems):
    mark_copy = pltpu.make_async_copy(marks_in, marks, sems.at[0])
    mark_copy.start()
    place_copy = pltpu.make_async_copy(places, pos, sems.at[1])
    place_copy.start()
    rows = pos.shape[1]
    copies = [None] * 4
    for j in range(MOVE_CAP):
        copies[MOVE_CAP + j] = pltpu.make_async_copy(pops.at[j], blocks.at[MOVE_CAP + j], sems.at[2 + MOVE_CAP + j])
        copies[MOVE_CAP + j].start()
    place_copy.wait()
    count = 0
    for row in range(rows):
        count = count + jnp.where(pos[0, row] >= 0, 1, 0)
    last = jnp.clip(count - MOVE_CAP, 0, rows - MOVE_CAP)
    for j in range(MOVE_CAP):
        copies[j] = pltpu.make_async_copy(pops.at[last + j], blocks.at[j], sems.at[2 + j])
        copies[j].start()
    fill_table(pos, table)
    slab_rows = []
    slab_copies = []
    for side in range(2):
        for bz in range(BZD):
            row = jnp.maximum(table[(2 - side) * BZD + bz], 0)
            n = side * BZD + bz
            first = (TILES - SLAB) * LANE if side == 0 else 0
            slab_rows.append(row)
            slab_copies.append(
                pltpu.make_async_copy(
                    pops.at[row, :, pl.ds(first, SLAB * LANE)], slabs.at[n], sems.at[2 + 2 * MOVE_CAP + n]
                )
            )
            slab_copies[n].start()
    mark_copy.wait()
    spread_marks(marks, dense)
    for side, out in ((1, down), (0, up)):
        for j in range(MOVE_CAP):
            row = j if side == 1 else last + j
            for k, axis in ((0, 0), (1, 2)):
                value = jnp.full((1, LANE), pos[axis, row], jnp.int32).astype(jnp.float32)
                out[pl.ds(SENT_META + 2 * j + k, 1), :] = value
            n = side * MOVE_CAP + j
            copies[n].wait()
            pack_block(out, j * BLOCK, blocks.at[n], dense, row, raw)
    for side, out in enumerate((up, down)):
        for bz in range(BZD):
            n = side * BZD + bz
            first = slab_rows[n] * ODD + (TILES - SLAB if side == 0 else 0)
            slab_copies[n].wait()
            moves = []
            for x in range(2):
                for yhi in range(2):
                    q = 2 * x + yhi
                    row = x * FACE + 2 * bz + yhi
                    for group, size in GROUPS:
                        value = slabs[n, group : group + size, q * LANE : (q + 1) * LANE]
                        moves.append((pl.ds(group * STRIP + row, size, stride=STRIP), value))
                row = POPS * STRIP + x * FACE + 2 * bz
                moves.append((pl.ds(row, 2), dense[pl.ds(first + 2 * x, 2), :]))
            for target, value in moves:
                strip[target, :] = value
        inner = 1 if side == 0 else 0
        for x in range(2):
            old = [strip[pl.ds(i * STRIP + x * FACE, FACE), :] for i in range(POPS)]
            mark = strip[pl.ds(POPS * STRIP + x * FACE, FACE), :] > 0.5
            post, _ = collide(old)
            if x == inner:
                pairs = [(i, i) for i in range(POPS)]
                marks_at = POPS
            else:
                pairs = [(PLANES + n, i) for n, i in enumerate(AHEAD if side == 0 else BACK)]
                marks_at = SLAB_PLANES - 1
            for plane, i in pairs:
                out[pl.ds(SENT_SLABS + plane * FACE, FACE), :] = jnp.where(mark, old[i], post[i])
            marks_of = strip[pl.ds(POPS * STRIP + x * FACE, FACE), :]
            out[pl.ds(SENT_SLABS + marks_at * FACE, FACE), :] = marks_of


def pack_edge(places, marks_in, pops, own, zpack, zup, zdown, pos, table, marks, dense, raw, stage, sems):
    column_z = lax.axis_index("cz")
    mark_copy = pltpu.make_async_copy(marks_in, marks, sems.at[LAYERS])
    mark_copy.start()
    place_copy = pltpu.make_async_copy(places, pos, sems.at[LAYERS + 1])
    place_copy.start()
    place_copy.wait()
    fill_table(pos, table)
    edge_bz = jnp.where(column_z == 0, BZD - 1, 0)
    first_c = jnp.where(column_z == 0, EDGE - 2, 0)
    found = [table[held * BZD + edge_bz] for held in range(LAYERS)]
    row_of = [jnp.maximum(row, 0) for row in found]
    copies = []
    for held in range(LAYERS):
        copies.append(pltpu.make_async_copy(pops.at[row_of[held]], stage.at[held], sems.at[held]))
        copies[held].start()
    mark_copy.wait()
    spread_marks(marks, dense)
    spot = (lanes() & (EDGE - 1)) >> 1
    sublane = lax.broadcasted_iota(jnp.int32, (8, LANE), 0)
    flags = jnp.zeros((8, LANE), jnp.int32)
    for held in range(LAYERS):
        copies[held].wait()
        base = pl.multiple_of((held * BZD + edge_bz) * BLOCK, 8)

        @pl.when(found[held] >= 0)
        def _(held=held, base=base):
            pack_block(own, base, stage.at[held], dense, row_of[held], raw)
            totals = []
            for group in range(ZGROUPS):
                for part in range(TILES // 8):
                    total = jnp.zeros((8, LANE), jnp.float32)
                    for k in range(min(8, PLANES - group * 8)):
                        value = own[pl.ds(base + (group * 8 + k) * TILES + part * 8, 8), :]
                        value = pltpu.roll(value, (2 * k - first_c + LANE) & (LANE - 1), 1)
                        total = jnp.where(spot == k, value, total)
                    totals.append((held * ZROWS + group * TILES + part * 8, total))
            for row, total in totals:
                zpack[pl.ds(row, 8), :] = total

        flags = jnp.where((sublane == held) & (found[held] >= 0), 1, flags)
    zpack[pl.ds(ZMETA, 8), :] = flags.astype(jnp.float32)
    zup[pl.ds(0, ZROWS), :] = zpack[pl.ds(3 * ZROWS, ZROWS), :]
    zdown[pl.ds(0, ZROWS), :] = zpack[pl.ds(0, ZROWS), :]
    for group in range(ZGROUPS):
        target = pl.ds(ZROWS + group * SLAB, SLAB)
        zup[target, :] = zpack[pl.ds(2 * ZROWS + group * TILES + TILES - SLAB, SLAB), :]
        zdown[target, :] = zpack[pl.ds(ZROWS + group * TILES, SLAB), :]


def pack_own(places, marks_in, pops, own_in, own, edge, flags, pos, table, marks, dense, raw, stage, sems):
    del own_in
    layer, _, column_z = place()
    edge_bz = jnp.where(column_z == 0, BZD - 1, 0)
    rows = pos.shape[1]
    mark_copy = pltpu.make_async_copy(marks_in, marks, sems.at[rows])
    mark_copy.start()
    place_copy = pltpu.make_async_copy(places, pos, sems.at[rows + 1])
    place_copy.start()
    copies = [pltpu.make_async_copy(pops.at[r], stage.at[r], sems.at[r]) for r in range(rows)]
    for copy in copies:
        copy.start()
    mark_copy.wait()
    spread_marks(marks, dense)
    place_copy.wait()

    def settle(row, carry):
        pltpu.make_async_copy(pops.at[row], stage.at[row], sems.at[row]).wait()
        slot = slot_of(pos, row, layer, column_z)

        @pl.when((pos[0, row] >= 0) & (slot % BZD != edge_bz))
        def _():
            pack_block(own, pl.multiple_of(slot * BLOCK, 8), stage.at[row], dense, row, raw)

        return carry

    lax.fori_loop(0, rows, settle, 0)
    fill_table(pos, table)
    line = lax.broadcasted_iota(jnp.int32, (FACE, LANE), 0) >> 1
    for side in range(2):
        here = jnp.zeros((FACE, LANE), jnp.int32)
        for bz in range(BZD):
            goal = (0 if side == 0 else LAYERS - 1) * BZD + bz
            present = table[goal] >= 0
            here = jnp.where((line == bz) & present, 1, here)

            @pl.when(present)
            def _(side=side, goal=goal, bz=bz):
                first = goal * BLOCK + (TILES - SLAB if side == 0 else 0)
                values = []
                for _, i, x in slab_planes(side):
                    shift = 2 * (x if side == 0 else x - 2)
                    values.append(own[pl.ds(first + i * TILES + shift, 2), :])
                for (_, i, x), value in zip(slab_planes(side), values):
                    edge[pl.ds((i * 4 + x) * FACE + 2 * bz, 2), :] = value

        flags[pl.ds(side * FACE, FACE), :] = here.astype(jnp.float32)


def slab_planes(side):
    inner, outer = (1, 0) if side == 0 else (2, 3)
    pairs = [(i, i, inner) for i in range(PLANES)]
    return pairs + [(PLANES + n, i, outer) for n, i in enumerate((AHEAD if side == 0 else BACK) + (POPS,))]


class Lanes:
    def __init__(self, column_z):
        lane = lanes()
        self.from_bz = [lane >= bz * EDGE for bz in range(BZD)]
        self.main = lane < SPAN_Z
        self.goal = jnp.where(column_z == 0, SPAN_Z, LANE - 2)

    def to_halo(self, ylo, spot):
        return (self.goal - (ylo * EDGE + 2 * spot) + LANE) & (LANE - 1)


def gathered(parts, zvalue, spot, ylo, masks):
    rows = parts[0].shape[0]
    total = None
    for bz in range(BZD):
        shift = (bz * EDGE - ylo * EDGE) % LANE
        value = pltpu.roll(parts[bz], shift, 1) if shift else parts[bz]
        total = value if total is None else jnp.where(masks.from_bz[bz][:rows], value, total)
    beyond = pltpu.roll(zvalue, masks.to_halo(ylo, spot), 1)
    return jnp.where(masks.main[:rows], total, beyond)


def inside_lanes(rows, column_z):
    lane = lanes()[:rows]
    low = (column_z == 0) & (lane >= SPAN_Z) & (lane < SPAN_Z + 2)
    high = (column_z != 0) & (lane >= LANE - 2)
    return (lane < SPAN_Z) | low | high


def walled(values, mark, inside):
    factor = jnp.where(mark > 0.5, ROTOR, 1.0)
    cap = jnp.where(inside, -OUTSIDE, OUTSIDE)
    return [jnp.minimum(value * factor, cap) for value in values]


def plane_parts(own, edge, zall, zedge, chunk, yhi, plane):
    group = plane >> 3
    if chunk is None:
        first = plane * 4 * FACE + yhi
        parts = [edge[pl.ds(first + 2 * bz, 4, stride=FACE), :] for bz in range(BZD)]
        return parts, zedge[pl.ds(group * 8 + yhi, 4, stride=2), :]
    held, half = 1 + (chunk >> 1), chunk & 1
    first = held * (BZD * BLOCK) + half * EDGE + yhi
    parts = [own[pl.ds(first + bz * BLOCK + plane * TILES, 8, stride=2), :] for bz in range(BZD)]
    first = held * ZROWS + half * EDGE + yhi
    return parts, zall[pl.ds(first + group * TILES, 8, stride=2), :]


def chunk_values(own, edge, zall, zedge, chunk, yhi, rows, masks):
    out = [[] for _ in rows]
    for plane in range(PLANES):
        taken = [n for n, (_, planes) in enumerate(rows) if plane in planes]
        if taken:
            parts, zvalue = plane_parts(own, edge, zall, zedge, chunk, yhi, plane)
        for n in taken:
            out[n].append(gathered(parts, zvalue, plane % 8, rows[n][0], masks))
    return out


def halo_x_inside(layer, layers):
    row = lax.broadcasted_iota(jnp.int32, (4, LANE), 0)
    low = (row < 2) & (layer > 0)
    high = (row >= 2) & (layer < layers - 1)
    return low | high


def settle_rim(layers, columns, depth, up, down, zin, zup, zdown, edge_own, flags, own_in, own, edge, zall, zedge, rim_up, rim_down, post_up, post_down):
    del own_in
    layer, column_y, column_z = place()
    codes = []
    for arrived in (up, down):
        first = layer == 0 if arrived is up else layer == layers - 1
        for j in range(MOVE_CAP):
            bx = arrived[pl.ds(SENT_META + 2 * j, 1), :].astype(jnp.int32)
            bz = arrived[pl.ds(SENT_META + 2 * j + 1, 1), :].astype(jnp.int32)
            code = (bx - layer * BXD) * BZD + (bz - column_z * BZD)
            mine = (bx >= layer * BXD) & (bx < (layer + 1) * BXD) & jnp.logical_not(first)
            codes.append((arrived, j, jnp.max(jnp.where(mine, code, -1))))
    for arrived, j, code in codes:

        @pl.when(code >= 0)
        def _(arrived=arrived, j=j, code=code):
            base = pl.multiple_of((jnp.clip(code, 0, BXD * BZD - 1) + BZD) * BLOCK, 8)
            for k in range(0, BLOCK, 128):
                values = [arrived[pl.ds(j * BLOCK + k + 8 * n, 8), :] for n in range(16)]
                for n, value in enumerate(values):
                    own[pl.ds(base + k + 8 * n, 8), :] = value

    for side, arrived in enumerate((up, down)):
        here = flags[pl.ds(side * FACE, FACE), :] > 0.5
        values = []
        for plane, i, x in slab_planes(side):
            row = (i * 4 + x) * FACE
            other = arrived[pl.ds(SENT_SLABS + plane * FACE, FACE), :]
            values.append((row, jnp.where(here, edge_own[pl.ds(row, FACE), :], other)))
        for row, value in values:
            edge[pl.ds(row, FACE), :] = value
    moves = []
    for held in range(LAYERS):
        flag = zin[pl.ds(ZMETA + held, 1), :] > 0.5
        for group in range(ZGROUPS):
            if held == 1 or held == 2:
                for part in range(TILES // 8):
                    rows = pl.ds(held * ZROWS + group * TILES + part * 8, 8)
                    source = zup if held == 1 else zdown
                    other = source[pl.ds(group * TILES + part * 8, 8), :]
                    moves.append((zall, rows, jnp.where(flag, zin[rows, :], other)))
            else:
                side = 0 if held == 0 else 1
                source = zup if held == 0 else zdown
                first = TILES - SLAB if held == 0 else 0
                mine = zin[pl.ds(held * ZROWS + group * TILES + first, SLAB), :]
                other = source[pl.ds(ZROWS + group * SLAB, SLAB), :]
                moves.append((zedge, pl.ds(group * 8 + side * SLAB, SLAB), jnp.where(flag, mine, other)))
    for target, rows, value in moves:
        target[rows, :] = value
    masks = Lanes(column_z)
    inside_box = inside_lanes(8, column_z)
    inside_halo = inside_lanes(4, column_z) & halo_x_inside(layer, layers)
    sides = ((0, 1, RIM_DOWN, RIM_UP, post_down), (SPAN_Y - 1, SPAN_Y - 2, RIM_UP, RIM_DOWN, post_up))
    for chunk in (0, 1, 2, 3, None):
        inside = inside_halo if chunk is None else inside_box
        for near, far, rim, _, target in sides:
            rows = ((near % YLO, range(PLANES)), (far % YLO, rim + (POPS,)))
            first, second = chunk_values(own, edge, zall, zedge, chunk, near // YLO, rows, masks)
            planes = walled(first[:POPS], first[POPS], inside)
            planes += walled(second[:TOWARD], second[TOWARD], inside)
            sent = [first[i] for i in rim] + [first[POPS]]
            spots = list(range(KEPT)) + [KEPT + STREAMED + 1 + n for n in range(len(sent))]
            for plane, value in zip(spots, planes + sent):
                row = plane * GRID_X
                if chunk is None:
                    target[pl.ds(row, 2), :] = value[:2]
                    target[pl.ds(row + EXT_X - 2, 2), :] = value[2:]
                else:
                    target[pl.ds(row + 2 + 8 * chunk, 8), :] = value
    drift_y, spin, centre_y = drifts_of(columns, depth)
    for near, _, rim, away, target in sides:
        drift_z = spin * ((column_y * SPAN_Y + near).astype(jnp.float32) - centre_y)
        wanted = [i for i in range(POPS) if i not in away]
        plane_of = {i: POPS + rim.index(i) if i in rim else i for i in wanted}
        for chunk in range(5):
            first = 1 + 8 * chunk

            def pull(i):
                step_x, _, step_z = VELOCITIES[i]
                return turned(target[pl.ds(plane_of[i] * GRID_X + first - step_x, 8), :], step_z)

            old = [target[pl.ds(i * GRID_X + first, 8), :] for i in range(POPS)]
            rho = total_of(old)
            values = streamed(pull, old, rho, drift_y, drift_z, wanted)
            size = min(8, EXT_X - 1 - first)
            for n, value in enumerate([values[i] for i in wanted] + [rho]):
                target[pl.ds((KEPT + n) * GRID_X + first, size), :] = value[:size]
    lane = lanes()
    for source, target in ((post_up, rim_up), (post_down, rim_down)):
        for chunk in range(5):
            size = min(8, EXT_X - 8 * chunk)
            values = []
            for plane in range(RIM):
                value = source[pl.ds((KEPT + plane) * GRID_X + 8 * chunk, 8), :]
                values.append(pltpu.roll(value, (plane * EXT_Z + 2 * column_z) & (LANE - 1), 1))
            totals = []
            for block in range(RIM_BLOCKS):
                total = jnp.zeros((8, LANE), jnp.float32)
                for plane in range(RIM):
                    begin = plane * EXT_Z - block * LANE
                    if begin >= LANE or begin + EXT_Z <= 0:
                        continue
                    total = jnp.where((lane >= begin) & (lane < begin + EXT_Z), values[plane], total)
                totals.append(total)
            for block in range(RIM_BLOCKS):
                target[pl.ds(block * EXT_X + 8 * chunk, size), :] = totals[block][:size]


def turned(value, step_z):
    return pltpu.roll(value, step_z % LANE, 1) if step_z else value


def drifts_of(columns, depth):
    _, _, column_z = place()
    lane = lanes()
    total_y = SPAN_Y * columns
    total_z = SPAN_Z * depth
    spin = 0.2 / (total_y + total_z)
    here_z = jnp.where(lane < SPAN_Z + 8, lane, lane - LANE) + column_z * SPAN_Z
    drift_y = -spin * (here_z.astype(jnp.float32) - (total_z - 1) / 2.0)
    return drift_y, spin, (total_y - 1) / 2.0


def first_step(columns, depth, field, later, begin, end, last):
    _, column_y, _ = place()
    drift_y, spin, centre_y = drifts_of(columns, depth)
    sublane = lax.broadcasted_iota(jnp.int32, (8, LANE), 0)

    def tile(base, drift_z):
        old = [field[pl.ds(i * FIELD + base, 8), :] for i in range(POPS)]
        values = streamed(pull_from(field, base), old, total_of(old), drift_y, drift_z)
        post, _ = collide(values)
        wall = old[0] < WALL_BELOW
        for i in range(POPS):
            later[pl.ds(i * FIELD + base, 8), :] = jnp.where(wall, old[i], post[i])

    def drift_at(y):
        return spin * ((y + column_y * SPAN_Y).astype(jnp.float32) - centre_y)

    def between(y):
        return jnp.where(sublane < 6, drift_at(y - 1), drift_at(y))

    def row(line, carry):
        y = line - 2
        base = pl.multiple_of(line * PITCH + (FIRST - 2 * PITCH), 8)
        tile(base - 8, between(y))
        for xc in range(STEP - 1):
            tile(base + 8 * xc, drift_at(y))
        return carry

    lax.fori_loop(begin + 2, end + 2, row, 0)
    if last:
        tile(FIRST + end * PITCH - 8, between(jnp.int32(end)))


def pull_from(field, base):
    def pull(i):
        step_x, step_y, step_z = VELOCITIES[i]
        return turned(field[pl.ds(i * FIELD + base - step_y * PITCH - step_x, 8), :], step_z)

    return pull


def settle_all(layers, columns, depth, own, edge, zall, zedge, field, later, turn):
    layer, _, column_z = place()
    masks = Lanes(column_z)
    lane = lanes()
    group_of = [((lane >> 4) & (BZD - 1)) == bz for bz in range(BZD)]
    inside_box = inside_lanes(8, column_z)
    inside_halo = inside_lanes(4, column_z) & halo_x_inside(layer, layers)

    def relay(chunk, yhi, inside, leave):
        for plane in range(PLANES):
            parts, zvalue = plane_parts(own, edge, zall, zedge, chunk, yhi, plane)
            size = zvalue.shape[0]
            main = masks.main[:size]
            for r in range(4):
                both = None
                for bz in range(BZD):
                    shift = (bz - r) * EDGE % LANE
                    value = pltpu.roll(parts[bz], shift, 1) if shift else parts[bz]
                    both = value if both is None else jnp.where(group_of[bz][:size], value, both)
                beyond = pltpu.roll(zvalue, masks.to_halo(r, plane % 8), 1)
                turn[pl.ds((plane * YLO + r) * 8, size), :] = jnp.where(main, both, beyond)
                turn[pl.ds((plane * YLO + r + 4) * 8, size), :] = jnp.where(main, beyond, both)
        for ylo in range(YLO):
            values = [turn[pl.ds((plane * YLO + ylo) * 8, size), :] for plane in range(PLANES)]
            if ylo >= 4:
                values = [pltpu.roll(value, SPAN_Z, 1) for value in values]
            leave(ylo, walled(values[:POPS], values[POPS], inside))

    def halves(yhi, carry):
        def chunks(chunk, carry):
            def leave(ylo, values):
                row = pl.multiple_of(FIRST + (YLO * yhi + ylo) * PITCH + 8 * chunk, 8)
                for i in range(POPS):
                    field[pl.ds(i * FIELD + row, 8), :] = values[i]

            relay(chunk, yhi, inside_box, leave)
            return carry

        lax.fori_loop(0, SPAN_X // 8, chunks, 0)

        def leave(ylo, values):
            row = FIRST + (YLO * yhi + ylo) * PITCH
            for i in range(POPS):
                field[pl.ds(i * FIELD + row - 2, 2), :] = values[i][:2]
                field[pl.ds(i * FIELD + row + SPAN_X, 2), :] = values[i][2:]

        relay(None, yhi, inside_halo, leave)
        return carry

    lax.fori_loop(0, SPAN_Y // YLO, halves, 0)
    first_step(columns, depth, field, later, 1, SPAN_Y - 1, False)


def finish(layers, columns, depth, rim_low, rim_high, field_in, later_in, out, field, later, low, high, turn, result, sems):
    del field_in, later_in
    layer, column_y, column_z = place()
    flat = (lanes() + 2 * column_z) & (LANE - 1)
    sides = (
        (rim_low, low, -1, RIM_UP, RIM_DOWN, column_y > 0),
        (rim_high, high, SPAN_Y, RIM_DOWN, RIM_UP, column_y < columns - 1),
    )
    sublane = lax.broadcasted_iota(jnp.int32, (8, LANE), 0)
    for source, ready, y, rim, _, there in sides:
        for chunk in range(5):
            size = min(8, EXT_X - 8 * chunk)
            blocks = [source[pl.ds(block * EXT_X + 8 * chunk, 8), :] for block in range(RIM_BLOCKS)]
            values = []
            for plane in range(RIM):
                block, begin = divmod(plane * EXT_Z, LANE)
                shift = (2 * LANE - begin - 2 * column_z) & (LANE - 1)
                value = pltpu.roll(blocks[block], shift, 1)
                if begin + EXT_Z > LANE:
                    value = jnp.where(flat < LANE - begin, value, pltpu.roll(blocks[block + 1], shift, 1))
                values.append(value)
            inside = (flat < EXT_Z) & there
            if chunk == 0:
                inside = inside & ((sublane >= 2) | (layer > 0))
            if chunk == 4:
                inside = inside & ((sublane < 2) | (layer < layers - 1))
            for n in range(STREAMED + 1):
                ready[pl.ds(n * GRID_X + 8 * chunk, 8), :] = values[n]
            for i, value in zip(rim, walled(values[STREAMED + 1 : RIM - 1], values[RIM - 1], inside)):
                field[pl.ds(i * FIELD + FIRST + y * PITCH - 2 + 8 * chunk, size), :] = value[:size]

    first_step(columns, depth, field, later, 0, 1, True)
    first_step(columns, depth, field, later, SPAN_Y - 1, SPAN_Y, True)
    drift_y, spin, centre_y = drifts_of(columns, depth)
    for _, ready, y, rim, away, _ in sides:
        drift_z = spin * ((column_y * SPAN_Y + y).astype(jnp.float32) - centre_y)
        for chunk in range(5):
            first = 1 + 8 * chunk
            base = FIRST + y * PITCH - 2 + first
            old = {i: field[pl.ds(i * FIELD + base, 8), :] for i in rim}
            rho = ready[pl.ds(STREAMED * GRID_X + first, 8), :]
            values = streamed(pull_from(field, base), old, rho, drift_y, drift_z, away)
            for n, i in enumerate([i for i in range(POPS) if i not in away]):
                values[i] = ready[pl.ds(n * GRID_X + first, 8), :]
            post, _ = collide(values)
            wall = old[rim[0]] < WALL_BELOW
            size = min(8, EXT_X - 1 - first)
            for i in rim:
                later[pl.ds(i * FIELD + base, size), :] = jnp.where(wall, old[i], post[i])[:size]

    drift_y, spin, centre_y = drifts_of(columns, depth)

    def leave(chunk, half):
        part = (slice(None), pl.ds(chunk * 8, 8), pl.ds(half * 8, 8))
        return pltpu.make_async_copy(result.at[part], out.at[part], sems.at[chunk, half])

    def second_step(chunk, carry):
        for half in range(SPAN_Y // 8):
            for k in range(8):
                y = 8 * half + k
                base = pl.multiple_of(FIRST + y * PITCH + 8 * chunk, 8)
                drift_z = spin * ((column_y * SPAN_Y + y).astype(jnp.float32) - centre_y)
                old = [later[pl.ds(i * FIELD + base, 8), :] for i in range(POPS)]
                values = streamed(pull_from(later, base), old, total_of(old), drift_y, drift_z)
                wall = old[0] < WALL_BELOW
                for i in range(POPS):
                    value = jnp.where(wall, old[i] * (1.0 / ROTOR), values[i])
                    turn[pl.ds(i * 8 * TURN + k * TURN, 8), :] = value
            for k in range(8):
                values = [turn[pl.ds(i * 8 * TURN + k, 8, stride=TURN), :] for i in range(POPS)]
                for i in range(POPS):
                    result[i, 8 * chunk + k, 8 * half : 8 * half + 8, :] = values[i][:, :SPAN_Z]
            leave(chunk, half).start()
        return carry

    lax.fori_loop(0, SPAN_X // 8, second_step, 0)
    for chunk in range(SPAN_X // 8):
        for half in range(SPAN_Y // 8):
            leave(chunk, half).wait()


def rows_of(count):
    return jax.ShapeDtypeStruct((count, LANE), jnp.float32)


def kept(count):
    return VMEM((count, LANE), jnp.float32)


def params(mib):
    return pltpu.CompilerParams(vmem_limit_bytes=mib * 2**20)


def shards(populations, solid_cells, block_pos):
    layers = lax.axis_size("stream")
    columns = lax.axis_size("cy")
    depth = lax.axis_size("cz")
    rows = block_pos.shape[0]
    vmem = pl.BlockSpec(memory_space=VMEM)
    hbm = pl.BlockSpec(memory_space=pltpu.HBM)
    populations = pltpu.with_memory_space_constraint(populations, pltpu.HBM)
    solid_cells = pltpu.with_memory_space_constraint(solid_cells, pltpu.HBM)
    places = pltpu.with_memory_space_constraint(block_pos.T, pltpu.HBM)
    place_scratch = SMEM((3, rows), jnp.int32)
    table_scratch = SMEM((LAYERS * BZD,), jnp.int32)
    mark_scratch = [
        VMEM((rows, EDGE**3), jnp.int32),
        VMEM((rows * ODD, LANE), jnp.float32),
        VMEM((POPS * ODD, LANE), jnp.float32),
    ]

    up = [(i, i + 1) for i in range(layers - 1)]
    down = [(i + 1, i) for i in range(layers - 1)]
    send_up, send_down = pl.pallas_call(
        pack_stream,
        out_shape=(kept(SENT_ROWS), kept(SENT_ROWS)),
        in_specs=[hbm, hbm, hbm],
        out_specs=(vmem, vmem),
        scratch_shapes=[place_scratch, table_scratch]
        + mark_scratch
        + [
            VMEM((2 * MOVE_CAP, POPS, EDGE**3), jnp.float32),
            VMEM((2 * BZD, POPS, SLAB * LANE), jnp.float32),
            VMEM((PLANES * STRIP, LANE), jnp.float32),
            pltpu.SemaphoreType.DMA((2 + 2 * MOVE_CAP + 2 * BZD,)),
        ],
        compiler_params=params(16),
        name="pack_stream",
    )(places, solid_cells, populations)
    from_low = lax.ppermute(send_up, "stream", up)
    from_high = lax.ppermute(send_down, "stream", down)

    own, zpack, zsend_up, zsend_down = pl.pallas_call(
        pack_edge,
        out_shape=(kept(LAYERS * BZD * BLOCK), kept(ZMETA + 8), kept(DIAG), kept(DIAG)),
        in_specs=[hbm, hbm, hbm],
        out_specs=(vmem,) * 4,
        scratch_shapes=[place_scratch, table_scratch]
        + mark_scratch
        + [
            VMEM((LAYERS, POPS, EDGE**3), jnp.float32),
            pltpu.SemaphoreType.DMA((LAYERS + 2,)),
        ],
        compiler_params=params(16),
        name="pack_edge",
    )(places, solid_cells, populations)
    swap = [(i, depth - 1 - i) for i in range(depth)]
    zin = lax.ppermute(zpack, "cz", swap)
    zup_pairs = [(s * depth + c, t * depth + d) for s, t in up for c, d in swap]
    zdown_pairs = [(s * depth + c, t * depth + d) for s, t in down for c, d in swap]
    z_low = lax.ppermute(zsend_up, ("stream", "cz"), zup_pairs)
    z_high = lax.ppermute(zsend_down, ("stream", "cz"), zdown_pairs)

    own, edge_own, flags = pl.pallas_call(
        pack_own,
        out_shape=(kept(LAYERS * BZD * BLOCK), kept(PLANES * 4 * FACE), kept(2 * FACE)),
        in_specs=[hbm, hbm, hbm, vmem],
        out_specs=(vmem,) * 3,
        scratch_shapes=[place_scratch, table_scratch]
        + mark_scratch
        + [
            VMEM((rows, POPS, EDGE**3), jnp.float32),
            pltpu.SemaphoreType.DMA((rows + 2,)),
        ],
        input_output_aliases={3: 0},
        compiler_params=params(16),
        name="pack_own",
    )(places, solid_cells, populations, own)

    own, edge, zall, zedge, rim_up, rim_down = pl.pallas_call(
        functools.partial(settle_rim, layers, columns, depth),
        out_shape=(
            kept(LAYERS * BZD * BLOCK),
            kept(PLANES * 4 * FACE),
            kept(LAYERS * ZROWS),
            kept(ZGROUPS * 8),
            kept(RIM_ROWS),
            kept(RIM_ROWS),
        ),
        in_specs=[vmem] * 8,
        out_specs=(vmem,) * 6,
        scratch_shapes=[
            VMEM(((KEPT + RIM) * GRID_X, LANE), jnp.float32),
            VMEM(((KEPT + RIM) * GRID_X, LANE), jnp.float32),
        ],
        input_output_aliases={7: 0},
        compiler_params=params(16),
        name="settle_rim",
    )(from_low, from_high, zin, z_low, z_high, edge_own, flags, own)
    cy_up = [(i, i + 1) for i in range(columns - 1)]
    cy_down = [(i + 1, i) for i in range(columns - 1)]
    rim_low = lax.ppermute(rim_up, "cy", cy_up)
    rim_high = lax.ppermute(rim_down, "cy", cy_down)

    field, later = pl.pallas_call(
        functools.partial(settle_all, layers, columns, depth),
        out_shape=(kept(POPS * FIELD), kept(POPS * FIELD)),
        in_specs=[vmem] * 4,
        out_specs=(vmem,) * 2,
        scratch_shapes=[VMEM((PLANES * YLO * 8, LANE), jnp.float32)],
        compiler_params=params(16),
        name="settle_all",
    )(own, edge, zall, zedge)

    out, _, _ = pl.pallas_call(
        functools.partial(finish, layers, columns, depth),
        out_shape=(
            jax.ShapeDtypeStruct((POPS, SPAN_X, SPAN_Y, SPAN_Z), jnp.float32),
            kept(POPS * FIELD),
            kept(POPS * FIELD),
        ),
        in_specs=[vmem] * 4,
        out_specs=(hbm, vmem, vmem),
        scratch_shapes=[
            VMEM(((STREAMED + 1) * GRID_X, LANE), jnp.float32),
            VMEM(((STREAMED + 1) * GRID_X, LANE), jnp.float32),
            VMEM((POPS * 8 * TURN, LANE), jnp.float32),
            VMEM((POPS, SPAN_X, SPAN_Y, SPAN_Z), jnp.float32),
            pltpu.SemaphoreType.DMA((SPAN_X // 8, SPAN_Y // 8)),
        ],
        input_output_aliases={2: 1, 3: 2},
        compiler_params=params(16),
        name="finish",
    )(rim_low, rim_high, field, later)
    return out


def solution(mesh):
    in_specs = (
        P(("stream", "cy", "cz"), None, None),
        P(("stream", "cy", "cz"), None),
        P(("stream", "cy", "cz"), None),
    )
    out_specs = P(None, "stream", "cy", "cz")
    return jax.shard_map(shards, mesh=mesh, in_specs=in_specs, out_specs=out_specs, check_vma=False)
```

```python
import functools

import jax
import jax.numpy as jnp
from jax import lax
from jax.experimental import pallas as pl
from jax.experimental.pallas import tpu as pltpu
from jax.sharding import PartitionSpec as P

EDGE = 16
BXD = 2
BYD = 1
BZD = 4
MOVE_CAP = 2

VELOCITIES = (
    (0, 0, 0),
    (1, 0, 0),
    (-1, 0, 0),
    (0, 1, 0),
    (0, -1, 0),
    (0, 0, 1),
    (0, 0, -1),
    (1, 1, 0),
    (-1, -1, 0),
    (1, -1, 0),
    (-1, 1, 0),
    (1, 0, 1),
    (-1, 0, -1),
    (1, 0, -1),
    (-1, 0, 1),
    (0, 1, 1),
    (0, -1, -1),
    (0, 1, -1),
    (0, -1, 1),
)
WEIGHTS = (1.0 / 3.0,) + (1.0 / 18.0,) * 6 + (1.0 / 36.0,) * 12
OPPOSITE = (0, 2, 1, 4, 3, 6, 5, 8, 7, 10, 9, 12, 11, 14, 13, 16, 15, 18, 17)
OMEGA_EVEN = 1.25
OMEGA_ODD = 1.0 / 1.125

POPS = 19
PLANES = 20
LANE = 128
TILES = EDGE**3 // LANE
BLOCK = PLANES * TILES
YLO = LANE // EDGE
SLAB = 4
ODD = TILES + 1
STRIP = 2 * 2 * BZD + 1
GROUPS = ((0, 8), (8, 8), (16, 3))
SENT_SLABS = MOVE_CAP * BLOCK
LAYERS = BXD + 2
ZGROUPS = 3
ZROWS = ZGROUPS * TILES
ZMETA = LAYERS * ZROWS
DIAG = ZROWS + ZGROUPS * SLAB

SPAN_X = BXD * EDGE
SPAN_Y = BYD * EDGE
SPAN_Z = BZD * EDGE
PITCH = SPAN_X + 8
STEP = PITCH // 8
FIRST = 96
FIELD = FIRST + (SPAN_Y + 1) * PITCH + 48
TURN = 9
EXT_X = SPAN_X + 4
EXT_Z = SPAN_Z + 2
RIM_UP = tuple(i for i in range(POPS) if VELOCITIES[i][1] == 1)
RIM_DOWN = tuple(i for i in range(POPS) if VELOCITIES[i][1] == -1)
TOWARD = len(RIM_UP)
SLAB_PLANES = PLANES + TOWARD + 1
STREAMED = POPS - TOWARD
RIM = STREAMED + 1 + TOWARD + 1
KEPT = POPS + TOWARD
AHEAD = tuple(i for i in range(POPS) if VELOCITIES[i][0] == 1)
BACK = tuple(i for i in range(POPS) if VELOCITIES[i][0] == -1)
FACE = 2 * BZD
SENT_META = SENT_SLABS + SLAB_PLANES * FACE
SENT_ROWS = SENT_META + 8
RIM_BLOCKS = -(-RIM * EXT_Z // LANE)
RIM_ROWS = RIM_BLOCKS * EXT_X + 4
GRID_X = 48

ROTOR = -(2.0**100)
OUTSIDE = -(2.0**110)
WALL_BELOW = -(2.0**80)
OUT_BELOW = -(2.0**105)

VMEM = pltpu.VMEM
SMEM = pltpu.SMEM


def lanes():
    return lax.broadcasted_iota(jnp.int32, (8, LANE), 1)


def collide(f):
    even = [None] * POPS
    odd = [None] * POPS
    for i in range(1, POPS, 2):
        even[i] = f[i] + f[i + 1]
        odd[i] = f[i] - f[i + 1]
    density = f[0]
    for i in range(1, POPS, 2):
        density = density + even[i]
    flow = []
    for axis in range(3):
        total = None
        for i in range(1, POPS, 2):
            sign = VELOCITIES[i][axis]
            if sign == 0:
                continue
            if total is None:
                total = odd[i] if sign == 1 else -odd[i]
            else:
                total = total + odd[i] if sign == 1 else total - odd[i]
        flow.append(total)
    inverse = 1.0 / density
    velocity = [part * inverse for part in flow]
    square = velocity[0] * velocity[0] + velocity[1] * velocity[1] + velocity[2] * velocity[2]
    base = density * (1.0 - 1.5 * square)
    post = [None] * POPS
    post[0] = (1.0 - OMEGA_EVEN) * f[0] + (OMEGA_EVEN * WEIGHTS[0]) * base
    shared = {}
    for weight in (WEIGHTS[1], WEIGHTS[7]):
        shared[weight] = ((OMEGA_EVEN * weight) * base, (OMEGA_EVEN * weight * 4.5) * density,
                          (OMEGA_ODD * weight * 3.0) * density)
    for i in range(1, POPS, 2):
        projected = None
        for axis in range(3):
            sign = VELOCITIES[i][axis]
            if sign == 0:
                continue
            if projected is None:
                projected = velocity[axis] if sign == 1 else -velocity[axis]
            else:
                projected = projected + velocity[axis] if sign == 1 else projected - velocity[axis]
        low, curve, slope = shared[WEIGHTS[i]]
        even_part = (0.5 - 0.5 * OMEGA_EVEN) * even[i] + (low + curve * (projected * projected))
        odd_part = (0.5 - 0.5 * OMEGA_ODD) * odd[i] + slope * projected
        post[i] = even_part + odd_part
        post[i + 1] = even_part - odd_part
    return post, density


def pushes(density, drift_y, drift_z):
    along_y = density * drift_y
    along_z = density * drift_z
    out = [None] * POPS
    for i in range(1, POPS):
        _, step_y, step_z = VELOCITIES[i]
        total = None
        for sign, part in ((step_y, along_y), (step_z, along_z)):
            if sign == 0:
                continue
            if total is None:
                total = part if sign == 1 else -part
            else:
                total = total + part if sign == 1 else total - part
        if total is not None:
            out[i] = (6.0 * WEIGHTS[i]) * total
    return out


def total_of(parts):
    parts = list(parts)
    while len(parts) > 1:
        pairs = [parts[n] + parts[n + 1] for n in range(0, len(parts) - 1, 2)]
        parts = pairs + parts[len(parts) - len(parts) % 2 :]
    return parts[0]


def streamed(pull, own, density, drift_y, drift_z, wanted=range(POPS)):
    push = pushes(density, drift_y, drift_z)
    out = {}
    for i in wanted:
        if i == 0:
            out[i] = own[0]
            continue
        pulled = pull(i)
        bounced = own[OPPOSITE[i]]
        blocked = pulled < WALL_BELOW
        if push[i] is not None:
            bounced = jnp.where(pulled < OUT_BELOW, bounced, bounced + push[i])
        out[i] = jnp.where(blocked, bounced, pulled)
    return out


def place():
    return lax.axis_index("stream"), lax.axis_index("cy"), lax.axis_index("cz")


def slot_of(pos, row, layer, column_z):
    slot = (pos[0, row] - (layer * BXD - 1)) * BZD + (pos[2, row] - column_z * BZD)
    return jnp.clip(slot, 0, LAYERS * BZD - 1)


def fill_table(pos, table):
    layer, _, column_z = place()
    for entry in range(LAYERS * BZD):
        table[entry] = -1
    for row in range(pos.shape[1]):

        @pl.when(pos[0, row] >= 0)
        def _(row=row):
            table[slot_of(pos, row, layer, column_z)] = row


def spread_marks(marks, dense):
    rows = marks.shape[0]
    for first in range(0, rows, 8):
        size = min(8, rows - first)
        for begin in range(0, TILES, 8):
            values = [marks[first : first + size, t * LANE : (t + 1) * LANE] for t in range(begin, begin + 8)]
            for k, value in enumerate(values):
                dense[pl.ds(first * ODD + begin + k, size, stride=ODD), :] = value.astype(jnp.float32)


def pack_block(out, base, stage, dense, row, raw):
    for first in range(0, TILES, 4):
        moves = []
        for tile in range(first, first + 4):
            for group, size in GROUPS:
                value = stage[group : group + size, tile * LANE : (tile + 1) * LANE]
                moves.append((pl.ds(group * ODD + tile, size, stride=ODD), value))
        for target, value in moves:
            raw[target, :] = value
    for part in range(TILES // 8):
        old = [raw[pl.ds(i * ODD + 8 * part, 8), :] for i in range(POPS)]
        mark = dense[pl.ds(row * ODD + 8 * part, 8), :]
        post, _ = collide(old)
        for i in range(POPS):
            out[pl.ds(base + i * TILES + 8 * part, 8), :] = jnp.where(mark > 0.5, old[i], post[i])
        out[pl.ds(base + POPS * TILES + 8 * part, 8), :] = mark


def pack_stream(places, marks_in, pops, up, down, pos, table, marks, dense, raw, blocks, slabs, strip, sems):
    mark_copy = pltpu.make_async_copy(marks_in, marks, sems.at[0])
    mark_copy.start()
    place_copy = pltpu.make_async_copy(places, pos, sems.at[1])
    place_copy.start()
    rows = pos.shape[1]
    copies = [None] * 4
    for j in range(MOVE_CAP):
        copies[MOVE_CAP + j] = pltpu.make_async_copy(pops.at[j], blocks.at[MOVE_CAP + j], sems.at[2 + MOVE_CAP + j])
        copies[MOVE_CAP + j].start()
    place_copy.wait()
    count = 0
    for row in range(rows):
        count = count + jnp.where(pos[0, row] >= 0, 1, 0)
    last = jnp.clip(count - MOVE_CAP, 0, rows - MOVE_CAP)
    for j in range(MOVE_CAP):
        copies[j] = pltpu.make_async_copy(pops.at[last + j], blocks.at[j], sems.at[2 + j])
        copies[j].start()
    fill_table(pos, table)
    slab_rows = []
    slab_copies = []
    for side in range(2):
        for bz in range(BZD):
            row = jnp.maximum(table[(2 - side) * BZD + bz], 0)
            n = side * BZD + bz
            first = (TILES - SLAB) * LANE if side == 0 else 0
            slab_rows.append(row)
            slab_copies.append(
                pltpu.make_async_copy(
                    pops.at[row, :, pl.ds(first, SLAB * LANE)], slabs.at[n], sems.at[2 + 2 * MOVE_CAP + n]
                )
            )
            slab_copies[n].start()
    mark_copy.wait()
    spread_marks(marks, dense)
    for side, out in ((1, down), (0, up)):
        for j in range(MOVE_CAP):
            row = j if side == 1 else last + j
            for k, axis in ((0, 0), (1, 2)):
                value = jnp.full((1, LANE), pos[axis, row], jnp.int32).astype(jnp.float32)
                out[pl.ds(SENT_META + 2 * j + k, 1), :] = value
            n = side * MOVE_CAP + j
            copies[n].wait()
            pack_block(out, j * BLOCK, blocks.at[n], dense, row, raw)
    for side, out in enumerate((up, down)):
        for bz in range(BZD):
            n = side * BZD + bz
            first = slab_rows[n] * ODD + (TILES - SLAB if side == 0 else 0)
            slab_copies[n].wait()
            moves = []
            for x in range(2):
                for yhi in range(2):
                    q = 2 * x + yhi
                    row = x * FACE + 2 * bz + yhi
                    for group, size in GROUPS:
                        value = slabs[n, group : group + size, q * LANE : (q + 1) * LANE]
                        moves.append((pl.ds(group * STRIP + row, size, stride=STRIP), value))
                row = POPS * STRIP + x * FACE + 2 * bz
                moves.append((pl.ds(row, 2), dense[pl.ds(first + 2 * x, 2), :]))
            for target, value in moves:
                strip[target, :] = value
        inner = 1 if side == 0 else 0
        for x in range(2):
            old = [strip[pl.ds(i * STRIP + x * FACE, FACE), :] for i in range(POPS)]
            mark = strip[pl.ds(POPS * STRIP + x * FACE, FACE), :] > 0.5
            post, _ = collide(old)
            if x == inner:
                pairs = [(i, i) for i in range(POPS)]
                marks_at = POPS
            else:
                pairs = [(PLANES + n, i) for n, i in enumerate(AHEAD if side == 0 else BACK)]
                marks_at = SLAB_PLANES - 1
            for plane, i in pairs:
                out[pl.ds(SENT_SLABS + plane * FACE, FACE), :] = jnp.where(mark, old[i], post[i])
            marks_of = strip[pl.ds(POPS * STRIP + x * FACE, FACE), :]
            out[pl.ds(SENT_SLABS + marks_at * FACE, FACE), :] = marks_of


def pack_edge(places, marks_in, pops, own, zpack, zup, zdown, pos, table, marks, dense, raw, stage, sems):
    column_z = lax.axis_index("cz")
    mark_copy = pltpu.make_async_copy(marks_in, marks, sems.at[LAYERS])
    mark_copy.start()
    place_copy = pltpu.make_async_copy(places, pos, sems.at[LAYERS + 1])
    place_copy.start()
    place_copy.wait()
    fill_table(pos, table)
    edge_bz = jnp.where(column_z == 0, BZD - 1, 0)
    first_c = jnp.where(column_z == 0, EDGE - 2, 0)
    found = [table[held * BZD + edge_bz] for held in range(LAYERS)]
    row_of = [jnp.maximum(row, 0) for row in found]
    copies = []
    for held in range(LAYERS):
        copies.append(pltpu.make_async_copy(pops.at[row_of[held]], stage.at[held], sems.at[held]))
        copies[held].start()
    mark_copy.wait()
    spread_marks(marks, dense)
    spot = (lanes() & (EDGE - 1)) >> 1
    sublane = lax.broadcasted_iota(jnp.int32, (8, LANE), 0)
    flags = jnp.zeros((8, LANE), jnp.int32)
    for held in range(LAYERS):
        copies[held].wait()
        base = pl.multiple_of((held * BZD + edge_bz) * BLOCK, 8)

        @pl.when(found[held] >= 0)
        def _(held=held, base=base):
            pack_block(own, base, stage.at[held], dense, row_of[held], raw)
            totals = []
            for group in range(ZGROUPS):
                for part in range(TILES // 8):
                    total = jnp.zeros((8, LANE), jnp.float32)
                    for k in range(min(8, PLANES - group * 8)):
                        value = own[pl.ds(base + (group * 8 + k) * TILES + part * 8, 8), :]
                        value = pltpu.roll(value, (2 * k - first_c + LANE) & (LANE - 1), 1)
                        total = jnp.where(spot == k, value, total)
                    totals.append((held * ZROWS + group * TILES + part * 8, total))
            for row, total in totals:
                zpack[pl.ds(row, 8), :] = total

        flags = jnp.where((sublane == held) & (found[held] >= 0), 1, flags)
    zpack[pl.ds(ZMETA, 8), :] = flags.astype(jnp.float32)
    zup[pl.ds(0, ZROWS), :] = zpack[pl.ds(3 * ZROWS, ZROWS), :]
    zdown[pl.ds(0, ZROWS), :] = zpack[pl.ds(0, ZROWS), :]
    for group in range(ZGROUPS):
        target = pl.ds(ZROWS + group * SLAB, SLAB)
        zup[target, :] = zpack[pl.ds(2 * ZROWS + group * TILES + TILES - SLAB, SLAB), :]
        zdown[target, :] = zpack[pl.ds(ZROWS + group * TILES, SLAB), :]


def pack_own(places, marks_in, pops, own_in, own, edge, flags, pos, table, marks, dense, raw, stage, sems):
    del own_in
    layer, _, column_z = place()
    edge_bz = jnp.where(column_z == 0, BZD - 1, 0)
    rows = pos.shape[1]
    mark_copy = pltpu.make_async_copy(marks_in, marks, sems.at[rows])
    mark_copy.start()
    place_copy = pltpu.make_async_copy(places, pos, sems.at[rows + 1])
    place_copy.start()
    copies = [pltpu.make_async_copy(pops.at[r], stage.at[r], sems.at[r]) for r in range(rows)]
    for copy in copies:
        copy.start()
    mark_copy.wait()
    spread_marks(marks, dense)
    place_copy.wait()

    def settle(row, carry):
        pltpu.make_async_copy(pops.at[row], stage.at[row], sems.at[row]).wait()
        slot = slot_of(pos, row, layer, column_z)

        @pl.when((pos[0, row] >= 0) & (slot % BZD != edge_bz))
        def _():
            pack_block(own, pl.multiple_of(slot * BLOCK, 8), stage.at[row], dense, row, raw)

        return carry

    lax.fori_loop(0, rows, settle, 0)
    fill_table(pos, table)
    line = lax.broadcasted_iota(jnp.int32, (FACE, LANE), 0) >> 1
    for side in range(2):
        here = jnp.zeros((FACE, LANE), jnp.int32)
        for bz in range(BZD):
            goal = (0 if side == 0 else LAYERS - 1) * BZD + bz
            present = table[goal] >= 0
            here = jnp.where((line == bz) & present, 1, here)

            @pl.when(present)
            def _(side=side, goal=goal, bz=bz):
                first = goal * BLOCK + (TILES - SLAB if side == 0 else 0)
                values = []
                for _, i, x in slab_planes(side):
                    shift = 2 * (x if side == 0 else x - 2)
                    values.append(own[pl.ds(first + i * TILES + shift, 2), :])
                for (_, i, x), value in zip(slab_planes(side), values):
                    edge[pl.ds((i * 4 + x) * FACE + 2 * bz, 2), :] = value

        flags[pl.ds(side * FACE, FACE), :] = here.astype(jnp.float32)


def slab_planes(side):
    inner, outer = (1, 0) if side == 0 else (2, 3)
    pairs = [(i, i, inner) for i in range(PLANES)]
    return pairs + [(PLANES + n, i, outer) for n, i in enumerate((AHEAD if side == 0 else BACK) + (POPS,))]


class Lanes:
    def __init__(self, column_z):
        lane = lanes()
        self.from_bz = [lane >= bz * EDGE for bz in range(BZD)]
        self.main = lane < SPAN_Z
        self.goal = jnp.where(column_z == 0, SPAN_Z, LANE - 2)

    def to_halo(self, ylo, spot):
        return (self.goal - (ylo * EDGE + 2 * spot) + LANE) & (LANE - 1)


def gathered(parts, zvalue, spot, ylo, masks):
    rows = parts[0].shape[0]
    total = None
    for bz in range(BZD):
        shift = (bz * EDGE - ylo * EDGE) % LANE
        value = pltpu.roll(parts[bz], shift, 1) if shift else parts[bz]
        total = value if total is None else jnp.where(masks.from_bz[bz][:rows], value, total)
    beyond = pltpu.roll(zvalue, masks.to_halo(ylo, spot), 1)
    return jnp.where(masks.main[:rows], total, beyond)


def inside_lanes(rows, column_z):
    lane = lanes()[:rows]
    low = (column_z == 0) & (lane >= SPAN_Z) & (lane < SPAN_Z + 2)
    high = (column_z != 0) & (lane >= LANE - 2)
    return (lane < SPAN_Z) | low | high


def walled(values, mark, inside):
    factor = jnp.where(mark > 0.5, ROTOR, 1.0)
    cap = jnp.where(inside, -OUTSIDE, OUTSIDE)
    return [jnp.minimum(value * factor, cap) for value in values]


def plane_parts(own, edge, zall, zedge, chunk, yhi, plane):
    group = plane >> 3
    if chunk is None:
        first = plane * 4 * FACE + yhi
        parts = [edge[pl.ds(first + 2 * bz, 4, stride=FACE), :] for bz in range(BZD)]
        return parts, zedge[pl.ds(group * 8 + yhi, 4, stride=2), :]
    held, half = 1 + (chunk >> 1), chunk & 1
    first = held * (BZD * BLOCK) + half * EDGE + yhi
    parts = [own[pl.ds(first + bz * BLOCK + plane * TILES, 8, stride=2), :] for bz in range(BZD)]
    first = held * ZROWS + half * EDGE + yhi
    return parts, zall[pl.ds(first + group * TILES, 8, stride=2), :]


def chunk_values(own, edge, zall, zedge, chunk, yhi, rows, masks):
    out = [[] for _ in rows]
    for plane in range(PLANES):
        taken = [n for n, (_, planes) in enumerate(rows) if plane in planes]
        if taken:
            parts, zvalue = plane_parts(own, edge, zall, zedge, chunk, yhi, plane)
        for n in taken:
            out[n].append(gathered(parts, zvalue, plane % 8, rows[n][0], masks))
    return out


def halo_x_inside(layer, layers):
    row = lax.broadcasted_iota(jnp.int32, (4, LANE), 0)
    low = (row < 2) & (layer > 0)
    high = (row >= 2) & (layer < layers - 1)
    return low | high


def settle_rim(layers, columns, depth, up, down, zin, zup, zdown, edge_own, flags, own_in, own, edge, zall, zedge, rim_up, rim_down, post_up, post_down):
    del own_in
    layer, column_y, column_z = place()
    codes = []
    for arrived in (up, down):
        first = layer == 0 if arrived is up else layer == layers - 1
        for j in range(MOVE_CAP):
            bx = arrived[pl.ds(SENT_META + 2 * j, 1), :].astype(jnp.int32)
            bz = arrived[pl.ds(SENT_META + 2 * j + 1, 1), :].astype(jnp.int32)
            code = (bx - layer * BXD) * BZD + (bz - column_z * BZD)
            mine = (bx >= layer * BXD) & (bx < (layer + 1) * BXD) & jnp.logical_not(first)
            codes.append((arrived, j, jnp.max(jnp.where(mine, code, -1))))
    for arrived, j, code in codes:

        @pl.when(code >= 0)
        def _(arrived=arrived, j=j, code=code):
            base = pl.multiple_of((jnp.clip(code, 0, BXD * BZD - 1) + BZD) * BLOCK, 8)
            for k in range(0, BLOCK, 128):
                values = [arrived[pl.ds(j * BLOCK + k + 8 * n, 8), :] for n in range(16)]
                for n, value in enumerate(values):
                    own[pl.ds(base + k + 8 * n, 8), :] = value

    for side, arrived in enumerate((up, down)):
        here = flags[pl.ds(side * FACE, FACE), :] > 0.5
        values = []
        for plane, i, x in slab_planes(side):
            row = (i * 4 + x) * FACE
            other = arrived[pl.ds(SENT_SLABS + plane * FACE, FACE), :]
            values.append((row, jnp.where(here, edge_own[pl.ds(row, FACE), :], other)))
        for row, value in values:
            edge[pl.ds(row, FACE), :] = value
    moves = []
    for held in range(LAYERS):
        flag = zin[pl.ds(ZMETA + held, 1), :] > 0.5
        for group in range(ZGROUPS):
            if held == 1 or held == 2:
                for part in range(TILES // 8):
                    rows = pl.ds(held * ZROWS + group * TILES + part * 8, 8)
                    source = zup if held == 1 else zdown
                    other = source[pl.ds(group * TILES + part * 8, 8), :]
                    moves.append((zall, rows, jnp.where(flag, zin[rows, :], other)))
            else:
                side = 0 if held == 0 else 1
                source = zup if held == 0 else zdown
                first = TILES - SLAB if held == 0 else 0
                mine = zin[pl.ds(held * ZROWS + group * TILES + first, SLAB), :]
                other = source[pl.ds(ZROWS + group * SLAB, SLAB), :]
                moves.append((zedge, pl.ds(group * 8 + side * SLAB, SLAB), jnp.where(flag, mine, other)))
    for target, rows, value in moves:
        target[rows, :] = value
    masks = Lanes(column_z)
    inside_box = inside_lanes(8, column_z)
    inside_halo = inside_lanes(4, column_z) & halo_x_inside(layer, layers)
    sides = ((0, 1, RIM_DOWN, RIM_UP, post_down), (SPAN_Y - 1, SPAN_Y - 2, RIM_UP, RIM_DOWN, post_up))
    for chunk in (0, 1, 2, 3, None):
        inside = inside_halo if chunk is None else inside_box
        for near, far, rim, _, target in sides:
            rows = ((near % YLO, range(PLANES)), (far % YLO, rim + (POPS,)))
            first, second = chunk_values(own, edge, zall, zedge, chunk, near // YLO, rows, masks)
            planes = walled(first[:POPS], first[POPS], inside)
            planes += walled(second[:TOWARD], second[TOWARD], inside)
            sent = [first[i] for i in rim] + [first[POPS]]
            spots = list(range(KEPT)) + [KEPT + STREAMED + 1 + n for n in range(len(sent))]
            for plane, value in zip(spots, planes + sent):
                row = plane * GRID_X
                if chunk is None:
                    target[pl.ds(row, 2), :] = value[:2]
                    target[pl.ds(row + EXT_X - 2, 2), :] = value[2:]
                else:
                    target[pl.ds(row + 2 + 8 * chunk, 8), :] = value
    drift_y, spin, centre_y = drifts_of(columns, depth)
    for near, _, rim, away, target in sides:
        drift_z = spin * ((column_y * SPAN_Y + near).astype(jnp.float32) - centre_y)
        wanted = [i for i in range(POPS) if i not in away]
        plane_of = {i: POPS + rim.index(i) if i in rim else i for i in wanted}
        for chunk in range(5):
            first = 1 + 8 * chunk

            def pull(i):
                step_x, _, step_z = VELOCITIES[i]
                return turned(target[pl.ds(plane_of[i] * GRID_X + first - step_x, 8), :], step_z)

            old = [target[pl.ds(i * GRID_X + first, 8), :] for i in range(POPS)]
            rho = total_of(old)
            values = streamed(pull, old, rho, drift_y, drift_z, wanted)
            size = min(8, EXT_X - 1 - first)
            for n, value in enumerate([values[i] for i in wanted] + [rho]):
                target[pl.ds((KEPT + n) * GRID_X + first, size), :] = value[:size]
    lane = lanes()
    for source, target in ((post_up, rim_up), (post_down, rim_down)):
        for chunk in range(5):
            size = min(8, EXT_X - 8 * chunk)
            values = []
            for plane in range(RIM):
                value = source[pl.ds((KEPT + plane) * GRID_X + 8 * chunk, 8), :]
                values.append(pltpu.roll(value, (plane * EXT_Z + 2 * column_z) & (LANE - 1), 1))
            totals = []
            for block in range(RIM_BLOCKS):
                total = jnp.zeros((8, LANE), jnp.float32)
                for plane in range(RIM):
                    begin = plane * EXT_Z - block * LANE
                    if begin >= LANE or begin + EXT_Z <= 0:
                        continue
                    total = jnp.where((lane >= begin) & (lane < begin + EXT_Z), values[plane], total)
                totals.append(total)
            for block in range(RIM_BLOCKS):
                target[pl.ds(block * EXT_X + 8 * chunk, size), :] = totals[block][:size]


def turned(value, step_z):
    return pltpu.roll(value, step_z % LANE, 1) if step_z else value


def drifts_of(columns, depth):
    _, _, column_z = place()
    lane = lanes()
    total_y = SPAN_Y * columns
    total_z = SPAN_Z * depth
    spin = 0.2 / (total_y + total_z)
    here_z = jnp.where(lane < SPAN_Z + 8, lane, lane - LANE) + column_z * SPAN_Z
    drift_y = -spin * (here_z.astype(jnp.float32) - (total_z - 1) / 2.0)
    return drift_y, spin, (total_y - 1) / 2.0


def first_step(columns, depth, field, later, begin, end, last):
    _, column_y, _ = place()
    drift_y, spin, centre_y = drifts_of(columns, depth)
    sublane = lax.broadcasted_iota(jnp.int32, (8, LANE), 0)

    def tile(base, drift_z):
        old = [field[pl.ds(i * FIELD + base, 8), :] for i in range(POPS)]
        values = streamed(pull_from(field, base), old, total_of(old), drift_y, drift_z)
        post, _ = collide(values)
        wall = old[0] < WALL_BELOW
        for i in range(POPS):
            later[pl.ds(i * FIELD + base, 8), :] = jnp.where(wall, old[i], post[i])

    def drift_at(y):
        return spin * ((y + column_y * SPAN_Y).astype(jnp.float32) - centre_y)

    def between(y):
        return jnp.where(sublane < 6, drift_at(y - 1), drift_at(y))

    def row(line, carry):
        y = line - 2
        base = pl.multiple_of(line * PITCH + (FIRST - 2 * PITCH), 8)
        tile(base - 8, between(y))
        for xc in range(STEP - 1):
            tile(base + 8 * xc, drift_at(y))
        return carry

    lax.fori_loop(begin + 2, end + 2, row, 0)
    if last:
        tile(FIRST + end * PITCH - 8, between(jnp.int32(end)))


def pull_from(field, base):
    def pull(i):
        step_x, step_y, step_z = VELOCITIES[i]
        return turned(field[pl.ds(i * FIELD + base - step_y * PITCH - step_x, 8), :], step_z)

    return pull


def settle_all(layers, columns, depth, own, edge, zall, zedge, field, later, half, turn):
    layer, _, column_z = place()
    masks = Lanes(column_z)
    lane = lanes()
    single = (lane & EDGE) != 0
    double = (lane & (2 * EDGE)) != 0
    inside_box = inside_lanes(8, column_z)
    inside_halo = inside_lanes(4, column_z) & halo_x_inside(layer, layers)

    def relay(chunk, yhi, inside, leave):
        for plane in range(PLANES):
            parts, zvalue = plane_parts(own, edge, zall, zedge, chunk, yhi, plane)
            size = zvalue.shape[0]
            for n in range(0, BZD, 2):
                even = jnp.where(single[:size], pltpu.roll(parts[n + 1], EDGE, 1), parts[n])
                odd = jnp.where(single[:size], parts[n + 1], pltpu.roll(parts[n], LANE - EDGE, 1))
                half[pl.ds((plane * 4 + n) * 8, size), :] = even
                half[pl.ds((plane * 4 + n + 1) * 8, size), :] = odd
        main = masks.main[:size]
        for plane in range(PLANES):
            _, zvalue = plane_parts(own, edge, zall, zedge, chunk, yhi, plane)
            for r in range(4):
                low = half[pl.ds((plane * 4 + r % 2) * 8, size), :]
                high = half[pl.ds((plane * 4 + 2 + r % 2) * 8, size), :]
                if r < 2:
                    both = jnp.where(double[:size], pltpu.roll(high, 2 * EDGE, 1), low)
                else:
                    both = jnp.where(double[:size], high, pltpu.roll(low, LANE - 2 * EDGE, 1))
                beyond = pltpu.roll(zvalue, masks.to_halo(r, plane % 8), 1)
                turn[pl.ds((plane * YLO + r) * 8, size), :] = jnp.where(main, both, beyond)
                turn[pl.ds((plane * YLO + r + 4) * 8, size), :] = jnp.where(main, beyond, both)
        for ylo in range(YLO):
            values = [turn[pl.ds((plane * YLO + ylo) * 8, size), :] for plane in range(PLANES)]
            if ylo >= 4:
                values = [pltpu.roll(value, SPAN_Z, 1) for value in values]
            leave(ylo, walled(values[:POPS], values[POPS], inside))

    def halves(yhi, carry):
        def chunks(chunk, carry):
            def leave(ylo, values):
                row = pl.multiple_of(FIRST + (YLO * yhi + ylo) * PITCH + 8 * chunk, 8)
                for i in range(POPS):
                    field[pl.ds(i * FIELD + row, 8), :] = values[i]

            relay(chunk, yhi, inside_box, leave)
            return carry

        lax.fori_loop(0, SPAN_X // 8, chunks, 0)

        def leave(ylo, values):
            row = FIRST + (YLO * yhi + ylo) * PITCH
            for i in range(POPS):
                field[pl.ds(i * FIELD + row - 2, 2), :] = values[i][:2]
                field[pl.ds(i * FIELD + row + SPAN_X, 2), :] = values[i][2:]

        relay(None, yhi, inside_halo, leave)
        return carry

    lax.fori_loop(0, SPAN_Y // YLO, halves, 0)
    first_step(columns, depth, field, later, 1, SPAN_Y - 1, False)


def finish(layers, columns, depth, rim_low, rim_high, field_in, later_in, out, field, later, low, high, turn, result, sems):
    del field_in, later_in
    layer, column_y, column_z = place()
    flat = (lanes() + 2 * column_z) & (LANE - 1)
    sides = (
        (rim_low, low, -1, RIM_UP, RIM_DOWN, column_y > 0),
        (rim_high, high, SPAN_Y, RIM_DOWN, RIM_UP, column_y < columns - 1),
    )
    sublane = lax.broadcasted_iota(jnp.int32, (8, LANE), 0)
    for source, ready, y, rim, _, there in sides:
        for chunk in range(5):
            size = min(8, EXT_X - 8 * chunk)
            blocks = [source[pl.ds(block * EXT_X + 8 * chunk, 8), :] for block in range(RIM_BLOCKS)]
            values = []
            for plane in range(RIM):
                block, begin = divmod(plane * EXT_Z, LANE)
                shift = (2 * LANE - begin - 2 * column_z) & (LANE - 1)
                value = pltpu.roll(blocks[block], shift, 1)
                if begin + EXT_Z > LANE:
                    value = jnp.where(flat < LANE - begin, value, pltpu.roll(blocks[block + 1], shift, 1))
                values.append(value)
            inside = (flat < EXT_Z) & there
            if chunk == 0:
                inside = inside & ((sublane >= 2) | (layer > 0))
            if chunk == 4:
                inside = inside & ((sublane < 2) | (layer < layers - 1))
            for n in range(STREAMED + 1):
                ready[pl.ds(n * GRID_X + 8 * chunk, 8), :] = values[n]
            for i, value in zip(rim, walled(values[STREAMED + 1 : RIM - 1], values[RIM - 1], inside)):
                field[pl.ds(i * FIELD + FIRST + y * PITCH - 2 + 8 * chunk, size), :] = value[:size]

    first_step(columns, depth, field, later, 0, 1, True)
    first_step(columns, depth, field, later, SPAN_Y - 1, SPAN_Y, True)
    drift_y, spin, centre_y = drifts_of(columns, depth)
    for _, ready, y, rim, away, _ in sides:
        drift_z = spin * ((column_y * SPAN_Y + y).astype(jnp.float32) - centre_y)
        for chunk in range(5):
            first = 1 + 8 * chunk
            base = FIRST + y * PITCH - 2 + first
            old = {i: field[pl.ds(i * FIELD + base, 8), :] for i in rim}
            rho = ready[pl.ds(STREAMED * GRID_X + first, 8), :]
            values = streamed(pull_from(field, base), old, rho, drift_y, drift_z, away)
            for n, i in enumerate([i for i in range(POPS) if i not in away]):
                values[i] = ready[pl.ds(n * GRID_X + first, 8), :]
            post, _ = collide(values)
            wall = old[rim[0]] < WALL_BELOW
            size = min(8, EXT_X - 1 - first)
            for i in rim:
                later[pl.ds(i * FIELD + base, size), :] = jnp.where(wall, old[i], post[i])[:size]

    drift_y, spin, centre_y = drifts_of(columns, depth)

    def leave(chunk, half):
        part = (slice(None), pl.ds(chunk * 8, 8), pl.ds(half * 8, 8))
        return pltpu.make_async_copy(result.at[part], out.at[part], sems.at[chunk, half])

    def second_step(chunk, carry):
        for half in range(SPAN_Y // 8):
            for k in range(8):
                y = 8 * half + k
                base = pl.multiple_of(FIRST + y * PITCH + 8 * chunk, 8)
                drift_z = spin * ((column_y * SPAN_Y + y).astype(jnp.float32) - centre_y)
                old = [later[pl.ds(i * FIELD + base, 8), :] for i in range(POPS)]
                values = streamed(pull_from(later, base), old, total_of(old), drift_y, drift_z)
                wall = old[0] < WALL_BELOW
                for i in range(POPS):
                    value = jnp.where(wall, old[i] * (1.0 / ROTOR), values[i])
                    turn[pl.ds(i * 8 * TURN + k * TURN, 8), :] = value
            for k in range(8):
                values = [turn[pl.ds(i * 8 * TURN + k, 8, stride=TURN), :] for i in range(POPS)]
                for i in range(POPS):
                    result[i, 8 * chunk + k, 8 * half : 8 * half + 8, :] = values[i][:, :SPAN_Z]
            leave(chunk, half).start()
        return carry

    lax.fori_loop(0, SPAN_X // 8, second_step, 0)
    for chunk in range(SPAN_X // 8):
        for half in range(SPAN_Y // 8):
            leave(chunk, half).wait()


def rows_of(count):
    return jax.ShapeDtypeStruct((count, LANE), jnp.float32)


def kept(count):
    return VMEM((count, LANE), jnp.float32)


def params(mib):
    return pltpu.CompilerParams(vmem_limit_bytes=mib * 2**20)


def shards(populations, solid_cells, block_pos):
    layers = lax.axis_size("stream")
    columns = lax.axis_size("cy")
    depth = lax.axis_size("cz")
    rows = block_pos.shape[0]
    vmem = pl.BlockSpec(memory_space=VMEM)
    hbm = pl.BlockSpec(memory_space=pltpu.HBM)
    populations = pltpu.with_memory_space_constraint(populations, pltpu.HBM)
    solid_cells = pltpu.with_memory_space_constraint(solid_cells, pltpu.HBM)
    places = pltpu.with_memory_space_constraint(block_pos.T, pltpu.HBM)
    place_scratch = SMEM((3, rows), jnp.int32)
    table_scratch = SMEM((LAYERS * BZD,), jnp.int32)
    mark_scratch = [
        VMEM((rows, EDGE**3), jnp.int32),
        VMEM((rows * ODD, LANE), jnp.float32),
        VMEM((POPS * ODD, LANE), jnp.float32),
    ]

    up = [(i, i + 1) for i in range(layers - 1)]
    down = [(i + 1, i) for i in range(layers - 1)]
    send_up, send_down = pl.pallas_call(
        pack_stream,
        out_shape=(kept(SENT_ROWS), kept(SENT_ROWS)),
        in_specs=[hbm, hbm, hbm],
        out_specs=(vmem, vmem),
        scratch_shapes=[place_scratch, table_scratch]
        + mark_scratch
        + [
            VMEM((2 * MOVE_CAP, POPS, EDGE**3), jnp.float32),
            VMEM((2 * BZD, POPS, SLAB * LANE), jnp.float32),
            VMEM((PLANES * STRIP, LANE), jnp.float32),
            pltpu.SemaphoreType.DMA((2 + 2 * MOVE_CAP + 2 * BZD,)),
        ],
        compiler_params=params(16),
        name="pack_stream",
    )(places, solid_cells, populations)
    from_low = lax.ppermute(send_up, "stream", up)
    from_high = lax.ppermute(send_down, "stream", down)

    own, zpack, zsend_up, zsend_down = pl.pallas_call(
        pack_edge,
        out_shape=(kept(LAYERS * BZD * BLOCK), kept(ZMETA + 8), kept(DIAG), kept(DIAG)),
        in_specs=[hbm, hbm, hbm],
        out_specs=(vmem,) * 4,
        scratch_shapes=[place_scratch, table_scratch]
        + mark_scratch
        + [
            VMEM((LAYERS, POPS, EDGE**3), jnp.float32),
            pltpu.SemaphoreType.DMA((LAYERS + 2,)),
        ],
        compiler_params=params(16),
        name="pack_edge",
    )(places, solid_cells, populations)
    swap = [(i, depth - 1 - i) for i in range(depth)]
    zin = lax.ppermute(zpack, "cz", swap)
    zup_pairs = [(s * depth + c, t * depth + d) for s, t in up for c, d in swap]
    zdown_pairs = [(s * depth + c, t * depth + d) for s, t in down for c, d in swap]
    z_low = lax.ppermute(zsend_up, ("stream", "cz"), zup_pairs)
    z_high = lax.ppermute(zsend_down, ("stream", "cz"), zdown_pairs)

    own, edge_own, flags = pl.pallas_call(
        pack_own,
        out_shape=(kept(LAYERS * BZD * BLOCK), kept(PLANES * 4 * FACE), kept(2 * FACE)),
        in_specs=[hbm, hbm, hbm, vmem],
        out_specs=(vmem,) * 3,
        scratch_shapes=[place_scratch, table_scratch]
        + mark_scratch
        + [
            VMEM((rows, POPS, EDGE**3), jnp.float32),
            pltpu.SemaphoreType.DMA((rows + 2,)),
        ],
        input_output_aliases={3: 0},
        compiler_params=params(16),
        name="pack_own",
    )(places, solid_cells, populations, own)

    own, edge, zall, zedge, rim_up, rim_down = pl.pallas_call(
        functools.partial(settle_rim, layers, columns, depth),
        out_shape=(
            kept(LAYERS * BZD * BLOCK),
            kept(PLANES * 4 * FACE),
            kept(LAYERS * ZROWS),
            kept(ZGROUPS * 8),
            kept(RIM_ROWS),
            kept(RIM_ROWS),
        ),
        in_specs=[vmem] * 8,
        out_specs=(vmem,) * 6,
        scratch_shapes=[
            VMEM(((KEPT + RIM) * GRID_X, LANE), jnp.float32),
            VMEM(((KEPT + RIM) * GRID_X, LANE), jnp.float32),
        ],
        input_output_aliases={7: 0},
        compiler_params=params(16),
        name="settle_rim",
    )(from_low, from_high, zin, z_low, z_high, edge_own, flags, own)
    cy_up = [(i, i + 1) for i in range(columns - 1)]
    cy_down = [(i + 1, i) for i in range(columns - 1)]
    rim_low = lax.ppermute(rim_up, "cy", cy_up)
    rim_high = lax.ppermute(rim_down, "cy", cy_down)

    field, later = pl.pallas_call(
        functools.partial(settle_all, layers, columns, depth),
        out_shape=(kept(POPS * FIELD), kept(POPS * FIELD)),
        in_specs=[vmem] * 4,
        out_specs=(vmem,) * 2,
        scratch_shapes=[
            VMEM((PLANES * 4 * 8, LANE), jnp.float32),
            VMEM((PLANES * YLO * 8, LANE), jnp.float32),
        ],
        compiler_params=params(16),
        name="settle_all",
    )(own, edge, zall, zedge)

    out, _, _ = pl.pallas_call(
        functools.partial(finish, layers, columns, depth),
        out_shape=(
            jax.ShapeDtypeStruct((POPS, SPAN_X, SPAN_Y, SPAN_Z), jnp.float32),
            kept(POPS * FIELD),
            kept(POPS * FIELD),
        ),
        in_specs=[vmem] * 4,
        out_specs=(hbm, vmem, vmem),
        scratch_shapes=[
            VMEM(((STREAMED + 1) * GRID_X, LANE), jnp.float32),
            VMEM(((STREAMED + 1) * GRID_X, LANE), jnp.float32),
            VMEM((POPS * 8 * TURN, LANE), jnp.float32),
            VMEM((POPS, SPAN_X, SPAN_Y, SPAN_Z), jnp.float32),
            pltpu.SemaphoreType.DMA((SPAN_X // 8, SPAN_Y // 8)),
        ],
        input_output_aliases={2: 1, 3: 2},
        compiler_params=params(16),
        name="finish",
    )(rim_low, rim_high, field, later)
    return out


def solution(mesh):
    in_specs = (
        P(("stream", "cy", "cz"), None, None),
        P(("stream", "cy", "cz"), None),
        P(("stream", "cy", "cz"), None),
    )
    out_specs = P(None, "stream", "cy", "cz")
    return jax.shard_map(shards, mesh=mesh, in_specs=in_specs, out_specs=out_specs, check_vma=False)
```

```python
import functools

import jax
import jax.numpy as jnp
from jax import lax
from jax.experimental import pallas as pl
from jax.experimental.pallas import tpu as pltpu
from jax.sharding import PartitionSpec as P

EDGE = 16
BXD = 2
BYD = 1
BZD = 4
MOVE_CAP = 2

VELOCITIES = (
    (0, 0, 0),
    (1, 0, 0),
    (-1, 0, 0),
    (0, 1, 0),
    (0, -1, 0),
    (0, 0, 1),
    (0, 0, -1),
    (1, 1, 0),
    (-1, -1, 0),
    (1, -1, 0),
    (-1, 1, 0),
    (1, 0, 1),
    (-1, 0, -1),
    (1, 0, -1),
    (-1, 0, 1),
    (0, 1, 1),
    (0, -1, -1),
    (0, 1, -1),
    (0, -1, 1),
)
WEIGHTS = (1.0 / 3.0,) + (1.0 / 18.0,) * 6 + (1.0 / 36.0,) * 12
OPPOSITE = (0, 2, 1, 4, 3, 6, 5, 8, 7, 10, 9, 12, 11, 14, 13, 16, 15, 18, 17)
OMEGA_EVEN = 1.25
OMEGA_ODD = 1.0 / 1.125

POPS = 19
PLANES = 20
LANE = 128
TILES = EDGE**3 // LANE
BLOCK = PLANES * TILES
YLO = LANE // EDGE
SLAB = 4
ODD = TILES + 1
STRIP = 2 * 2 * BZD + 1
GROUPS = ((0, 8), (8, 8), (16, 3))
SENT_SLABS = MOVE_CAP * BLOCK
LAYERS = BXD + 2
ZGROUPS = 3
ZROWS = ZGROUPS * TILES
ZMETA = LAYERS * ZROWS
DIAG = ZROWS + ZGROUPS * SLAB

SPAN_X = BXD * EDGE
SPAN_Y = BYD * EDGE
SPAN_Z = BZD * EDGE
PITCH = SPAN_X + 8
STEP = PITCH // 8
FIRST = 96
FIELD = FIRST + (SPAN_Y + 1) * PITCH + 48
TURN = 9
EXT_X = SPAN_X + 4
EXT_Z = SPAN_Z + 2
RIM_UP = tuple(i for i in range(POPS) if VELOCITIES[i][1] == 1)
RIM_DOWN = tuple(i for i in range(POPS) if VELOCITIES[i][1] == -1)
TOWARD = len(RIM_UP)
SLAB_PLANES = PLANES + TOWARD + 1
STREAMED = POPS - TOWARD
RIM = STREAMED + 1 + TOWARD + 1
KEPT = POPS + TOWARD
AHEAD = tuple(i for i in range(POPS) if VELOCITIES[i][0] == 1)
BACK = tuple(i for i in range(POPS) if VELOCITIES[i][0] == -1)
FACE = 2 * BZD
SENT_META = SENT_SLABS + SLAB_PLANES * FACE
SENT_ROWS = SENT_META + 8
RIM_BLOCKS = -(-RIM * EXT_Z // LANE)
RIM_ROWS = RIM_BLOCKS * EXT_X + 4
GRID_X = 48

ROTOR = -(2.0**100)
OUTSIDE = -(2.0**110)
WALL_BELOW = -(2.0**80)
OUT_BELOW = -(2.0**105)

VMEM = pltpu.VMEM
SMEM = pltpu.SMEM


def lanes():
    return lax.broadcasted_iota(jnp.int32, (8, LANE), 1)


def collide(f):
    even = [None] * POPS
    odd = [None] * POPS
    for i in range(1, POPS, 2):
        even[i] = f[i] + f[i + 1]
        odd[i] = f[i] - f[i + 1]
    density = f[0]
    for i in range(1, POPS, 2):
        density = density + even[i]
    flow = []
    for axis in range(3):
        total = None
        for i in range(1, POPS, 2):
            sign = VELOCITIES[i][axis]
            if sign == 0:
                continue
            if total is None:
                total = odd[i] if sign == 1 else -odd[i]
            else:
                total = total + odd[i] if sign == 1 else total - odd[i]
        flow.append(total)
    inverse = 1.0 / density
    velocity = [part * inverse for part in flow]
    square = velocity[0] * velocity[0] + velocity[1] * velocity[1] + velocity[2] * velocity[2]
    base = density * (1.0 - 1.5 * square)
    post = [None] * POPS
    post[0] = (1.0 - OMEGA_EVEN) * f[0] + (OMEGA_EVEN * WEIGHTS[0]) * base
    shared = {}
    for weight in (WEIGHTS[1], WEIGHTS[7]):
        shared[weight] = ((OMEGA_EVEN * weight) * base, (OMEGA_EVEN * weight * 4.5) * density,
                          (OMEGA_ODD * weight * 3.0) * density)
    for i in range(1, POPS, 2):
        projected = None
        for axis in range(3):
            sign = VELOCITIES[i][axis]
            if sign == 0:
                continue
            if projected is None:
                projected = velocity[axis] if sign == 1 else -velocity[axis]
            else:
                projected = projected + velocity[axis] if sign == 1 else projected - velocity[axis]
        low, curve, slope = shared[WEIGHTS[i]]
        even_part = (0.5 - 0.5 * OMEGA_EVEN) * even[i] + (low + curve * (projected * projected))
        odd_part = (0.5 - 0.5 * OMEGA_ODD) * odd[i] + slope * projected
        post[i] = even_part + odd_part
        post[i + 1] = even_part - odd_part
    return post, density


def pushes(density, drift_y, drift_z):
    along_y = density * drift_y
    along_z = density * drift_z
    out = [None] * POPS
    for i in range(1, POPS):
        _, step_y, step_z = VELOCITIES[i]
        total = None
        for sign, part in ((step_y, along_y), (step_z, along_z)):
            if sign == 0:
                continue
            if total is None:
                total = part if sign == 1 else -part
            else:
                total = total + part if sign == 1 else total - part
        if total is not None:
            out[i] = (6.0 * WEIGHTS[i]) * total
    return out


def total_of(parts):
    parts = list(parts)
    while len(parts) > 1:
        pairs = [parts[n] + parts[n + 1] for n in range(0, len(parts) - 1, 2)]
        parts = pairs + parts[len(parts) - len(parts) % 2 :]
    return parts[0]


def streamed(pull, own, density, drift_y, drift_z, wanted=range(POPS)):
    push = pushes(density, drift_y, drift_z)
    out = {}
    for i in wanted:
        if i == 0:
            out[i] = own[0]
            continue
        pulled = pull(i)
        bounced = own[OPPOSITE[i]]
        blocked = pulled < WALL_BELOW
        if push[i] is not None:
            bounced = jnp.where(pulled < OUT_BELOW, bounced, bounced + push[i])
        out[i] = jnp.where(blocked, bounced, pulled)
    return out


def place():
    return lax.axis_index("stream"), lax.axis_index("cy"), lax.axis_index("cz")


def slot_of(pos, row, layer, column_z):
    slot = (pos[0, row] - (layer * BXD - 1)) * BZD + (pos[2, row] - column_z * BZD)
    return jnp.clip(slot, 0, LAYERS * BZD - 1)


def fill_table(pos, table):
    layer, _, column_z = place()
    for entry in range(LAYERS * BZD):
        table[entry] = -1
    for row in range(pos.shape[1]):

        @pl.when(pos[0, row] >= 0)
        def _(row=row):
            table[slot_of(pos, row, layer, column_z)] = row


def spread_marks(marks, dense):
    rows = marks.shape[0]
    for first in range(0, rows, 8):
        size = min(8, rows - first)
        for begin in range(0, TILES, 8):
            values = [marks[first : first + size, t * LANE : (t + 1) * LANE] for t in range(begin, begin + 8)]
            for k, value in enumerate(values):
                dense[pl.ds(first * ODD + begin + k, size, stride=ODD), :] = value.astype(jnp.float32)


def pack_block(out, base, stage, dense, row, raw):
    for first in range(0, TILES, 4):
        moves = []
        for tile in range(first, first + 4):
            for group, size in GROUPS:
                value = stage[group : group + size, tile * LANE : (tile + 1) * LANE]
                moves.append((pl.ds(group * ODD + tile, size, stride=ODD), value))
        for target, value in moves:
            raw[target, :] = value
    for part in range(TILES // 8):
        old = [raw[pl.ds(i * ODD + 8 * part, 8), :] for i in range(POPS)]
        mark = dense[pl.ds(row * ODD + 8 * part, 8), :]
        post, _ = collide(old)
        for i in range(POPS):
            out[pl.ds(base + i * TILES + 8 * part, 8), :] = jnp.where(mark > 0.5, old[i], post[i])
        out[pl.ds(base + POPS * TILES + 8 * part, 8), :] = mark


def pack_stream(places, marks_in, pops, up, down, pos, table, marks, dense, raw, blocks, slabs, strip, sems):
    mark_copy = pltpu.make_async_copy(marks_in, marks, sems.at[0])
    mark_copy.start()
    place_copy = pltpu.make_async_copy(places, pos, sems.at[1])
    place_copy.start()
    rows = pos.shape[1]
    copies = [None] * 4
    for j in range(MOVE_CAP):
        copies[MOVE_CAP + j] = pltpu.make_async_copy(pops.at[j], blocks.at[MOVE_CAP + j], sems.at[2 + MOVE_CAP + j])
        copies[MOVE_CAP + j].start()
    place_copy.wait()
    count = 0
    for row in range(rows):
        count = count + jnp.where(pos[0, row] >= 0, 1, 0)
    last = jnp.clip(count - MOVE_CAP, 0, rows - MOVE_CAP)
    for j in range(MOVE_CAP):
        copies[j] = pltpu.make_async_copy(pops.at[last + j], blocks.at[j], sems.at[2 + j])
        copies[j].start()
    fill_table(pos, table)
    slab_rows = []
    slab_copies = []
    for side in range(2):
        for bz in range(BZD):
            row = jnp.maximum(table[(2 - side) * BZD + bz], 0)
            n = side * BZD + bz
            first = (TILES - SLAB) * LANE if side == 0 else 0
            slab_rows.append(row)
            slab_copies.append(
                pltpu.make_async_copy(
                    pops.at[row, :, pl.ds(first, SLAB * LANE)], slabs.at[n], sems.at[2 + 2 * MOVE_CAP + n]
                )
            )
            slab_copies[n].start()
    mark_copy.wait()
    spread_marks(marks, dense)
    for side, out in ((1, down), (0, up)):
        for j in range(MOVE_CAP):
            row = j if side == 1 else last + j
            for k, axis in ((0, 0), (1, 2)):
                value = jnp.full((1, LANE), pos[axis, row], jnp.int32).astype(jnp.float32)
                out[pl.ds(SENT_META + 2 * j + k, 1), :] = value
            n = side * MOVE_CAP + j
            copies[n].wait()
            pack_block(out, j * BLOCK, blocks.at[n], dense, row, raw)
    for side, out in enumerate((up, down)):
        for bz in range(BZD):
            n = side * BZD + bz
            first = slab_rows[n] * ODD + (TILES - SLAB if side == 0 else 0)
            slab_copies[n].wait()
            moves = []
            for x in range(2):
                for yhi in range(2):
                    q = 2 * x + yhi
                    row = x * FACE + 2 * bz + yhi
                    for group, size in GROUPS:
                        value = slabs[n, group : group + size, q * LANE : (q + 1) * LANE]
                        moves.append((pl.ds(group * STRIP + row, size, stride=STRIP), value))
                row = POPS * STRIP + x * FACE + 2 * bz
                moves.append((pl.ds(row, 2), dense[pl.ds(first + 2 * x, 2), :]))
            for target, value in moves:
                strip[target, :] = value
        inner = 1 if side == 0 else 0
        for x in range(2):
            old = [strip[pl.ds(i * STRIP + x * FACE, FACE), :] for i in range(POPS)]
            mark = strip[pl.ds(POPS * STRIP + x * FACE, FACE), :] > 0.5
            post, _ = collide(old)
            if x == inner:
                pairs = [(i, i) for i in range(POPS)]
                marks_at = POPS
            else:
                pairs = [(PLANES + n, i) for n, i in enumerate(AHEAD if side == 0 else BACK)]
                marks_at = SLAB_PLANES - 1
            for plane, i in pairs:
                out[pl.ds(SENT_SLABS + plane * FACE, FACE), :] = jnp.where(mark, old[i], post[i])
            marks_of = strip[pl.ds(POPS * STRIP + x * FACE, FACE), :]
            out[pl.ds(SENT_SLABS + marks_at * FACE, FACE), :] = marks_of


def pack_edge(places, marks_in, pops, own, zpack, zup, zdown, pos, table, marks, dense, raw, stage, sems):
    column_z = lax.axis_index("cz")
    mark_copy = pltpu.make_async_copy(marks_in, marks, sems.at[LAYERS])
    mark_copy.start()
    place_copy = pltpu.make_async_copy(places, pos, sems.at[LAYERS + 1])
    place_copy.start()
    place_copy.wait()
    fill_table(pos, table)
    edge_bz = jnp.where(column_z == 0, BZD - 1, 0)
    first_c = jnp.where(column_z == 0, EDGE - 2, 0)
    found = [table[held * BZD + edge_bz] for held in range(LAYERS)]
    row_of = [jnp.maximum(row, 0) for row in found]
    copies = []
    for held in range(LAYERS):
        copies.append(pltpu.make_async_copy(pops.at[row_of[held]], stage.at[held], sems.at[held]))
        copies[held].start()
    mark_copy.wait()
    spread_marks(marks, dense)
    spot = (lanes() & (EDGE - 1)) >> 1
    sublane = lax.broadcasted_iota(jnp.int32, (8, LANE), 0)
    flags = jnp.zeros((8, LANE), jnp.int32)
    for held in range(LAYERS):
        copies[held].wait()
        base = pl.multiple_of((held * BZD + edge_bz) * BLOCK, 8)

        @pl.when(found[held] >= 0)
        def _(held=held, base=base):
            pack_block(own, base, stage.at[held], dense, row_of[held], raw)
            totals = []
            for group in range(ZGROUPS):
                for part in range(TILES // 8):
                    total = jnp.zeros((8, LANE), jnp.float32)
                    for k in range(min(8, PLANES - group * 8)):
                        value = own[pl.ds(base + (group * 8 + k) * TILES + part * 8, 8), :]
                        value = pltpu.roll(value, (2 * k - first_c + LANE) & (LANE - 1), 1)
                        total = jnp.where(spot == k, value, total)
                    totals.append((held * ZROWS + group * TILES + part * 8, total))
            for row, total in totals:
                zpack[pl.ds(row, 8), :] = total

        flags = jnp.where((sublane == held) & (found[held] >= 0), 1, flags)
    zpack[pl.ds(ZMETA, 8), :] = flags.astype(jnp.float32)
    zup[pl.ds(0, ZROWS), :] = zpack[pl.ds(3 * ZROWS, ZROWS), :]
    zdown[pl.ds(0, ZROWS), :] = zpack[pl.ds(0, ZROWS), :]
    for group in range(ZGROUPS):
        target = pl.ds(ZROWS + group * SLAB, SLAB)
        zup[target, :] = zpack[pl.ds(2 * ZROWS + group * TILES + TILES - SLAB, SLAB), :]
        zdown[target, :] = zpack[pl.ds(ZROWS + group * TILES, SLAB), :]


def pack_own(places, marks_in, pops, own_in, own, edge, flags, pos, table, marks, dense, raw, stage, sems):
    del own_in
    layer, _, column_z = place()
    edge_bz = jnp.where(column_z == 0, BZD - 1, 0)
    rows = pos.shape[1]
    mark_copy = pltpu.make_async_copy(marks_in, marks, sems.at[rows])
    mark_copy.start()
    place_copy = pltpu.make_async_copy(places, pos, sems.at[rows + 1])
    place_copy.start()
    copies = [pltpu.make_async_copy(pops.at[r], stage.at[r], sems.at[r]) for r in range(rows)]
    for copy in copies:
        copy.start()
    mark_copy.wait()
    spread_marks(marks, dense)
    place_copy.wait()

    def settle(row, carry):
        pltpu.make_async_copy(pops.at[row], stage.at[row], sems.at[row]).wait()
        slot = slot_of(pos, row, layer, column_z)

        @pl.when((pos[0, row] >= 0) & (slot % BZD != edge_bz))
        def _():
            pack_block(own, pl.multiple_of(slot * BLOCK, 8), stage.at[row], dense, row, raw)

        return carry

    lax.fori_loop(0, rows, settle, 0)
    fill_table(pos, table)
    line = lax.broadcasted_iota(jnp.int32, (FACE, LANE), 0) >> 1
    for side in range(2):
        here = jnp.zeros((FACE, LANE), jnp.int32)
        for bz in range(BZD):
            goal = (0 if side == 0 else LAYERS - 1) * BZD + bz
            present = table[goal] >= 0
            here = jnp.where((line == bz) & present, 1, here)

            @pl.when(present)
            def _(side=side, goal=goal, bz=bz):
                first = goal * BLOCK + (TILES - SLAB if side == 0 else 0)
                values = []
                for _, i, x in slab_planes(side):
                    shift = 2 * (x if side == 0 else x - 2)
                    values.append(own[pl.ds(first + i * TILES + shift, 2), :])
                for (_, i, x), value in zip(slab_planes(side), values):
                    edge[pl.ds((i * 4 + x) * FACE + 2 * bz, 2), :] = value

        flags[pl.ds(side * FACE, FACE), :] = here.astype(jnp.float32)


def slab_planes(side):
    inner, outer = (1, 0) if side == 0 else (2, 3)
    pairs = [(i, i, inner) for i in range(PLANES)]
    return pairs + [(PLANES + n, i, outer) for n, i in enumerate((AHEAD if side == 0 else BACK) + (POPS,))]


class Lanes:
    def __init__(self, column_z):
        lane = lanes()
        self.from_bz = [lane >= bz * EDGE for bz in range(BZD)]
        self.main = lane < SPAN_Z
        self.goal = jnp.where(column_z == 0, SPAN_Z, LANE - 2)

    def to_halo(self, ylo, spot):
        return (self.goal - (ylo * EDGE + 2 * spot) + LANE) & (LANE - 1)


def gathered(parts, zvalue, spot, ylo, masks):
    rows = parts[0].shape[0]
    total = None
    for bz in range(BZD):
        shift = (bz * EDGE - ylo * EDGE) % LANE
        value = pltpu.roll(parts[bz], shift, 1) if shift else parts[bz]
        total = value if total is None else jnp.where(masks.from_bz[bz][:rows], value, total)
    beyond = pltpu.roll(zvalue, masks.to_halo(ylo, spot), 1)
    return jnp.where(masks.main[:rows], total, beyond)


def inside_lanes(rows, column_z):
    lane = lanes()[:rows]
    low = (column_z == 0) & (lane >= SPAN_Z) & (lane < SPAN_Z + 2)
    high = (column_z != 0) & (lane >= LANE - 2)
    return (lane < SPAN_Z) | low | high


def walled(values, mark, inside):
    factor = jnp.where(mark > 0.5, ROTOR, 1.0)
    cap = jnp.where(inside, -OUTSIDE, OUTSIDE)
    return [jnp.minimum(value * factor, cap) for value in values]


def plane_parts(own, edge, zall, zedge, chunk, yhi, plane):
    group = plane >> 3
    if chunk is None:
        first = plane * 4 * FACE + yhi
        parts = [edge[pl.ds(first + 2 * bz, 4, stride=FACE), :] for bz in range(BZD)]
        return parts, zedge[pl.ds(group * 8 + yhi, 4, stride=2), :]
    held, half = 1 + (chunk >> 1), chunk & 1
    first = held * (BZD * BLOCK) + half * EDGE + yhi
    parts = [own[pl.ds(first + bz * BLOCK + plane * TILES, 8, stride=2), :] for bz in range(BZD)]
    first = held * ZROWS + half * EDGE + yhi
    return parts, zall[pl.ds(first + group * TILES, 8, stride=2), :]


def chunk_values(own, edge, zall, zedge, chunk, yhi, rows, masks):
    out = [[] for _ in rows]
    for plane in range(PLANES):
        taken = [n for n, (_, planes) in enumerate(rows) if plane in planes]
        if taken:
            parts, zvalue = plane_parts(own, edge, zall, zedge, chunk, yhi, plane)
        for n in taken:
            out[n].append(gathered(parts, zvalue, plane % 8, rows[n][0], masks))
    return out


def halo_x_inside(layer, layers):
    row = lax.broadcasted_iota(jnp.int32, (4, LANE), 0)
    low = (row < 2) & (layer > 0)
    high = (row >= 2) & (layer < layers - 1)
    return low | high


def settle_rim(layers, columns, depth, up, down, zin, zup, zdown, edge_own, flags, own_in, own, edge, zall, zedge, rim_up, rim_down, post_up, post_down):
    del own_in
    layer, column_y, column_z = place()
    codes = []
    for arrived in (up, down):
        first = layer == 0 if arrived is up else layer == layers - 1
        for j in range(MOVE_CAP):
            bx = arrived[pl.ds(SENT_META + 2 * j, 1), :].astype(jnp.int32)
            bz = arrived[pl.ds(SENT_META + 2 * j + 1, 1), :].astype(jnp.int32)
            code = (bx - layer * BXD) * BZD + (bz - column_z * BZD)
            mine = (bx >= layer * BXD) & (bx < (layer + 1) * BXD) & jnp.logical_not(first)
            codes.append((arrived, j, jnp.max(jnp.where(mine, code, -1))))
    for arrived, j, code in codes:

        @pl.when(code >= 0)
        def _(arrived=arrived, j=j, code=code):
            base = pl.multiple_of((jnp.clip(code, 0, BXD * BZD - 1) + BZD) * BLOCK, 8)
            for k in range(0, BLOCK, 128):
                values = [arrived[pl.ds(j * BLOCK + k + 8 * n, 8), :] for n in range(16)]
                for n, value in enumerate(values):
                    own[pl.ds(base + k + 8 * n, 8), :] = value

    for side, arrived in enumerate((up, down)):
        here = flags[pl.ds(side * FACE, FACE), :] > 0.5
        values = []
        for plane, i, x in slab_planes(side):
            row = (i * 4 + x) * FACE
            other = arrived[pl.ds(SENT_SLABS + plane * FACE, FACE), :]
            values.append((row, jnp.where(here, edge_own[pl.ds(row, FACE), :], other)))
        for row, value in values:
            edge[pl.ds(row, FACE), :] = value
    moves = []
    for held in range(LAYERS):
        flag = zin[pl.ds(ZMETA + held, 1), :] > 0.5
        for group in range(ZGROUPS):
            if held == 1 or held == 2:
                for part in range(TILES // 8):
                    rows = pl.ds(held * ZROWS + group * TILES + part * 8, 8)
                    source = zup if held == 1 else zdown
                    other = source[pl.ds(group * TILES + part * 8, 8), :]
                    moves.append((zall, rows, jnp.where(flag, zin[rows, :], other)))
            else:
                side = 0 if held == 0 else 1
                source = zup if held == 0 else zdown
                first = TILES - SLAB if held == 0 else 0
                mine = zin[pl.ds(held * ZROWS + group * TILES + first, SLAB), :]
                other = source[pl.ds(ZROWS + group * SLAB, SLAB), :]
                moves.append((zedge, pl.ds(group * 8 + side * SLAB, SLAB), jnp.where(flag, mine, other)))
    for target, rows, value in moves:
        target[rows, :] = value
    masks = Lanes(column_z)
    inside_box = inside_lanes(8, column_z)
    inside_halo = inside_lanes(4, column_z) & halo_x_inside(layer, layers)
    sides = ((0, 1, RIM_DOWN, RIM_UP, post_down), (SPAN_Y - 1, SPAN_Y - 2, RIM_UP, RIM_DOWN, post_up))
    for chunk in (0, 1, 2, 3, None):
        inside = inside_halo if chunk is None else inside_box
        for near, far, rim, _, target in sides:
            rows = ((near % YLO, range(PLANES)), (far % YLO, rim + (POPS,)))
            first, second = chunk_values(own, edge, zall, zedge, chunk, near // YLO, rows, masks)
            planes = walled(first[:POPS], first[POPS], inside)
            planes += walled(second[:TOWARD], second[TOWARD], inside)
            sent = [first[i] for i in rim] + [first[POPS]]
            spots = list(range(KEPT)) + [KEPT + STREAMED + 1 + n for n in range(len(sent))]
            for plane, value in zip(spots, planes + sent):
                row = plane * GRID_X
                if chunk is None:
                    target[pl.ds(row, 2), :] = value[:2]
                    target[pl.ds(row + EXT_X - 2, 2), :] = value[2:]
                else:
                    target[pl.ds(row + 2 + 8 * chunk, 8), :] = value
    drift_y, spin, centre_y = drifts_of(columns, depth)
    for near, _, rim, away, target in sides:
        drift_z = spin * ((column_y * SPAN_Y + near).astype(jnp.float32) - centre_y)
        wanted = [i for i in range(POPS) if i not in away]
        plane_of = {i: POPS + rim.index(i) if i in rim else i for i in wanted}
        for chunk in range(5):
            first = 1 + 8 * chunk

            def pull(i):
                step_x, _, step_z = VELOCITIES[i]
                return turned(target[pl.ds(plane_of[i] * GRID_X + first - step_x, 8), :], step_z)

            old = [target[pl.ds(i * GRID_X + first, 8), :] for i in range(POPS)]
            rho = total_of(old)
            values = streamed(pull, old, rho, drift_y, drift_z, wanted)
            size = min(8, EXT_X - 1 - first)
            for n, value in enumerate([values[i] for i in wanted] + [rho]):
                target[pl.ds((KEPT + n) * GRID_X + first, size), :] = value[:size]
    lane = lanes()
    for source, target in ((post_up, rim_up), (post_down, rim_down)):
        for chunk in range(5):
            size = min(8, EXT_X - 8 * chunk)
            values = []
            for plane in range(RIM):
                value = source[pl.ds((KEPT + plane) * GRID_X + 8 * chunk, 8), :]
                values.append(pltpu.roll(value, (plane * EXT_Z + 2 * column_z) & (LANE - 1), 1))
            totals = []
            for block in range(RIM_BLOCKS):
                total = jnp.zeros((8, LANE), jnp.float32)
                for plane in range(RIM):
                    begin = plane * EXT_Z - block * LANE
                    if begin >= LANE or begin + EXT_Z <= 0:
                        continue
                    total = jnp.where((lane >= begin) & (lane < begin + EXT_Z), values[plane], total)
                totals.append(total)
            for block in range(RIM_BLOCKS):
                target[pl.ds(block * EXT_X + 8 * chunk, size), :] = totals[block][:size]


def turned(value, step_z):
    return pltpu.roll(value, step_z % LANE, 1) if step_z else value


def drifts_of(columns, depth):
    _, _, column_z = place()
    lane = lanes()
    total_y = SPAN_Y * columns
    total_z = SPAN_Z * depth
    spin = 0.2 / (total_y + total_z)
    here_z = jnp.where(lane < SPAN_Z + 8, lane, lane - LANE) + column_z * SPAN_Z
    drift_y = -spin * (here_z.astype(jnp.float32) - (total_z - 1) / 2.0)
    return drift_y, spin, (total_y - 1) / 2.0


def first_step(columns, depth, field, later, begin, end, last):
    _, column_y, _ = place()
    drift_y, spin, centre_y = drifts_of(columns, depth)
    sublane = lax.broadcasted_iota(jnp.int32, (8, LANE), 0)

    def tile(base, drift_z):
        old = [field[pl.ds(i * FIELD + base, 8), :] for i in range(POPS)]
        values = streamed(pull_from(field, base), old, total_of(old), drift_y, drift_z)
        post, _ = collide(values)
        wall = old[0] < WALL_BELOW
        for i in range(POPS):
            later[pl.ds(i * FIELD + base, 8), :] = jnp.where(wall, old[i], post[i])

    def drift_at(y):
        return spin * ((y + column_y * SPAN_Y).astype(jnp.float32) - centre_y)

    def between(y):
        return jnp.where(sublane < 6, drift_at(y - 1), drift_at(y))

    def row(line, carry):
        y = line - 2
        base = pl.multiple_of(line * PITCH + (FIRST - 2 * PITCH), 8)
        tile(base - 8, between(y))
        for xc in range(STEP - 1):
            tile(base + 8 * xc, drift_at(y))
        return carry

    lax.fori_loop(begin + 2, end + 2, row, 0)
    if last:
        tile(FIRST + end * PITCH - 8, between(jnp.int32(end)))


def pull_from(field, base):
    def pull(i):
        step_x, step_y, step_z = VELOCITIES[i]
        return turned(field[pl.ds(i * FIELD + base - step_y * PITCH - step_x, 8), :], step_z)

    return pull


def settle_all(layers, columns, depth, own, edge, zall, zedge, field, later, half, turn):
    layer, _, column_z = place()
    masks = Lanes(column_z)
    lane = lanes()
    single = (lane & EDGE) != 0
    double = (lane & (2 * EDGE)) != 0
    inside_box = inside_lanes(8, column_z)
    inside_halo = inside_lanes(4, column_z) & halo_x_inside(layer, layers)

    def relay(chunk, yhi, inside, leave):
        for plane in range(PLANES):
            parts, zvalue = plane_parts(own, edge, zall, zedge, chunk, yhi, plane)
            size = zvalue.shape[0]
            for n in range(0, BZD, 2):
                even = jnp.where(single[:size], pltpu.roll(parts[n + 1], EDGE, 1), parts[n])
                odd = jnp.where(single[:size], parts[n + 1], pltpu.roll(parts[n], LANE - EDGE, 1))
                half[pl.ds((plane * 4 + n) * 8, size), :] = even
                half[pl.ds((plane * 4 + n + 1) * 8, size), :] = odd
        main = masks.main[:size]
        for plane in range(PLANES):
            _, zvalue = plane_parts(own, edge, zall, zedge, chunk, yhi, plane)
            for r in range(4):
                low = half[pl.ds((plane * 4 + r % 2) * 8, size), :]
                high = half[pl.ds((plane * 4 + 2 + r % 2) * 8, size), :]
                if r < 2:
                    both = jnp.where(double[:size], pltpu.roll(high, 2 * EDGE, 1), low)
                else:
                    both = jnp.where(double[:size], high, pltpu.roll(low, LANE - 2 * EDGE, 1))
                beyond = pltpu.roll(zvalue, masks.to_halo(r, plane % 8), 1)
                turn[pl.ds((plane * YLO + r) * 8, size), :] = jnp.where(main, both, beyond)
                turn[pl.ds((plane * YLO + r + 4) * 8, size), :] = jnp.where(main, beyond, both)
        for ylo in range(YLO):
            values = [turn[pl.ds((plane * YLO + ylo) * 8, size), :] for plane in range(PLANES)]
            if ylo >= 4:
                values = [pltpu.roll(value, SPAN_Z, 1) for value in values]
            leave(ylo, walled(values[:POPS], values[POPS], inside))

    def halves(yhi, carry):
        def chunks(chunk, carry):
            def leave(ylo, values):
                row = pl.multiple_of(FIRST + (YLO * yhi + ylo) * PITCH + 8 * chunk, 8)
                for i in range(POPS):
                    field[pl.ds(i * FIELD + row, 8), :] = values[i]

            relay(chunk, yhi, inside_box, leave)
            return carry

        lax.fori_loop(0, SPAN_X // 8, chunks, 0)

        def leave(ylo, values):
            row = FIRST + (YLO * yhi + ylo) * PITCH
            for i in range(POPS):
                field[pl.ds(i * FIELD + row - 2, 2), :] = values[i][:2]
                field[pl.ds(i * FIELD + row + SPAN_X, 2), :] = values[i][2:]

        relay(None, yhi, inside_halo, leave)
        return carry

    lax.fori_loop(0, SPAN_Y // YLO, halves, 0)
    first_step(columns, depth, field, later, 1, SPAN_Y - 1, False)


def finish(layers, columns, depth, rim_low, rim_high, field_in, later_in, out, field, later, low, high, turn, result, sems):
    del field_in, later_in
    layer, column_y, column_z = place()
    flat = (lanes() + 2 * column_z) & (LANE - 1)
    sides = (
        (rim_low, low, -1, RIM_UP, RIM_DOWN, column_y > 0),
        (rim_high, high, SPAN_Y, RIM_DOWN, RIM_UP, column_y < columns - 1),
    )
    sublane = lax.broadcasted_iota(jnp.int32, (8, LANE), 0)
    for source, ready, y, rim, _, there in sides:
        for chunk in range(5):
            size = min(8, EXT_X - 8 * chunk)
            blocks = [source[pl.ds(block * EXT_X + 8 * chunk, 8), :] for block in range(RIM_BLOCKS)]
            values = []
            for plane in range(RIM):
                block, begin = divmod(plane * EXT_Z, LANE)
                shift = (2 * LANE - begin - 2 * column_z) & (LANE - 1)
                value = pltpu.roll(blocks[block], shift, 1)
                if begin + EXT_Z > LANE:
                    value = jnp.where(flat < LANE - begin, value, pltpu.roll(blocks[block + 1], shift, 1))
                values.append(value)
            inside = (flat < EXT_Z) & there
            if chunk == 0:
                inside = inside & ((sublane >= 2) | (layer > 0))
            if chunk == 4:
                inside = inside & ((sublane < 2) | (layer < layers - 1))
            for n in range(STREAMED + 1):
                ready[pl.ds(n * GRID_X + 8 * chunk, 8), :] = values[n]
            for i, value in zip(rim, walled(values[STREAMED + 1 : RIM - 1], values[RIM - 1], inside)):
                field[pl.ds(i * FIELD + FIRST + y * PITCH - 2 + 8 * chunk, size), :] = value[:size]

    first_step(columns, depth, field, later, 0, 1, True)
    first_step(columns, depth, field, later, SPAN_Y - 1, SPAN_Y, True)
    drift_y, spin, centre_y = drifts_of(columns, depth)
    for _, ready, y, rim, away, _ in sides:
        drift_z = spin * ((column_y * SPAN_Y + y).astype(jnp.float32) - centre_y)
        for chunk in range(5):
            first = 1 + 8 * chunk
            base = FIRST + y * PITCH - 2 + first
            old = {i: field[pl.ds(i * FIELD + base, 8), :] for i in rim}
            rho = ready[pl.ds(STREAMED * GRID_X + first, 8), :]
            values = streamed(pull_from(field, base), old, rho, drift_y, drift_z, away)
            for n, i in enumerate([i for i in range(POPS) if i not in away]):
                values[i] = ready[pl.ds(n * GRID_X + first, 8), :]
            post, _ = collide(values)
            wall = old[rim[0]] < WALL_BELOW
            size = min(8, EXT_X - 1 - first)
            for i in rim:
                later[pl.ds(i * FIELD + base, size), :] = jnp.where(wall, old[i], post[i])[:size]

    drift_y, spin, centre_y = drifts_of(columns, depth)

    def leave(chunk, half):
        part = (slice(None), pl.ds(chunk * 8, 8), pl.ds(half * 8, 8))
        return pltpu.make_async_copy(result.at[part], out.at[part], sems.at[chunk, half])

    def second_step(chunk, carry):
        def tile(half, k):
            y = 8 * half + k
            base = pl.multiple_of(FIRST + y * PITCH + 8 * chunk, 8)
            drift_z = spin * ((column_y * SPAN_Y + y).astype(jnp.float32) - centre_y)
            old = [later[pl.ds(i * FIELD + base, 8), :] for i in range(POPS)]
            values = streamed(pull_from(later, base), old, total_of(old), drift_y, drift_z)
            wall = old[0] < WALL_BELOW
            for i in range(POPS):
                value = jnp.where(wall, old[i] * (1.0 / ROTOR), values[i])
                turn[pl.ds(((half * POPS + i) * 8 + k) * TURN, 8), :] = value

        def place_row(half, k):
            values = [turn[pl.ds((half * POPS + i) * 8 * TURN + k, 8, stride=TURN), :] for i in range(POPS)]
            for i in range(POPS):
                result[i, 8 * chunk + k, 8 * half : 8 * half + 8, :] = values[i][:, :SPAN_Z]

        halves = SPAN_Y // 8
        for half in range(halves + 1):
            for k in range(8):
                if half < halves:
                    tile(half, k)
                if half > 0:
                    place_row(half - 1, k)
            if half > 0:
                leave(chunk, half - 1).start()
        return carry

    lax.fori_loop(0, SPAN_X // 8, second_step, 0)
    for chunk in range(SPAN_X // 8):
        for half in range(SPAN_Y // 8):
            leave(chunk, half).wait()


def rows_of(count):
    return jax.ShapeDtypeStruct((count, LANE), jnp.float32)


def kept(count):
    return VMEM((count, LANE), jnp.float32)


def params(mib):
    return pltpu.CompilerParams(vmem_limit_bytes=mib * 2**20)


def shards(populations, solid_cells, block_pos):
    layers = lax.axis_size("stream")
    columns = lax.axis_size("cy")
    depth = lax.axis_size("cz")
    rows = block_pos.shape[0]
    vmem = pl.BlockSpec(memory_space=VMEM)
    hbm = pl.BlockSpec(memory_space=pltpu.HBM)
    populations = pltpu.with_memory_space_constraint(populations, pltpu.HBM)
    solid_cells = pltpu.with_memory_space_constraint(solid_cells, pltpu.HBM)
    places = pltpu.with_memory_space_constraint(block_pos.T, pltpu.HBM)
    place_scratch = SMEM((3, rows), jnp.int32)
    table_scratch = SMEM((LAYERS * BZD,), jnp.int32)
    mark_scratch = [
        VMEM((rows, EDGE**3), jnp.int32),
        VMEM((rows * ODD, LANE), jnp.float32),
        VMEM((POPS * ODD, LANE), jnp.float32),
    ]

    up = [(i, i + 1) for i in range(layers - 1)]
    down = [(i + 1, i) for i in range(layers - 1)]
    send_up, send_down = pl.pallas_call(
        pack_stream,
        out_shape=(kept(SENT_ROWS), kept(SENT_ROWS)),
        in_specs=[hbm, hbm, hbm],
        out_specs=(vmem, vmem),
        scratch_shapes=[place_scratch, table_scratch]
        + mark_scratch
        + [
            VMEM((2 * MOVE_CAP, POPS, EDGE**3), jnp.float32),
            VMEM((2 * BZD, POPS, SLAB * LANE), jnp.float32),
            VMEM((PLANES * STRIP, LANE), jnp.float32),
            pltpu.SemaphoreType.DMA((2 + 2 * MOVE_CAP + 2 * BZD,)),
        ],
        compiler_params=params(16),
        name="pack_stream",
    )(places, solid_cells, populations)
    from_low = lax.ppermute(send_up, "stream", up)
    from_high = lax.ppermute(send_down, "stream", down)

    own, zpack, zsend_up, zsend_down = pl.pallas_call(
        pack_edge,
        out_shape=(kept(LAYERS * BZD * BLOCK), kept(ZMETA + 8), kept(DIAG), kept(DIAG)),
        in_specs=[hbm, hbm, hbm],
        out_specs=(vmem,) * 4,
        scratch_shapes=[place_scratch, table_scratch]
        + mark_scratch
        + [
            VMEM((LAYERS, POPS, EDGE**3), jnp.float32),
            pltpu.SemaphoreType.DMA((LAYERS + 2,)),
        ],
        compiler_params=params(16),
        name="pack_edge",
    )(places, solid_cells, populations)
    swap = [(i, depth - 1 - i) for i in range(depth)]
    zin = lax.ppermute(zpack, "cz", swap)
    zup_pairs = [(s * depth + c, t * depth + d) for s, t in up for c, d in swap]
    zdown_pairs = [(s * depth + c, t * depth + d) for s, t in down for c, d in swap]
    z_low = lax.ppermute(zsend_up, ("stream", "cz"), zup_pairs)
    z_high = lax.ppermute(zsend_down, ("stream", "cz"), zdown_pairs)

    own, edge_own, flags = pl.pallas_call(
        pack_own,
        out_shape=(kept(LAYERS * BZD * BLOCK), kept(PLANES * 4 * FACE), kept(2 * FACE)),
        in_specs=[hbm, hbm, hbm, vmem],
        out_specs=(vmem,) * 3,
        scratch_shapes=[place_scratch, table_scratch]
        + mark_scratch
        + [
            VMEM((rows, POPS, EDGE**3), jnp.float32),
            pltpu.SemaphoreType.DMA((rows + 2,)),
        ],
        input_output_aliases={3: 0},
        compiler_params=params(16),
        name="pack_own",
    )(places, solid_cells, populations, own)

    own, edge, zall, zedge, rim_up, rim_down = pl.pallas_call(
        functools.partial(settle_rim, layers, columns, depth),
        out_shape=(
            kept(LAYERS * BZD * BLOCK),
            kept(PLANES * 4 * FACE),
            kept(LAYERS * ZROWS),
            kept(ZGROUPS * 8),
            kept(RIM_ROWS),
            kept(RIM_ROWS),
        ),
        in_specs=[vmem] * 8,
        out_specs=(vmem,) * 6,
        scratch_shapes=[
            VMEM(((KEPT + RIM) * GRID_X, LANE), jnp.float32),
            VMEM(((KEPT + RIM) * GRID_X, LANE), jnp.float32),
        ],
        input_output_aliases={7: 0},
        compiler_params=params(16),
        name="settle_rim",
    )(from_low, from_high, zin, z_low, z_high, edge_own, flags, own)
    cy_up = [(i, i + 1) for i in range(columns - 1)]
    cy_down = [(i + 1, i) for i in range(columns - 1)]
    rim_low = lax.ppermute(rim_up, "cy", cy_up)
    rim_high = lax.ppermute(rim_down, "cy", cy_down)

    field, later = pl.pallas_call(
        functools.partial(settle_all, layers, columns, depth),
        out_shape=(kept(POPS * FIELD), kept(POPS * FIELD)),
        in_specs=[vmem] * 4,
        out_specs=(vmem,) * 2,
        scratch_shapes=[
            VMEM((PLANES * 4 * 8, LANE), jnp.float32),
            VMEM((PLANES * YLO * 8, LANE), jnp.float32),
        ],
        compiler_params=params(16),
        name="settle_all",
    )(own, edge, zall, zedge)

    out, _, _ = pl.pallas_call(
        functools.partial(finish, layers, columns, depth),
        out_shape=(
            jax.ShapeDtypeStruct((POPS, SPAN_X, SPAN_Y, SPAN_Z), jnp.float32),
            kept(POPS * FIELD),
            kept(POPS * FIELD),
        ),
        in_specs=[vmem] * 4,
        out_specs=(hbm, vmem, vmem),
        scratch_shapes=[
            VMEM(((STREAMED + 1) * GRID_X, LANE), jnp.float32),
            VMEM(((STREAMED + 1) * GRID_X, LANE), jnp.float32),
            VMEM((SPAN_Y // 8 * POPS * 8 * TURN, LANE), jnp.float32),
            VMEM((POPS, SPAN_X, SPAN_Y, SPAN_Z), jnp.float32),
            pltpu.SemaphoreType.DMA((SPAN_X // 8, SPAN_Y // 8)),
        ],
        input_output_aliases={2: 1, 3: 2},
        compiler_params=params(16),
        name="finish",
    )(rim_low, rim_high, field, later)
    return out


def solution(mesh):
    in_specs = (
        P(("stream", "cy", "cz"), None, None),
        P(("stream", "cy", "cz"), None),
        P(("stream", "cy", "cz"), None),
    )
    out_specs = P(None, "stream", "cy", "cz")
    return jax.shard_map(shards, mesh=mesh, in_specs=in_specs, out_specs=out_specs, check_vma=False)
```
